32 devices in a mesh: dp: 16 (over z, y, core), fsdp: 2 (over x).
Axes of the slice: x: 2, y: 2, z: 4, core: 2. Of those that a mesh axis runs over, the one named last changes fastest.
Arguments:
- tokens: bfloat16 [32, 512, 1024], P(('dp', 'fsdp')), may hold values from -6 to 6
- lengths: int32 [32], P(('dp', 'fsdp')), may hold values from 76 to 512, as said below
- local_project: bfloat16 [1024, 4096], P('dp', 'fsdp'), may hold values from -0.1875 to 0.1875
- local_output: bfloat16 [1024, 1024], P('dp', 'fsdp'), may hold values from -0.1875 to 0.1875
- local_expand: bfloat16 [1024, 5632], P('dp', 'fsdp'), may hold values from -0.1875 to 0.1875
- local_shrink: bfloat16 [2816, 1024], P('dp', 'fsdp'), may hold values from -0.109375 to 0.109375
- linear_project: bfloat16 [1024, 4096], P('dp', 'fsdp'), may hold values from -0.1875 to 0.1875
- linear_output: bfloat16 [1024, 1024], P('dp', 'fsdp'), may hold values from -0.1875 to 0.1875
- linear_expand: bfloat16 [1024, 5632], P('dp', 'fsdp'), may hold values from -0.1875 to 0.1875
- linear_shrink: bfloat16 [2816, 1024], P('dp', 'fsdp'), may hold values from -0.109375 to 0.109375
- cotangent: bfloat16 [32, 512, 1024], P(('dp', 'fsdp')), may hold values from -6 to 6
Outputs:
- mixed_out: bfloat16 [32, 512, 1024], P(('dp', 'fsdp'))
- tokens_gradient: float32 [32, 512, 1024], P(('dp', 'fsdp'))
- local_project_gradient: float32 [1024, 4096], P('dp', 'fsdp')
- local_output_gradient: float32 [1024, 1024], P('dp', 'fsdp')
- local_expand_gradient: float32 [1024, 5632], P('dp', 'fsdp')
- local_shrink_gradient: float32 [2816, 1024], P('dp', 'fsdp')
- linear_project_gradient: float32 [1024, 4096], P('dp', 'fsdp')
- linear_output_gradient: float32 [1024, 1024], P('dp', 'fsdp')
- linear_expand_gradient: float32 [1024, 5632], P('dp', 'fsdp')
- linear_shrink_gradient: float32 [2816, 1024], P('dp', 'fsdp')
The draws below stay inside these ranges and needn't reach their ends.
Inputs may be any that keep to these rules, and one draw needn't show every extreme that they name: `lengths`: number of real tokens of each sequence; slots from there to 512 are padding; some sequence fills all 512 slots.
All inputs are finite; a program needn't handle non-finite values.
Results may differ from the reference program's by a relative error of at most 0.023.
Values may be sent and summed in bfloat16 or wider, within the bound.
A program may use at most 320 MiB of HBM per device.

```python
import math
import jax
import jax.numpy as jnp
from jax import lax

D = 1024
HEADS = 16
HEAD = 64
FF = 2816
BLOCK = 64
SEQ = 512
SEQS = 32


def draw_lengths(key, part):
    key = jax.random.fold_in(key, 7)
    first_key, second_key = jax.random.split(key)
    drawn = jax.random.randint(first_key, (SEQS,), SEQ * 3 // 20, SEQ + 1, dtype=jnp.int32)
    chosen = jax.random.randint(second_key, (), 0, SEQS, dtype=jnp.int32)
    return jnp.where(jnp.arange(SEQS, dtype=jnp.int32) == chosen, SEQ, drawn).astype(jnp.int32)


def spiked(values, rng, source, target, parts, factor):
    def block_of(position):
        return (jnp.arange(values.shape[position]) // (values.shape[position] // parts)).reshape((-1,) + (1,) * (values.ndim - 1 - position))

    near = jax.random.permutation(rng, parts)[block_of(target)]
    far = (block_of(target) + parts // 2) % parts
    return jnp.where((block_of(source) == near) | (block_of(source) == far), factor * values, values)


def block_scale(key, extent, cuts, low, high):
    def one(dim, shards_of):
        draws = jax.random.uniform(jax.random.fold_in(jax.random.fold_in(key, 6), dim), (shards_of,), jnp.float32, low / len(cuts), high / len(cuts))
        return jnp.repeat(jnp.exp(draws), extent[dim] // shards_of).reshape((-1,) + (1,) * (len(extent) - dim - 1))

    factor_of = one(*cuts[0])
    for cut in cuts[1:]:
        factor_of = factor_of * one(*cut)
    return factor_of


def noise(key, extent, deviation, most, shards=(), kind=jnp.bfloat16):
    entries = jax.random.normal(key, extent, jnp.float32) * deviation
    if len(shards) > 0:
        entries = block_scale(key, extent, shards, -0.22, 0.18) * entries
    return jnp.clip(entries, min=-most, max=most).astype(kind)


def heavy_noise(own_key, shape, spread, bound, cuts, heavy, held_as=jnp.bfloat16):
    result = spread * jax.random.normal(own_key, shape, jnp.float32)
    if cuts:
        result = result * block_scale(own_key, shape, cuts, -0.22, 0.18)
    return jnp.clip(spiked(result, jax.random.fold_in(own_key, 3), *heavy), -bound, bound).astype(held_as)


def setup_inputs(seed: int = 0) -> dict:
    streams_of = jax.random.split(jax.random.key(seed), 12)
    return {
        "tokens": noise(streams_of[0], (SEQS, SEQ, D), 1.0, 6.0, ((0, 32),)),
        "lengths": draw_lengths(jax.random.fold_in(streams_of[11], 71), 0),
        "local_project": noise(streams_of[2], (D, 4 * D), D ** -0.5, 0.1875, ((0, 16), (1, 2))),
        "local_output": noise(streams_of[3], (D, D), D ** -0.5, 0.1875, ((0, 16), (1, 2))),
        "local_expand": noise(streams_of[4], (D, 2 * FF), D ** -0.5, 0.1875, ((0, 16), (1, 2))),
        "local_shrink": noise(streams_of[5], (FF, D), FF ** -0.5, 0.109375, ((0, 16), (1, 2))),
        "linear_project": noise(streams_of[6], (D, 4 * D), D ** -0.5, 0.1875, ((0, 16), (1, 2))),
        "linear_output": noise(streams_of[7], (D, D), D ** -0.5, 0.1875, ((0, 16), (1, 2))),
        "linear_expand": noise(streams_of[8], (D, 2 * FF), D ** -0.5, 0.1875, ((0, 16), (1, 2))),
        "linear_shrink": noise(streams_of[9], (FF, D), FF ** -0.5, 0.109375, ((0, 16), (1, 2))),
        "cotangent": heavy_noise(streams_of[10], (SEQS, SEQ, D), 1.0, 6.0, ((0, 32),), (0, 2, 32, 2.75)),
    }


epsilon = 1e-05
highest = lax.Precision.HIGHEST

@jax.custom_vjp
def low(v):
    return lax.optimization_barrier(v.astype(jnp.bfloat16)).astype(jnp.float32)

@jax.custom_vjp
def low_back(v):
    return v

def low_keep(v):
    return (low(v), None)

def low_pass(kept, grad):
    return (grad,)

def back_keep(v):
    return (v, None)

def back_low(kept, grad):
    return (low(grad),)
low.defvjp(low_keep, low_pass)
low_back.defvjp(back_keep, back_low)

def simple_norm(values):
    return values * lax.rsqrt(lax.optimization_barrier(jnp.mean(values * values, axis=-1, keepdims=True)) + epsilon)

def head_norm(values):
    shaped = values.reshape(values.shape[0], HEADS, HEAD)
    return simple_norm(shaped).reshape(values.shape)

def product(first_matrix, second_matrix):
    return jnp.matmul(first_matrix, second_matrix, precision=highest)

def causal_table():
    places = jnp.arange(BLOCK, dtype=jnp.int32)
    return places[:, None] >= places[None, :]

def local_mix(queries, keys_all, values, validity):
    shape = (SEQ // BLOCK, BLOCK, HEADS, HEAD)
    scores = jnp.einsum('bihd,bjhd->bhij', queries.reshape(shape), keys_all.reshape(shape), precision=highest) * HEAD ** (-0.5)
    scores = jnp.where(causal_table(), low_back(scores), -1e+30)
    attend = low(jax.nn.softmax(scores, axis=-1))
    mixture = jnp.einsum('bhij,bjhd->bihd', attend, values.reshape(shape), precision=highest)
    return mixture.reshape(SEQ, D) * validity[:, None]

def linear_mix(queries, keys_all, values):
    shape = (SEQ // BLOCK, BLOCK, HEADS, HEAD)
    feature_q = low(jax.nn.softplus(queries)).reshape(shape)
    feature_k = low(jax.nn.softplus(keys_all)).reshape(shape)
    value_blocks = values.reshape(shape)
    causal = causal_table().astype(jnp.float32)
    inner_scores = jnp.einsum('bihd,bjhd->bhij', feature_q, feature_k, precision=highest) * causal
    inner_scores = low(low_back(inner_scores))
    states = jnp.einsum('bjhd,bjhe->bhde', feature_k, value_blocks, precision=highest)
    running = jnp.cumsum(states, axis=0)
    prior_states = jnp.concatenate([jnp.zeros_like(states[:1]), running[:-1]], axis=0)
    mixture = jnp.einsum('bhij,bjhe->bihe', inner_scores, value_blocks, precision=highest)
    mixture = mixture + jnp.einsum('bihd,bhde->bihe', feature_q, prior_states, precision=highest)
    return mixture.reshape(SEQ, D)

def attention_layer(layer_in, validity, weights, local):
    project, output, expand, shrink = weights
    normed = low(simple_norm(layer_in))
    projected = low_back(product(normed, project))
    queries, keys_all, values, update = jnp.split(projected, 4, axis=-1)
    if local:
        mixture = local_mix(low(queries), low(keys_all), low(values), validity)
    else:
        mixture = linear_mix(queries, keys_all, low(values))
    mixture = low_back(mixture)
    gated_rows = low(head_norm(mixture) * jax.nn.silu(update))
    middle = layer_in + low_back(product(gated_rows, output))
    second = low(simple_norm(middle))
    expanded = low_back(product(second, expand))
    first_half, second_half = jnp.split(expanded, 2, axis=-1)
    hidden = low(first_half * second_half)
    return middle + low_back(product(hidden, shrink))

def network(layer_in, validity, weights):
    layer_in = layer_in * validity[:, None]
    between = attention_layer(layer_in, validity, weights[:4], True)
    return attention_layer(between, validity, weights[4:], False) * validity[:, None]

def reference(tokens, lengths, local_project, local_output, local_expand, local_shrink, linear_project, linear_output, linear_expand, linear_shrink, cotangent):
    weights = tuple((item.astype(jnp.float32) for item in (local_project, local_output, local_expand, local_shrink, linear_project, linear_output, linear_expand, linear_shrink)))
    group_size = math.gcd(SEQS, max(1, 4096 // SEQ))
    places = jnp.arange(SEQ, dtype=jnp.int32)
    validity = (places[None, :] < lengths.astype(jnp.int32)[:, None]).astype(jnp.float32)
    inputs = tokens.astype(jnp.float32).reshape(SEQS // group_size, group_size, SEQ, D)
    cotangents = cotangent.astype(jnp.float32).reshape(SEQS // group_size, group_size, SEQ, D)
    validity = validity.reshape(SEQS // group_size, group_size, SEQ)

    def accumulate(totals, batch_item):
        rows_in, valid_rows, cotangent_rows = batch_item

        def batched(layer_rows, *params):

            def single(one_row, one_valid):
                return network(one_row, one_valid, params)
            return jax.vmap(single)(layer_rows, valid_rows)
        outputs, pullback = jax.vjp(batched, rows_in, *weights)
        grads = pullback(cotangent_rows)
        totals = tuple((left_sum + right_sum for left_sum, right_sum in zip(totals, grads[1:])))
        return (totals, (outputs.astype(jnp.bfloat16), grads[0]))
    start = tuple((jnp.zeros_like(item) for item in weights))
    totals, (outputs, token_grads) = lax.scan(accumulate, start, (inputs, validity, cotangents))
    return (outputs.reshape(SEQS, SEQ, D), token_grads.reshape(SEQS, SEQ, D), totals[0], totals[1], totals[2], totals[3], totals[4], totals[5], totals[6], totals[7])
```

```python
import functools

import jax
import jax.numpy as jnp
from jax import lax
from jax.experimental import pallas as pl
from jax.experimental.pallas import tpu as pltpu
from jax.sharding import PartitionSpec as P

HEADS = 16
HEAD = 64
BLOCK = 64


epsilon = 1e-05
highest = lax.Precision.HIGHEST


def simple_norm(values):
    return values * lax.rsqrt(jnp.mean(values * values, axis=-1, keepdims=True) + epsilon)


def norm_back(values, upstream):
    inverse_rms = lax.rsqrt(jnp.mean(values * values, axis=-1, keepdims=True) + epsilon)
    return inverse_rms * (
        upstream
        - values * (inverse_rms * inverse_rms) * jnp.mean(upstream * values, axis=-1, keepdims=True)
    )


def head_norm(values):
    shaped = values.reshape(values.shape[0], HEADS, HEAD)
    return simple_norm(shaped).reshape(values.shape)


def head_back(values, upstream):
    shaped = values.reshape(values.shape[0], HEADS, HEAD)
    coming = upstream.reshape(values.shape[0], HEADS, HEAD)
    return norm_back(shaped, coming).reshape(values.shape)


def silu_slope(values):
    logistic = jax.nn.sigmoid(values)
    return logistic * (1.0 + values * (1.0 - logistic))


def contract_rows(first_matrix, second_matrix):
    return lax.dot_general(
        first_matrix, second_matrix, (((0,), (0,)), ((), ())), preferred_element_type=jnp.float32
    )


def contract_cols(first_matrix, second_matrix):
    return lax.dot_general(
        first_matrix, second_matrix, (((1,), (1,)), ((), ())), preferred_element_type=jnp.float32
    )


def causal_table():
    return lax.broadcasted_iota(jnp.int32, (BLOCK, BLOCK), 0) >= lax.broadcasted_iota(
        jnp.int32, (BLOCK, BLOCK), 1
    )


def split_heads(values):
    return values.reshape(values.shape[0] // BLOCK, BLOCK, HEADS, HEAD)


def join_heads(values):
    return values.reshape(values.shape[0] * BLOCK, HEADS * HEAD)


MESH = pl.DeviceIdType.MESH
ANY = pl.BlockSpec(memory_space=pl.ANY)
WEIGHTS = 8
AXIS_NAMES = ("f", "zh", "zl", "y", "c")
AXIS_OF = {"c": "c", "y": "y", "x": "f", "z1": "zl", "z2": "zh"}
GATHER_LAG = 3
GATHER_SLOTS = 8
SCATTER_LAG = 3
SCATTER_SLOTS = 3 * SCATTER_LAG + 1
TERM_SLOTS = SCATTER_LAG + 1
TALL = 64
TALL_WIDTH = 256
OTHER_WIDTH = 128


def neighbours():
    dp = lax.axis_index("dp")
    x = lax.axis_index("fsdp")
    z = dp // 4
    y = (dp // 2) % 2
    c = dp % 2
    places = {"f": x, "zh": z // 2, "zl": z % 2, "y": y, "c": c}
    targets = {
        "z1": ((z + 1 - 2 * (z % 2)) * 4 + y * 2 + c, x),
        "z2": (lax.rem(z + 2, 4) * 4 + y * 2 + c, x),
        "y": (z * 4 + (1 - y) * 2 + c, x),
        "c": (z * 4 + y * 2 + (1 - c), x),
        "x": (dp, 1 - x),
    }
    return places, targets


def greet(targets):
    barrier = pltpu.get_barrier_semaphore()
    for target in targets.values():
        pl.semaphore_signal(barrier, inc=1, device_id=target, device_id_type=MESH)
    return barrier


def late_z(chunk):
    return chunk % 5 == 3


def gather_kernel(chunks, *refs):
    own = refs[:WEIGHTS]
    held = refs[WEIGHTS : 2 * WEIGHTS]
    local_sem, send_sem, recv_sem = refs[2 * WEIGHTS :]
    places, targets = neighbours()
    x, zh, zl, y, c = (places[name] for name in AXIS_NAMES)
    barrier = greet(targets)
    local = [
        pltpu.make_async_copy(own[i], held[i].at[x, zh, zl, y, c], local_sem.at[i])
        for i in range(WEIGHTS)
    ]
    for copy in local:
        copy.start()
    pl.semaphore_wait(barrier, len(targets))

    def messages(phase, chunk):
        weight, start, width = chunks[chunk]
        ref = held[weight]
        half = width // 2
        every = pl.ds(start, width)
        first = pl.ds(start, half)
        second = pl.ds(start + half, half)

        def message(block, target, part):
            slot = chunk % GATHER_SLOTS
            return pltpu.make_async_remote_copy(
                src_ref=block,
                dst_ref=block,
                send_sem=send_sem.at[2 * phase + part, slot],
                recv_sem=recv_sem.at[2 * phase + part, slot],
                device_id=targets[target],
                device_id_type=MESH,
            )

        if phase == 4:
            return [message(ref.at[:, :, :, :, c, :, every], "c", 0)]
        if late_z(chunk):
            if phase == 0:
                return [
                    message(ref.at[x, zh, zl, y, c, :, first], "x", 0),
                    message(ref.at[x, zh, zl, y, c, :, second], "y", 1),
                ]
            if phase == 1:
                return [
                    message(ref.at[:, zh, zl, y, c, :, first], "y", 0),
                    message(ref.at[x, zh, zl, :, c, :, second], "x", 1),
                ]
            if phase == 2:
                return [message(ref.at[:, zh, zl, :, c, :, every], "z2", 0)]
            return [message(ref.at[:, :, zl, :, c, :, every], "z1", 0)]
        if phase == 0:
            return [message(ref.at[x, zh, zl, y, c, :, every], "z2", 0)]
        if phase == 1:
            return [message(ref.at[x, :, zl, y, c, :, every], "z1", 0)]
        if phase == 2:
            return [
                message(ref.at[x, :, :, y, c, :, first], "x", 0),
                message(ref.at[x, :, :, y, c, :, second], "y", 1),
            ]
        return [
            message(ref.at[:, :, :, y, c, :, first], "y", 0),
            message(ref.at[x, :, :, :, c, :, second], "x", 1),
        ]

    phases = 5
    landed = set()
    live = {}
    for step in range(len(chunks) + phases * GATHER_LAG):
        for phase in range(phases, -1, -1):
            chunk = step - phase * GATHER_LAG
            if not 0 <= chunk < len(chunks):
                continue
            if phase >= 1:
                for copy in live.pop((phase - 1, chunk)):
                    copy.wait()
            weight = chunks[chunk][0]
            if phase == 0 and weight not in landed:
                local[weight].wait()
                landed.add(weight)
            if phase < phases:
                live[(phase, chunk)] = messages(phase, chunk)
                for copy in live[(phase, chunk)]:
                    copy.start()


def gather_all(shards_of):
    chunks = [
        (i, start, 256) for i in range(WEIGHTS) for start in range(0, shards_of[i].shape[1], 256)
    ]
    return pl.pallas_call(
        functools.partial(gather_kernel, chunks),
        out_shape=tuple(
            jax.ShapeDtypeStruct((2, 2, 2, 2, 2) + item.shape, item.dtype) for item in shards_of
        ),
        in_specs=[ANY] * WEIGHTS,
        out_specs=(ANY,) * WEIGHTS,
        scratch_shapes=[
            pltpu.SemaphoreType.DMA((WEIGHTS,)),
            pltpu.SemaphoreType.DMA((10, GATHER_SLOTS)),
            pltpu.SemaphoreType.DMA((10, GATHER_SLOTS)),
        ],
        compiler_params=pltpu.CompilerParams(collective_id=0, has_side_effects=True),
    )(*shards_of)


class Scatter:
    def __init__(self, chunks, rows_of, terms, outs, sems, buffers):
        self.chunks = chunks
        self.rows_of = rows_of
        self.terms = terms
        self.outs = outs
        self.load_sem, self.store_sem, self.send_sem, self.recv_sem = sems
        self.buffers = buffers
        self.places, self.targets = neighbours()

    def load(self, chunk):
        weight, start, width = self.chunks[chunk]
        return pltpu.make_async_copy(
            self.terms[weight].at[..., pl.ds(start, width)],
            self.buffers[self.rows_of[weight]][0].at[chunk % TERM_SLOTS],
            self.load_sem.at[chunk % TERM_SLOTS],
        )

    def store(self, chunk):
        weight, start, width = self.chunks[chunk]
        return pltpu.make_async_copy(
            self.result(chunk),
            self.outs[weight].at[:, pl.ds(start, width)],
            self.store_sem.at[chunk % 2],
        )

    def result(self, chunk):
        return self.buffers[self.rows_of[self.chunks[chunk][0]]][6].at[chunk % 2]

    def parts(self, chunk):
        weight, start, width = self.chunks[chunk]
        if self.rows_of[weight] == TALL:
            halves = [(0, width // 2, 0), (width // 2, width // 2, 1)]
        else:
            halves = [(0, width, chunk % 2)]
        out = []
        for begin, extent, turn in halves:
            plane = ("y", "x") if turn == 0 else ("x", "y")
            order = ("z1", "z2") + plane if late_z(chunk) else plane + ("z1", "z2")
            out.append((begin, extent, ("c",) + order))
        return out

    def arrived(self, chunk, phase):
        rows = self.rows_of[self.chunks[chunk][0]]
        return self.buffers[rows][1 + phase].at[chunk % SCATTER_SLOTS]

    def dims_after(self, order, phase):
        used = set(AXIS_OF[target] for target in order[: phase + 1])
        return [name for name in AXIS_NAMES if name not in used]

    def source(self, chunk, phase, order):
        rows = self.rows_of[self.chunks[chunk][0]]
        if phase == 0:
            return self.buffers[rows][0].at[chunk % TERM_SLOTS], list(AXIS_NAMES)
        return self.arrived(chunk, phase - 1), self.dims_after(order, phase - 1)

    def messages(self, phase, chunk):
        parts = self.parts(chunk)
        if len(set(order[: phase + 1] for _, _, order in parts)) == 1:
            parts = [(0, self.chunks[chunk][2], parts[0][2])]
        out = []
        for part, (begin, extent, order) in enumerate(parts):
            source, dims = self.source(chunk, phase, order)
            target = order[phase]
            cut = AXIS_OF[target]
            lanes = pl.ds(begin, extent)
            away = tuple(1 - self.places[d] if d == cut else slice(None) for d in dims)
            whole = tuple(slice(None) for _ in self.dims_after(order, phase))
            slot = chunk % SCATTER_SLOTS
            out.append(
                pltpu.make_async_remote_copy(
                    src_ref=source.at[away + (slice(None), lanes)],
                    dst_ref=self.arrived(chunk, phase).at[whole + (slice(None), lanes)],
                    send_sem=self.send_sem.at[2 * phase + part, slot],
                    recv_sem=self.recv_sem.at[2 * phase + part, slot],
                    device_id=self.targets[target],
                    device_id_type=MESH,
                )
            )
        return out

    def add(self, phase, chunk):
        for begin, extent, order in self.parts(chunk):
            source, dims = self.source(chunk, phase, order)
            cut = AXIS_OF[order[phase]]
            kept = self.dims_after(order, phase)
            ref = self.arrived(chunk, phase)
            lanes = pl.ds(begin, extent)
            result = self.result(chunk)

            def body(unit, carry):
                index = tuple((unit >> (len(kept) - 1 - b)) & 1 for b in range(len(kept)))
                where = dict(zip(kept, index))
                where[cut] = self.places[cut]
                mine = source[tuple(where[d] for d in dims) + (slice(None), lanes)]
                came = ref[index + (slice(None), lanes)]
                if phase < 4:
                    ref[index + (slice(None), lanes)] = came + mine
                else:
                    result[:, lanes] = came.astype(jnp.float32) + mine.astype(jnp.float32)
                return carry

            if kept:
                lax.fori_loop(0, 2 ** len(kept), body, 0)
            else:
                body(0, 0)


def scatter_kernel(chunks, rows_of, *refs):
    terms = refs[:WEIGHTS]
    outs = refs[WEIGHTS : 2 * WEIGHTS]
    scratch = refs[2 * WEIGHTS :]
    buffers = {TALL: scratch[4:11], rows_of[3]: scratch[11:18]}
    work = Scatter(chunks, rows_of, terms, outs, scratch[:4], buffers)
    barrier = greet(work.targets)
    loads = {0: work.load(0)}
    loads[0].start()
    pl.semaphore_wait(barrier, len(work.targets))
    phases = 5
    live = {}
    stores = {}
    for step in range(len(chunks) + phases * SCATTER_LAG):
        for phase in range(phases, -1, -1):
            chunk = step - phase * SCATTER_LAG
            if not 0 <= chunk < len(chunks):
                continue
            if phase == 0:
                loads.pop(chunk).wait()
            else:
                for copy in live.pop((phase - 1, chunk)):
                    copy.wait()
                if phase == phases and chunk - 2 in stores:
                    stores.pop(chunk - 2).wait()
                work.add(phase - 1, chunk)
            if phase < phases:
                live[(phase, chunk)] = work.messages(phase, chunk)
                for copy in live[(phase, chunk)]:
                    copy.start()
            else:
                stores[chunk] = work.store(chunk)
                stores[chunk].start()
        if step + 1 < len(chunks):
            loads[step + 1] = work.load(step + 1)
            loads[step + 1].start()
    for copy in stores.values():
        copy.wait()


def scatter_buffers(rows, width):
    low = jnp.bfloat16
    out = [pltpu.VMEM((TERM_SLOTS, 2, 2, 2, 2, 2, rows, width), low)]
    for phase in range(5):
        out.append(pltpu.VMEM((SCATTER_SLOTS,) + (2,) * (4 - phase) + (rows, width), low))
    out.append(pltpu.VMEM((2, rows, width), jnp.float32))
    return out


def scatter_all(terms):
    shapes = [item.shape[5:] for item in terms]
    rows_of = [shape[0] for shape in shapes]
    chunks = []
    for i in range(WEIGHTS - 1, -1, -1):
        width = TALL_WIDTH if rows_of[i] == TALL else OTHER_WIDTH
        chunks += [(i, start, width) for start in range(0, shapes[i][1], width)]
    return pl.pallas_call(
        functools.partial(scatter_kernel, chunks, rows_of),
        out_shape=tuple(jax.ShapeDtypeStruct(shape, jnp.float32) for shape in shapes),
        in_specs=[ANY] * WEIGHTS,
        out_specs=(ANY,) * WEIGHTS,
        scratch_shapes=[
            pltpu.SemaphoreType.DMA((TERM_SLOTS,)),
            pltpu.SemaphoreType.DMA((2,)),
            pltpu.SemaphoreType.DMA((10, SCATTER_SLOTS)),
            pltpu.SemaphoreType.DMA((10, SCATTER_SLOTS)),
        ]
        + scatter_buffers(TALL, TALL_WIDTH)
        + scatter_buffers(rows_of[3], OTHER_WIDTH),
        compiler_params=pltpu.CompilerParams(
            collective_id=1, has_side_effects=True, vmem_limit_bytes=60 << 20
        ),
    )(*terms)


def gather_weights(shards_of, direct):
    if direct:
        return [
            item.reshape(2, 16 * item.shape[5], item.shape[6]) for item in gather_all(shards_of)
        ]
    wide = [
        lax.all_gather(lax.all_gather(item, "fsdp", axis=1, tiled=True), "dp", axis=0, tiled=True)
        for item in shards_of
    ]
    return [
        item.reshape(item.shape[0], 2, item.shape[1] // 2).transpose(1, 0, 2) for item in wide
    ]


def settle_gradients(terms, direct):
    if direct:
        return scatter_all(
            [
                item.reshape(2, 2, 2, 2, 2, item.shape[1] // 16, item.shape[2])
                for item in terms
            ]
        )
    wide = [
        item.transpose(1, 0, 2).reshape(item.shape[1], 2 * item.shape[2]) for item in terms
    ]
    tall = [lax.psum_scatter(item, "dp", scatter_dimension=0, tiled=True) for item in wide]
    return [
        lax.psum_scatter(item, "fsdp", scatter_dimension=1, tiled=True).astype(jnp.float32)
        for item in tall
    ]


def halves(matrix):
    return matrix.reshape(matrix.shape[0], 2, matrix.shape[1] // 2).transpose(1, 0, 2)


def joined(stack):
    return stack.transpose(1, 0, 2).reshape(stack.shape[1], 2 * stack.shape[2])


def local_scores(queries, keys_all):
    query_blocks = split_heads(queries.astype(jnp.bfloat16))
    key_blocks = split_heads(keys_all.astype(jnp.bfloat16))
    scores = jnp.einsum(
        "bihd,bjhd->bhij", query_blocks, key_blocks, preferred_element_type=jnp.float32
    ) * HEAD ** (-0.5)
    return (query_blocks, key_blocks, jnp.where(causal_table(), scores, -1e30))


def local_forward(queries, keys_all, values_low, validity):
    query_blocks, key_blocks, scores = local_scores(queries, keys_all)
    highest_score = jnp.max(scores, axis=-1, keepdims=True)
    expweights = jnp.exp(scores - highest_score)
    row_total = jnp.sum(expweights, axis=-1, keepdims=True)
    attend = (expweights / row_total).astype(jnp.bfloat16)
    mixture = jnp.einsum(
        "bhij,bjhd->bihd", attend, split_heads(values_low), preferred_element_type=jnp.float32
    )
    return (join_heads(mixture) * validity, highest_score + jnp.log(row_total))


def local_backward(queries, keys_all, values_low, validity, logsum, back_mixture):
    query_blocks, key_blocks, scores = local_scores(queries, keys_all)
    value_blocks = split_heads(values_low)
    coming = split_heads(back_mixture * validity.astype(jnp.bfloat16))
    attend = jnp.exp(scores - logsum)
    back_values = jnp.einsum(
        "bhij,bihd->bjhd", attend.astype(jnp.bfloat16), coming, preferred_element_type=jnp.float32
    )
    back_attend = jnp.einsum(
        "bihd,bjhd->bhij", coming, value_blocks, preferred_element_type=jnp.float32
    )
    back_scores = (
        attend * (back_attend - jnp.sum(back_attend * attend, axis=-1, keepdims=True))
    ).astype(jnp.bfloat16)
    back_queries = jnp.einsum(
        "bhij,bjhd->bihd", back_scores, key_blocks, preferred_element_type=jnp.float32
    ) * HEAD ** (-0.5)
    back_keys = jnp.einsum(
        "bhij,bihd->bjhd", back_scores, query_blocks, preferred_element_type=jnp.float32
    ) * HEAD ** (-0.5)
    return (join_heads(back_queries), join_heads(back_keys), join_heads(back_values))


def linear_parts(queries, keys_all, values_low):
    feature_q = split_heads(jax.nn.softplus(queries).astype(jnp.bfloat16))
    feature_k = split_heads(jax.nn.softplus(keys_all).astype(jnp.bfloat16))
    value_blocks = split_heads(values_low)
    causal = causal_table().astype(jnp.float32)
    inner_scores = (
        jnp.einsum("bihd,bjhd->bhij", feature_q, feature_k, preferred_element_type=jnp.float32)
        * causal
    ).astype(jnp.bfloat16)
    states = jnp.einsum(
        "bjhd,bjhe->bhde", feature_k, value_blocks, preferred_element_type=jnp.float32
    )
    running = jnp.cumsum(states, axis=0)
    prior_states = jnp.concatenate([jnp.zeros_like(states[:1]), running[:-1]], axis=0)
    return (feature_q, feature_k, value_blocks, causal, inner_scores, prior_states)


def linear_forward(queries, keys_all, values_low):
    feature_q, feature_k, value_blocks, causal, inner_scores, prior_states = linear_parts(
        queries, keys_all, values_low
    )
    mixture = jnp.einsum(
        "bhij,bjhe->bihe", inner_scores, value_blocks, preferred_element_type=jnp.float32
    )
    mixture = mixture + jnp.einsum(
        "bihd,bhde->bihe", feature_q.astype(jnp.float32), prior_states, precision=highest
    )
    return join_heads(mixture)


def linear_backward(queries, keys_all, values_low, back_mixture):
    feature_q, feature_k, value_blocks, causal, inner_scores, prior_states = linear_parts(
        queries, keys_all, values_low
    )
    coming = split_heads(back_mixture)
    coming_wide = coming.astype(jnp.float32)
    back_inner = (
        jnp.einsum("bihe,bjhe->bhij", coming, value_blocks, preferred_element_type=jnp.float32)
        * causal
    ).astype(jnp.bfloat16)
    back_feature_q = jnp.einsum(
        "bhij,bjhd->bihd", back_inner, feature_k, preferred_element_type=jnp.float32
    )
    back_feature_q = back_feature_q + jnp.einsum(
        "bihe,bhde->bihd", coming_wide, prior_states, precision=highest
    )
    back_feature_k = jnp.einsum(
        "bhij,bihd->bjhd", back_inner, feature_q, preferred_element_type=jnp.float32
    )
    back_values = jnp.einsum(
        "bhij,bihe->bjhe", inner_scores, coming, preferred_element_type=jnp.float32
    )
    back_prior = jnp.einsum(
        "bihd,bihe->bhde", feature_q.astype(jnp.float32), coming_wide, precision=highest
    )
    running = jnp.cumsum(back_prior[::-1], axis=0)[::-1]
    later_states = jnp.concatenate([running[1:], jnp.zeros_like(running[:1])], axis=0)
    back_feature_k = back_feature_k + jnp.einsum(
        "bjhe,bhde->bjhd", value_blocks.astype(jnp.float32), later_states, precision=highest
    )
    back_values = back_values + jnp.einsum(
        "bjhd,bhde->bjhe", feature_k.astype(jnp.float32), later_states, precision=highest
    )
    return (
        join_heads(back_feature_q) * jax.nn.sigmoid(queries),
        join_heads(back_feature_k) * jax.nn.sigmoid(keys_all),
        join_heads(back_values),
    )


def forward_layer(layer_in, validity, weights, local):
    project, output, expand, shrink = weights
    normed = simple_norm(layer_in).astype(jnp.bfloat16)
    projected = jnp.dot(normed, project, preferred_element_type=jnp.float32)
    queries, keys_all, values, update = jnp.split(projected, 4, axis=1)
    values_low = values.astype(jnp.bfloat16)
    if local:
        mixture, logsum = local_forward(queries, keys_all, values_low, validity)
    else:
        mixture = linear_forward(queries, keys_all, values_low)
        logsum = None
    gated_rows = (head_norm(mixture) * jax.nn.silu(update)).astype(jnp.bfloat16)
    middle = layer_in + jnp.dot(gated_rows, output, preferred_element_type=jnp.float32)
    second = simple_norm(middle).astype(jnp.bfloat16)
    expanded = jnp.dot(second, expand, preferred_element_type=jnp.float32)
    half_width = expanded.shape[1] // 2
    hidden = (expanded[:, :half_width] * expanded[:, half_width:]).astype(jnp.bfloat16)
    result = middle + jnp.dot(hidden, shrink, preferred_element_type=jnp.float32)
    return (
        result,
        (layer_in, normed, projected, values_low, mixture, logsum, gated_rows, middle, second),
    )


def backward_layer(upstream, saved, weights, validity, local):
    project, output, expand, shrink = weights
    layer_in, normed, projected, values_low, mixture, logsum, gated_rows, middle, second = saved
    expanded = jnp.dot(second, expand, preferred_element_type=jnp.float32)
    half_width = expanded.shape[1] // 2
    first_half = expanded[:, :half_width]
    second_half = expanded[:, half_width:]
    hidden = (first_half * second_half).astype(jnp.bfloat16)
    back_branch = upstream.astype(jnp.bfloat16)
    shrink_term = contract_rows(hidden, back_branch)
    back_hidden = contract_cols(back_branch, shrink)
    back_expanded = jnp.concatenate(
        [back_hidden * second_half, back_hidden * first_half], axis=1
    ).astype(jnp.bfloat16)
    expand_term = contract_rows(second, back_expanded)
    back_second = contract_cols(back_expanded, expand)
    back_middle = upstream + norm_back(middle, back_second)
    back_gated = back_middle.astype(jnp.bfloat16)
    output_term = contract_rows(gated_rows, back_gated)
    back_rows_gated = contract_cols(back_gated, output)
    queries, keys_all, unused_values, update = jnp.split(projected, 4, axis=1)
    back_update = back_rows_gated * head_norm(mixture) * silu_slope(update)
    back_mixture = head_back(mixture, back_rows_gated * jax.nn.silu(update)).astype(jnp.bfloat16)
    if local:
        back_queries, back_keys, back_values = local_backward(
            queries, keys_all, values_low, validity, logsum, back_mixture
        )
    else:
        back_queries, back_keys, back_values = linear_backward(
            queries, keys_all, values_low, back_mixture
        )
    back_projected = jnp.concatenate(
        [back_queries, back_keys, back_values, back_update], axis=1
    ).astype(jnp.bfloat16)
    project_term = contract_rows(normed, back_projected)
    back_normed = contract_cols(back_projected, project)
    back_input = back_middle + norm_back(layer_in, back_normed)
    return (back_input, (project_term, output_term, expand_term, shrink_term))


def shards(
    direct,
    tokens,
    lengths,
    local_project,
    local_output,
    local_expand,
    local_shrink,
    linear_project,
    linear_output,
    linear_expand,
    linear_shrink,
    cotangent,
):
    positions = lax.broadcasted_iota(jnp.int32, (tokens.shape[1], 1), 0)
    validity = (positions < lengths[0]).astype(jnp.float32)
    layer_in = tokens[0].astype(jnp.float32) * validity
    gathered = gather_weights(
        [
            local_project,
            local_output,
            local_expand,
            local_shrink,
            linear_project,
            linear_output,
            linear_expand,
            linear_shrink,
        ],
        direct,
    )
    whole = [joined(item) for item in gathered]
    local_weights = whole[:4]
    linear_weights = whole[4:]
    between, local_saved = forward_layer(layer_in, validity, local_weights, True)
    result, linear_saved = forward_layer(between, validity, linear_weights, False)
    result = result * validity
    upstream = cotangent[0].astype(jnp.float32) * validity
    back_between, linear_terms = backward_layer(
        upstream, linear_saved, linear_weights, validity, False
    )
    back_input, local_terms = backward_layer(
        back_between, local_saved, local_weights, validity, True
    )
    sums = settle_gradients(
        [halves(item.astype(jnp.bfloat16)) for item in local_terms + linear_terms], direct
    )
    return (
        result.astype(jnp.bfloat16)[None],
        (back_input * validity)[None],
    ) + tuple(sums)


def solution(mesh):
    in_specs = (
        P(("dp", "fsdp"), None, None),
        P(("dp", "fsdp")),
        P("dp", "fsdp"),
        P("dp", "fsdp"),
        P("dp", "fsdp"),
        P("dp", "fsdp"),
        P("dp", "fsdp"),
        P("dp", "fsdp"),
        P("dp", "fsdp"),
        P("dp", "fsdp"),
        P(("dp", "fsdp"), None, None),
    )
    out_specs = (
        P(("dp", "fsdp"), None, None),
        P(("dp", "fsdp"), None, None),
        P("dp", "fsdp"),
        P("dp", "fsdp"),
        P("dp", "fsdp"),
        P("dp", "fsdp"),
        P("dp", "fsdp"),
        P("dp", "fsdp"),
        P("dp", "fsdp"),
        P("dp", "fsdp"),
    )
    direct = dict(mesh.shape) == {"dp": 16, "fsdp": 2}
    return jax.shard_map(functools.partial(shards, direct), mesh=mesh, in_specs=in_specs, out_specs=out_specs, check_vma=False)
```

```python
import functools

import jax
import jax.numpy as jnp
from jax import lax
from jax.experimental import pallas as pl
from jax.experimental.pallas import tpu as pltpu
from jax.sharding import PartitionSpec as P

HEADS = 16
HEAD = 64
BLOCK = 64


epsilon = 1e-05
highest = lax.Precision.HIGHEST


def simple_norm(values):
    return values * lax.rsqrt(jnp.mean(values * values, axis=-1, keepdims=True) + epsilon)


def norm_back(values, upstream):
    inverse_rms = lax.rsqrt(jnp.mean(values * values, axis=-1, keepdims=True) + epsilon)
    return inverse_rms * (
        upstream
        - values * (inverse_rms * inverse_rms) * jnp.mean(upstream * values, axis=-1, keepdims=True)
    )


def head_norm(values):
    shaped = values.reshape(values.shape[0], HEADS, HEAD)
    return simple_norm(shaped).reshape(values.shape)


def head_back(values, upstream):
    shaped = values.reshape(values.shape[0], HEADS, HEAD)
    coming = upstream.reshape(values.shape[0], HEADS, HEAD)
    return norm_back(shaped, coming).reshape(values.shape)


def silu_slope(values):
    logistic = jax.nn.sigmoid(values)
    return logistic * (1.0 + values * (1.0 - logistic))


def contract_rows(first_matrix, second_matrix):
    return lax.dot_general(
        first_matrix, second_matrix, (((0,), (0,)), ((), ())), preferred_element_type=jnp.float32
    )


def contract_cols(first_matrix, second_matrix):
    return lax.dot_general(
        first_matrix, second_matrix, (((1,), (1,)), ((), ())), preferred_element_type=jnp.float32
    )


def causal_table():
    return lax.broadcasted_iota(jnp.int32, (BLOCK, BLOCK), 0) >= lax.broadcasted_iota(
        jnp.int32, (BLOCK, BLOCK), 1
    )


def split_heads(values):
    return values.reshape(values.shape[0] // BLOCK, BLOCK, HEADS, HEAD)


def join_heads(values):
    return values.reshape(values.shape[0] * BLOCK, HEADS * HEAD)


MESH = pl.DeviceIdType.MESH
ANY = pl.BlockSpec(memory_space=pl.ANY)
FULL = pl.BlockSpec(memory_space=pltpu.VMEM)
WEIGHTS = 8
WIDTH = 256
LAG = 3
PHASES = 5
HEAD_GROUPS = 4
PROJECT_CHUNKS = 8
OUTPUT_CHUNKS = 2
EXPAND_CHUNKS = 11
LAYER_CHUNKS = PROJECT_CHUNKS + OUTPUT_CHUNKS + EXPAND_CHUNKS
CHUNKS = 2 * LAYER_CHUNKS
SHRINK_PARTS = 4
SHRINK_WIDTH = 128
GATHER_SLOTS = 8
LOAD_SLOTS = 3
LOW = jnp.bfloat16
WIDE = jnp.float32
ROWS = 512


def neighbours():
    dp = lax.axis_index("dp")
    x = lax.axis_index("fsdp")
    z = dp // 4
    y = (dp // 2) % 2
    c = dp % 2
    places = {"f": x, "zh": z // 2, "zl": z % 2, "y": y, "c": c}
    targets = {
        "z1": ((z + 1 - 2 * (z % 2)) * 4 + y * 2 + c, x),
        "z2": (lax.rem(z + 2, 4) * 4 + y * 2 + c, x),
        "y": (z * 4 + (1 - y) * 2 + c, x),
        "c": (z * 4 + y * 2 + (1 - c), x),
        "x": (dp, 1 - x),
    }
    return places, targets


def greet(targets):
    barrier = pltpu.get_barrier_semaphore()
    for target in targets.values():
        pl.semaphore_signal(barrier, inc=1, device_id=target, device_id_type=MESH)
    pl.semaphore_wait(barrier, len(targets))


def dot(left, right):
    return jnp.dot(left, right, preferred_element_type=WIDE)


def softplus(values):
    return jnp.maximum(values, 0.0) + jnp.log1p(jnp.exp(-jnp.abs(values)))


def logistic(values):
    return 1.0 / (1.0 + jnp.exp(-values))


def first_lanes(rows):
    return lax.broadcasted_iota(jnp.int32, (rows, 128), 1) < HEAD


def pair_mean(values, first):
    left = jnp.sum(jnp.where(first, values, 0.0), axis=-1, keepdims=True)
    right = jnp.sum(jnp.where(first, 0.0, values), axis=-1, keepdims=True)
    return jnp.where(first, left, right) * (1.0 / HEAD)


def block_mask(rows):
    i = lax.broadcasted_iota(jnp.int32, (rows, rows), 0)
    j = lax.broadcasted_iota(jnp.int32, (rows, rows), 1)
    return (i // BLOCK == j // BLOCK) & (j <= i)


def norm_into(source, target):
    def body(t, carry):
        rows = pl.ds(pl.multiple_of(t * 128, 128), 128)
        target[rows, :] = simple_norm(source[rows, :]).astype(LOW)
        return carry

    lax.fori_loop(0, ROWS // 128, body, 0)


def local_mixer(group, parts, validity, gated, stage):
    def body(turn, carry):
        t = turn // 2
        rows = pl.ds(pl.multiple_of(t * 128, 128), 128)
        pair = turn % 2
        lanes = pl.ds(pl.multiple_of(pair * 128, 128), 128)
        first = first_lanes(128)
        q = parts[0, 0, rows, lanes].astype(LOW)
        k = parts[1, 0, rows, lanes].astype(LOW)
        v = parts[0, 1, rows, lanes].astype(LOW)
        u = parts[1, 1, rows, lanes]
        keep = block_mask(128)
        mixed = []
        for head in range(2):
            mine = jnp.where(first == (head == 0), q, jnp.zeros_like(q))
            scores = contract_cols(mine, k) * HEAD ** (-0.5)
            scores = jnp.where(keep, scores, -1e30)
            highest_score = jnp.max(scores, axis=-1, keepdims=True)
            weights = jnp.exp(scores - highest_score)
            attend = weights / jnp.sum(weights, axis=-1, keepdims=True)
            mixed.append(dot(attend.astype(LOW), v))
        mixture = jnp.where(first, mixed[0], mixed[1]) * validity[rows, :]
        scale = lax.rsqrt(pair_mean(mixture * mixture, first) + epsilon)
        columns = pl.ds(pl.multiple_of(group * WIDTH + pair * 128, 128), 128)
        gated[rows, columns] = (mixture * scale * (u * logistic(u))).astype(LOW)
        stage[4, rows, lanes] = mixture.astype(LOW)
        return carry

    lax.fori_loop(0, 2 * ROWS // 128, body, 0)


def linear_mixer(group, parts, gated, stage):
    half = ROWS // 2

    def body(pair, carry):
        lanes = pl.ds(pl.multiple_of(pair * 128, 128), 128)
        columns = pl.ds(pl.multiple_of(group * WIDTH + pair * 128, 128), 128)
        first = first_lanes(half)
        fk = softplus(parts[1, 0, :, lanes]).astype(LOW)
        v = parts[0, 1, :, lanes].astype(LOW)
        for t in range(2):
            rows = pl.ds(t * half, half)
            reach = (t + 1) * half
            fq = softplus(parts[0, 0, rows, lanes]).astype(LOW)
            i = lax.broadcasted_iota(jnp.int32, (half, reach), 0) + t * half
            j = lax.broadcasted_iota(jnp.int32, (half, reach), 1)
            mixed = []
            for head in range(2):
                mine = jnp.where(first == (head == 0), fq, jnp.zeros_like(fq))
                scores = jnp.where(j <= i, contract_cols(mine, fk[:reach]), 0.0).astype(LOW)
                mixed.append(dot(scores, v[:reach]))
            mixture = jnp.where(first, mixed[0], mixed[1])
            scale = lax.rsqrt(pair_mean(mixture * mixture, first) + epsilon)
            u = parts[1, 1, rows, lanes]
            gated[rows, columns] = (mixture * scale * (u * logistic(u))).astype(LOW)
            stage[4, rows, lanes] = mixture.astype(LOW)
        return carry

    lax.fori_loop(0, 2, body, 0)


def chunk_columns(weight, part):
    if weight == 0:
        return (part % 2) * 1024 + (part // 2) * WIDTH
    return part * WIDTH


class Gather:
    def __init__(self, own, held, tall, sems):
        self.own, self.held, self.tall = own, held, tall
        self.local_sem, self.send_sem, self.recv_sem, self.tall_send, self.tall_recv = sems
        self.places, self.targets = neighbours()
        self.at = tuple(self.places[name] for name in ("f", "zh", "zl", "y", "c"))

    def begin(self):
        counts = (PROJECT_CHUNKS, OUTPUT_CHUNKS, EXPAND_CHUNKS)
        for layer in range(2):
            chunk = LAYER_CHUNKS * layer
            for weight in range(3):
                for part in range(counts[weight]):
                    start = chunk_columns(weight, part)
                    pltpu.make_async_copy(
                        self.own[4 * layer + weight].at[:, pl.ds(start, WIDTH)],
                        self.held.at[(chunk,) + self.at],
                        self.local_sem.at[chunk],
                    ).start()
                    chunk += 1
            pltpu.make_async_copy(
                self.own[4 * layer + 3],
                self.tall.at[(layer,) + self.at],
                self.local_sem.at[CHUNKS + layer],
            ).start()
        greet(self.targets)

    def message(self, block, target, sems, place):
        return pltpu.make_async_remote_copy(
            src_ref=block,
            dst_ref=block,
            send_sem=sems[0].at[place],
            recv_sem=sems[1].at[place],
            device_id=self.targets[target],
            device_id_type=MESH,
        )

    def wide_messages(self, phase, chunk):
        x, zh, zl, y, c = self.at
        ref = self.held
        sems = (self.send_sem, self.recv_sem)
        slot = chunk % GATHER_SLOTS
        half = WIDTH // 2
        low, high = pl.ds(0, half), pl.ds(half, half)

        def one(index, target, part):
            return self.message(ref.at[(chunk,) + index], target, sems, (2 * phase + part, slot))

        a = slice(None)
        if phase == 0:
            return [one((x, zh, zl, y, c), "z2", 0)]
        if phase == 1:
            return [one((x, a, zl, y, c), "z1", 0)]
        if phase == 2:
            return [one((x, a, a, y, c, a, low), "x", 0), one((x, a, a, y, c, a, high), "y", 1)]
        if phase == 3:
            return [one((a, a, a, y, c, a, low), "y", 0), one((x, a, a, a, c, a, high), "x", 1)]
        return [one((a, a, a, a, c), "c", 0)]

    def tall_message(self, phase, layer, part, odd):
        x, zh, zl, y, c = self.at
        a = slice(None)
        lanes = pl.ds(pl.multiple_of(part * SHRINK_WIDTH, SHRINK_WIDTH), SHRINK_WIDTH)
        index, target = {
            (0, 0): ((x, zh, zl, y, c), "x"),
            (0, 1): ((x, zh, zl, y, c), "y"),
            (1, 0): ((a, zh, zl, y, c), "y"),
            (1, 1): ((x, zh, zl, a, c), "x"),
            (2, 0): ((a, zh, zl, a, c), "z2"),
            (3, 0): ((a, a, zl, a, c), "z1"),
            (4, 0): ((a, a, a, a, c), "c"),
        }[(phase, odd)]
        return self.message(
            self.tall.at[(layer,) + index + (a, lanes)],
            target,
            (self.tall_send, self.tall_recv),
            (phase, layer * SHRINK_PARTS + part),
        )

    def tall_turn(self, chunk):
        layer = chunk // LAYER_CHUNKS
        place = chunk % LAYER_CHUNKS
        return layer, place // 5, place % 5 == 4

    def for_tall(self, phase, chunk, act):
        layer, part, due = self.tall_turn(chunk)
        if phase >= 2:
            pl.when(due)(lambda: act(self.tall_message(phase, layer, part, 0)))
        else:
            for odd in range(2):
                pl.when(due & (part % 2 == odd))(
                    lambda odd=odd: act(self.tall_message(phase, layer, part, odd))
                )

    def step(self, step):
        for phase in range(PHASES, -1, -1):
            chunk = step - phase * LAG

            @pl.when((chunk >= 0) & (chunk < CHUNKS))
            def _(phase=phase, chunk=chunk):
                if phase >= 1:
                    for copy in self.wide_messages(phase - 1, chunk):
                        copy.wait()
                    self.for_tall(phase - 1, chunk, lambda copy: copy.wait())
                else:
                    pltpu.make_async_copy(
                        self.own[0].at[:, pl.ds(0, WIDTH)],
                        self.held.at[(chunk,) + self.at],
                        self.local_sem.at[chunk],
                    ).wait()
                    layer = chunk // LAYER_CHUNKS

                    @pl.when(chunk % LAYER_CHUNKS == 4)
                    def _():
                        pltpu.make_async_copy(
                            self.own[3],
                            self.tall.at[(layer,) + self.at],
                            self.local_sem.at[CHUNKS + layer],
                        ).wait()

                if phase < PHASES:
                    for copy in self.wide_messages(phase, chunk):
                        copy.start()
                    self.for_tall(phase, chunk, lambda copy: copy.start())


def forward_kernel(*refs):
    own = refs[:WEIGHTS]
    tokens, validity = refs[WEIGHTS : WEIGHTS + 2]
    held, tall, mixed_out, between, middles, gates, stages, halves_out = refs[10:18]
    scratch = refs[18:]
    sems, (load_sem, tall_sem, stage_sem, half_sem, misc_sem) = scratch[:5], scratch[5:10]
    loaded, shrink, x, middle, normed, gated, hidden, parts, stage, half_stage, final = scratch[10:]
    gather = Gather(own, held, tall, sems)
    gather.begin()

    def rows_of(t):
        return pl.ds(pl.multiple_of(t * 128, 128), 128)

    def start_rows(t, carry):
        rows = rows_of(t)
        x[rows, :] = tokens[rows, :].astype(WIDE) * validity[rows, :]
        return carry

    lax.fori_loop(0, ROWS // 128, start_rows, 0)
    norm_into(x, normed)

    def load(chunk):
        return pltpu.make_async_copy(
            held.at[chunk], loaded.at[chunk % LOAD_SLOTS], load_sem.at[chunk % LOAD_SLOTS]
        )

    def load_tall(layer):
        return pltpu.make_async_copy(tall.at[layer], shrink, tall_sem)

    def keep_stage(layer, group):
        return pltpu.make_async_copy(stage, stages.at[layer, group], stage_sem)

    def keep_half(layer, part):
        return pltpu.make_async_copy(
            half_stage.at[part % 2], halves_out.at[layer, part], half_sem.at[part % 2]
        )

    def keep(kind, layer):
        source, target = ((gated, gates), (middle, middles))[kind]
        return pltpu.make_async_copy(source, target.at[layer], misc_sem.at[kind])

    def keep_between():
        return pltpu.make_async_copy(x, between, misc_sem.at[2])

    def weight(slot, f):
        return loaded[slot, f].reshape(1024, WIDTH)

    def project_step(layer, place, slot):
        group = place // 2
        for f in range(2):
            parts[place % 2, f] = dot(normed[...], weight(slot, f))

        @pl.when(place % 2 == 1)
        def _():
            @pl.when((layer > 0) | (group > 0))
            def _():
                keep_stage(layer, group).wait()

            @pl.when((layer > 0) & (group == 0))
            def _():
                keep(0, 0).wait()

            for kind in range(4):
                stage[kind] = parts[kind % 2, kind // 2].astype(LOW)
            pl.when(layer == 0)(lambda: local_mixer(group, parts, validity, gated, stage))
            pl.when(layer > 0)(lambda: linear_mixer(group, parts, gated, stage))
            keep_stage(layer, group).start()

    def output_step(layer, part, slot):
        @pl.when(part == 0)
        def _():
            keep(0, layer).start()

            @pl.when(layer > 0)
            def _():
                keep(1, 0).wait()

        for f in range(2):
            lanes = pl.ds(pl.multiple_of(f * 512 + part * WIDTH, WIDTH), WIDTH)
            middle[:, lanes] = x[:, lanes] + dot(gated[...], weight(slot, f))

        @pl.when(part == OUTPUT_CHUNKS - 1)
        def _():
            keep(1, layer).start()
            norm_into(middle, normed)

    def expand_step(layer, part, slot):
        @pl.when((layer > 0) | (part > 1))
        def _():
            keep_half(layer, part).wait()

        first = dot(normed[...], weight(slot, 0))
        second = dot(normed[...], weight(slot, 1))
        half_stage[part % 2, 0] = first.astype(LOW)
        half_stage[part % 2, 1] = second.astype(LOW)
        hidden[:, pl.ds(pl.multiple_of(part * WIDTH, WIDTH), WIDTH)] = (first * second).astype(LOW)
        keep_half(layer, part).start()

    def shrink_step(layer):
        load_tall(layer).wait()

        @pl.when(layer > 0)
        def _():
            keep_between().wait()

        def body(turn, carry):
            f = turn // 2
            columns = pl.ds(pl.multiple_of((turn % 2) * WIDTH, WIDTH), WIDTH)
            lanes = pl.ds(pl.multiple_of(turn * WIDTH, WIDTH), WIDTH)
            matrix = shrink[f, :, :, :, :, :, columns].reshape(hidden.shape[1], WIDTH)
            x[:, lanes] = middle[:, lanes] + dot(hidden[...], matrix)
            return carry

        lax.fori_loop(0, 4, body, 0)

        @pl.when(layer == 0)
        def _():
            keep_between().start()
            norm_into(x, normed)

        @pl.when(layer > 0)
        def _():
            def last_rows(t, carry):
                rows = rows_of(t)
                final[rows, :] = (x[rows, :] * validity[rows, :]).astype(LOW)
                return carry

            lax.fori_loop(0, ROWS // 128, last_rows, 0)

    def body(step, carry):
        gather.step(step)
        arrived = step - PHASES * LAG

        @pl.when((arrived >= 0) & (arrived < CHUNKS))
        def _():
            load(arrived).start()

            @pl.when(arrived % LAYER_CHUNKS == LAYER_CHUNKS - 2)
            def _():
                load_tall(arrived // LAYER_CHUNKS).start()

        ready = arrived - 1

        @pl.when((ready >= 0) & (ready < CHUNKS))
        def _():
            load(ready).wait()
            layer = ready // LAYER_CHUNKS
            place = ready % LAYER_CHUNKS
            slot = ready % LOAD_SLOTS
            pl.when(place < PROJECT_CHUNKS)(lambda: project_step(layer, place, slot))
            pl.when((place >= PROJECT_CHUNKS) & (place < PROJECT_CHUNKS + OUTPUT_CHUNKS))(
                lambda: output_step(layer, place - PROJECT_CHUNKS, slot)
            )
            pl.when(place >= PROJECT_CHUNKS + OUTPUT_CHUNKS)(
                lambda: expand_step(layer, place - PROJECT_CHUNKS - OUTPUT_CHUNKS, slot)
            )
            pl.when(place == LAYER_CHUNKS - 1)(lambda: shrink_step(layer))

        return carry

    lax.fori_loop(0, CHUNKS + PHASES * LAG + 1, body, 0)
    last = pltpu.make_async_copy(final, mixed_out, misc_sem.at[3])
    last.start()
    keep_stage(1, HEAD_GROUPS - 1).wait()
    keep(0, 1).wait()
    keep(1, 1).wait()
    keep_half(1, EXPAND_CHUNKS - 2).wait()
    keep_half(1, EXPAND_CHUNKS - 1).wait()
    last.wait()


def run_forward(shards_of, tokens, validity):
    bits = (2, 2, 2, 2, 2)
    struct = jax.ShapeDtypeStruct
    return pl.pallas_call(
        forward_kernel,
        out_shape=(
            struct((CHUNKS,) + bits + (64, WIDTH), LOW),
            struct((2,) + bits + (176, 512), LOW),
            struct((ROWS, 1024), LOW),
            struct((ROWS, 1024), WIDE),
            struct((2, ROWS, 1024), WIDE),
            struct((2, ROWS, 1024), LOW),
            struct((2, HEAD_GROUPS, 5, ROWS, WIDTH), LOW),
            struct((2, EXPAND_CHUNKS, 2, ROWS, WIDTH), LOW),
        ),
        in_specs=[ANY] * WEIGHTS + [FULL, FULL],
        out_specs=(ANY,) * 8,
        scratch_shapes=[
            pltpu.SemaphoreType.DMA((CHUNKS + 2,)),
            pltpu.SemaphoreType.DMA((10, GATHER_SLOTS)),
            pltpu.SemaphoreType.DMA((10, GATHER_SLOTS)),
            pltpu.SemaphoreType.DMA((PHASES, 2 * SHRINK_PARTS)),
            pltpu.SemaphoreType.DMA((PHASES, 2 * SHRINK_PARTS)),
            pltpu.SemaphoreType.DMA((LOAD_SLOTS,)),
            pltpu.SemaphoreType.DMA,
            pltpu.SemaphoreType.DMA,
            pltpu.SemaphoreType.DMA((2,)),
            pltpu.SemaphoreType.DMA((4,)),
            pltpu.VMEM((LOAD_SLOTS,) + bits + (64, WIDTH), LOW),
            pltpu.VMEM(bits + (176, 512), LOW),
            pltpu.VMEM((ROWS, 1024), WIDE),
            pltpu.VMEM((ROWS, 1024), WIDE),
            pltpu.VMEM((ROWS, 1024), LOW),
            pltpu.VMEM((ROWS, 1024), LOW),
            pltpu.VMEM((ROWS, 2816), LOW),
            pltpu.VMEM((2, 2, ROWS, WIDTH), WIDE),
            pltpu.VMEM((5, ROWS, WIDTH), LOW),
            pltpu.VMEM((2, 2, ROWS, WIDTH), LOW),
            pltpu.VMEM((ROWS, 1024), LOW),
        ],
        compiler_params=pltpu.CompilerParams(
            collective_id=0, has_side_effects=True, vmem_limit_bytes=60 << 20
        ),
    )(*shards_of, tokens, validity)

AXIS_NAMES = ("f", "zh", "zl", "y", "c")
AXIS_OF = {"c": "c", "y": "y", "x": "f", "z1": "zl", "z2": "zh"}
SCATTER_LAG = 3
SCATTER_SLOTS = 3 * SCATTER_LAG + 1
TERM_SLOTS = SCATTER_LAG + 1
TALL = 64
TALL_WIDTH = 256
OTHER_WIDTH = 128


def late_z(chunk):
    return chunk % 5 == 3


class Scatter:
    def __init__(self, chunks, rows_of, terms, outs, sems, buffers):
        self.chunks = chunks
        self.rows_of = rows_of
        self.terms = terms
        self.outs = outs
        self.load_sem, self.store_sem, self.send_sem, self.recv_sem = sems
        self.buffers = buffers
        self.places, self.targets = neighbours()

    def load(self, chunk):
        weight, start, width = self.chunks[chunk]
        return pltpu.make_async_copy(
            self.terms[weight].at[..., pl.ds(start, width)],
            self.buffers[self.rows_of[weight]][0].at[chunk % TERM_SLOTS],
            self.load_sem.at[chunk % TERM_SLOTS],
        )

    def store(self, chunk):
        weight, start, width = self.chunks[chunk]
        return pltpu.make_async_copy(
            self.result(chunk),
            self.outs[weight].at[:, pl.ds(start, width)],
            self.store_sem.at[chunk % 2],
        )

    def result(self, chunk):
        return self.buffers[self.rows_of[self.chunks[chunk][0]]][6].at[chunk % 2]

    def parts(self, chunk):
        weight, start, width = self.chunks[chunk]
        if self.rows_of[weight] == TALL:
            halves = [(0, width // 2, 0), (width // 2, width // 2, 1)]
        else:
            halves = [(0, width, chunk % 2)]
        out = []
        for begin, extent, turn in halves:
            plane = ("y", "x") if turn == 0 else ("x", "y")
            order = ("z1", "z2") + plane if late_z(chunk) else plane + ("z1", "z2")
            out.append((begin, extent, ("c",) + order))
        return out

    def arrived(self, chunk, phase):
        rows = self.rows_of[self.chunks[chunk][0]]
        return self.buffers[rows][1 + phase].at[chunk % SCATTER_SLOTS]

    def dims_after(self, order, phase):
        used = set(AXIS_OF[target] for target in order[: phase + 1])
        return [name for name in AXIS_NAMES if name not in used]

    def source(self, chunk, phase, order):
        rows = self.rows_of[self.chunks[chunk][0]]
        if phase == 0:
            return self.buffers[rows][0].at[chunk % TERM_SLOTS], list(AXIS_NAMES)
        return self.arrived(chunk, phase - 1), self.dims_after(order, phase - 1)

    def messages(self, phase, chunk):
        parts = self.parts(chunk)
        if len(set(order[: phase + 1] for _, _, order in parts)) == 1:
            parts = [(0, self.chunks[chunk][2], parts[0][2])]
        out = []
        for part, (begin, extent, order) in enumerate(parts):
            source, dims = self.source(chunk, phase, order)
            target = order[phase]
            cut = AXIS_OF[target]
            lanes = pl.ds(begin, extent)
            away = tuple(1 - self.places[d] if d == cut else slice(None) for d in dims)
            whole = tuple(slice(None) for _ in self.dims_after(order, phase))
            slot = chunk % SCATTER_SLOTS
            out.append(
                pltpu.make_async_remote_copy(
                    src_ref=source.at[away + (slice(None), lanes)],
                    dst_ref=self.arrived(chunk, phase).at[whole + (slice(None), lanes)],
                    send_sem=self.send_sem.at[2 * phase + part, slot],
                    recv_sem=self.recv_sem.at[2 * phase + part, slot],
                    device_id=self.targets[target],
                    device_id_type=MESH,
                )
            )
        return out

    def add(self, phase, chunk):
        for begin, extent, order in self.parts(chunk):
            source, dims = self.source(chunk, phase, order)
            cut = AXIS_OF[order[phase]]
            kept = self.dims_after(order, phase)
            ref = self.arrived(chunk, phase)
            lanes = pl.ds(begin, extent)
            result = self.result(chunk)

            def body(unit, carry):
                index = tuple((unit >> (len(kept) - 1 - b)) & 1 for b in range(len(kept)))
                where = dict(zip(kept, index))
                where[cut] = self.places[cut]
                mine = source[tuple(where[d] for d in dims) + (slice(None), lanes)]
                came = ref[index + (slice(None), lanes)]
                if phase < 4:
                    ref[index + (slice(None), lanes)] = came + mine
                else:
                    result[:, lanes] = came.astype(jnp.float32) + mine.astype(jnp.float32)
                return carry

            if kept:
                lax.fori_loop(0, 2 ** len(kept), body, 0)
            else:
                body(0, 0)


def scatter_kernel(chunks, rows_of, *refs):
    terms = refs[:WEIGHTS]
    outs = refs[WEIGHTS : 2 * WEIGHTS]
    scratch = refs[2 * WEIGHTS :]
    buffers = {TALL: scratch[4:11], rows_of[3]: scratch[11:18]}
    work = Scatter(chunks, rows_of, terms, outs, scratch[:4], buffers)
    greet(work.targets)
    loads = {0: work.load(0)}
    loads[0].start()
    phases = 5
    live = {}
    stores = {}
    for step in range(len(chunks) + phases * SCATTER_LAG):
        for phase in range(phases, -1, -1):
            chunk = step - phase * SCATTER_LAG
            if not 0 <= chunk < len(chunks):
                continue
            if phase == 0:
                loads.pop(chunk).wait()
            else:
                for copy in live.pop((phase - 1, chunk)):
                    copy.wait()
                if phase == phases and chunk - 2 in stores:
                    stores.pop(chunk - 2).wait()
                work.add(phase - 1, chunk)
            if phase < phases:
                live[(phase, chunk)] = work.messages(phase, chunk)
                for copy in live[(phase, chunk)]:
                    copy.start()
            else:
                stores[chunk] = work.store(chunk)
                stores[chunk].start()
        if step + 1 < len(chunks):
            loads[step + 1] = work.load(step + 1)
            loads[step + 1].start()
    for copy in stores.values():
        copy.wait()


def scatter_buffers(rows, width):
    low = jnp.bfloat16
    out = [pltpu.VMEM((TERM_SLOTS, 2, 2, 2, 2, 2, rows, width), low)]
    for phase in range(5):
        out.append(pltpu.VMEM((SCATTER_SLOTS,) + (2,) * (4 - phase) + (rows, width), low))
    out.append(pltpu.VMEM((2, rows, width), jnp.float32))
    return out


def scatter_all(terms):
    shapes = [item.shape[5:] for item in terms]
    rows_of = [shape[0] for shape in shapes]
    chunks = []
    for i in range(WEIGHTS - 1, -1, -1):
        width = TALL_WIDTH if rows_of[i] == TALL else OTHER_WIDTH
        chunks += [(i, start, width) for start in range(0, shapes[i][1], width)]
    return pl.pallas_call(
        functools.partial(scatter_kernel, chunks, rows_of),
        out_shape=tuple(jax.ShapeDtypeStruct(shape, jnp.float32) for shape in shapes),
        in_specs=[ANY] * WEIGHTS,
        out_specs=(ANY,) * WEIGHTS,
        scratch_shapes=[
            pltpu.SemaphoreType.DMA((TERM_SLOTS,)),
            pltpu.SemaphoreType.DMA((2,)),
            pltpu.SemaphoreType.DMA((10, SCATTER_SLOTS)),
            pltpu.SemaphoreType.DMA((10, SCATTER_SLOTS)),
        ]
        + scatter_buffers(TALL, TALL_WIDTH)
        + scatter_buffers(rows_of[3], OTHER_WIDTH),
        compiler_params=pltpu.CompilerParams(
            collective_id=1, has_side_effects=True, vmem_limit_bytes=60 << 20
        ),
    )(*terms)


def gather_weights(shards_of):
    wide = [
        lax.all_gather(lax.all_gather(item, "fsdp", axis=1, tiled=True), "dp", axis=0, tiled=True)
        for item in shards_of
    ]
    return [
        item.reshape(item.shape[0], 2, item.shape[1] // 2).transpose(1, 0, 2) for item in wide
    ]


def settle_gradients(terms, direct):
    if direct:
        return scatter_all(
            [
                item.reshape(2, 2, 2, 2, 2, item.shape[1] // 16, item.shape[2])
                for item in terms
            ]
        )
    wide = [
        item.transpose(1, 0, 2).reshape(item.shape[1], 2 * item.shape[2]) for item in terms
    ]
    tall = [lax.psum_scatter(item, "dp", scatter_dimension=0, tiled=True) for item in wide]
    return [
        lax.psum_scatter(item, "fsdp", scatter_dimension=1, tiled=True).astype(jnp.float32)
        for item in tall
    ]


def halves(matrix):
    return matrix.reshape(matrix.shape[0], 2, matrix.shape[1] // 2).transpose(1, 0, 2)


def joined(stack):
    return stack.transpose(1, 0, 2).reshape(stack.shape[1], 2 * stack.shape[2])


def local_scores(queries, keys_all):
    query_blocks = split_heads(queries.astype(jnp.bfloat16))
    key_blocks = split_heads(keys_all.astype(jnp.bfloat16))
    scores = jnp.einsum(
        "bihd,bjhd->bhij", query_blocks, key_blocks, preferred_element_type=jnp.float32
    ) * HEAD ** (-0.5)
    return (query_blocks, key_blocks, jnp.where(causal_table(), scores, -1e30))


def local_forward(queries, keys_all, values_low, validity):
    query_blocks, key_blocks, scores = local_scores(queries, keys_all)
    highest_score = jnp.max(scores, axis=-1, keepdims=True)
    expweights = jnp.exp(scores - highest_score)
    row_total = jnp.sum(expweights, axis=-1, keepdims=True)
    attend = (expweights / row_total).astype(jnp.bfloat16)
    mixture = jnp.einsum(
        "bhij,bjhd->bihd", attend, split_heads(values_low), preferred_element_type=jnp.float32
    )
    return (join_heads(mixture) * validity, highest_score + jnp.log(row_total))


def local_backward(queries, keys_all, values_low, validity, logsum, back_mixture):
    query_blocks, key_blocks, scores = local_scores(queries, keys_all)
    value_blocks = split_heads(values_low)
    coming = split_heads(back_mixture * validity.astype(jnp.bfloat16))
    attend = jnp.exp(scores - logsum)
    back_values = jnp.einsum(
        "bhij,bihd->bjhd", attend.astype(jnp.bfloat16), coming, preferred_element_type=jnp.float32
    )
    back_attend = jnp.einsum(
        "bihd,bjhd->bhij", coming, value_blocks, preferred_element_type=jnp.float32
    )
    back_scores = (
        attend * (back_attend - jnp.sum(back_attend * attend, axis=-1, keepdims=True))
    ).astype(jnp.bfloat16)
    back_queries = jnp.einsum(
        "bhij,bjhd->bihd", back_scores, key_blocks, preferred_element_type=jnp.float32
    ) * HEAD ** (-0.5)
    back_keys = jnp.einsum(
        "bhij,bihd->bjhd", back_scores, query_blocks, preferred_element_type=jnp.float32
    ) * HEAD ** (-0.5)
    return (join_heads(back_queries), join_heads(back_keys), join_heads(back_values))


def linear_parts(queries, keys_all, values_low):
    feature_q = split_heads(jax.nn.softplus(queries).astype(jnp.bfloat16))
    feature_k = split_heads(jax.nn.softplus(keys_all).astype(jnp.bfloat16))
    value_blocks = split_heads(values_low)
    causal = causal_table().astype(jnp.float32)
    inner_scores = (
        jnp.einsum("bihd,bjhd->bhij", feature_q, feature_k, preferred_element_type=jnp.float32)
        * causal
    ).astype(jnp.bfloat16)
    states = jnp.einsum(
        "bjhd,bjhe->bhde", feature_k, value_blocks, preferred_element_type=jnp.float32
    )
    running = jnp.cumsum(states, axis=0)
    prior_states = jnp.concatenate([jnp.zeros_like(states[:1]), running[:-1]], axis=0)
    return (feature_q, feature_k, value_blocks, causal, inner_scores, prior_states)


def linear_forward(queries, keys_all, values_low):
    feature_q, feature_k, value_blocks, causal, inner_scores, prior_states = linear_parts(
        queries, keys_all, values_low
    )
    mixture = jnp.einsum(
        "bhij,bjhe->bihe", inner_scores, value_blocks, preferred_element_type=jnp.float32
    )
    mixture = mixture + jnp.einsum(
        "bihd,bhde->bihe", feature_q.astype(jnp.float32), prior_states, precision=highest
    )
    return join_heads(mixture)


def linear_backward(queries, keys_all, values_low, back_mixture):
    feature_q, feature_k, value_blocks, causal, inner_scores, prior_states = linear_parts(
        queries, keys_all, values_low
    )
    coming = split_heads(back_mixture)
    coming_wide = coming.astype(jnp.float32)
    back_inner = (
        jnp.einsum("bihe,bjhe->bhij", coming, value_blocks, preferred_element_type=jnp.float32)
        * causal
    ).astype(jnp.bfloat16)
    back_feature_q = jnp.einsum(
        "bhij,bjhd->bihd", back_inner, feature_k, preferred_element_type=jnp.float32
    )
    back_feature_q = back_feature_q + jnp.einsum(
        "bihe,bhde->bihd", coming_wide, prior_states, precision=highest
    )
    back_feature_k = jnp.einsum(
        "bhij,bihd->bjhd", back_inner, feature_q, preferred_element_type=jnp.float32
    )
    back_values = jnp.einsum(
        "bhij,bihe->bjhe", inner_scores, coming, preferred_element_type=jnp.float32
    )
    back_prior = jnp.einsum(
        "bihd,bihe->bhde", feature_q.astype(jnp.float32), coming_wide, precision=highest
    )
    running = jnp.cumsum(back_prior[::-1], axis=0)[::-1]
    later_states = jnp.concatenate([running[1:], jnp.zeros_like(running[:1])], axis=0)
    back_feature_k = back_feature_k + jnp.einsum(
        "bjhe,bhde->bjhd", value_blocks.astype(jnp.float32), later_states, precision=highest
    )
    back_values = back_values + jnp.einsum(
        "bjhd,bhde->bjhe", feature_k.astype(jnp.float32), later_states, precision=highest
    )
    return (
        join_heads(back_feature_q) * jax.nn.sigmoid(queries),
        join_heads(back_feature_k) * jax.nn.sigmoid(keys_all),
        join_heads(back_values),
    )


def forward_layer(layer_in, validity, weights, local):
    project, output, expand, shrink = weights
    normed = simple_norm(layer_in).astype(jnp.bfloat16)
    projected = jnp.dot(normed, project, preferred_element_type=jnp.float32)
    queries, keys_all, values, update = jnp.split(projected, 4, axis=1)
    values_low = values.astype(jnp.bfloat16)
    if local:
        mixture, logsum = local_forward(queries, keys_all, values_low, validity)
    else:
        mixture = linear_forward(queries, keys_all, values_low)
        logsum = None
    gated_rows = (head_norm(mixture) * jax.nn.silu(update)).astype(jnp.bfloat16)
    middle = layer_in + jnp.dot(gated_rows, output, preferred_element_type=jnp.float32)
    second = simple_norm(middle).astype(jnp.bfloat16)
    expanded = jnp.dot(second, expand, preferred_element_type=jnp.float32)
    half_width = expanded.shape[1] // 2
    hidden = (expanded[:, :half_width] * expanded[:, half_width:]).astype(jnp.bfloat16)
    result = middle + jnp.dot(hidden, shrink, preferred_element_type=jnp.float32)
    return (
        result,
        (layer_in, normed, projected, values_low, mixture, logsum, gated_rows, middle, second),
    )


def backward_layer(upstream, saved, weights, validity, local):
    project, output, expand, shrink = weights
    layer_in, normed, projected, values_low, mixture, logsum, gated_rows, middle, second = saved
    expanded = jnp.dot(second, expand, preferred_element_type=jnp.float32)
    half_width = expanded.shape[1] // 2
    first_half = expanded[:, :half_width]
    second_half = expanded[:, half_width:]
    hidden = (first_half * second_half).astype(jnp.bfloat16)
    back_branch = upstream.astype(jnp.bfloat16)
    shrink_term = contract_rows(hidden, back_branch)
    back_hidden = contract_cols(back_branch, shrink)
    back_expanded = jnp.concatenate(
        [back_hidden * second_half, back_hidden * first_half], axis=1
    ).astype(jnp.bfloat16)
    expand_term = contract_rows(second, back_expanded)
    back_second = contract_cols(back_expanded, expand)
    back_middle = upstream + norm_back(middle, back_second)
    back_gated = back_middle.astype(jnp.bfloat16)
    output_term = contract_rows(gated_rows, back_gated)
    back_rows_gated = contract_cols(back_gated, output)
    queries, keys_all, unused_values, update = jnp.split(projected, 4, axis=1)
    back_update = back_rows_gated * head_norm(mixture) * silu_slope(update)
    back_mixture = head_back(mixture, back_rows_gated * jax.nn.silu(update)).astype(jnp.bfloat16)
    if local:
        back_queries, back_keys, back_values = local_backward(
            queries, keys_all, values_low, validity, logsum, back_mixture
        )
    else:
        back_queries, back_keys, back_values = linear_backward(
            queries, keys_all, values_low, back_mixture
        )
    back_projected = jnp.concatenate(
        [back_queries, back_keys, back_values, back_update], axis=1
    ).astype(jnp.bfloat16)
    project_term = contract_rows(normed, back_projected)
    back_normed = contract_cols(back_projected, project)
    back_input = back_middle + norm_back(layer_in, back_normed)
    return (back_input, (project_term, output_term, expand_term, shrink_term))


def shards(
    direct,
    tokens,
    lengths,
    local_project,
    local_output,
    local_expand,
    local_shrink,
    linear_project,
    linear_output,
    linear_expand,
    linear_shrink,
    cotangent,
):
    positions = lax.broadcasted_iota(jnp.int32, (tokens.shape[1], 1), 0)
    validity = (positions < lengths[0]).astype(jnp.float32)
    layer_in = tokens[0].astype(jnp.float32) * validity
    shards_of = [
        local_project,
        local_output,
        local_expand,
        local_shrink,
        linear_project,
        linear_output,
        linear_expand,
        linear_shrink,
    ]
    if direct:
        held, tall, result, between, middles, gates, stages, kept = run_forward(
            shards_of, tokens[0], validity
        )
        whole = []
        saved = []
        for layer in range(2):
            mats = held.reshape(2, LAYER_CHUNKS, 2, 1024, WIDTH)[layer]
            project = mats[:8].reshape(4, 2, 2, 1024, WIDTH).transpose(3, 2, 1, 0, 4)
            output = mats[8:10].transpose(2, 1, 0, 3)
            expand = mats[10:].transpose(2, 1, 0, 3)
            whole += [
                project.reshape(1024, 4096),
                output.reshape(1024, 1024),
                expand.reshape(1024, 5632),
                joined(tall[layer].reshape(2, 2816, 512)),
            ]
            source = (layer_in, between)[layer]
            five = stages[layer].transpose(1, 2, 0, 3).reshape(5, ROWS, 1024).astype(jnp.float32)
            projected = jnp.concatenate([five[0], five[1], five[2], five[3]], axis=1)
            projected = jnp.concatenate([five[0], five[1], five[2], five[3]], axis=1)
            queries, keys_all = five[0], five[1]
            logsum = None
            if layer == 0:
                scores = local_scores(queries, keys_all)[2]
                logsum = jax.nn.logsumexp(scores, axis=-1, keepdims=True)
            saved.append(
                (
                    source,
                    simple_norm(source).astype(jnp.bfloat16),
                    projected,
                    five[2].astype(jnp.bfloat16),
                    five[4],
                    logsum,
                    gates[layer],
                    middles[layer],
                    simple_norm(middles[layer]).astype(jnp.bfloat16),
                )
            )
        local_weights, linear_weights = whole[:4], whole[4:]
        local_saved, linear_saved = saved
    else:
        whole = [joined(item) for item in gather_weights(shards_of)]
        local_weights = whole[:4]
        linear_weights = whole[4:]
        between, local_saved = forward_layer(layer_in, validity, local_weights, True)
        result, linear_saved = forward_layer(between, validity, linear_weights, False)
        result = (result * validity).astype(jnp.bfloat16)
    upstream = cotangent[0].astype(jnp.float32) * validity
    back_between, linear_terms = backward_layer(
        upstream, linear_saved, linear_weights, validity, False
    )
    back_input, local_terms = backward_layer(
        back_between, local_saved, local_weights, validity, True
    )
    sums = settle_gradients(
        [halves(item.astype(jnp.bfloat16)) for item in local_terms + linear_terms], direct
    )
    return (
        result[None],
        (back_input * validity)[None],
    ) + tuple(sums)


def solution(mesh):
    in_specs = (
        P(("dp", "fsdp"), None, None),
        P(("dp", "fsdp")),
        P("dp", "fsdp"),
        P("dp", "fsdp"),
        P("dp", "fsdp"),
        P("dp", "fsdp"),
        P("dp", "fsdp"),
        P("dp", "fsdp"),
        P("dp", "fsdp"),
        P("dp", "fsdp"),
        P(("dp", "fsdp"), None, None),
    )
    out_specs = (
        P(("dp", "fsdp"), None, None),
        P(("dp", "fsdp"), None, None),
        P("dp", "fsdp"),
        P("dp", "fsdp"),
        P("dp", "fsdp"),
        P("dp", "fsdp"),
        P("dp", "fsdp"),
        P("dp", "fsdp"),
        P("dp", "fsdp"),
        P("dp", "fsdp"),
    )
    direct = dict(mesh.shape) == {"dp": 16, "fsdp": 2}
    return jax.shard_map(functools.partial(shards, direct), mesh=mesh, in_specs=in_specs, out_specs=out_specs, check_vma=False)
```

```python
import functools

import jax
import jax.numpy as jnp
from jax import lax
from jax.experimental import pallas as pl
from jax.experimental.pallas import tpu as pltpu
from jax.sharding import PartitionSpec as P

HEADS = 16
HEAD = 64
BLOCK = 64


epsilon = 1e-05
highest = lax.Precision.HIGHEST


def simple_norm(values):
    return values * lax.rsqrt(jnp.mean(values * values, axis=-1, keepdims=True) + epsilon)


def norm_back(values, upstream):
    inverse_rms = lax.rsqrt(jnp.mean(values * values, axis=-1, keepdims=True) + epsilon)
    return inverse_rms * (
        upstream
        - values * (inverse_rms * inverse_rms) * jnp.mean(upstream * values, axis=-1, keepdims=True)
    )


def head_norm(values):
    shaped = values.reshape(values.shape[0], HEADS, HEAD)
    return simple_norm(shaped).reshape(values.shape)


def head_back(values, upstream):
    shaped = values.reshape(values.shape[0], HEADS, HEAD)
    coming = upstream.reshape(values.shape[0], HEADS, HEAD)
    return norm_back(shaped, coming).reshape(values.shape)


def silu_slope(values):
    logistic = jax.nn.sigmoid(values)
    return logistic * (1.0 + values * (1.0 - logistic))


def contract_rows(first_matrix, second_matrix):
    return lax.dot_general(
        first_matrix, second_matrix, (((0,), (0,)), ((), ())), preferred_element_type=jnp.float32
    )


def contract_cols(first_matrix, second_matrix):
    return lax.dot_general(
        first_matrix, second_matrix, (((1,), (1,)), ((), ())), preferred_element_type=jnp.float32
    )


def causal_table():
    return lax.broadcasted_iota(jnp.int32, (BLOCK, BLOCK), 0) >= lax.broadcasted_iota(
        jnp.int32, (BLOCK, BLOCK), 1
    )


def split_heads(values):
    return values.reshape(values.shape[0] // BLOCK, BLOCK, HEADS, HEAD)


def join_heads(values):
    return values.reshape(values.shape[0] * BLOCK, HEADS * HEAD)


AXIS_NAMES = ("f", "zh", "zl", "y", "c")
AXIS_OF = {"c": "c", "y": "y", "x": "f", "z1": "zl", "z2": "zh"}
MESH = pl.DeviceIdType.MESH
ANY = pl.BlockSpec(memory_space=pl.ANY)
FULL = pl.BlockSpec(memory_space=pltpu.VMEM)
WEIGHTS = 8
WIDTH = 256
LAG = 3
PHASES = 5
HEAD_GROUPS = 4
PROJECT_CHUNKS = 8
OUTPUT_CHUNKS = 2
EXPAND_CHUNKS = 11
LAYER_CHUNKS = PROJECT_CHUNKS + OUTPUT_CHUNKS + EXPAND_CHUNKS
CHUNKS = 2 * LAYER_CHUNKS
SHRINK_PARTS = 4
SHRINK_WIDTH = 128
GATHER_SLOTS = 8
LOAD_SLOTS = 3
LOW = jnp.bfloat16
WIDE = jnp.float32
ROWS = 512


def neighbours():
    dp = lax.axis_index("dp")
    x = lax.axis_index("fsdp")
    z = dp // 4
    y = (dp // 2) % 2
    c = dp % 2
    places = {"f": x, "zh": z // 2, "zl": z % 2, "y": y, "c": c}
    targets = {
        "z1": ((z + 1 - 2 * (z % 2)) * 4 + y * 2 + c, x),
        "z2": (lax.rem(z + 2, 4) * 4 + y * 2 + c, x),
        "y": (z * 4 + (1 - y) * 2 + c, x),
        "c": (z * 4 + y * 2 + (1 - c), x),
        "x": (dp, 1 - x),
    }
    return places, targets


def greet(targets):
    barrier = pltpu.get_barrier_semaphore()
    for target in targets.values():
        pl.semaphore_signal(barrier, inc=1, device_id=target, device_id_type=MESH)
    pl.semaphore_wait(barrier, len(targets))


def dot(left, right):
    return jnp.dot(left, right, preferred_element_type=WIDE)


def softplus(values):
    return jnp.maximum(values, 0.0) + jnp.log1p(jnp.exp(-jnp.abs(values)))


def logistic(values):
    return 1.0 / (1.0 + jnp.exp(-values))


def first_lanes(rows):
    return lax.broadcasted_iota(jnp.int32, (rows, 128), 1) < HEAD


def pair_mean(values, first):
    left = jnp.sum(jnp.where(first, values, 0.0), axis=-1, keepdims=True)
    right = jnp.sum(jnp.where(first, 0.0, values), axis=-1, keepdims=True)
    return jnp.where(first, left, right) * (1.0 / HEAD)


def block_mask(rows):
    i = lax.broadcasted_iota(jnp.int32, (rows, rows), 0)
    j = lax.broadcasted_iota(jnp.int32, (rows, rows), 1)
    return (i // BLOCK == j // BLOCK) & (j <= i)


def norm_into(source, target):
    def body(t, carry):
        rows = pl.ds(pl.multiple_of(t * 128, 128), 128)
        target[rows, :] = simple_norm(source[rows, :]).astype(LOW)
        return carry

    lax.fori_loop(0, ROWS // 128, body, 0)


def local_mixer(group, parts, validity, gated, stage):
    def body(turn, carry):
        t = turn // 2
        rows = pl.ds(pl.multiple_of(t * 128, 128), 128)
        pair = turn % 2
        lanes = pl.ds(pl.multiple_of(pair * 128, 128), 128)
        first = first_lanes(128)
        q = parts[0, 0, rows, lanes].astype(LOW)
        k = parts[1, 0, rows, lanes].astype(LOW)
        v = parts[0, 1, rows, lanes].astype(LOW)
        u = parts[1, 1, rows, lanes]
        keep = block_mask(128)
        mixed = []
        for head in range(2):
            mine = jnp.where(first == (head == 0), q, jnp.zeros_like(q))
            scores = contract_cols(mine, k) * HEAD ** (-0.5)
            scores = jnp.where(keep, scores, -1e30)
            highest_score = jnp.max(scores, axis=-1, keepdims=True)
            weights = jnp.exp(scores - highest_score)
            attend = weights / jnp.sum(weights, axis=-1, keepdims=True)
            mixed.append(dot(attend.astype(LOW), v))
        mixture = jnp.where(first, mixed[0], mixed[1]) * validity[rows, :]
        scale = lax.rsqrt(pair_mean(mixture * mixture, first) + epsilon)
        columns = pl.ds(pl.multiple_of(group * WIDTH + pair * 128, 128), 128)
        gated[rows, columns] = (mixture * scale * (u * logistic(u))).astype(LOW)
        stage[4, rows, lanes] = mixture.astype(LOW)
        return carry

    lax.fori_loop(0, 2 * ROWS // 128, body, 0)


def linear_mixer(group, parts, gated, stage):
    half = ROWS // 2

    def body(pair, carry):
        lanes = pl.ds(pl.multiple_of(pair * 128, 128), 128)
        columns = pl.ds(pl.multiple_of(group * WIDTH + pair * 128, 128), 128)
        first = first_lanes(half)
        fk = softplus(parts[1, 0, :, lanes]).astype(LOW)
        v = parts[0, 1, :, lanes].astype(LOW)
        for t in range(2):
            rows = pl.ds(t * half, half)
            reach = (t + 1) * half
            fq = softplus(parts[0, 0, rows, lanes]).astype(LOW)
            i = lax.broadcasted_iota(jnp.int32, (half, reach), 0) + t * half
            j = lax.broadcasted_iota(jnp.int32, (half, reach), 1)
            mixed = []
            for head in range(2):
                mine = jnp.where(first == (head == 0), fq, jnp.zeros_like(fq))
                scores = jnp.where(j <= i, contract_cols(mine, fk[:reach]), 0.0).astype(LOW)
                mixed.append(dot(scores, v[:reach]))
            mixture = jnp.where(first, mixed[0], mixed[1])
            scale = lax.rsqrt(pair_mean(mixture * mixture, first) + epsilon)
            u = parts[1, 1, rows, lanes]
            gated[rows, columns] = (mixture * scale * (u * logistic(u))).astype(LOW)
            stage[4, rows, lanes] = mixture.astype(LOW)
        return carry

    lax.fori_loop(0, 2, body, 0)


def chunk_columns(weight, part):
    if weight == 0:
        return (part % 2) * 1024 + (part // 2) * WIDTH
    return part * WIDTH


class Gather:
    def __init__(self, own, held, tall, sems):
        self.own, self.held, self.tall = own, held, tall
        self.local_sem, self.send_sem, self.recv_sem, self.tall_send, self.tall_recv = sems
        self.places, self.targets = neighbours()
        self.at = tuple(self.places[name] for name in ("f", "zh", "zl", "y", "c"))

    def begin(self):
        counts = (PROJECT_CHUNKS, OUTPUT_CHUNKS, EXPAND_CHUNKS)
        for layer in range(2):
            chunk = LAYER_CHUNKS * layer
            for weight in range(3):
                for part in range(counts[weight]):
                    start = chunk_columns(weight, part)
                    pltpu.make_async_copy(
                        self.own[4 * layer + weight].at[:, pl.ds(start, WIDTH)],
                        self.held.at[(chunk,) + self.at],
                        self.local_sem.at[chunk],
                    ).start()
                    chunk += 1
            pltpu.make_async_copy(
                self.own[4 * layer + 3],
                self.tall.at[(layer,) + self.at],
                self.local_sem.at[CHUNKS + layer],
            ).start()
        greet(self.targets)

    def message(self, block, target, sems, place):
        return pltpu.make_async_remote_copy(
            src_ref=block,
            dst_ref=block,
            send_sem=sems[0].at[place],
            recv_sem=sems[1].at[place],
            device_id=self.targets[target],
            device_id_type=MESH,
        )

    def wide_messages(self, phase, chunk):
        x, zh, zl, y, c = self.at
        ref = self.held
        sems = (self.send_sem, self.recv_sem)
        slot = chunk % GATHER_SLOTS
        half = WIDTH // 2
        low, high = pl.ds(0, half), pl.ds(half, half)

        def one(index, target, part):
            return self.message(ref.at[(chunk,) + index], target, sems, (2 * phase + part, slot))

        a = slice(None)
        if phase == 0:
            return [one((x, zh, zl, y, c), "z2", 0)]
        if phase == 1:
            return [one((x, a, zl, y, c), "z1", 0)]
        if phase == 2:
            return [one((x, a, a, y, c, a, low), "x", 0), one((x, a, a, y, c, a, high), "y", 1)]
        if phase == 3:
            return [one((a, a, a, y, c, a, low), "y", 0), one((x, a, a, a, c, a, high), "x", 1)]
        return [one((a, a, a, a, c), "c", 0)]

    def tall_message(self, phase, layer, part, odd):
        x, zh, zl, y, c = self.at
        a = slice(None)
        lanes = pl.ds(pl.multiple_of(part * SHRINK_WIDTH, SHRINK_WIDTH), SHRINK_WIDTH)
        index, target = {
            (0, 0): ((x, zh, zl, y, c), "x"),
            (0, 1): ((x, zh, zl, y, c), "y"),
            (1, 0): ((a, zh, zl, y, c), "y"),
            (1, 1): ((x, zh, zl, a, c), "x"),
            (2, 0): ((a, zh, zl, a, c), "z2"),
            (3, 0): ((a, a, zl, a, c), "z1"),
            (4, 0): ((a, a, a, a, c), "c"),
        }[(phase, odd)]
        return self.message(
            self.tall.at[(layer,) + index + (a, lanes)],
            target,
            (self.tall_send, self.tall_recv),
            (phase, layer * SHRINK_PARTS + part),
        )

    def tall_turn(self, chunk):
        layer = chunk // LAYER_CHUNKS
        place = chunk % LAYER_CHUNKS
        return layer, place // 5, place % 5 == 4

    def for_tall(self, phase, chunk, act):
        layer, part, due = self.tall_turn(chunk)
        if phase >= 2:
            pl.when(due)(lambda: act(self.tall_message(phase, layer, part, 0)))
        else:
            for odd in range(2):
                pl.when(due & (part % 2 == odd))(
                    lambda odd=odd: act(self.tall_message(phase, layer, part, odd))
                )

    def step(self, step):
        for phase in range(PHASES, -1, -1):
            chunk = step - phase * LAG

            @pl.when((chunk >= 0) & (chunk < CHUNKS))
            def _(phase=phase, chunk=chunk):
                if phase >= 1:
                    for copy in self.wide_messages(phase - 1, chunk):
                        copy.wait()
                    self.for_tall(phase - 1, chunk, lambda copy: copy.wait())
                else:
                    pltpu.make_async_copy(
                        self.own[0].at[:, pl.ds(0, WIDTH)],
                        self.held.at[(chunk,) + self.at],
                        self.local_sem.at[chunk],
                    ).wait()
                    layer = chunk // LAYER_CHUNKS

                    @pl.when(chunk % LAYER_CHUNKS == 4)
                    def _():
                        pltpu.make_async_copy(
                            self.own[3],
                            self.tall.at[(layer,) + self.at],
                            self.local_sem.at[CHUNKS + layer],
                        ).wait()

                if phase < PHASES:
                    for copy in self.wide_messages(phase, chunk):
                        copy.start()
                    self.for_tall(phase, chunk, lambda copy: copy.start())


def forward_kernel(*refs):
    own = refs[:WEIGHTS]
    tokens, validity = refs[WEIGHTS : WEIGHTS + 2]
    held, tall, mixed_out, between, middles, gates, stages, halves_out = refs[10:18]
    scratch = refs[18:]
    sems, (load_sem, tall_sem, stage_sem, half_sem, misc_sem) = scratch[:5], scratch[5:10]
    loaded, shrink, x, middle, normed, gated, hidden, parts, stage, half_stage, final = scratch[10:]
    gather = Gather(own, held, tall, sems)
    gather.begin()

    def rows_of(t):
        return pl.ds(pl.multiple_of(t * 128, 128), 128)

    def start_rows(t, carry):
        rows = rows_of(t)
        x[rows, :] = tokens[rows, :].astype(WIDE) * validity[rows, :]
        return carry

    lax.fori_loop(0, ROWS // 128, start_rows, 0)
    norm_into(x, normed)

    def load(chunk):
        return pltpu.make_async_copy(
            held.at[chunk], loaded.at[chunk % LOAD_SLOTS], load_sem.at[chunk % LOAD_SLOTS]
        )

    def load_tall(layer):
        return pltpu.make_async_copy(tall.at[layer], shrink, tall_sem)

    def keep_stage(layer, group):
        return pltpu.make_async_copy(stage, stages.at[layer, group], stage_sem)

    def keep_half(layer, part):
        return pltpu.make_async_copy(
            half_stage.at[part % 2], halves_out.at[layer, part], half_sem.at[part % 2]
        )

    def keep(kind, layer):
        source, target = ((gated, gates), (middle, middles))[kind]
        return pltpu.make_async_copy(source, target.at[layer], misc_sem.at[kind])

    def keep_between():
        return pltpu.make_async_copy(x, between, misc_sem.at[2])

    def weight(slot, f):
        return loaded[slot, f].reshape(1024, WIDTH)

    def project_step(layer, place, slot):
        group = place // 2
        for f in range(2):
            parts[place % 2, f] = dot(normed[...], weight(slot, f))

        @pl.when(place % 2 == 1)
        def _():
            @pl.when((layer > 0) | (group > 0))
            def _():
                keep_stage(layer, group).wait()

            @pl.when((layer > 0) & (group == 0))
            def _():
                keep(0, 0).wait()

            for kind in range(4):
                stage[kind] = parts[kind % 2, kind // 2].astype(LOW)
            pl.when(layer == 0)(lambda: local_mixer(group, parts, validity, gated, stage))
            pl.when(layer > 0)(lambda: linear_mixer(group, parts, gated, stage))
            keep_stage(layer, group).start()

    def output_step(layer, part, slot):
        @pl.when(part == 0)
        def _():
            keep(0, layer).start()

            @pl.when(layer > 0)
            def _():
                keep(1, 0).wait()

        for f in range(2):
            lanes = pl.ds(pl.multiple_of(f * 512 + part * WIDTH, WIDTH), WIDTH)
            middle[:, lanes] = x[:, lanes] + dot(gated[...], weight(slot, f))

        @pl.when(part == OUTPUT_CHUNKS - 1)
        def _():
            keep(1, layer).start()
            norm_into(middle, normed)

    def expand_step(layer, part, slot):
        @pl.when((layer > 0) | (part > 1))
        def _():
            keep_half(layer, part).wait()

        first = dot(normed[...], weight(slot, 0))
        second = dot(normed[...], weight(slot, 1))
        half_stage[part % 2, 0] = first.astype(LOW)
        half_stage[part % 2, 1] = second.astype(LOW)
        hidden[:, pl.ds(pl.multiple_of(part * WIDTH, WIDTH), WIDTH)] = (first * second).astype(LOW)
        keep_half(layer, part).start()

    def shrink_step(layer):
        load_tall(layer).wait()

        @pl.when(layer > 0)
        def _():
            keep_between().wait()

        def body(turn, carry):
            f = turn // 2
            columns = pl.ds(pl.multiple_of((turn % 2) * WIDTH, WIDTH), WIDTH)
            lanes = pl.ds(pl.multiple_of(turn * WIDTH, WIDTH), WIDTH)
            matrix = shrink[f, :, :, :, :, :, columns].reshape(hidden.shape[1], WIDTH)
            x[:, lanes] = middle[:, lanes] + dot(hidden[...], matrix)
            return carry

        lax.fori_loop(0, 4, body, 0)

        @pl.when(layer == 0)
        def _():
            keep_between().start()
            norm_into(x, normed)

        @pl.when(layer > 0)
        def _():
            def last_rows(t, carry):
                rows = rows_of(t)
                final[rows, :] = (x[rows, :] * validity[rows, :]).astype(LOW)
                return carry

            lax.fori_loop(0, ROWS // 128, last_rows, 0)

    def body(step, carry):
        gather.step(step)
        arrived = step - PHASES * LAG

        @pl.when((arrived >= 0) & (arrived < CHUNKS))
        def _():
            load(arrived).start()

            @pl.when(arrived % LAYER_CHUNKS == LAYER_CHUNKS - 2)
            def _():
                load_tall(arrived // LAYER_CHUNKS).start()

        ready = arrived - 1

        @pl.when((ready >= 0) & (ready < CHUNKS))
        def _():
            load(ready).wait()
            layer = ready // LAYER_CHUNKS
            place = ready % LAYER_CHUNKS
            slot = ready % LOAD_SLOTS
            pl.when(place < PROJECT_CHUNKS)(lambda: project_step(layer, place, slot))
            pl.when((place >= PROJECT_CHUNKS) & (place < PROJECT_CHUNKS + OUTPUT_CHUNKS))(
                lambda: output_step(layer, place - PROJECT_CHUNKS, slot)
            )
            pl.when(place >= PROJECT_CHUNKS + OUTPUT_CHUNKS)(
                lambda: expand_step(layer, place - PROJECT_CHUNKS - OUTPUT_CHUNKS, slot)
            )
            pl.when(place == LAYER_CHUNKS - 1)(lambda: shrink_step(layer))

        return carry

    lax.fori_loop(0, CHUNKS + PHASES * LAG + 1, body, 0)
    last = pltpu.make_async_copy(final, mixed_out, misc_sem.at[3])
    last.start()
    keep_stage(1, HEAD_GROUPS - 1).wait()
    keep(0, 1).wait()
    keep(1, 1).wait()
    keep_half(1, EXPAND_CHUNKS - 2).wait()
    keep_half(1, EXPAND_CHUNKS - 1).wait()
    last.wait()


def run_forward(shards_of, tokens, validity):
    bits = (2, 2, 2, 2, 2)
    struct = jax.ShapeDtypeStruct
    return pl.pallas_call(
        forward_kernel,
        out_shape=(
            struct((CHUNKS,) + bits + (64, WIDTH), LOW),
            struct((2,) + bits + (176, 512), LOW),
            struct((ROWS, 1024), LOW),
            struct((ROWS, 1024), WIDE),
            struct((2, ROWS, 1024), WIDE),
            struct((2, ROWS, 1024), LOW),
            struct((2, HEAD_GROUPS, 5, ROWS, WIDTH), LOW),
            struct((2, EXPAND_CHUNKS, 2, ROWS, WIDTH), LOW),
        ),
        in_specs=[ANY] * WEIGHTS + [FULL, FULL],
        out_specs=(ANY,) * 8,
        scratch_shapes=[
            pltpu.SemaphoreType.DMA((CHUNKS + 2,)),
            pltpu.SemaphoreType.DMA((10, GATHER_SLOTS)),
            pltpu.SemaphoreType.DMA((10, GATHER_SLOTS)),
            pltpu.SemaphoreType.DMA((PHASES, 2 * SHRINK_PARTS)),
            pltpu.SemaphoreType.DMA((PHASES, 2 * SHRINK_PARTS)),
            pltpu.SemaphoreType.DMA((LOAD_SLOTS,)),
            pltpu.SemaphoreType.DMA,
            pltpu.SemaphoreType.DMA,
            pltpu.SemaphoreType.DMA((2,)),
            pltpu.SemaphoreType.DMA((4,)),
            pltpu.VMEM((LOAD_SLOTS,) + bits + (64, WIDTH), LOW),
            pltpu.VMEM(bits + (176, 512), LOW),
            pltpu.VMEM((ROWS, 1024), WIDE),
            pltpu.VMEM((ROWS, 1024), WIDE),
            pltpu.VMEM((ROWS, 1024), LOW),
            pltpu.VMEM((ROWS, 1024), LOW),
            pltpu.VMEM((ROWS, 2816), LOW),
            pltpu.VMEM((2, 2, ROWS, WIDTH), WIDE),
            pltpu.VMEM((5, ROWS, WIDTH), LOW),
            pltpu.VMEM((2, 2, ROWS, WIDTH), LOW),
            pltpu.VMEM((ROWS, 1024), LOW),
        ],
        compiler_params=pltpu.CompilerParams(
            collective_id=0, has_side_effects=True, vmem_limit_bytes=60 << 20
        ),
    )(*shards_of, tokens, validity)


SCATTER_LAG = 3
SCATTER_SLOTS = 3 * SCATTER_LAG + 1
TERM_SLOTS = SCATTER_LAG
TALL_SLOTS = 6
TALL_TERM_SLOTS = 2
OUTPUT_TURN = EXPAND_CHUNKS
PROJECT_TURN = EXPAND_CHUNKS + OUTPUT_CHUNKS
TALL_ROWS = 176


class Scatter:
    def __init__(self, outs, sems, wide, tall):
        self.outs, self.tall_outs = outs
        self.send_sem, self.recv_sem, self.tall_send, self.tall_recv = sems[:4]
        self.store_sem, self.tall_store = sems[4:]
        self.wide, self.tall = wide[:6], tall[:6]
        self.result, self.tall_result = wide[6], tall[6]
        self.places, self.targets = neighbours()

    def tall_turn(self, chunk):
        layer = chunk // LAYER_CHUNKS
        turn = chunk % LAYER_CHUNKS - OUTPUT_TURN
        due = (turn >= 0) & (turn < 2 * SHRINK_PARTS) & (turn % 2 == 0)
        return layer * SHRINK_PARTS + turn // 2, turn // 2, due

    def wide_parts(self):
        half = WIDTH // 2
        return (
            (pl.ds(0, half), ("c", "y", "x", "z1", "z2")),
            (pl.ds(half, half), ("c", "x", "y", "z1", "z2")),
        )

    def tall_parts(self, odd):
        plane = ("x", "y") if odd else ("y", "x")
        return ((pl.ds(0, SHRINK_WIDTH), ("c", "z1", "z2") + plane),)

    def left(self, order, phase):
        used = set(AXIS_OF[target] for target in order[: phase + 1])
        return [name for name in AXIS_NAMES if name not in used]

    def source(self, buffers, slots, phase, order):
        if phase == 0:
            return buffers[0].at[slots[0]], list(AXIS_NAMES)
        return buffers[phase].at[slots[1]], self.left(order, phase - 1)

    def messages(self, buffers, slots, sems, phase, parts):
        if phase == 0 and len(parts) == 2:
            parts = ((pl.ds(0, WIDTH), parts[0][1]),)
        out = []
        for part, (lanes, order) in enumerate(parts):
            source, dims = self.source(buffers, slots, phase, order)
            target = order[phase]
            away = tuple(
                1 - self.places[d] if d == AXIS_OF[target] else slice(None) for d in dims
            )
            whole = tuple(slice(None) for _ in self.left(order, phase))
            place = (2 * phase + part, slots[1])
            out.append(
                pltpu.make_async_remote_copy(
                    src_ref=source.at[away + (slice(None), lanes)],
                    dst_ref=buffers[1 + phase].at[(slots[1],) + whole + (slice(None), lanes)],
                    send_sem=sems[0].at[place],
                    recv_sem=sems[1].at[place],
                    device_id=self.targets[target],
                    device_id_type=MESH,
                )
            )
        return out

    def add(self, buffers, slots, phase, parts, result):
        for lanes, order in parts:
            source, dims = self.source(buffers, slots, phase, order)
            cut = AXIS_OF[order[phase]]
            kept = self.left(order, phase)
            ref = buffers[1 + phase].at[slots[1]]

            def body(unit, carry):
                index = tuple((unit // 2 ** (len(kept) - 1 - b)) % 2 for b in range(len(kept)))
                where = dict(zip(kept, index))
                where[cut] = self.places[cut]
                mine = source[tuple(where[d] for d in dims) + (slice(None), lanes)]
                came = ref[index + (slice(None), lanes)]
                if phase < 4:
                    ref[index + (slice(None), lanes)] = came + mine
                else:
                    result[:, lanes] = came.astype(WIDE) + mine.astype(WIDE)
                return carry

            if kept:
                lax.fori_loop(0, 2 ** len(kept), body, 0)
            else:
                body(0, 0)

    def wide_slots(self, chunk):
        return (chunk % TERM_SLOTS, chunk % SCATTER_SLOTS)

    def tall_slots(self, place):
        return (place % TALL_TERM_SLOTS, place % TALL_SLOTS)

    def wide_messages(self, phase, chunk):
        return self.messages(
            self.wide,
            self.wide_slots(chunk),
            (self.send_sem, self.recv_sem),
            phase,
            self.wide_parts(),
        )

    def tall_messages(self, phase, place, odd):
        return self.messages(
            self.tall,
            self.tall_slots(place),
            (self.tall_send, self.tall_recv),
            phase,
            self.tall_parts(odd),
        )

    def store(self, chunk):
        return pltpu.make_async_copy(
            self.result.at[chunk % 2], self.outs.at[chunk], self.store_sem.at[chunk % 2]
        )

    def store_tall(self, place):
        return pltpu.make_async_copy(
            self.tall_result.at[place % 2], self.tall_outs.at[place], self.tall_store.at[place % 2]
        )

    def start(self, phase, chunk):
        for copy in self.wide_messages(phase, chunk):
            copy.start()
        place, part, due = self.tall_turn(chunk)
        for odd in range(2):

            @pl.when(due & (part % 2 == odd))
            def _(odd=odd):
                for copy in self.tall_messages(phase, place, odd):
                    copy.start()

    def take(self, phase, chunk):
        for copy in self.wide_messages(phase, chunk):
            copy.wait()
        if phase == PHASES - 1:
            pl.when(chunk >= 2)(lambda: self.store(chunk).wait())
        self.add(
            self.wide, self.wide_slots(chunk), phase, self.wide_parts(), self.result.at[chunk % 2]
        )
        place, part, due = self.tall_turn(chunk)
        for odd in range(2):

            @pl.when(due & (part % 2 == odd))
            def _(odd=odd):
                for copy in self.tall_messages(phase, place, odd):
                    copy.wait()
                if phase == PHASES - 1:
                    pl.when(place >= 2)(lambda: self.store_tall(place).wait())
                self.add(
                    self.tall,
                    self.tall_slots(place),
                    phase,
                    self.tall_parts(odd),
                    self.tall_result.at[place % 2],
                )
                if phase == PHASES - 1:
                    self.store_tall(place).start()

        if phase == PHASES - 1:
            self.store(chunk).start()

    def older(self, step):
        for phase in range(PHASES, 0, -1):
            chunk = step - phase * SCATTER_LAG

            @pl.when((chunk >= 0) & (chunk < CHUNKS))
            def _(phase=phase, chunk=chunk):
                self.take(phase - 1, chunk)
                if phase < PHASES:
                    self.start(phase, chunk)

    def finish(self):
        for chunk in (CHUNKS - 2, CHUNKS - 1):
            self.store(chunk).wait()
        for place in (2 * SHRINK_PARTS - 2, 2 * SHRINK_PARTS - 1):
            self.store_tall(place).wait()


def norm_slope(values, inverse, upstream, mean):
    return inverse * (upstream - values * (inverse * inverse) * mean)


def gate_back(update, mixture, coming, first):
    inverse = lax.rsqrt(pair_mean(mixture * mixture, first) + epsilon)
    curve = logistic(update)
    back_update = coming * (mixture * inverse) * (curve * (1.0 + update * (1.0 - curve)))
    gate = coming * (update * curve)
    back_mixture = norm_slope(mixture, inverse, gate, pair_mean(gate * mixture, first))
    return back_update, back_mixture


def local_mixer_back(group, stage, validity, coming, back):
    def body(turn, carry):
        rows = pl.ds(pl.multiple_of((turn // 2) * 128, 128), 128)
        lanes = pl.ds(pl.multiple_of((turn % 2) * 128, 128), 128)
        columns = pl.ds(pl.multiple_of(group * WIDTH + (turn % 2) * 128, 128), 128)
        first = first_lanes(128)
        q, k, v = stage[0, rows, lanes], stage[1, rows, lanes], stage[2, rows, lanes]
        update = stage[3, rows, lanes].astype(WIDE)
        mixture = stage[4, rows, lanes].astype(WIDE)
        back_update, back_mixture = gate_back(update, mixture, coming[rows, columns], first)
        back[1, 1, rows, lanes] = back_update.astype(LOW)
        grad = (back_mixture.astype(LOW).astype(WIDE) * validity[rows, :]).astype(LOW)
        keep = block_mask(128)
        zero = jnp.zeros_like(q)
        out = []
        for head in range(2):
            here = first == (head == 0)
            scores = contract_cols(jnp.where(here, q, zero), k) * HEAD ** (-0.5)
            scores = jnp.where(keep, scores, -1e30)
            weights = jnp.exp(scores - jnp.max(scores, axis=-1, keepdims=True))
            attend = weights / jnp.sum(weights, axis=-1, keepdims=True)
            back_attend = contract_cols(jnp.where(here, grad, zero), v)
            total = jnp.sum(back_attend * attend, axis=-1, keepdims=True)
            back_scores = (attend * (back_attend - total)).astype(LOW)
            out.append(
                (
                    dot(back_scores, k) * HEAD ** (-0.5),
                    contract_rows(back_scores, q) * HEAD ** (-0.5),
                    contract_rows(attend.astype(LOW), grad),
                )
            )
        for kind, (i, j) in enumerate(((0, 0), (1, 0), (0, 1))):
            back[i, j, rows, lanes] = jnp.where(first, out[0][kind], out[1][kind]).astype(LOW)
        return carry

    lax.fori_loop(0, 2 * ROWS // 128, body, 0)


def linear_mixer_back(group, stage, coming, back):
    half = ROWS // 2

    def body(pair, carry):
        lanes = pl.ds(pl.multiple_of(pair * 128, 128), 128)
        columns = pl.ds(pl.multiple_of(group * WIDTH + pair * 128, 128), 128)
        first = first_lanes(ROWS)
        queries = stage[0, :, lanes].astype(WIDE)
        keys_all = stage[1, :, lanes].astype(WIDE)
        v = stage[2, :, lanes]
        fq = softplus(queries).astype(LOW)
        fk = softplus(keys_all).astype(LOW)
        update = stage[3, :, lanes].astype(WIDE)
        mixture = stage[4, :, lanes].astype(WIDE)
        back_update, back_mixture = gate_back(update, mixture, coming[:, columns], first)
        back[1, 1, :, lanes] = back_update.astype(LOW)
        grad = back_mixture.astype(LOW)
        zero = jnp.zeros((half, 128), LOW)
        tiles = []
        for t in range(2):
            reach = (t + 1) * half
            i = lax.broadcasted_iota(jnp.int32, (half, reach), 0) + t * half
            j = lax.broadcasted_iota(jnp.int32, (half, reach), 1)
            mine_q = fq[t * half : reach]
            mine_g = grad[t * half : reach]
            out = []
            for head in range(2):
                here = first[:half] == (head == 0)
                scores = contract_cols(jnp.where(here, mine_q, zero), fk[:reach])
                scores = jnp.where(j <= i, scores, 0.0).astype(LOW)
                inner = contract_cols(jnp.where(here, mine_g, zero), v[:reach])
                inner = jnp.where(j <= i, inner, 0.0).astype(LOW)
                out.append(
                    (dot(inner, fk[:reach]), contract_rows(inner, mine_q), contract_rows(scores, mine_g))
                )
            tiles.append(
                [jnp.where(first[: out[0][n].shape[0]], out[0][n], out[1][n]) for n in range(3)]
            )
        for t in range(2):
            rows = pl.ds(t * half, half)
            span = slice(t * half, (t + 1) * half)
            back_q = tiles[t][0]
            back_k = tiles[1][1][span]
            back_v = tiles[1][2][span]
            if t == 0:
                back_k = back_k + tiles[0][1]
                back_v = back_v + tiles[0][2]
            back[0, 0, rows, lanes] = (back_q * logistic(queries[span])).astype(LOW)
            back[1, 0, rows, lanes] = (back_k * logistic(keys_all[span])).astype(LOW)
            back[0, 1, rows, lanes] = back_v.astype(LOW)
        return carry

    lax.fori_loop(0, 2, body, 0)


def over_rows(act):
    def body(t, carry):
        act(pl.ds(pl.multiple_of(t * 128, 128), 128))
        return carry

    lax.fori_loop(0, ROWS // 128, body, 0)


def backward_kernel(*refs):
    cotangent, tokens, validity = refs[:3]
    held, tall, between, middles, gates, stages, halves_in = refs[3:10]
    tokens_out, outs, tall_outs = refs[10:13]
    scratch = refs[13:]
    scatter_sems, loads = scratch[:6], scratch[6:10]
    load_sem, half_sem, stage_sem, misc_sem = loads
    wide_buffers, tall_buffers = scratch[10:17], scratch[17:24]
    (
        loaded,
        half_in,
        stage,
        shrink,
        hidden_turned,
        branch,
        gated_branch,
        up,
        sums,
        middle,
        layer_in,
        gated,
        turned,
        back,
    ) = scratch[24:]
    scatter = Scatter((outs, tall_outs), scatter_sems, wide_buffers, tall_buffers)

    def load(chunk, number):
        return pltpu.make_async_copy(
            held.at[chunk], loaded.at[number % 2], load_sem.at[number % 2]
        )

    def load_half(layer, part, number):
        return pltpu.make_async_copy(
            halves_in.at[layer, part], half_in.at[number % 2], half_sem.at[number % 2]
        )

    def load_stage(layer, group):
        return pltpu.make_async_copy(stages.at[layer, group], stage, stage_sem)

    def fetch(kind, layer):
        source, target = (
            (tall, shrink),
            (middles, middle),
            (gates, gated),
        )[kind]
        return pltpu.make_async_copy(source.at[layer], target, misc_sem.at[kind])

    def fetch_between():
        return pltpu.make_async_copy(between, layer_in, misc_sem.at[3])

    def prefetch(number):
        layer = 1 - number // LAYER_CHUNKS
        turn = number % LAYER_CHUNKS
        base = LAYER_CHUNKS * layer

        @pl.when(turn < OUTPUT_TURN)
        def _():
            load(base + PROJECT_CHUNKS + OUTPUT_CHUNKS + turn, number).start()
            load_half(layer, turn, number).start()

        @pl.when((turn >= OUTPUT_TURN) & (turn < PROJECT_TURN))
        def _():
            load(base + PROJECT_CHUNKS + turn - OUTPUT_TURN, number).start()

        @pl.when(turn >= PROJECT_TURN)
        def _():
            load(base + turn - PROJECT_TURN, number).start()

            @pl.when((turn - PROJECT_TURN) % 2 == 0)
            def _():
                load_stage(layer, (turn - PROJECT_TURN) // 2).start()

    prefetch(jnp.int32(0))
    for kind in range(3):
        fetch(kind, 1).start()
    fetch_between().start()

    def begin_rows(rows):
        up[rows, :] = cotangent[rows, :].astype(WIDE) * validity[rows, :]

    over_rows(begin_rows)
    greet(scatter.targets)

    def turn_norm(source):
        def act(rows):
            turned[:, rows] = simple_norm(source[rows, :]).astype(LOW).T

        over_rows(act)

    def expand_start(layer):
        fetch(0, 1).wait()
        fetch(1, 1).wait()

        def act(rows):
            branch[rows, :] = up[rows, :].astype(LOW)
            sums[0, rows, :] = jnp.zeros((128, 1024), WIDE)

        over_rows(act)
        turn_norm(middle)

    def expand_turn(part, number):
        load_half(0, 0, number).wait()
        rows = pl.ds(pl.multiple_of(part * WIDTH, WIDTH), WIDTH)
        back_hidden = contract_cols(branch[:, :512], shrink[0, rows, :])
        back_hidden = back_hidden + contract_cols(branch[:, 512:], shrink[1, rows, :])
        first = half_in[number % 2, 0].astype(WIDE)
        second = half_in[number % 2, 1].astype(WIDE)
        back[0, 0] = (back_hidden * second).astype(LOW)
        back[0, 1] = (back_hidden * first).astype(LOW)
        hidden_turned[rows, :] = (first * second).astype(LOW).T

    def output_start(layer):
        fetch(2, 1).wait()

        def act(rows):
            values = middle[rows, :]
            back_second = sums[0, rows, :]
            new = up[rows, :] + norm_back(values, back_second)
            up[rows, :] = new
            gated_branch[rows, :] = new.astype(LOW)
            sums[1, rows, :] = jnp.zeros((128, 1024), WIDE)
            turned[:, rows] = gated[rows, :].T

        over_rows(act)

        @pl.when(layer == 1)
        def _():
            fetch(0, 0).start()

    def output_turn(part):
        for f in range(2):
            lanes = pl.ds(pl.multiple_of(f * 512 + part * WIDTH, WIDTH), WIDTH)
            back[0, f] = gated_branch[:, lanes]

    def project_start(layer):
        @pl.when(layer == 1)
        def _():
            fetch_between().wait()
            fetch(1, 0).start()
            fetch(2, 0).start()

        @pl.when(layer == 0)
        def _():
            def act(rows):
                layer_in[rows, :] = tokens[rows, :].astype(WIDE) * validity[rows, :]

            over_rows(act)

        def clear(rows):
            sums[0, rows, :] = jnp.zeros((128, 1024), WIDE)

        over_rows(clear)
        turn_norm(layer_in)

    def project_turn(layer, group):
        load_stage(0, 0).wait()
        coming = sums.at[1]
        pl.when(layer == 1)(lambda: linear_mixer_back(group, stage, coming, back))
        pl.when(layer == 0)(lambda: local_mixer_back(group, stage, validity, coming, back))

    def finish_layer(layer):
        def act(rows):
            up[rows, :] = up[rows, :] + norm_back(layer_in[rows, :], sums[0, rows, :])

        over_rows(act)

    def terms(number, which):
        slot = number % TERM_SLOTS
        out = wide_buffers[0]

        def body(tile, carry):
            f = tile // 4
            rows = pl.ds(pl.multiple_of((tile % 4) * 256, 256), 256)
            value = dot(turned[rows, :], back[which, f]).astype(LOW)
            out[slot, f, (tile % 4) // 2, tile % 2] = value.reshape(2, 2, 64, WIDTH)
            return carry

        lax.fori_loop(0, 8, body, 0)

    def tall_terms(place, part):
        slot = place % TALL_TERM_SLOTS
        out = tall_buffers[0]

        def body(tile, carry):
            f = tile // 4
            rows = pl.ds(pl.multiple_of((tile % 4) * 4 * TALL_ROWS, 4 * TALL_ROWS), 4 * TALL_ROWS)
            lanes = pl.ds(pl.multiple_of(f * 512 + part * SHRINK_WIDTH, 128), SHRINK_WIDTH)
            value = dot(hidden_turned[rows, :], branch[:, lanes]).astype(LOW)
            out[slot, f, (tile % 4) // 2, tile % 2] = value.reshape(2, 2, TALL_ROWS, SHRINK_WIDTH)
            return carry

        lax.fori_loop(0, 8, body, 0)

    def spread(number, which, kind):
        def body(t, carry):
            rows = pl.ds(pl.multiple_of(t * 256, 256), 256)
            value = contract_cols(back[which, 0, rows, :], loaded[number % 2, 0])
            value = value + contract_cols(back[which, 1, rows, :], loaded[number % 2, 1])
            sums[kind, rows, :] = sums[kind, rows, :] + value
            return carry

        lax.fori_loop(0, 2, body, 0)

    def body(step, carry):
        pl.when(step + 1 < CHUNKS)(lambda: prefetch(step + 1))
        scatter.older(step)

        @pl.when(step < CHUNKS)
        def _():
            layer = 1 - step // LAYER_CHUNKS
            turn = step % LAYER_CHUNKS
            pl.when(turn == 0)(lambda: expand_start(layer))
            pl.when(turn == OUTPUT_TURN)(lambda: output_start(layer))
            pl.when(turn == PROJECT_TURN)(lambda: project_start(layer))
            pl.when(turn < OUTPUT_TURN)(lambda: expand_turn(turn, step))
            pl.when((turn >= OUTPUT_TURN) & (turn < PROJECT_TURN))(
                lambda: output_turn(turn - OUTPUT_TURN)
            )
            pl.when((turn >= PROJECT_TURN) & ((turn - PROJECT_TURN) % 2 == 0))(
                lambda: project_turn(layer, (turn - PROJECT_TURN) // 2)
            )
            in_project = jnp.minimum(jnp.maximum(turn - PROJECT_TURN + 1, 0), 1)
            in_output = jnp.minimum(jnp.maximum(turn - OUTPUT_TURN + 1, 0), 1) - in_project
            which = in_project * ((turn + PROJECT_TURN) % 2)
            terms(step, which)
            place, part, due = scatter.tall_turn(step)
            pl.when(due)(lambda: tall_terms(place, part))
            scatter.start(0, step)
            load(0, step).wait()
            spread(step, which, in_output)
            pl.when(turn == LAYER_CHUNKS - 1)(lambda: finish_layer(layer))

            @pl.when(step == CHUNKS - 1)
            def _():
                def act(rows):
                    up[rows, :] = up[rows, :] * validity[rows, :]

                over_rows(act)
                pltpu.make_async_copy(up, tokens_out, misc_sem.at[3]).start()

        return carry

    lax.fori_loop(0, CHUNKS + PHASES * SCATTER_LAG, body, 0)
    pltpu.make_async_copy(up, tokens_out, misc_sem.at[3]).wait()
    scatter.finish()


def scatter_buffers(terms, slots, rows, width):
    bits = [(2,) * (4 - phase) for phase in range(5)]
    return (
        [pltpu.VMEM((terms, 2, 2, 2, 2, 2, rows, width), LOW)]
        + [pltpu.VMEM((slots,) + lead + (rows, width), LOW) for lead in bits]
        + [pltpu.VMEM((2, rows, width), WIDE)]
    )


def run_backward(cotangent, tokens, validity, forward):
    struct = jax.ShapeDtypeStruct
    held, tall, mixed_out, between, middles, gates, stages, kept = forward
    return pl.pallas_call(
        backward_kernel,
        out_shape=(
            struct((ROWS, 1024), WIDE),
            struct((CHUNKS, 64, WIDTH), WIDE),
            struct((2 * SHRINK_PARTS, TALL_ROWS, SHRINK_WIDTH), WIDE),
        ),
        in_specs=[FULL] * 3 + [ANY] * 7,
        out_specs=(ANY,) * 3,
        scratch_shapes=[
            pltpu.SemaphoreType.DMA((10, SCATTER_SLOTS)),
            pltpu.SemaphoreType.DMA((10, SCATTER_SLOTS)),
            pltpu.SemaphoreType.DMA((10, TALL_SLOTS)),
            pltpu.SemaphoreType.DMA((10, TALL_SLOTS)),
            pltpu.SemaphoreType.DMA((2,)),
            pltpu.SemaphoreType.DMA((2,)),
            pltpu.SemaphoreType.DMA((2,)),
            pltpu.SemaphoreType.DMA((2,)),
            pltpu.SemaphoreType.DMA,
            pltpu.SemaphoreType.DMA((4,)),
        ]
        + scatter_buffers(TERM_SLOTS, SCATTER_SLOTS, 64, WIDTH)
        + scatter_buffers(TALL_TERM_SLOTS, TALL_SLOTS, TALL_ROWS, SHRINK_WIDTH)
        + [
            pltpu.VMEM((2, 2, 1024, WIDTH), LOW),
            pltpu.VMEM((2, 2, ROWS, WIDTH), LOW),
            pltpu.VMEM((5, ROWS, WIDTH), LOW),
            pltpu.VMEM((2, 2816, 512), LOW),
            pltpu.VMEM((2816, ROWS), LOW),
            pltpu.VMEM((ROWS, 1024), LOW),
            pltpu.VMEM((ROWS, 1024), LOW),
            pltpu.VMEM((ROWS, 1024), WIDE),
            pltpu.VMEM((2, ROWS, 1024), WIDE),
            pltpu.VMEM((ROWS, 1024), WIDE),
            pltpu.VMEM((ROWS, 1024), WIDE),
            pltpu.VMEM((ROWS, 1024), LOW),
            pltpu.VMEM((1024, ROWS), LOW),
            pltpu.VMEM((2, 2, ROWS, WIDTH), LOW),
        ],
        compiler_params=pltpu.CompilerParams(
            collective_id=1, has_side_effects=True, vmem_limit_bytes=62 << 20
        ),
    )(
        cotangent,
        tokens,
        validity,
        held.reshape(CHUNKS, 2, 1024, WIDTH),
        tall.reshape(2, 2, 2816, 512),
        between,
        middles,
        gates,
        stages,
        kept,
    )


def unpack_kernel(mixed_in, tokens_in, chunks, parts, *refs):
    outs, sem = refs[:-1], refs[-1]
    copies = [(mixed_in, outs[0]), (tokens_in, outs[1])]
    for order in range(2):
        layer = 1 - order
        for turn in range(LAYER_CHUNKS):
            number = order * LAYER_CHUNKS + turn
            if turn < OUTPUT_TURN:
                weight, start = 2, chunk_columns(2, turn)
            elif turn < PROJECT_TURN:
                weight, start = 1, chunk_columns(1, turn - OUTPUT_TURN)
            else:
                weight, start = 0, chunk_columns(0, turn - PROJECT_TURN)
            target = outs[2 + 4 * layer + weight].at[:, pl.ds(start, WIDTH)]
            copies.append((chunks.at[number], target))
        for part in range(SHRINK_PARTS):
            target = outs[5 + 4 * layer].at[:, pl.ds(part * SHRINK_WIDTH, SHRINK_WIDTH)]
            copies.append((parts.at[order * SHRINK_PARTS + part], target))
    copies = [
        pltpu.make_async_copy(source, target, sem.at[i])
        for i, (source, target) in enumerate(copies)
    ]
    for copy in copies:
        copy.start()
    for copy in copies:
        copy.wait()


def unpack(mixed_out, tokens_gradient, chunks, parts, shards_of):
    struct = jax.ShapeDtypeStruct
    count = 2 + CHUNKS + 2 * SHRINK_PARTS
    return pl.pallas_call(
        unpack_kernel,
        out_shape=(struct(mixed_out.shape, LOW), struct(tokens_gradient.shape, WIDE))
        + tuple(struct(item.shape, WIDE) for item in shards_of),
        in_specs=[FULL] * 4,
        out_specs=(ANY,) * (2 + WEIGHTS),
        scratch_shapes=[pltpu.SemaphoreType.DMA((count,))],
        compiler_params=pltpu.CompilerParams(vmem_limit_bytes=32 << 20),
    )(mixed_out, tokens_gradient, chunks, parts)


def gather_weights(shards_of):
    return [
        lax.all_gather(lax.all_gather(item, "fsdp", axis=1, tiled=True), "dp", axis=0, tiled=True)
        for item in shards_of
    ]


def settle_gradients(terms):
    tall = [
        lax.psum_scatter(item.astype(jnp.bfloat16), "dp", scatter_dimension=0, tiled=True)
        for item in terms
    ]
    return [
        lax.psum_scatter(item, "fsdp", scatter_dimension=1, tiled=True).astype(jnp.float32)
        for item in tall
    ]


def local_scores(queries, keys_all):
    query_blocks = split_heads(queries.astype(jnp.bfloat16))
    key_blocks = split_heads(keys_all.astype(jnp.bfloat16))
    scores = jnp.einsum(
        "bihd,bjhd->bhij", query_blocks, key_blocks, preferred_element_type=jnp.float32
    ) * HEAD ** (-0.5)
    return (query_blocks, key_blocks, jnp.where(causal_table(), scores, -1e30))


def local_forward(queries, keys_all, values_low, validity):
    query_blocks, key_blocks, scores = local_scores(queries, keys_all)
    highest_score = jnp.max(scores, axis=-1, keepdims=True)
    expweights = jnp.exp(scores - highest_score)
    row_total = jnp.sum(expweights, axis=-1, keepdims=True)
    attend = (expweights / row_total).astype(jnp.bfloat16)
    mixture = jnp.einsum(
        "bhij,bjhd->bihd", attend, split_heads(values_low), preferred_element_type=jnp.float32
    )
    return (join_heads(mixture) * validity, highest_score + jnp.log(row_total))


def local_backward(queries, keys_all, values_low, validity, logsum, back_mixture):
    query_blocks, key_blocks, scores = local_scores(queries, keys_all)
    value_blocks = split_heads(values_low)
    coming = split_heads(back_mixture * validity.astype(jnp.bfloat16))
    attend = jnp.exp(scores - logsum)
    back_values = jnp.einsum(
        "bhij,bihd->bjhd", attend.astype(jnp.bfloat16), coming, preferred_element_type=jnp.float32
    )
    back_attend = jnp.einsum(
        "bihd,bjhd->bhij", coming, value_blocks, preferred_element_type=jnp.float32
    )
    back_scores = (
        attend * (back_attend - jnp.sum(back_attend * attend, axis=-1, keepdims=True))
    ).astype(jnp.bfloat16)
    back_queries = jnp.einsum(
        "bhij,bjhd->bihd", back_scores, key_blocks, preferred_element_type=jnp.float32
    ) * HEAD ** (-0.5)
    back_keys = jnp.einsum(
        "bhij,bihd->bjhd", back_scores, query_blocks, preferred_element_type=jnp.float32
    ) * HEAD ** (-0.5)
    return (join_heads(back_queries), join_heads(back_keys), join_heads(back_values))


def linear_parts(queries, keys_all, values_low):
    feature_q = split_heads(jax.nn.softplus(queries).astype(jnp.bfloat16))
    feature_k = split_heads(jax.nn.softplus(keys_all).astype(jnp.bfloat16))
    value_blocks = split_heads(values_low)
    causal = causal_table().astype(jnp.float32)
    inner_scores = (
        jnp.einsum("bihd,bjhd->bhij", feature_q, feature_k, preferred_element_type=jnp.float32)
        * causal
    ).astype(jnp.bfloat16)
    states = jnp.einsum(
        "bjhd,bjhe->bhde", feature_k, value_blocks, preferred_element_type=jnp.float32
    )
    running = jnp.cumsum(states, axis=0)
    prior_states = jnp.concatenate([jnp.zeros_like(states[:1]), running[:-1]], axis=0)
    return (feature_q, feature_k, value_blocks, causal, inner_scores, prior_states)


def linear_forward(queries, keys_all, values_low):
    feature_q, feature_k, value_blocks, causal, inner_scores, prior_states = linear_parts(
        queries, keys_all, values_low
    )
    mixture = jnp.einsum(
        "bhij,bjhe->bihe", inner_scores, value_blocks, preferred_element_type=jnp.float32
    )
    mixture = mixture + jnp.einsum(
        "bihd,bhde->bihe", feature_q.astype(jnp.float32), prior_states, precision=highest
    )
    return join_heads(mixture)


def linear_backward(queries, keys_all, values_low, back_mixture):
    feature_q, feature_k, value_blocks, causal, inner_scores, prior_states = linear_parts(
        queries, keys_all, values_low
    )
    coming = split_heads(back_mixture)
    coming_wide = coming.astype(jnp.float32)
    back_inner = (
        jnp.einsum("bihe,bjhe->bhij", coming, value_blocks, preferred_element_type=jnp.float32)
        * causal
    ).astype(jnp.bfloat16)
    back_feature_q = jnp.einsum(
        "bhij,bjhd->bihd", back_inner, feature_k, preferred_element_type=jnp.float32
    )
    back_feature_q = back_feature_q + jnp.einsum(
        "bihe,bhde->bihd", coming_wide, prior_states, precision=highest
    )
    back_feature_k = jnp.einsum(
        "bhij,bihd->bjhd", back_inner, feature_q, preferred_element_type=jnp.float32
    )
    back_values = jnp.einsum(
        "bhij,bihe->bjhe", inner_scores, coming, preferred_element_type=jnp.float32
    )
    back_prior = jnp.einsum(
        "bihd,bihe->bhde", feature_q.astype(jnp.float32), coming_wide, precision=highest
    )
    running = jnp.cumsum(back_prior[::-1], axis=0)[::-1]
    later_states = jnp.concatenate([running[1:], jnp.zeros_like(running[:1])], axis=0)
    back_feature_k = back_feature_k + jnp.einsum(
        "bjhe,bhde->bjhd", value_blocks.astype(jnp.float32), later_states, precision=highest
    )
    back_values = back_values + jnp.einsum(
        "bjhd,bhde->bjhe", feature_k.astype(jnp.float32), later_states, precision=highest
    )
    return (
        join_heads(back_feature_q) * jax.nn.sigmoid(queries),
        join_heads(back_feature_k) * jax.nn.sigmoid(keys_all),
        join_heads(back_values),
    )


def forward_layer(layer_in, validity, weights, local):
    project, output, expand, shrink = weights
    normed = simple_norm(layer_in).astype(jnp.bfloat16)
    projected = jnp.dot(normed, project, preferred_element_type=jnp.float32)
    queries, keys_all, values, update = jnp.split(projected, 4, axis=1)
    values_low = values.astype(jnp.bfloat16)
    if local:
        mixture, logsum = local_forward(queries, keys_all, values_low, validity)
    else:
        mixture = linear_forward(queries, keys_all, values_low)
        logsum = None
    gated_rows = (head_norm(mixture) * jax.nn.silu(update)).astype(jnp.bfloat16)
    middle = layer_in + jnp.dot(gated_rows, output, preferred_element_type=jnp.float32)
    second = simple_norm(middle).astype(jnp.bfloat16)
    expanded = jnp.dot(second, expand, preferred_element_type=jnp.float32)
    half_width = expanded.shape[1] // 2
    hidden = (expanded[:, :half_width] * expanded[:, half_width:]).astype(jnp.bfloat16)
    result = middle + jnp.dot(hidden, shrink, preferred_element_type=jnp.float32)
    return (
        result,
        (layer_in, normed, projected, values_low, mixture, logsum, gated_rows, middle, second),
    )


def backward_layer(upstream, saved, weights, validity, local):
    project, output, expand, shrink = weights
    layer_in, normed, projected, values_low, mixture, logsum, gated_rows, middle, second = saved
    expanded = jnp.dot(second, expand, preferred_element_type=jnp.float32)
    half_width = expanded.shape[1] // 2
    first_half = expanded[:, :half_width]
    second_half = expanded[:, half_width:]
    hidden = (first_half * second_half).astype(jnp.bfloat16)
    back_branch = upstream.astype(jnp.bfloat16)
    shrink_term = contract_rows(hidden, back_branch)
    back_hidden = contract_cols(back_branch, shrink)
    back_expanded = jnp.concatenate(
        [back_hidden * second_half, back_hidden * first_half], axis=1
    ).astype(jnp.bfloat16)
    expand_term = contract_rows(second, back_expanded)
    back_second = contract_cols(back_expanded, expand)
    back_middle = upstream + norm_back(middle, back_second)
    back_gated = back_middle.astype(jnp.bfloat16)
    output_term = contract_rows(gated_rows, back_gated)
    back_rows_gated = contract_cols(back_gated, output)
    queries, keys_all, unused_values, update = jnp.split(projected, 4, axis=1)
    back_update = back_rows_gated * head_norm(mixture) * silu_slope(update)
    back_mixture = head_back(mixture, back_rows_gated * jax.nn.silu(update)).astype(jnp.bfloat16)
    if local:
        back_queries, back_keys, back_values = local_backward(
            queries, keys_all, values_low, validity, logsum, back_mixture
        )
    else:
        back_queries, back_keys, back_values = linear_backward(
            queries, keys_all, values_low, back_mixture
        )
    back_projected = jnp.concatenate(
        [back_queries, back_keys, back_values, back_update], axis=1
    ).astype(jnp.bfloat16)
    project_term = contract_rows(normed, back_projected)
    back_normed = contract_cols(back_projected, project)
    back_input = back_middle + norm_back(layer_in, back_normed)
    return (back_input, (project_term, output_term, expand_term, shrink_term))


def shards(
    direct,
    tokens,
    lengths,
    local_project,
    local_output,
    local_expand,
    local_shrink,
    linear_project,
    linear_output,
    linear_expand,
    linear_shrink,
    cotangent,
):
    positions = lax.broadcasted_iota(jnp.int32, (tokens.shape[1], 1), 0)
    validity = (positions < lengths[0]).astype(jnp.float32)
    shards_of = [
        local_project,
        local_output,
        local_expand,
        local_shrink,
        linear_project,
        linear_output,
        linear_expand,
        linear_shrink,
    ]
    if direct:
        forward = run_forward(shards_of, tokens[0], validity)
        back_tokens, chunks, parts = run_backward(cotangent[0], tokens[0], validity, forward)
        outs = unpack(forward[2], back_tokens, chunks, parts, shards_of)
        return (outs[0][None], outs[1][None]) + tuple(outs[2:])
    layer_in = tokens[0].astype(jnp.float32) * validity
    whole = gather_weights(shards_of)
    local_weights = whole[:4]
    linear_weights = whole[4:]
    between, local_saved = forward_layer(layer_in, validity, local_weights, True)
    result, linear_saved = forward_layer(between, validity, linear_weights, False)
    result = (result * validity).astype(jnp.bfloat16)
    upstream = cotangent[0].astype(jnp.float32) * validity
    back_between, linear_terms = backward_layer(
        upstream, linear_saved, linear_weights, validity, False
    )
    back_input, local_terms = backward_layer(
        back_between, local_saved, local_weights, validity, True
    )
    sums = settle_gradients(local_terms + linear_terms)
    return (
        result[None],
        (back_input * validity)[None],
    ) + tuple(sums)


def solution(mesh):
    in_specs = (
        P(("dp", "fsdp"), None, None),
        P(("dp", "fsdp")),
        P("dp", "fsdp"),
        P("dp", "fsdp"),
        P("dp", "fsdp"),
        P("dp", "fsdp"),
        P("dp", "fsdp"),
        P("dp", "fsdp"),
        P("dp", "fsdp"),
        P("dp", "fsdp"),
        P(("dp", "fsdp"), None, None),
    )
    out_specs = (
        P(("dp", "fsdp"), None, None),
        P(("dp", "fsdp"), None, None),
        P("dp", "fsdp"),
        P("dp", "fsdp"),
        P("dp", "fsdp"),
        P("dp", "fsdp"),
        P("dp", "fsdp"),
        P("dp", "fsdp"),
        P("dp", "fsdp"),
        P("dp", "fsdp"),
    )
    direct = dict(mesh.shape) == {"dp": 16, "fsdp": 2}
    return jax.shard_map(functools.partial(shards, direct), mesh=mesh, in_specs=in_specs, out_specs=out_specs, check_vma=False)
```

```python
import functools

import jax
import jax.numpy as jnp
from jax import lax
from jax.experimental import pallas as pl
from jax.experimental.pallas import tpu as pltpu
from jax.sharding import PartitionSpec as P

HEADS = 16
HEAD = 64
BLOCK = 64


epsilon = 1e-05
highest = lax.Precision.HIGHEST


def simple_norm(values):
    return values * lax.rsqrt(jnp.mean(values * values, axis=-1, keepdims=True) + epsilon)


def norm_back(values, upstream):
    inverse_rms = lax.rsqrt(jnp.mean(values * values, axis=-1, keepdims=True) + epsilon)
    return inverse_rms * (
        upstream
        - values * (inverse_rms * inverse_rms) * jnp.mean(upstream * values, axis=-1, keepdims=True)
    )


def head_norm(values):
    shaped = values.reshape(values.shape[0], HEADS, HEAD)
    return simple_norm(shaped).reshape(values.shape)


def head_back(values, upstream):
    shaped = values.reshape(values.shape[0], HEADS, HEAD)
    coming = upstream.reshape(values.shape[0], HEADS, HEAD)
    return norm_back(shaped, coming).reshape(values.shape)


def silu_slope(values):
    logistic = jax.nn.sigmoid(values)
    return logistic * (1.0 + values * (1.0 - logistic))


def contract_rows(first_matrix, second_matrix):
    return lax.dot_general(
        first_matrix, second_matrix, (((0,), (0,)), ((), ())), preferred_element_type=jnp.float32
    )


def contract_cols(first_matrix, second_matrix):
    return lax.dot_general(
        first_matrix, second_matrix, (((1,), (1,)), ((), ())), preferred_element_type=jnp.float32
    )


def causal_table():
    return lax.broadcasted_iota(jnp.int32, (BLOCK, BLOCK), 0) >= lax.broadcasted_iota(
        jnp.int32, (BLOCK, BLOCK), 1
    )


def split_heads(values):
    return values.reshape(values.shape[0] // BLOCK, BLOCK, HEADS, HEAD)


def join_heads(values):
    return values.reshape(values.shape[0] * BLOCK, HEADS * HEAD)


AXIS_NAMES = ("f", "zh", "zl", "y", "c")
AXIS_OF = {"c": "c", "y": "y", "x": "f", "z1": "zl", "z2": "zh"}
MESH = pl.DeviceIdType.MESH
ANY = pl.BlockSpec(memory_space=pl.ANY)
FULL = pl.BlockSpec(memory_space=pltpu.VMEM)
WEIGHTS = 8
WIDTH = 256
LAG = 3
PHASES = 5
HEAD_GROUPS = 4
PROJECT_CHUNKS = 8
OUTPUT_CHUNKS = 2
EXPAND_CHUNKS = 11
LAYER_CHUNKS = PROJECT_CHUNKS + OUTPUT_CHUNKS + EXPAND_CHUNKS
CHUNKS = 2 * LAYER_CHUNKS
SHRINK_PARTS = 4
SHRINK_WIDTH = 128
GATHER_SLOTS = 8
LOAD_SLOTS = 3
LOW = jnp.bfloat16
WIDE = jnp.float32
ROWS = 512


def neighbours():
    dp = lax.axis_index("dp")
    x = lax.axis_index("fsdp")
    z = dp // 4
    y = (dp // 2) % 2
    c = dp % 2
    places = {"f": x, "zh": z // 2, "zl": z % 2, "y": y, "c": c}
    targets = {
        "z1": ((z + 1 - 2 * (z % 2)) * 4 + y * 2 + c, x),
        "z2": (lax.rem(z + 2, 4) * 4 + y * 2 + c, x),
        "y": (z * 4 + (1 - y) * 2 + c, x),
        "c": (z * 4 + y * 2 + (1 - c), x),
        "x": (dp, 1 - x),
    }
    return places, targets


def greet(targets):
    barrier = pltpu.get_barrier_semaphore()
    for target in targets.values():
        pl.semaphore_signal(barrier, inc=1, device_id=target, device_id_type=MESH)
    pl.semaphore_wait(barrier, len(targets))


def dot(left, right):
    return jnp.dot(left, right, preferred_element_type=WIDE)


def softplus(values):
    return jnp.maximum(values, 0.0) + jnp.log1p(jnp.exp(-jnp.abs(values)))


def logistic(values):
    return 1.0 / (1.0 + jnp.exp(-values))


def first_lanes(rows):
    return lax.broadcasted_iota(jnp.int32, (rows, 128), 1) < HEAD


def pair_mean(values, first):
    left = jnp.sum(jnp.where(first, values, 0.0), axis=-1, keepdims=True)
    right = jnp.sum(jnp.where(first, 0.0, values), axis=-1, keepdims=True)
    return jnp.where(first, left, right) * (1.0 / HEAD)


def block_mask(rows):
    i = lax.broadcasted_iota(jnp.int32, (rows, rows), 0)
    j = lax.broadcasted_iota(jnp.int32, (rows, rows), 1)
    return (i // BLOCK == j // BLOCK) & (j <= i)


def norm_into(source, target):
    def body(t, carry):
        rows = pl.ds(pl.multiple_of(t * 128, 128), 128)
        target[rows, :] = simple_norm(source[rows, :]).astype(LOW)
        return carry

    lax.fori_loop(0, ROWS // 128, body, 0)


def local_mixer(group, parts, validity, gated, stage, attends):
    def body(turn, carry):
        t = turn // 2
        rows = pl.ds(pl.multiple_of(t * 128, 128), 128)
        pair = turn % 2
        lanes = pl.ds(pl.multiple_of(pair * 128, 128), 128)
        first = first_lanes(128)
        q = parts[0, 0, rows, lanes].astype(LOW)
        k = parts[1, 0, rows, lanes].astype(LOW)
        v = parts[0, 1, rows, lanes].astype(LOW)
        u = parts[1, 1, rows, lanes]
        keep = block_mask(128)
        mixed = []
        for head in range(2):
            mine = jnp.where(first == (head == 0), q, jnp.zeros_like(q))
            scores = contract_cols(mine, k) * HEAD ** (-0.5)
            scores = jnp.where(keep, scores, -1e30)
            highest_score = jnp.max(scores, axis=-1, keepdims=True)
            weights = jnp.exp(scores - highest_score)
            attend = (weights / jnp.sum(weights, axis=-1, keepdims=True)).astype(LOW)
            attends[turn, head] = attend
            mixed.append(dot(attend, v))
        mixture = jnp.where(first, mixed[0], mixed[1]) * validity[rows, :]
        scale = lax.rsqrt(pair_mean(mixture * mixture, first) + epsilon)
        columns = pl.ds(pl.multiple_of(group * WIDTH + pair * 128, 128), 128)
        gated[rows, columns] = (mixture * scale * (u * logistic(u))).astype(LOW)
        stage[4, rows, lanes] = mixture.astype(LOW)
        return carry

    lax.fori_loop(0, 2 * ROWS // 128, body, 0)


def linear_mixer(group, parts, gated, stage):
    half = ROWS // 2

    def body(pair, carry):
        lanes = pl.ds(pl.multiple_of(pair * 128, 128), 128)
        columns = pl.ds(pl.multiple_of(group * WIDTH + pair * 128, 128), 128)
        first = first_lanes(half)
        fk = softplus(parts[1, 0, :, lanes]).astype(LOW)
        v = parts[0, 1, :, lanes].astype(LOW)
        for t in range(2):
            rows = pl.ds(t * half, half)
            reach = (t + 1) * half
            fq = softplus(parts[0, 0, rows, lanes]).astype(LOW)
            i = lax.broadcasted_iota(jnp.int32, (half, reach), 0) + t * half
            j = lax.broadcasted_iota(jnp.int32, (half, reach), 1)
            mixed = []
            for head in range(2):
                mine = jnp.where(first == (head == 0), fq, jnp.zeros_like(fq))
                scores = jnp.where(j <= i, contract_cols(mine, fk[:reach]), 0.0).astype(LOW)
                mixed.append(dot(scores, v[:reach]))
            mixture = jnp.where(first, mixed[0], mixed[1])
            scale = lax.rsqrt(pair_mean(mixture * mixture, first) + epsilon)
            u = parts[1, 1, rows, lanes]
            gated[rows, columns] = (mixture * scale * (u * logistic(u))).astype(LOW)
            stage[4, rows, lanes] = mixture.astype(LOW)
        return carry

    lax.fori_loop(0, 2, body, 0)


def chunk_columns(weight, part):
    if weight == 0:
        return (part % 2) * 1024 + (part // 2) * WIDTH
    return part * WIDTH


class Gather:
    def __init__(self, own, held, tall, sems):
        self.own, self.held, self.tall = own, held, tall
        self.local_sem, self.send_sem, self.recv_sem, self.tall_send, self.tall_recv = sems
        self.places, self.targets = neighbours()
        self.at = tuple(self.places[name] for name in ("f", "zh", "zl", "y", "c"))

    def begin(self):
        counts = (PROJECT_CHUNKS, OUTPUT_CHUNKS, EXPAND_CHUNKS)
        for layer in range(2):
            chunk = LAYER_CHUNKS * layer
            for weight in range(3):
                for part in range(counts[weight]):
                    start = chunk_columns(weight, part)
                    pltpu.make_async_copy(
                        self.own[4 * layer + weight].at[:, pl.ds(start, WIDTH)],
                        self.held.at[(chunk,) + self.at],
                        self.local_sem.at[chunk],
                    ).start()
                    chunk += 1
            pltpu.make_async_copy(
                self.own[4 * layer + 3],
                self.tall.at[(layer,) + self.at],
                self.local_sem.at[CHUNKS + layer],
            ).start()
        greet(self.targets)

    def message(self, block, target, sems, place):
        return pltpu.make_async_remote_copy(
            src_ref=block,
            dst_ref=block,
            send_sem=sems[0].at[place],
            recv_sem=sems[1].at[place],
            device_id=self.targets[target],
            device_id_type=MESH,
        )

    def wide_messages(self, phase, chunk):
        x, zh, zl, y, c = self.at
        ref = self.held
        sems = (self.send_sem, self.recv_sem)
        slot = chunk % GATHER_SLOTS
        half = WIDTH // 2
        low, high = pl.ds(0, half), pl.ds(half, half)

        def one(index, target, part):
            return self.message(ref.at[(chunk,) + index], target, sems, (2 * phase + part, slot))

        a = slice(None)
        if phase == 0:
            return [one((x, zh, zl, y, c), "z2", 0)]
        if phase == 1:
            return [one((x, a, zl, y, c), "z1", 0)]
        if phase == 2:
            return [one((x, a, a, y, c, a, low), "x", 0), one((x, a, a, y, c, a, high), "y", 1)]
        if phase == 3:
            return [one((a, a, a, y, c, a, low), "y", 0), one((x, a, a, a, c, a, high), "x", 1)]
        return [one((a, a, a, a, c), "c", 0)]

    def tall_message(self, phase, layer, part, odd):
        x, zh, zl, y, c = self.at
        a = slice(None)
        lanes = pl.ds(pl.multiple_of(part * SHRINK_WIDTH, SHRINK_WIDTH), SHRINK_WIDTH)
        index, target = {
            (0, 0): ((x, zh, zl, y, c), "x"),
            (0, 1): ((x, zh, zl, y, c), "y"),
            (1, 0): ((a, zh, zl, y, c), "y"),
            (1, 1): ((x, zh, zl, a, c), "x"),
            (2, 0): ((a, zh, zl, a, c), "z2"),
            (3, 0): ((a, a, zl, a, c), "z1"),
            (4, 0): ((a, a, a, a, c), "c"),
        }[(phase, odd)]
        return self.message(
            self.tall.at[(layer,) + index + (a, lanes)],
            target,
            (self.tall_send, self.tall_recv),
            (phase, layer * SHRINK_PARTS + part),
        )

    def tall_turn(self, chunk):
        layer = chunk // LAYER_CHUNKS
        place = chunk % LAYER_CHUNKS
        return layer, place // 5, place % 5 == 4

    def for_tall(self, phase, chunk, act):
        layer, part, due = self.tall_turn(chunk)
        if phase >= 2:
            pl.when(due)(lambda: act(self.tall_message(phase, layer, part, 0)))
        else:
            for odd in range(2):
                pl.when(due & (part % 2 == odd))(
                    lambda odd=odd: act(self.tall_message(phase, layer, part, odd))
                )

    def step(self, step):
        for phase in range(PHASES, -1, -1):
            chunk = step - phase * LAG

            @pl.when((chunk >= 0) & (chunk < CHUNKS))
            def _(phase=phase, chunk=chunk):
                if phase >= 1:
                    for copy in self.wide_messages(phase - 1, chunk):
                        copy.wait()
                    self.for_tall(phase - 1, chunk, lambda copy: copy.wait())
                else:
                    pltpu.make_async_copy(
                        self.own[0].at[:, pl.ds(0, WIDTH)],
                        self.held.at[(chunk,) + self.at],
                        self.local_sem.at[chunk],
                    ).wait()
                    layer = chunk // LAYER_CHUNKS

                    @pl.when(chunk % LAYER_CHUNKS == 4)
                    def _():
                        pltpu.make_async_copy(
                            self.own[3],
                            self.tall.at[(layer,) + self.at],
                            self.local_sem.at[CHUNKS + layer],
                        ).wait()

                if phase < PHASES:
                    for copy in self.wide_messages(phase, chunk):
                        copy.start()
                    self.for_tall(phase, chunk, lambda copy: copy.start())


def forward_kernel(*refs):
    own = refs[:WEIGHTS]
    tokens, validity = refs[WEIGHTS : WEIGHTS + 2]
    held, tall, mixed_out, between, middles, turns, stages, halves_out = refs[10:18]
    hidden_out, attends_out = refs[18:20]
    scratch = refs[20:]
    sems, (load_sem, tall_sem, stage_sem, half_sem, hidden_sem, misc_sem) = scratch[:5], scratch[5:11]
    loaded, shrink, x, middle, normed, gated, hidden, parts, stage, half_stage, final = scratch[11:22]
    turned, hidden_stage, attends = scratch[22:]
    gather = Gather(own, held, tall, sems)
    gather.begin()

    def rows_of(t):
        return pl.ds(pl.multiple_of(t * 128, 128), 128)

    def start_rows(t, carry):
        rows = rows_of(t)
        x[rows, :] = tokens[rows, :].astype(WIDE) * validity[rows, :]
        return carry

    def keep_turned(layer, kind):
        return pltpu.make_async_copy(turned, turns.at[layer, kind], misc_sem.at[0])

    def turn(source, layer, kind):
        def act(t, carry):
            rows = rows_of(t)
            turned[:, rows] = source[rows, :].T
            return carry

        lax.fori_loop(0, ROWS // 128, act, 0)
        keep_turned(layer, kind).start()

    lax.fori_loop(0, ROWS // 128, start_rows, 0)
    norm_into(x, normed)
    turn(normed, 0, 0)

    def load(chunk):
        return pltpu.make_async_copy(
            held.at[chunk], loaded.at[chunk % LOAD_SLOTS], load_sem.at[chunk % LOAD_SLOTS]
        )

    def load_tall(layer):
        return pltpu.make_async_copy(tall.at[layer], shrink, tall_sem)

    def keep_stage(layer, group):
        return pltpu.make_async_copy(stage, stages.at[layer, group], stage_sem)

    def keep_half(layer, part):
        return pltpu.make_async_copy(
            half_stage.at[part % 2], halves_out.at[layer, part], half_sem.at[part % 2]
        )

    def keep_hidden(layer, part):
        rows = pl.ds(pl.multiple_of(part * WIDTH, WIDTH), WIDTH)
        return pltpu.make_async_copy(
            hidden_stage.at[part % 2], hidden_out.at[layer, rows, :], hidden_sem.at[part % 2]
        )

    def keep_attends(group):
        return pltpu.make_async_copy(attends, attends_out.at[group], misc_sem.at[4])

    def keep_middle(layer):
        return pltpu.make_async_copy(middle, middles.at[layer], misc_sem.at[1])

    def keep_between():
        return pltpu.make_async_copy(x, between, misc_sem.at[2])

    def weight(slot, f):
        return loaded[slot, f].reshape(1024, WIDTH)

    def project_step(layer, place, slot):
        group = place // 2
        for f in range(2):
            parts[place % 2, f] = dot(normed[...], weight(slot, f))

        @pl.when(place % 2 == 1)
        def _():
            @pl.when((layer > 0) | (group > 0))
            def _():
                keep_stage(layer, group).wait()

            @pl.when((layer == 0) & (group > 0))
            def _():
                keep_attends(0).wait()

            for kind in range(4):
                stage[kind] = parts[kind % 2, kind // 2].astype(LOW)

            @pl.when(layer == 0)
            def _():
                local_mixer(group, parts, validity, gated, stage, attends)
                keep_attends(group).start()

            pl.when(layer > 0)(lambda: linear_mixer(group, parts, gated, stage))
            keep_stage(layer, group).start()

    def output_step(layer, part, slot):
        @pl.when(part == 0)
        def _():
            keep_turned(0, 0).wait()
            turn(gated, layer, 1)

            @pl.when(layer > 0)
            def _():
                keep_middle(0).wait()

        for f in range(2):
            lanes = pl.ds(pl.multiple_of(f * 512 + part * WIDTH, WIDTH), WIDTH)
            middle[:, lanes] = x[:, lanes] + dot(gated[...], weight(slot, f))

        @pl.when(part == OUTPUT_CHUNKS - 1)
        def _():
            keep_middle(layer).start()
            norm_into(middle, normed)
            keep_turned(0, 0).wait()
            turn(normed, layer, 2)

    def expand_step(layer, part, slot):
        @pl.when((layer > 0) | (part > 1))
        def _():
            keep_half(layer, part).wait()
            keep_hidden(layer, part).wait()

        first = dot(normed[...], weight(slot, 0))
        second = dot(normed[...], weight(slot, 1))
        half_stage[part % 2, 0] = first.astype(LOW)
        half_stage[part % 2, 1] = second.astype(LOW)
        both = (first * second).astype(LOW)
        hidden[:, pl.ds(pl.multiple_of(part * WIDTH, WIDTH), WIDTH)] = both
        hidden_stage[part % 2] = both.T
        keep_half(layer, part).start()
        keep_hidden(layer, part).start()

    def shrink_step(layer):
        load_tall(layer).wait()

        @pl.when(layer > 0)
        def _():
            keep_between().wait()

        def body(turn, carry):
            f = turn // 2
            columns = pl.ds(pl.multiple_of((turn % 2) * WIDTH, WIDTH), WIDTH)
            lanes = pl.ds(pl.multiple_of(turn * WIDTH, WIDTH), WIDTH)
            matrix = shrink[f, :, :, :, :, :, columns].reshape(hidden.shape[1], WIDTH)
            x[:, lanes] = middle[:, lanes] + dot(hidden[...], matrix)
            return carry

        lax.fori_loop(0, 4, body, 0)

        @pl.when(layer == 0)
        def _():
            keep_between().start()
            norm_into(x, normed)
            keep_turned(0, 0).wait()
            turn(normed, 1, 0)

        @pl.when(layer > 0)
        def _():
            def last_rows(t, carry):
                rows = rows_of(t)
                final[rows, :] = (x[rows, :] * validity[rows, :]).astype(LOW)
                return carry

            lax.fori_loop(0, ROWS // 128, last_rows, 0)

    def body(step, carry):
        gather.step(step)
        arrived = step - PHASES * LAG

        @pl.when((arrived >= 0) & (arrived < CHUNKS))
        def _():
            load(arrived).start()

            @pl.when(arrived % LAYER_CHUNKS == LAYER_CHUNKS - 2)
            def _():
                load_tall(arrived // LAYER_CHUNKS).start()

        ready = arrived - 1

        @pl.when((ready >= 0) & (ready < CHUNKS))
        def _():
            load(ready).wait()
            layer = ready // LAYER_CHUNKS
            place = ready % LAYER_CHUNKS
            slot = ready % LOAD_SLOTS
            pl.when(place < PROJECT_CHUNKS)(lambda: project_step(layer, place, slot))
            pl.when((place >= PROJECT_CHUNKS) & (place < PROJECT_CHUNKS + OUTPUT_CHUNKS))(
                lambda: output_step(layer, place - PROJECT_CHUNKS, slot)
            )
            pl.when(place >= PROJECT_CHUNKS + OUTPUT_CHUNKS)(
                lambda: expand_step(layer, place - PROJECT_CHUNKS - OUTPUT_CHUNKS, slot)
            )
            pl.when(place == LAYER_CHUNKS - 1)(lambda: shrink_step(layer))

        return carry

    lax.fori_loop(0, CHUNKS + PHASES * LAG + 1, body, 0)
    last = pltpu.make_async_copy(final, mixed_out, misc_sem.at[3])
    last.start()
    keep_stage(1, HEAD_GROUPS - 1).wait()
    keep_attends(0).wait()
    keep_turned(0, 0).wait()
    keep_middle(1).wait()
    keep_half(1, EXPAND_CHUNKS - 2).wait()
    keep_half(1, EXPAND_CHUNKS - 1).wait()
    keep_hidden(1, EXPAND_CHUNKS - 2).wait()
    keep_hidden(1, EXPAND_CHUNKS - 1).wait()
    last.wait()


def run_forward(shards_of, tokens, validity):
    bits = (2, 2, 2, 2, 2)
    struct = jax.ShapeDtypeStruct
    return pl.pallas_call(
        forward_kernel,
        out_shape=(
            struct((CHUNKS,) + bits + (64, WIDTH), LOW),
            struct((2,) + bits + (176, 512), LOW),
            struct((ROWS, 1024), LOW),
            struct((ROWS, 1024), WIDE),
            struct((2, ROWS, 1024), WIDE),
            struct((2, 3, 1024, ROWS), LOW),
            struct((2, HEAD_GROUPS, 5, ROWS, WIDTH), LOW),
            struct((2, EXPAND_CHUNKS, 2, ROWS, WIDTH), LOW),
            struct((2, 2816, ROWS), LOW),
            struct((HEAD_GROUPS, 8, 2, 128, 128), LOW),
        ),
        in_specs=[FULL] * (WEIGHTS + 2),
        out_specs=(ANY,) * 10,
        scratch_shapes=[
            pltpu.SemaphoreType.DMA((CHUNKS + 2,)),
            pltpu.SemaphoreType.DMA((10, GATHER_SLOTS)),
            pltpu.SemaphoreType.DMA((10, GATHER_SLOTS)),
            pltpu.SemaphoreType.DMA((PHASES, 2 * SHRINK_PARTS)),
            pltpu.SemaphoreType.DMA((PHASES, 2 * SHRINK_PARTS)),
            pltpu.SemaphoreType.DMA((LOAD_SLOTS,)),
            pltpu.SemaphoreType.DMA,
            pltpu.SemaphoreType.DMA,
            pltpu.SemaphoreType.DMA((2,)),
            pltpu.SemaphoreType.DMA((2,)),
            pltpu.SemaphoreType.DMA((5,)),
            pltpu.VMEM((LOAD_SLOTS,) + bits + (64, WIDTH), LOW),
            pltpu.VMEM(bits + (176, 512), LOW),
            pltpu.VMEM((ROWS, 1024), WIDE),
            pltpu.VMEM((ROWS, 1024), WIDE),
            pltpu.VMEM((ROWS, 1024), LOW),
            pltpu.VMEM((ROWS, 1024), LOW),
            pltpu.VMEM((ROWS, 2816), LOW),
            pltpu.VMEM((2, 2, ROWS, WIDTH), WIDE),
            pltpu.VMEM((5, ROWS, WIDTH), LOW),
            pltpu.VMEM((2, 2, ROWS, WIDTH), LOW),
            pltpu.VMEM((ROWS, 1024), LOW),
            pltpu.VMEM((1024, ROWS), LOW),
            pltpu.VMEM((2, WIDTH, ROWS), LOW),
            pltpu.VMEM((8, 2, 128, 128), LOW),
        ],
        compiler_params=pltpu.CompilerParams(
            collective_id=0, has_side_effects=True, vmem_limit_bytes=60 << 20
        ),
    )(*shards_of, tokens, validity)


SCATTER_LAG = 3
SCATTER_SLOTS = 3 * SCATTER_LAG + 1
TERM_SLOTS = SCATTER_LAG
TALL_SLOTS = 3
OUTPUT_TURN = EXPAND_CHUNKS
PROJECT_TURN = EXPAND_CHUNKS + OUTPUT_CHUNKS
TALL_ROWS = 176


class Scatter:
    def __init__(self, outs, sems, wide, tall):
        self.outs, self.tall_outs = outs
        self.send_sem, self.recv_sem, self.tall_send, self.tall_recv = sems[:4]
        self.store_sem, self.tall_store = sems[4:]
        self.wide, self.tall = wide[:6], tall[:6]
        self.result, self.tall_result = wide[6], tall[6]
        self.places, self.targets = neighbours()

    def tall_turn(self, chunk):
        layer = chunk // LAYER_CHUNKS
        turn = chunk % LAYER_CHUNKS
        return layer * SHRINK_PARTS + turn // 5, turn // 5, turn % 5 == 4

    def wide_parts(self):
        half = WIDTH // 2
        return (
            (pl.ds(0, half), ("c", "y", "x", "z1", "z2")),
            (pl.ds(half, half), ("c", "x", "y", "z1", "z2")),
        )

    def tall_parts(self, odd):
        plane = ("x", "y") if odd else ("y", "x")
        return ((pl.ds(0, SHRINK_WIDTH), ("c", "z1", "z2") + plane),)

    def left(self, order, phase):
        used = set(AXIS_OF[target] for target in order[: phase + 1])
        return [name for name in AXIS_NAMES if name not in used]

    def source(self, buffers, slots, phase, order):
        if phase == 0:
            return buffers[0].at[slots[0]], list(AXIS_NAMES)
        return buffers[phase].at[slots[1]], self.left(order, phase - 1)

    def messages(self, buffers, slots, sems, phase, parts):
        if phase == 0 and len(parts) == 2:
            parts = ((pl.ds(0, WIDTH), parts[0][1]),)
        out = []
        for part, (lanes, order) in enumerate(parts):
            source, dims = self.source(buffers, slots, phase, order)
            target = order[phase]
            away = tuple(
                1 - self.places[d] if d == AXIS_OF[target] else slice(None) for d in dims
            )
            whole = tuple(slice(None) for _ in self.left(order, phase))
            place = (2 * phase + part, slots[1])
            out.append(
                pltpu.make_async_remote_copy(
                    src_ref=source.at[away + (slice(None), lanes)],
                    dst_ref=buffers[1 + phase].at[(slots[1],) + whole + (slice(None), lanes)],
                    send_sem=sems[0].at[place],
                    recv_sem=sems[1].at[place],
                    device_id=self.targets[target],
                    device_id_type=MESH,
                )
            )
        return out

    def add(self, buffers, slots, phase, parts, result):
        if phase == 0 and len(parts) == 2:
            parts = ((pl.ds(0, WIDTH), parts[0][1]),)
        for lanes, order in parts:
            source, dims = self.source(buffers, slots, phase, order)
            cut = AXIS_OF[order[phase]]
            near = tuple(self.places[d] if d == cut else slice(None) for d in dims)
            whole = tuple(slice(None) for _ in self.left(order, phase))
            ref = buffers[1 + phase].at[slots[1]]
            mine = source[near + (slice(None), lanes)]
            came = ref[whole + (slice(None), lanes)]
            if phase < 4:
                ref[whole + (slice(None), lanes)] = came + mine
            else:
                result[:, lanes] = came.astype(WIDE) + mine.astype(WIDE)

    def wide_slots(self, chunk):
        return (chunk % TERM_SLOTS, chunk % SCATTER_SLOTS)

    def tall_slots(self, place):
        return (0, place % TALL_SLOTS)

    def wide_messages(self, phase, chunk):
        return self.messages(
            self.wide,
            self.wide_slots(chunk),
            (self.send_sem, self.recv_sem),
            phase,
            self.wide_parts(),
        )

    def tall_messages(self, phase, place, odd):
        return self.messages(
            self.tall,
            self.tall_slots(place),
            (self.tall_send, self.tall_recv),
            phase,
            self.tall_parts(odd),
        )

    def store(self, chunk):
        return pltpu.make_async_copy(
            self.result.at[chunk % 2], self.outs.at[chunk], self.store_sem.at[chunk % 2]
        )

    def store_tall(self, place):
        return pltpu.make_async_copy(
            self.tall_result.at[place % 2], self.tall_outs.at[place], self.tall_store.at[place % 2]
        )

    def start(self, phase, chunk):
        for copy in self.wide_messages(phase, chunk):
            copy.start()
        place, part, due = self.tall_turn(chunk)
        for odd in range(2):

            @pl.when(due & (part % 2 == odd))
            def _(odd=odd):
                for copy in self.tall_messages(phase, place, odd):
                    copy.start()

    def take(self, phase, chunk):
        for copy in self.wide_messages(phase, chunk):
            copy.wait()
        if phase == PHASES - 1:
            pl.when(chunk >= 2)(lambda: self.store(chunk).wait())
        self.add(
            self.wide, self.wide_slots(chunk), phase, self.wide_parts(), self.result.at[chunk % 2]
        )
        place, part, due = self.tall_turn(chunk)
        for odd in range(2):

            @pl.when(due & (part % 2 == odd))
            def _(odd=odd):
                for copy in self.tall_messages(phase, place, odd):
                    copy.wait()
                if phase == PHASES - 1:
                    pl.when(place >= 2)(lambda: self.store_tall(place).wait())
                self.add(
                    self.tall,
                    self.tall_slots(place),
                    phase,
                    self.tall_parts(odd),
                    self.tall_result.at[place % 2],
                )
                if phase == PHASES - 1:
                    self.store_tall(place).start()

        if phase == PHASES - 1:
            self.store(chunk).start()

    def older(self, step):
        for phase in range(PHASES, 0, -1):
            chunk = step - phase * SCATTER_LAG

            @pl.when((chunk >= 0) & (chunk < CHUNKS))
            def _(phase=phase, chunk=chunk):
                self.take(phase - 1, chunk)
                if phase < PHASES:
                    self.start(phase, chunk)

    def finish(self):
        for chunk in (CHUNKS - 2, CHUNKS - 1):
            self.store(chunk).wait()
        for place in (2 * SHRINK_PARTS - 2, 2 * SHRINK_PARTS - 1):
            self.store_tall(place).wait()


def norm_slope(values, inverse, upstream, mean):
    return inverse * (upstream - values * (inverse * inverse) * mean)


def gate_back(update, mixture, coming, first):
    inverse = lax.rsqrt(pair_mean(mixture * mixture, first) + epsilon)
    curve = logistic(update)
    back_update = coming * (mixture * inverse) * (curve * (1.0 + update * (1.0 - curve)))
    gate = coming * (update * curve)
    back_mixture = norm_slope(mixture, inverse, gate, pair_mean(gate * mixture, first))
    return back_update, back_mixture


def local_mixer_back(group, stage, attends, validity, coming, back):
    def body(turn, carry):
        rows = pl.ds(pl.multiple_of((turn // 2) * 128, 128), 128)
        lanes = pl.ds(pl.multiple_of((turn % 2) * 128, 128), 128)
        columns = pl.ds(pl.multiple_of(group * WIDTH + (turn % 2) * 128, 128), 128)
        first = first_lanes(128)

        def put(i, j, value):
            start = j * WIDTH + (turn % 2) * 128
            back[i, rows, pl.ds(pl.multiple_of(start, 128), 128)] = value.astype(LOW)

        q, k, v = stage[0, rows, lanes], stage[1, rows, lanes], stage[2, rows, lanes]
        update = stage[3, rows, lanes].astype(WIDE)
        mixture = stage[4, rows, lanes].astype(WIDE)
        back_update, back_mixture = gate_back(update, mixture, coming[rows, columns], first)
        put(1, 1, back_update)
        grad = (back_mixture.astype(LOW).astype(WIDE) * validity[rows, :]).astype(LOW)
        zero = jnp.zeros_like(q)
        out = []
        for head in range(2):
            here = first == (head == 0)
            attend = attends[turn, head].astype(WIDE)
            back_attend = contract_cols(jnp.where(here, grad, zero), v)
            total = jnp.sum(back_attend * attend, axis=-1, keepdims=True)
            back_scores = (attend * (back_attend - total)).astype(LOW)
            out.append(
                (
                    dot(back_scores, k) * HEAD ** (-0.5),
                    contract_rows(back_scores, q) * HEAD ** (-0.5),
                    contract_rows(attends[turn, head], grad),
                )
            )
        for kind, (i, j) in enumerate(((0, 0), (1, 0), (0, 1))):
            put(i, j, jnp.where(first, out[0][kind], out[1][kind]))
        return carry

    lax.fori_loop(0, 2 * ROWS // 128, body, 0, unroll=4)


def linear_mixer_back(group, stage, coming, back):
    half = ROWS // 2

    def body(pair, carry):
        lanes = pl.ds(pl.multiple_of(pair * 128, 128), 128)
        columns = pl.ds(pl.multiple_of(group * WIDTH + pair * 128, 128), 128)
        first = first_lanes(ROWS)
        queries = stage[0, :, lanes].astype(WIDE)
        keys_all = stage[1, :, lanes].astype(WIDE)
        v = stage[2, :, lanes]
        fq = softplus(queries).astype(LOW)
        fk = softplus(keys_all).astype(LOW)
        update = stage[3, :, lanes].astype(WIDE)
        mixture = stage[4, :, lanes].astype(WIDE)
        back_update, back_mixture = gate_back(update, mixture, coming[:, columns], first)

        def put(i, j, rows, value):
            start = j * WIDTH + pair * 128
            back[i, rows, pl.ds(pl.multiple_of(start, 128), 128)] = value.astype(LOW)

        put(1, 1, slice(None), back_update)
        grad = back_mixture.astype(LOW)
        zero = jnp.zeros((half, 128), LOW)
        tiles = []
        for t in range(2):
            reach = (t + 1) * half
            i = lax.broadcasted_iota(jnp.int32, (half, reach), 0) + t * half
            j = lax.broadcasted_iota(jnp.int32, (half, reach), 1)
            mine_q = fq[t * half : reach]
            mine_g = grad[t * half : reach]
            out = []
            for head in range(2):
                here = first[:half] == (head == 0)
                scores = contract_cols(jnp.where(here, mine_q, zero), fk[:reach])
                scores = jnp.where(j <= i, scores, 0.0).astype(LOW)
                inner = contract_cols(jnp.where(here, mine_g, zero), v[:reach])
                inner = jnp.where(j <= i, inner, 0.0).astype(LOW)
                out.append(
                    (dot(inner, fk[:reach]), contract_rows(inner, mine_q), contract_rows(scores, mine_g))
                )
            tiles.append(
                [jnp.where(first[: out[0][n].shape[0]], out[0][n], out[1][n]) for n in range(3)]
            )
        for t in range(2):
            rows = pl.ds(t * half, half)
            span = slice(t * half, (t + 1) * half)
            back_q = tiles[t][0]
            back_k = tiles[1][1][span]
            back_v = tiles[1][2][span]
            if t == 0:
                back_k = back_k + tiles[0][1]
                back_v = back_v + tiles[0][2]
            put(0, 0, rows, back_q * logistic(queries[span]))
            put(1, 0, rows, back_k * logistic(keys_all[span]))
            put(0, 1, rows, back_v)
        return carry

    lax.fori_loop(0, 2, body, 0)


def over_rows(act):
    def body(t, carry):
        act(pl.ds(pl.multiple_of(t * 128, 128), 128))
        return carry

    lax.fori_loop(0, ROWS // 128, body, 0)


def backward_kernel(*refs):
    cotangent, tokens, validity = refs[:3]
    held, tall, between, middles, turns, stages, halves_in, hidden_in, attends_in = refs[3:12]
    tokens_out, outs, tall_outs = refs[12:15]
    scratch = refs[15:]
    scatter_sems, loads = scratch[:6], scratch[6:12]
    load_sem, half_sem, shrink_sem, stage_sem, turn_sem, misc_sem = loads
    wide_buffers, tall_buffers = scratch[12:19], scratch[19:26]
    (
        loaded,
        half_in,
        stage,
        attends,
        shrink,
        hidden_turned,
        branch,
        gated_branch,
        up,
        sums,
        middle,
        layer_in,
        turned,
        back,
    ) = scratch[26:]
    scatter = Scatter((outs, tall_outs), scatter_sems, wide_buffers, tall_buffers)

    class Load:
        def __init__(self, chunk, number):
            self.copies = [
                pltpu.make_async_copy(
                    held.at[chunk, f],
                    loaded.at[number % 2, :, pl.ds(f * WIDTH, WIDTH)],
                    load_sem.at[number % 2, f],
                )
                for f in range(2)
            ]

        def start(self):
            for copy in self.copies:
                copy.start()

        def wait(self):
            for copy in self.copies:
                copy.wait()

    def load_turned(layer, kind, order):
        return pltpu.make_async_copy(
            turns.at[layer, kind], turned.at[order % 2], turn_sem.at[order % 2]
        )

    def load_attends(group):
        return pltpu.make_async_copy(attends_in.at[group], attends, misc_sem.at[4])

    def load_half(layer, part, number):
        return pltpu.make_async_copy(
            halves_in.at[layer, part], half_in.at[number % 2], half_sem.at[number % 2]
        )

    def load_shrink(layer, part, number):
        rows = pl.ds(pl.multiple_of(part * WIDTH, WIDTH), WIDTH)
        return pltpu.make_async_copy(
            tall.at[layer, :, rows, :], shrink.at[number % 2], shrink_sem.at[number % 2]
        )

    def load_stage(layer, group):
        return pltpu.make_async_copy(stages.at[layer, group], stage, stage_sem)

    def fetch(kind, layer):
        source, target = (
            (None, None),
            (middles, middle),
            (hidden_in, hidden_turned),
        )[kind]
        return pltpu.make_async_copy(source.at[layer], target, misc_sem.at[kind])

    def fetch_between():
        return pltpu.make_async_copy(between, layer_in, misc_sem.at[3])

    def prefetch(number):
        layer = 1 - number // LAYER_CHUNKS
        turn = number % LAYER_CHUNKS
        base = LAYER_CHUNKS * layer

        @pl.when(turn < OUTPUT_TURN)
        def _():
            Load(base + PROJECT_CHUNKS + OUTPUT_CHUNKS + turn, number).start()
            load_half(layer, turn, number).start()
            load_shrink(layer, turn, number).start()

        @pl.when((turn >= OUTPUT_TURN) & (turn < PROJECT_TURN))
        def _():
            Load(base + PROJECT_CHUNKS + turn - OUTPUT_TURN, number).start()

        @pl.when(turn >= PROJECT_TURN)
        def _():
            Load(base + turn - PROJECT_TURN, number).start()

            @pl.when((turn - PROJECT_TURN) % 2 == 0)
            def _():
                load_stage(layer, (turn - PROJECT_TURN) // 2).start()
                pl.when(layer == 0)(lambda: load_attends((turn - PROJECT_TURN) // 2).start())

    prefetch(jnp.int32(0))
    load_turned(1, 2, 0).start()
    load_turned(1, 1, 1).start()
    fetch(2, 1).start()
    fetch(1, 1).start()
    fetch_between().start()

    def begin_rows(rows):
        up[rows, :] = cotangent[rows, :].astype(WIDE) * validity[rows, :]

    over_rows(begin_rows)
    greet(scatter.targets)

    def expand_start(layer):
        def act(rows):
            branch[rows, :] = up[rows, :].astype(LOW)
            sums[0, rows, :] = jnp.zeros((128, 1024), WIDE)

        over_rows(act)
        load_turned(0, 0, 1 - layer).wait()
        pl.when(layer == 0)(lambda: load_turned(0, 1, 4).start())

    def expand_turn(part, number):
        load_half(0, 0, number).wait()
        load_shrink(0, 0, number).wait()
        low, high = pl.ds(0, WIDTH), pl.ds(WIDTH, WIDTH)
        back_hidden = contract_cols(branch[:, :512], shrink[number % 2, 0])
        back_hidden = back_hidden + contract_cols(branch[:, 512:], shrink[number % 2, 1])
        first = half_in[number % 2, 0].astype(WIDE)
        second = half_in[number % 2, 1].astype(WIDE)
        back[0, :, low] = (back_hidden * second).astype(LOW)
        back[0, :, high] = (back_hidden * first).astype(LOW)

    def output_start(layer):
        load_turned(0, 0, 2 - layer).wait()
        load_turned(layer, 0, 3 - layer).start()
        fetch(1, 1).wait()

        def act(rows):
            values = middle[rows, :]
            back_second = sums[0, rows, :]
            new = up[rows, :] + norm_back(values, back_second)
            up[rows, :] = new
            gated_branch[rows, :] = new.astype(LOW)
            sums[1, rows, :] = jnp.zeros((128, 1024), WIDE)

        over_rows(act)

    def output_turn(part):
        for f in range(2):
            lanes = pl.ds(pl.multiple_of(f * 512 + part * WIDTH, WIDTH), WIDTH)
            back[0, :, pl.ds(f * WIDTH, WIDTH)] = gated_branch[:, lanes]

    def project_start(layer):
        @pl.when(layer == 1)
        def _():
            fetch_between().wait()
            fetch(1, 0).start()
            load_turned(0, 2, 3).start()

        @pl.when(layer == 0)
        def _():
            def act(rows):
                layer_in[rows, :] = tokens[rows, :].astype(WIDE) * validity[rows, :]

            over_rows(act)

        def clear(rows):
            sums[0, rows, :] = jnp.zeros((128, 1024), WIDE)

        over_rows(clear)
        load_turned(0, 0, 1 - layer).wait()

    def project_turn(layer, group):
        load_stage(0, 0).wait()
        coming = sums.at[1]
        pl.when(layer == 1)(lambda: linear_mixer_back(group, stage, coming, back))

        @pl.when(layer == 0)
        def _():
            load_attends(0).wait()
            local_mixer_back(group, stage, attends, validity, coming, back)

    def finish_layer(layer):
        def act(rows):
            up[rows, :] = up[rows, :] + norm_back(layer_in[rows, :], sums[0, rows, :])

        over_rows(act)

    def terms(number, which, order):
        slot = number % TERM_SLOTS
        out = wide_buffers[0]

        def body(tile, carry):
            rows = pl.ds(pl.multiple_of(tile * 512, 512), 512)
            value = dot(turned[order % 2, rows, :], back[which]).astype(LOW)
            for f in range(2):
                part = value[:, f * WIDTH : (f + 1) * WIDTH]
                out[slot, f, tile] = part.reshape(2, 2, 2, 64, WIDTH)
            return carry

        lax.fori_loop(0, 2, body, 0)

    def tall_terms(part, number):
        out = tall_buffers[0]
        pl.when(part == 0)(lambda: fetch(2, 0).wait())
        lanes = [pl.ds(pl.multiple_of(f * 512 + part * 128, 128), 128) for f in range(2)]
        both = jnp.concatenate([branch[:, lanes[0]], branch[:, lanes[1]]], axis=1)

        def body(tile, carry):
            rows = pl.ds(pl.multiple_of(tile * 8 * TALL_ROWS, 8 * TALL_ROWS), 8 * TALL_ROWS)
            value = dot(hidden_turned[rows, :], both).astype(LOW)
            for f in range(2):
                out[0, f, tile] = value[:, f * 128 : f * 128 + 128].reshape(
                    2, 2, 2, TALL_ROWS, SHRINK_WIDTH
                )
            return carry

        lax.fori_loop(0, 2, body, 0)

        @pl.when((part == SHRINK_PARTS - 1) & (number < LAYER_CHUNKS))
        def _():
            fetch(2, 0).start()

    def spread(number, which, kind):
        def body(t, carry):
            rows = pl.ds(pl.multiple_of(t * 512, 512), 512)
            value = contract_cols(back[which], loaded[number % 2, rows, :])
            sums[kind, :, rows] = sums[kind, :, rows] + value
            return carry

        lax.fori_loop(0, 2, body, 0)

    def body(step, carry):
        pl.when(step + 1 < CHUNKS)(lambda: prefetch(step + 1))
        scatter.older(step)

        @pl.when(step < CHUNKS)
        def _():
            layer = 1 - step // LAYER_CHUNKS
            turn = step % LAYER_CHUNKS
            pl.when(turn == 0)(lambda: expand_start(layer))
            pl.when(turn == OUTPUT_TURN)(lambda: output_start(layer))
            pl.when(turn == PROJECT_TURN)(lambda: project_start(layer))
            pl.when(turn < OUTPUT_TURN)(lambda: expand_turn(turn, step))
            pl.when((turn >= OUTPUT_TURN) & (turn < PROJECT_TURN))(
                lambda: output_turn(turn - OUTPUT_TURN)
            )
            pl.when((turn >= PROJECT_TURN) & ((turn - PROJECT_TURN) % 2 == 0))(
                lambda: project_turn(layer, (turn - PROJECT_TURN) // 2)
            )
            in_project = jnp.minimum(jnp.maximum(turn - PROJECT_TURN + 1, 0), 1)
            in_output = jnp.minimum(jnp.maximum(turn - OUTPUT_TURN + 1, 0), 1) - in_project
            which = in_project * ((turn + PROJECT_TURN) % 2)
            terms(step, which, 1 - layer + in_output)
            place, part, due = scatter.tall_turn(step)
            pl.when(due)(lambda: tall_terms(part, step))
            scatter.start(0, step)
            Load(0, step).wait()
            spread(step, which, in_output)
            pl.when(turn == LAYER_CHUNKS - 1)(lambda: finish_layer(layer))

            @pl.when(step == CHUNKS - 1)
            def _():
                def act(rows):
                    up[rows, :] = up[rows, :] * validity[rows, :]

                over_rows(act)
                pltpu.make_async_copy(up, tokens_out, misc_sem.at[3]).start()

        return carry

    lax.fori_loop(0, CHUNKS + PHASES * SCATTER_LAG, body, 0)
    pltpu.make_async_copy(up, tokens_out, misc_sem.at[3]).wait()
    scatter.finish()


def scatter_buffers(terms, slots, rows, width):
    bits = [(2,) * (4 - phase) for phase in range(5)]
    return (
        [pltpu.VMEM((terms, 2, 2, 2, 2, 2, rows, width), LOW)]
        + [pltpu.VMEM((slots,) + lead + (rows, width), LOW) for lead in bits]
        + [pltpu.VMEM((2, rows, width), WIDE)]
    )


def run_backward(cotangent, tokens, validity, forward):
    struct = jax.ShapeDtypeStruct
    held, tall, mixed_out, between, middles, turns, stages, kept, hidden, attends = forward
    return pl.pallas_call(
        backward_kernel,
        out_shape=(
            struct((ROWS, 1024), WIDE),
            struct((CHUNKS, 64, WIDTH), WIDE),
            struct((2 * SHRINK_PARTS, TALL_ROWS, SHRINK_WIDTH), WIDE),
        ),
        in_specs=[FULL] * 3 + [ANY] * 9,
        out_specs=(ANY,) * 3,
        scratch_shapes=[
            pltpu.SemaphoreType.DMA((10, SCATTER_SLOTS)),
            pltpu.SemaphoreType.DMA((10, SCATTER_SLOTS)),
            pltpu.SemaphoreType.DMA((10, TALL_SLOTS)),
            pltpu.SemaphoreType.DMA((10, TALL_SLOTS)),
            pltpu.SemaphoreType.DMA((2,)),
            pltpu.SemaphoreType.DMA((2,)),
            pltpu.SemaphoreType.DMA((2, 2)),
            pltpu.SemaphoreType.DMA((2,)),
            pltpu.SemaphoreType.DMA((2,)),
            pltpu.SemaphoreType.DMA,
            pltpu.SemaphoreType.DMA((2,)),
            pltpu.SemaphoreType.DMA((5,)),
        ]
        + scatter_buffers(TERM_SLOTS, SCATTER_SLOTS, 64, WIDTH)
        + scatter_buffers(1, TALL_SLOTS, TALL_ROWS, SHRINK_WIDTH)
        + [
            pltpu.VMEM((2, 1024, 2 * WIDTH), LOW),
            pltpu.VMEM((2, 2, ROWS, WIDTH), LOW),
            pltpu.VMEM((5, ROWS, WIDTH), LOW),
            pltpu.VMEM((8, 2, 128, 128), LOW),
            pltpu.VMEM((2, 2, WIDTH, 512), LOW),
            pltpu.VMEM((2816, ROWS), LOW),
            pltpu.VMEM((ROWS, 1024), LOW),
            pltpu.VMEM((ROWS, 1024), LOW),
            pltpu.VMEM((ROWS, 1024), WIDE),
            pltpu.VMEM((2, ROWS, 1024), WIDE),
            pltpu.VMEM((ROWS, 1024), WIDE),
            pltpu.VMEM((ROWS, 1024), WIDE),
            pltpu.VMEM((2, 1024, ROWS), LOW),
            pltpu.VMEM((2, ROWS, 2 * WIDTH), LOW),
        ],
        compiler_params=pltpu.CompilerParams(
            collective_id=1, has_side_effects=True, vmem_limit_bytes=62 << 20
        ),
    )(
        cotangent,
        tokens,
        validity,
        held.reshape(CHUNKS, 2, 1024, WIDTH),
        tall.reshape(2, 2, 2816, 512),
        between,
        middles,
        turns,
        stages,
        kept,
        hidden,
        attends,
    )


def unpack_kernel(mixed_in, tokens_in, chunks, parts, *refs):
    outs, sem = refs[:-1], refs[-1]
    copies = [(mixed_in, outs[0]), (tokens_in, outs[1])]
    for order in range(2):
        layer = 1 - order
        for turn in range(LAYER_CHUNKS):
            number = order * LAYER_CHUNKS + turn
            if turn < OUTPUT_TURN:
                weight, start = 2, chunk_columns(2, turn)
            elif turn < PROJECT_TURN:
                weight, start = 1, chunk_columns(1, turn - OUTPUT_TURN)
            else:
                weight, start = 0, chunk_columns(0, turn - PROJECT_TURN)
            target = outs[2 + 4 * layer + weight].at[:, pl.ds(start, WIDTH)]
            copies.append((chunks.at[number], target))
        for part in range(SHRINK_PARTS):
            target = outs[5 + 4 * layer].at[:, pl.ds(part * SHRINK_WIDTH, SHRINK_WIDTH)]
            copies.append((parts.at[order * SHRINK_PARTS + part], target))
    copies = [
        pltpu.make_async_copy(source, target, sem.at[i])
        for i, (source, target) in enumerate(copies)
    ]
    for copy in copies:
        copy.start()
    for copy in copies:
        copy.wait()


def unpack(mixed_out, tokens_gradient, chunks, parts, shards_of):
    struct = jax.ShapeDtypeStruct
    count = 2 + CHUNKS + 2 * SHRINK_PARTS
    return pl.pallas_call(
        unpack_kernel,
        out_shape=(struct(mixed_out.shape, LOW), struct(tokens_gradient.shape, WIDE))
        + tuple(struct(item.shape, WIDE) for item in shards_of),
        in_specs=[FULL] * 4,
        out_specs=(ANY,) * (2 + WEIGHTS),
        scratch_shapes=[pltpu.SemaphoreType.DMA((count,))],
        compiler_params=pltpu.CompilerParams(vmem_limit_bytes=32 << 20),
    )(mixed_out, tokens_gradient, chunks, parts)


def gather_weights(shards_of):
    return [
        lax.all_gather(lax.all_gather(item, "fsdp", axis=1, tiled=True), "dp", axis=0, tiled=True)
        for item in shards_of
    ]


def settle_gradients(terms):
    tall = [
        lax.psum_scatter(item.astype(jnp.bfloat16), "dp", scatter_dimension=0, tiled=True)
        for item in terms
    ]
    return [
        lax.psum_scatter(item, "fsdp", scatter_dimension=1, tiled=True).astype(jnp.float32)
        for item in tall
    ]


def local_scores(queries, keys_all):
    query_blocks = split_heads(queries.astype(jnp.bfloat16))
    key_blocks = split_heads(keys_all.astype(jnp.bfloat16))
    scores = jnp.einsum(
        "bihd,bjhd->bhij", query_blocks, key_blocks, preferred_element_type=jnp.float32
    ) * HEAD ** (-0.5)
    return (query_blocks, key_blocks, jnp.where(causal_table(), scores, -1e30))


def local_forward(queries, keys_all, values_low, validity):
    query_blocks, key_blocks, scores = local_scores(queries, keys_all)
    highest_score = jnp.max(scores, axis=-1, keepdims=True)
    expweights = jnp.exp(scores - highest_score)
    row_total = jnp.sum(expweights, axis=-1, keepdims=True)
    attend = (expweights / row_total).astype(jnp.bfloat16)
    mixture = jnp.einsum(
        "bhij,bjhd->bihd", attend, split_heads(values_low), preferred_element_type=jnp.float32
    )
    return (join_heads(mixture) * validity, highest_score + jnp.log(row_total))


def local_backward(queries, keys_all, values_low, validity, logsum, back_mixture):
    query_blocks, key_blocks, scores = local_scores(queries, keys_all)
    value_blocks = split_heads(values_low)
    coming = split_heads(back_mixture * validity.astype(jnp.bfloat16))
    attend = jnp.exp(scores - logsum)
    back_values = jnp.einsum(
        "bhij,bihd->bjhd", attend.astype(jnp.bfloat16), coming, preferred_element_type=jnp.float32
    )
    back_attend = jnp.einsum(
        "bihd,bjhd->bhij", coming, value_blocks, preferred_element_type=jnp.float32
    )
    back_scores = (
        attend * (back_attend - jnp.sum(back_attend * attend, axis=-1, keepdims=True))
    ).astype(jnp.bfloat16)
    back_queries = jnp.einsum(
        "bhij,bjhd->bihd", back_scores, key_blocks, preferred_element_type=jnp.float32
    ) * HEAD ** (-0.5)
    back_keys = jnp.einsum(
        "bhij,bihd->bjhd", back_scores, query_blocks, preferred_element_type=jnp.float32
    ) * HEAD ** (-0.5)
    return (join_heads(back_queries), join_heads(back_keys), join_heads(back_values))


def linear_parts(queries, keys_all, values_low):
    feature_q = split_heads(jax.nn.softplus(queries).astype(jnp.bfloat16))
    feature_k = split_heads(jax.nn.softplus(keys_all).astype(jnp.bfloat16))
    value_blocks = split_heads(values_low)
    causal = causal_table().astype(jnp.float32)
    inner_scores = (
        jnp.einsum("bihd,bjhd->bhij", feature_q, feature_k, preferred_element_type=jnp.float32)
        * causal
    ).astype(jnp.bfloat16)
    states = jnp.einsum(
        "bjhd,bjhe->bhde", feature_k, value_blocks, preferred_element_type=jnp.float32
    )
    running = jnp.cumsum(states, axis=0)
    prior_states = jnp.concatenate([jnp.zeros_like(states[:1]), running[:-1]], axis=0)
    return (feature_q, feature_k, value_blocks, causal, inner_scores, prior_states)


def linear_forward(queries, keys_all, values_low):
    feature_q, feature_k, value_blocks, causal, inner_scores, prior_states = linear_parts(
        queries, keys_all, values_low
    )
    mixture = jnp.einsum(
        "bhij,bjhe->bihe", inner_scores, value_blocks, preferred_element_type=jnp.float32
    )
    mixture = mixture + jnp.einsum(
        "bihd,bhde->bihe", feature_q.astype(jnp.float32), prior_states, precision=highest
    )
    return join_heads(mixture)


def linear_backward(queries, keys_all, values_low, back_mixture):
    feature_q, feature_k, value_blocks, causal, inner_scores, prior_states = linear_parts(
        queries, keys_all, values_low
    )
    coming = split_heads(back_mixture)
    coming_wide = coming.astype(jnp.float32)
    back_inner = (
        jnp.einsum("bihe,bjhe->bhij", coming, value_blocks, preferred_element_type=jnp.float32)
        * causal
    ).astype(jnp.bfloat16)
    back_feature_q = jnp.einsum(
        "bhij,bjhd->bihd", back_inner, feature_k, preferred_element_type=jnp.float32
    )
    back_feature_q = back_feature_q + jnp.einsum(
        "bihe,bhde->bihd", coming_wide, prior_states, precision=highest
    )
    back_feature_k = jnp.einsum(
        "bhij,bihd->bjhd", back_inner, feature_q, preferred_element_type=jnp.float32
    )
    back_values = jnp.einsum(
        "bhij,bihe->bjhe", inner_scores, coming, preferred_element_type=jnp.float32
    )
    back_prior = jnp.einsum(
        "bihd,bihe->bhde", feature_q.astype(jnp.float32), coming_wide, precision=highest
    )
    running = jnp.cumsum(back_prior[::-1], axis=0)[::-1]
    later_states = jnp.concatenate([running[1:], jnp.zeros_like(running[:1])], axis=0)
    back_feature_k = back_feature_k + jnp.einsum(
        "bjhe,bhde->bjhd", value_blocks.astype(jnp.float32), later_states, precision=highest
    )
    back_values = back_values + jnp.einsum(
        "bjhd,bhde->bjhe", feature_k.astype(jnp.float32), later_states, precision=highest
    )
    return (
        join_heads(back_feature_q) * jax.nn.sigmoid(queries),
        join_heads(back_feature_k) * jax.nn.sigmoid(keys_all),
        join_heads(back_values),
    )


def forward_layer(layer_in, validity, weights, local):
    project, output, expand, shrink = weights
    normed = simple_norm(layer_in).astype(jnp.bfloat16)
    projected = jnp.dot(normed, project, preferred_element_type=jnp.float32)
    queries, keys_all, values, update = jnp.split(projected, 4, axis=1)
    values_low = values.astype(jnp.bfloat16)
    if local:
        mixture, logsum = local_forward(queries, keys_all, values_low, validity)
    else:
        mixture = linear_forward(queries, keys_all, values_low)
        logsum = None
    gated_rows = (head_norm(mixture) * jax.nn.silu(update)).astype(jnp.bfloat16)
    middle = layer_in + jnp.dot(gated_rows, output, preferred_element_type=jnp.float32)
    second = simple_norm(middle).astype(jnp.bfloat16)
    expanded = jnp.dot(second, expand, preferred_element_type=jnp.float32)
    half_width = expanded.shape[1] // 2
    hidden = (expanded[:, :half_width] * expanded[:, half_width:]).astype(jnp.bfloat16)
    result = middle + jnp.dot(hidden, shrink, preferred_element_type=jnp.float32)
    return (
        result,
        (layer_in, normed, projected, values_low, mixture, logsum, gated_rows, middle, second),
    )


def backward_layer(upstream, saved, weights, validity, local):
    project, output, expand, shrink = weights
    layer_in, normed, projected, values_low, mixture, logsum, gated_rows, middle, second = saved
    expanded = jnp.dot(second, expand, preferred_element_type=jnp.float32)
    half_width = expanded.shape[1] // 2
    first_half = expanded[:, :half_width]
    second_half = expanded[:, half_width:]
    hidden = (first_half * second_half).astype(jnp.bfloat16)
    back_branch = upstream.astype(jnp.bfloat16)
    shrink_term = contract_rows(hidden, back_branch)
    back_hidden = contract_cols(back_branch, shrink)
    back_expanded = jnp.concatenate(
        [back_hidden * second_half, back_hidden * first_half], axis=1
    ).astype(jnp.bfloat16)
    expand_term = contract_rows(second, back_expanded)
    back_second = contract_cols(back_expanded, expand)
    back_middle = upstream + norm_back(middle, back_second)
    back_gated = back_middle.astype(jnp.bfloat16)
    output_term = contract_rows(gated_rows, back_gated)
    back_rows_gated = contract_cols(back_gated, output)
    queries, keys_all, unused_values, update = jnp.split(projected, 4, axis=1)
    back_update = back_rows_gated * head_norm(mixture) * silu_slope(update)
    back_mixture = head_back(mixture, back_rows_gated * jax.nn.silu(update)).astype(jnp.bfloat16)
    if local:
        back_queries, back_keys, back_values = local_backward(
            queries, keys_all, values_low, validity, logsum, back_mixture
        )
    else:
        back_queries, back_keys, back_values = linear_backward(
            queries, keys_all, values_low, back_mixture
        )
    back_projected = jnp.concatenate(
        [back_queries, back_keys, back_values, back_update], axis=1
    ).astype(jnp.bfloat16)
    project_term = contract_rows(normed, back_projected)
    back_normed = contract_cols(back_projected, project)
    back_input = back_middle + norm_back(layer_in, back_normed)
    return (back_input, (project_term, output_term, expand_term, shrink_term))


def shards(
    direct,
    tokens,
    lengths,
    local_project,
    local_output,
    local_expand,
    local_shrink,
    linear_project,
    linear_output,
    linear_expand,
    linear_shrink,
    cotangent,
):
    positions = lax.broadcasted_iota(jnp.int32, (tokens.shape[1], 1), 0)
    validity = (positions < lengths[0]).astype(jnp.float32)
    shards_of = [
        local_project,
        local_output,
        local_expand,
        local_shrink,
        linear_project,
        linear_output,
        linear_expand,
        linear_shrink,
    ]
    if direct:
        forward = run_forward(shards_of, tokens[0], validity)
        back_tokens, chunks, parts = run_backward(cotangent[0], tokens[0], validity, forward)
        outs = unpack(forward[2], back_tokens, chunks, parts, shards_of)
        return (outs[0][None], outs[1][None]) + tuple(outs[2:])
    layer_in = tokens[0].astype(jnp.float32) * validity
    whole = gather_weights(shards_of)
    local_weights = whole[:4]
    linear_weights = whole[4:]
    between, local_saved = forward_layer(layer_in, validity, local_weights, True)
    result, linear_saved = forward_layer(between, validity, linear_weights, False)
    result = (result * validity).astype(jnp.bfloat16)
    upstream = cotangent[0].astype(jnp.float32) * validity
    back_between, linear_terms = backward_layer(
        upstream, linear_saved, linear_weights, validity, False
    )
    back_input, local_terms = backward_layer(
        back_between, local_saved, local_weights, validity, True
    )
    sums = settle_gradients(local_terms + linear_terms)
    return (
        result[None],
        (back_input * validity)[None],
    ) + tuple(sums)


def solution(mesh):
    in_specs = (
        P(("dp", "fsdp"), None, None),
        P(("dp", "fsdp")),
        P("dp", "fsdp"),
        P("dp", "fsdp"),
        P("dp", "fsdp"),
        P("dp", "fsdp"),
        P("dp", "fsdp"),
        P("dp", "fsdp"),
        P("dp", "fsdp"),
        P("dp", "fsdp"),
        P(("dp", "fsdp"), None, None),
    )
    out_specs = (
        P(("dp", "fsdp"), None, None),
        P(("dp", "fsdp"), None, None),
        P("dp", "fsdp"),
        P("dp", "fsdp"),
        P("dp", "fsdp"),
        P("dp", "fsdp"),
        P("dp", "fsdp"),
        P("dp", "fsdp"),
        P("dp", "fsdp"),
        P("dp", "fsdp"),
    )
    direct = dict(mesh.shape) == {"dp": 16, "fsdp": 2}
    return jax.shard_map(functools.partial(shards, direct), mesh=mesh, in_specs=in_specs, out_specs=out_specs, check_vma=False)
```

```python
import functools

import jax
import jax.numpy as jnp
from jax import lax
from jax.experimental import pallas as pl
from jax.experimental.pallas import tpu as pltpu
from jax.sharding import PartitionSpec as P

HEADS = 16
HEAD = 64
BLOCK = 64


epsilon = 1e-05
highest = lax.Precision.HIGHEST


def simple_norm(values):
    return values * lax.rsqrt(jnp.mean(values * values, axis=-1, keepdims=True) + epsilon)


def norm_back(values, upstream):
    inverse_rms = lax.rsqrt(jnp.mean(values * values, axis=-1, keepdims=True) + epsilon)
    return inverse_rms * (
        upstream
        - values * (inverse_rms * inverse_rms) * jnp.mean(upstream * values, axis=-1, keepdims=True)
    )


def head_norm(values):
    shaped = values.reshape(values.shape[0], HEADS, HEAD)
    return simple_norm(shaped).reshape(values.shape)


def head_back(values, upstream):
    shaped = values.reshape(values.shape[0], HEADS, HEAD)
    coming = upstream.reshape(values.shape[0], HEADS, HEAD)
    return norm_back(shaped, coming).reshape(values.shape)


def silu_slope(values):
    logistic = jax.nn.sigmoid(values)
    return logistic * (1.0 + values * (1.0 - logistic))


def contract_rows(first_matrix, second_matrix):
    return lax.dot_general(
        first_matrix, second_matrix, (((0,), (0,)), ((), ())), preferred_element_type=jnp.float32
    )


def contract_cols(first_matrix, second_matrix):
    return lax.dot_general(
        first_matrix, second_matrix, (((1,), (1,)), ((), ())), preferred_element_type=jnp.float32
    )


def causal_table():
    return lax.broadcasted_iota(jnp.int32, (BLOCK, BLOCK), 0) >= lax.broadcasted_iota(
        jnp.int32, (BLOCK, BLOCK), 1
    )


def split_heads(values):
    return values.reshape(values.shape[0] // BLOCK, BLOCK, HEADS, HEAD)


def join_heads(values):
    return values.reshape(values.shape[0] * BLOCK, HEADS * HEAD)


AXIS_NAMES = ("f", "zh", "zl", "y", "c")
AXIS_OF = {"c": "c", "y": "y", "x": "f", "z1": "zl", "z2": "zh"}
MESH = pl.DeviceIdType.MESH
ANY = pl.BlockSpec(memory_space=pl.ANY)
FULL = pl.BlockSpec(memory_space=pltpu.VMEM)
WEIGHTS = 8
WIDTH = 256
PHASES = 5
GATHER_STEPS = (0, 3, 6, 9, 12, 15)
HEAD_GROUPS = 4
PROJECT_CHUNKS = 8
OUTPUT_CHUNKS = 2
EXPAND_CHUNKS = 11
LAYER_CHUNKS = PROJECT_CHUNKS + OUTPUT_CHUNKS + EXPAND_CHUNKS
CHUNKS = 2 * LAYER_CHUNKS
SHRINK_PARTS = 4
SHRINK_WIDTH = 128
GATHER_SLOTS = 8
LOAD_SLOTS = 3
LOW = jnp.bfloat16
WIDE = jnp.float32
ROWS = 512


def neighbours():
    dp = lax.axis_index("dp")
    x = lax.axis_index("fsdp")
    z = dp // 4
    y = (dp // 2) % 2
    c = dp % 2
    places = {"f": x, "zh": z // 2, "zl": z % 2, "y": y, "c": c}
    targets = {
        "z1": ((z + 1 - 2 * (z % 2)) * 4 + y * 2 + c, x),
        "z2": (lax.rem(z + 2, 4) * 4 + y * 2 + c, x),
        "y": (z * 4 + (1 - y) * 2 + c, x),
        "c": (z * 4 + y * 2 + (1 - c), x),
        "x": (dp, 1 - x),
    }
    return places, targets


def greet(targets):
    barrier = pltpu.get_barrier_semaphore()
    for target in targets.values():
        pl.semaphore_signal(barrier, inc=1, device_id=target, device_id_type=MESH)
    pl.semaphore_wait(barrier, len(targets))


def dot(left, right):
    return jnp.dot(left, right, preferred_element_type=WIDE)


def softplus(values):
    return jnp.maximum(values, 0.0) + jnp.log1p(jnp.exp(-jnp.abs(values)))


def logistic(values):
    return 1.0 / (1.0 + jnp.exp(-values))


def first_lanes(rows):
    return lax.broadcasted_iota(jnp.int32, (rows, 128), 1) < HEAD


def pair_mean(values, first):
    left = jnp.sum(jnp.where(first, values, 0.0), axis=-1, keepdims=True)
    right = jnp.sum(jnp.where(first, 0.0, values), axis=-1, keepdims=True)
    return jnp.where(first, left, right) * (1.0 / HEAD)


def block_mask(rows):
    i = lax.broadcasted_iota(jnp.int32, (rows, rows), 0)
    j = lax.broadcasted_iota(jnp.int32, (rows, rows), 1)
    return (i // BLOCK == j // BLOCK) & (j <= i)


def norm_into(source, target):
    def body(t, carry):
        rows = pl.ds(pl.multiple_of(t * 128, 128), 128)
        target[rows, :] = simple_norm(source[rows, :]).astype(LOW)
        return carry

    lax.fori_loop(0, ROWS // 128, body, 0)


def local_mixer(group, parts, validity, gated, stage, attends):
    def body(turn, carry):
        t = turn // 2
        rows = pl.ds(pl.multiple_of(t * 128, 128), 128)
        pair = turn % 2
        lanes = pl.ds(pl.multiple_of(pair * 128, 128), 128)
        first = first_lanes(128)
        q = parts[0, 0, rows, lanes].astype(LOW)
        k = parts[1, 0, rows, lanes].astype(LOW)
        v = parts[0, 1, rows, lanes].astype(LOW)
        u = parts[1, 1, rows, lanes]
        keep = block_mask(128)
        mixed = []
        for head in range(2):
            mine = jnp.where(first == (head == 0), q, jnp.zeros_like(q))
            scores = contract_cols(mine, k) * HEAD ** (-0.5)
            scores = jnp.where(keep, scores, -1e30)
            highest_score = jnp.max(scores, axis=-1, keepdims=True)
            weights = jnp.exp(scores - highest_score)
            attend = (weights / jnp.sum(weights, axis=-1, keepdims=True)).astype(LOW)
            attends[turn, head] = attend
            mixed.append(dot(attend, v))
        mixture = jnp.where(first, mixed[0], mixed[1]) * validity[rows, :]
        scale = lax.rsqrt(pair_mean(mixture * mixture, first) + epsilon)
        columns = pl.ds(pl.multiple_of(group * WIDTH + pair * 128, 128), 128)
        gated[rows, columns] = (mixture * scale * (u * logistic(u))).astype(LOW)
        stage[4, rows, lanes] = mixture.astype(LOW)
        return carry

    lax.fori_loop(0, 2 * ROWS // 128, body, 0)


def linear_mixer(group, parts, gated, stage):
    half = ROWS // 2

    def body(pair, carry):
        lanes = pl.ds(pl.multiple_of(pair * 128, 128), 128)
        columns = pl.ds(pl.multiple_of(group * WIDTH + pair * 128, 128), 128)
        first = first_lanes(half)
        fk = softplus(parts[1, 0, :, lanes]).astype(LOW)
        v = parts[0, 1, :, lanes].astype(LOW)
        for t in range(2):
            rows = pl.ds(t * half, half)
            reach = (t + 1) * half
            fq = softplus(parts[0, 0, rows, lanes]).astype(LOW)
            i = lax.broadcasted_iota(jnp.int32, (half, reach), 0) + t * half
            j = lax.broadcasted_iota(jnp.int32, (half, reach), 1)
            mixed = []
            for head in range(2):
                mine = jnp.where(first == (head == 0), fq, jnp.zeros_like(fq))
                scores = jnp.where(j <= i, contract_cols(mine, fk[:reach]), 0.0).astype(LOW)
                mixed.append(dot(scores, v[:reach]))
            mixture = jnp.where(first, mixed[0], mixed[1])
            scale = lax.rsqrt(pair_mean(mixture * mixture, first) + epsilon)
            u = parts[1, 1, rows, lanes]
            gated[rows, columns] = (mixture * scale * (u * logistic(u))).astype(LOW)
            stage[4, rows, lanes] = mixture.astype(LOW)
        return carry

    lax.fori_loop(0, 2, body, 0)


def chunk_columns(weight, part):
    if weight == 0:
        return (part % 2) * 1024 + (part // 2) * WIDTH
    return part * WIDTH


class Gather:
    def __init__(self, own, held, tall, sems):
        self.own, self.held, self.tall = own, held, tall
        self.local_sem, self.send_sem, self.recv_sem, self.tall_send, self.tall_recv = sems
        self.places, self.targets = neighbours()
        self.at = tuple(self.places[name] for name in ("f", "zh", "zl", "y", "c"))

    def begin(self):
        counts = (PROJECT_CHUNKS, OUTPUT_CHUNKS, EXPAND_CHUNKS)
        for layer in range(2):
            chunk = LAYER_CHUNKS * layer
            for weight in range(3):
                for part in range(counts[weight]):
                    start = chunk_columns(weight, part)
                    pltpu.make_async_copy(
                        self.own[4 * layer + weight].at[:, pl.ds(start, WIDTH)],
                        self.held.at[(chunk,) + self.at],
                        self.local_sem.at[chunk],
                    ).start()
                    chunk += 1
            pltpu.make_async_copy(
                self.own[4 * layer + 3],
                self.tall.at[(layer,) + self.at],
                self.local_sem.at[CHUNKS + layer],
            ).start()
        greet(self.targets)

    def message(self, block, target, sems, place):
        return pltpu.make_async_remote_copy(
            src_ref=block,
            dst_ref=block,
            send_sem=sems[0].at[place],
            recv_sem=sems[1].at[place],
            device_id=self.targets[target],
            device_id_type=MESH,
        )

    def wide_messages(self, phase, chunk):
        x, zh, zl, y, c = self.at
        ref = self.held
        sems = (self.send_sem, self.recv_sem)
        slot = chunk % GATHER_SLOTS
        half = WIDTH // 2
        low, high = pl.ds(0, half), pl.ds(half, half)

        def one(index, target, part):
            return self.message(ref.at[(chunk,) + index], target, sems, (2 * phase + part, slot))

        a = slice(None)
        if phase == 0:
            return [one((x, zh, zl, y, c), "z2", 0)]
        if phase == 1:
            return [one((x, a, zl, y, c), "z1", 0)]
        if phase == 2:
            return [one((x, a, a, y, c, a, low), "x", 0), one((x, a, a, y, c, a, high), "y", 1)]
        if phase == 3:
            return [one((a, a, a, y, c, a, low), "y", 0), one((x, a, a, a, c, a, high), "x", 1)]
        return [one((a, a, a, a, c), "c", 0)]

    def tall_message(self, phase, layer, part, odd):
        x, zh, zl, y, c = self.at
        a = slice(None)
        lanes = pl.ds(pl.multiple_of(part * SHRINK_WIDTH, SHRINK_WIDTH), SHRINK_WIDTH)
        index, target = {
            (0, 0): ((x, zh, zl, y, c), "x"),
            (0, 1): ((x, zh, zl, y, c), "y"),
            (1, 0): ((a, zh, zl, y, c), "y"),
            (1, 1): ((x, zh, zl, a, c), "x"),
            (2, 0): ((a, zh, zl, a, c), "z2"),
            (3, 0): ((a, a, zl, a, c), "z1"),
            (4, 0): ((a, a, a, a, c), "c"),
        }[(phase, odd)]
        return self.message(
            self.tall.at[(layer,) + index + (a, lanes)],
            target,
            (self.tall_send, self.tall_recv),
            (phase, layer * SHRINK_PARTS + part),
        )

    def tall_turn(self, chunk):
        layer = chunk // LAYER_CHUNKS
        place = chunk % LAYER_CHUNKS
        return layer, place // 5, place % 5 == 4

    def for_tall(self, phase, chunk, act):
        layer, part, due = self.tall_turn(chunk)
        if phase >= 2:
            pl.when(due)(lambda: act(self.tall_message(phase, layer, part, 0)))
        else:
            for odd in range(2):
                pl.when(due & (part % 2 == odd))(
                    lambda odd=odd: act(self.tall_message(phase, layer, part, odd))
                )

    def step(self, step):
        for phase in range(PHASES, -1, -1):
            chunk = step - GATHER_STEPS[phase]

            @pl.when((chunk >= 0) & (chunk < CHUNKS))
            def _(phase=phase, chunk=chunk):
                if phase >= 1:
                    for copy in self.wide_messages(phase - 1, chunk):
                        copy.wait()
                    self.for_tall(phase - 1, chunk, lambda copy: copy.wait())
                else:
                    pltpu.make_async_copy(
                        self.own[0].at[:, pl.ds(0, WIDTH)],
                        self.held.at[(chunk,) + self.at],
                        self.local_sem.at[chunk],
                    ).wait()
                    layer = chunk // LAYER_CHUNKS

                    @pl.when(chunk % LAYER_CHUNKS == 4)
                    def _():
                        pltpu.make_async_copy(
                            self.own[3],
                            self.tall.at[(layer,) + self.at],
                            self.local_sem.at[CHUNKS + layer],
                        ).wait()

                if phase < PHASES:
                    for copy in self.wide_messages(phase, chunk):
                        copy.start()
                    self.for_tall(phase, chunk, lambda copy: copy.start())


def forward_kernel(*refs):
    own = refs[:WEIGHTS]
    tokens, validity = refs[WEIGHTS : WEIGHTS + 2]
    held, tall, mixed_out, between, middles, turns, stages, halves_out = refs[10:18]
    hidden_out, attends_out = refs[18:20]
    scratch = refs[20:]
    sems, (load_sem, tall_sem, stage_sem, half_sem, hidden_sem, misc_sem) = scratch[:5], scratch[5:11]
    loaded, shrink, x, middle, normed, gated, hidden, parts, stage, half_stage, final = scratch[11:22]
    turned, hidden_stage, attends = scratch[22:]
    gather = Gather(own, held, tall, sems)
    gather.begin()

    def rows_of(t):
        return pl.ds(pl.multiple_of(t * 128, 128), 128)

    def start_rows(t, carry):
        rows = rows_of(t)
        x[rows, :] = tokens[rows, :].astype(WIDE) * validity[rows, :]
        return carry

    def keep_turned(layer, kind):
        return pltpu.make_async_copy(turned, turns.at[layer, kind], misc_sem.at[0])

    def turn(source, layer, kind):
        def act(t, carry):
            rows = rows_of(t)
            turned[:, rows] = source[rows, :].T
            return carry

        lax.fori_loop(0, ROWS // 128, act, 0)
        keep_turned(layer, kind).start()

    lax.fori_loop(0, ROWS // 128, start_rows, 0)
    norm_into(x, normed)
    turn(normed, 0, 0)

    def load(chunk):
        return pltpu.make_async_copy(
            held.at[chunk], loaded.at[chunk % LOAD_SLOTS], load_sem.at[chunk % LOAD_SLOTS]
        )

    def load_tall(layer):
        return pltpu.make_async_copy(tall.at[layer], shrink, tall_sem)

    def keep_stage(layer, group):
        return pltpu.make_async_copy(stage, stages.at[layer, group], stage_sem)

    def keep_half(layer, part):
        return pltpu.make_async_copy(
            half_stage.at[part % 2], halves_out.at[layer, part], half_sem.at[part % 2]
        )

    def keep_hidden(layer, part):
        rows = pl.ds(pl.multiple_of(part * WIDTH, WIDTH), WIDTH)
        return pltpu.make_async_copy(
            hidden_stage.at[part % 2], hidden_out.at[layer, rows, :], hidden_sem.at[part % 2]
        )

    def keep_attends(group):
        return pltpu.make_async_copy(attends, attends_out.at[group], misc_sem.at[4])

    def keep_middle(layer):
        return pltpu.make_async_copy(middle, middles.at[layer], misc_sem.at[1])

    def keep_between():
        return pltpu.make_async_copy(x, between, misc_sem.at[2])

    def weight(slot, f):
        return loaded[slot, f].reshape(1024, WIDTH)

    def project_step(layer, place, slot):
        group = place // 2
        for f in range(2):
            parts[place % 2, f] = dot(normed[...], weight(slot, f))

        @pl.when(place % 2 == 1)
        def _():
            @pl.when((layer > 0) | (group > 0))
            def _():
                keep_stage(layer, group).wait()

            @pl.when((layer == 0) & (group > 0))
            def _():
                keep_attends(0).wait()

            for kind in range(4):
                stage[kind] = parts[kind % 2, kind // 2].astype(LOW)

            @pl.when(layer == 0)
            def _():
                local_mixer(group, parts, validity, gated, stage, attends)
                keep_attends(group).start()

            pl.when(layer > 0)(lambda: linear_mixer(group, parts, gated, stage))
            keep_stage(layer, group).start()

    def output_step(layer, part, slot):
        @pl.when(part == 0)
        def _():
            keep_turned(0, 0).wait()
            turn(gated, layer, 1)

            @pl.when(layer > 0)
            def _():
                keep_middle(0).wait()

        for f in range(2):
            lanes = pl.ds(pl.multiple_of(f * 512 + part * WIDTH, WIDTH), WIDTH)
            middle[:, lanes] = x[:, lanes] + dot(gated[...], weight(slot, f))

        @pl.when(part == OUTPUT_CHUNKS - 1)
        def _():
            keep_middle(layer).start()
            norm_into(middle, normed)
            keep_turned(0, 0).wait()
            turn(normed, layer, 2)

    def expand_step(layer, part, slot):
        @pl.when((layer > 0) | (part > 1))
        def _():
            keep_half(layer, part).wait()
            keep_hidden(layer, part).wait()

        first = dot(normed[...], weight(slot, 0))
        second = dot(normed[...], weight(slot, 1))
        half_stage[part % 2, 0] = first.astype(LOW)
        half_stage[part % 2, 1] = second.astype(LOW)
        both = (first * second).astype(LOW)
        hidden[:, pl.ds(pl.multiple_of(part * WIDTH, WIDTH), WIDTH)] = both
        hidden_stage[part % 2] = both.T
        keep_half(layer, part).start()
        keep_hidden(layer, part).start()

    def shrink_step(layer):
        load_tall(layer).wait()

        @pl.when(layer > 0)
        def _():
            keep_between().wait()

        def body(turn, carry):
            f = turn // 2
            columns = pl.ds(pl.multiple_of((turn % 2) * WIDTH, WIDTH), WIDTH)
            lanes = pl.ds(pl.multiple_of(turn * WIDTH, WIDTH), WIDTH)
            matrix = shrink[f, :, :, :, :, :, columns].reshape(hidden.shape[1], WIDTH)
            x[:, lanes] = middle[:, lanes] + dot(hidden[...], matrix)
            return carry

        lax.fori_loop(0, 4, body, 0)

        @pl.when(layer == 0)
        def _():
            keep_between().start()
            norm_into(x, normed)
            keep_turned(0, 0).wait()
            turn(normed, 1, 0)

        @pl.when(layer > 0)
        def _():
            def last_rows(t, carry):
                rows = rows_of(t)
                final[rows, :] = (x[rows, :] * validity[rows, :]).astype(LOW)
                return carry

            lax.fori_loop(0, ROWS // 128, last_rows, 0)

    def body(step, carry):
        gather.step(step)
        arrived = step - GATHER_STEPS[PHASES]

        @pl.when((arrived >= 0) & (arrived < CHUNKS))
        def _():
            load(arrived).start()

            @pl.when(arrived % LAYER_CHUNKS == LAYER_CHUNKS - 2)
            def _():
                load_tall(arrived // LAYER_CHUNKS).start()

        ready = arrived - 1

        @pl.when((ready >= 0) & (ready < CHUNKS))
        def _():
            load(ready).wait()
            layer = ready // LAYER_CHUNKS
            place = ready % LAYER_CHUNKS
            slot = ready % LOAD_SLOTS
            pl.when(place < PROJECT_CHUNKS)(lambda: project_step(layer, place, slot))
            pl.when((place >= PROJECT_CHUNKS) & (place < PROJECT_CHUNKS + OUTPUT_CHUNKS))(
                lambda: output_step(layer, place - PROJECT_CHUNKS, slot)
            )
            pl.when(place >= PROJECT_CHUNKS + OUTPUT_CHUNKS)(
                lambda: expand_step(layer, place - PROJECT_CHUNKS - OUTPUT_CHUNKS, slot)
            )
            pl.when(place == LAYER_CHUNKS - 1)(lambda: shrink_step(layer))

        return carry

    lax.fori_loop(0, CHUNKS + GATHER_STEPS[PHASES] + 1, body, 0)
    last = pltpu.make_async_copy(final, mixed_out, misc_sem.at[3])
    last.start()
    keep_stage(1, HEAD_GROUPS - 1).wait()
    keep_attends(0).wait()
    keep_turned(0, 0).wait()
    keep_middle(1).wait()
    keep_half(1, EXPAND_CHUNKS - 2).wait()
    keep_half(1, EXPAND_CHUNKS - 1).wait()
    keep_hidden(1, EXPAND_CHUNKS - 2).wait()
    keep_hidden(1, EXPAND_CHUNKS - 1).wait()
    last.wait()


def run_forward(shards_of, tokens, validity):
    bits = (2, 2, 2, 2, 2)
    struct = jax.ShapeDtypeStruct
    return pl.pallas_call(
        forward_kernel,
        out_shape=(
            struct((CHUNKS,) + bits + (64, WIDTH), LOW),
            struct((2,) + bits + (176, 512), LOW),
            struct((ROWS, 1024), LOW),
            struct((ROWS, 1024), WIDE),
            struct((2, ROWS, 1024), WIDE),
            struct((2, 3, 1024, ROWS), LOW),
            struct((2, HEAD_GROUPS, 5, ROWS, WIDTH), LOW),
            struct((2, EXPAND_CHUNKS, 2, ROWS, WIDTH), LOW),
            struct((2, 2816, ROWS), LOW),
            struct((HEAD_GROUPS, 8, 2, 128, 128), LOW),
        ),
        in_specs=[FULL] * (WEIGHTS + 2),
        out_specs=(ANY,) * 10,
        scratch_shapes=[
            pltpu.SemaphoreType.DMA((CHUNKS + 2,)),
            pltpu.SemaphoreType.DMA((10, GATHER_SLOTS)),
            pltpu.SemaphoreType.DMA((10, GATHER_SLOTS)),
            pltpu.SemaphoreType.DMA((PHASES, 2 * SHRINK_PARTS)),
            pltpu.SemaphoreType.DMA((PHASES, 2 * SHRINK_PARTS)),
            pltpu.SemaphoreType.DMA((LOAD_SLOTS,)),
            pltpu.SemaphoreType.DMA,
            pltpu.SemaphoreType.DMA,
            pltpu.SemaphoreType.DMA((2,)),
            pltpu.SemaphoreType.DMA((2,)),
            pltpu.SemaphoreType.DMA((5,)),
            pltpu.VMEM((LOAD_SLOTS,) + bits + (64, WIDTH), LOW),
            pltpu.VMEM(bits + (176, 512), LOW),
            pltpu.VMEM((ROWS, 1024), WIDE),
            pltpu.VMEM((ROWS, 1024), WIDE),
            pltpu.VMEM((ROWS, 1024), LOW),
            pltpu.VMEM((ROWS, 1024), LOW),
            pltpu.VMEM((ROWS, 2816), LOW),
            pltpu.VMEM((2, 2, ROWS, WIDTH), WIDE),
            pltpu.VMEM((5, ROWS, WIDTH), LOW),
            pltpu.VMEM((2, 2, ROWS, WIDTH), LOW),
            pltpu.VMEM((ROWS, 1024), LOW),
            pltpu.VMEM((1024, ROWS), LOW),
            pltpu.VMEM((2, WIDTH, ROWS), LOW),
            pltpu.VMEM((8, 2, 128, 128), LOW),
        ],
        compiler_params=pltpu.CompilerParams(
            collective_id=0, has_side_effects=True, vmem_limit_bytes=60 << 20
        ),
    )(*shards_of, tokens, validity)


SCATTER_STEPS = (0, 2, 5, 8, 11, 14)
SCATTER_SLOTS = 10
TERM_SLOTS = SCATTER_STEPS[1]
TALL_SLOTS = 3
OUTPUT_TURN = EXPAND_CHUNKS
PROJECT_TURN = EXPAND_CHUNKS + OUTPUT_CHUNKS
TALL_ROWS = 176


class Scatter:
    def __init__(self, outs, sems, wide, tall):
        self.outs, self.tall_outs = outs
        self.send_sem, self.recv_sem, self.tall_send, self.tall_recv = sems[:4]
        self.store_sem, self.tall_store = sems[4:]
        self.wide, self.tall = wide[:6], tall[:6]
        self.result, self.tall_result = wide[6], tall[6]
        self.places, self.targets = neighbours()

    def tall_turn(self, chunk):
        layer = chunk // LAYER_CHUNKS
        turn = chunk % LAYER_CHUNKS
        return layer * SHRINK_PARTS + turn // 5, turn // 5, turn % 5 == 4

    def wide_parts(self):
        half = WIDTH // 2
        return (
            (pl.ds(0, half), ("c", "y", "x", "z1", "z2")),
            (pl.ds(half, half), ("c", "x", "y", "z1", "z2")),
        )

    def tall_parts(self, odd):
        plane = ("x", "y") if odd else ("y", "x")
        return ((pl.ds(0, SHRINK_WIDTH), ("c", "z1", "z2") + plane),)

    def left(self, order, phase):
        used = set(AXIS_OF[target] for target in order[: phase + 1])
        return [name for name in AXIS_NAMES if name not in used]

    def source(self, buffers, slots, phase, order):
        if phase == 0:
            return buffers[0].at[slots[0]], list(AXIS_NAMES)
        return buffers[phase].at[slots[1]], self.left(order, phase - 1)

    def messages(self, buffers, slots, sems, phase, parts):
        if phase == 0 and len(parts) == 2:
            parts = ((pl.ds(0, WIDTH), parts[0][1]),)
        out = []
        for part, (lanes, order) in enumerate(parts):
            source, dims = self.source(buffers, slots, phase, order)
            target = order[phase]
            away = tuple(
                1 - self.places[d] if d == AXIS_OF[target] else slice(None) for d in dims
            )
            whole = tuple(slice(None) for _ in self.left(order, phase))
            place = (2 * phase + part, slots[1])
            out.append(
                pltpu.make_async_remote_copy(
                    src_ref=source.at[away + (slice(None), lanes)],
                    dst_ref=buffers[1 + phase].at[(slots[1],) + whole + (slice(None), lanes)],
                    send_sem=sems[0].at[place],
                    recv_sem=sems[1].at[place],
                    device_id=self.targets[target],
                    device_id_type=MESH,
                )
            )
        return out

    def add(self, buffers, slots, phase, parts, result):
        if phase == 0 and len(parts) == 2:
            parts = ((pl.ds(0, WIDTH), parts[0][1]),)
        for lanes, order in parts:
            source, dims = self.source(buffers, slots, phase, order)
            cut = AXIS_OF[order[phase]]
            near = tuple(self.places[d] if d == cut else slice(None) for d in dims)
            whole = tuple(slice(None) for _ in self.left(order, phase))
            ref = buffers[1 + phase].at[slots[1]]
            mine = source[near + (slice(None), lanes)]
            came = ref[whole + (slice(None), lanes)]
            if phase < 4:
                ref[whole + (slice(None), lanes)] = came + mine
            else:
                result[:, lanes] = came.astype(WIDE) + mine.astype(WIDE)

    def wide_slots(self, chunk):
        return (chunk % TERM_SLOTS, chunk % SCATTER_SLOTS)

    def tall_slots(self, place):
        return (0, place % TALL_SLOTS)

    def wide_messages(self, phase, chunk):
        return self.messages(
            self.wide,
            self.wide_slots(chunk),
            (self.send_sem, self.recv_sem),
            phase,
            self.wide_parts(),
        )

    def tall_messages(self, phase, place, odd):
        return self.messages(
            self.tall,
            self.tall_slots(place),
            (self.tall_send, self.tall_recv),
            phase,
            self.tall_parts(odd),
        )

    def store(self, chunk):
        return pltpu.make_async_copy(
            self.result.at[chunk % 2], self.outs.at[chunk], self.store_sem.at[chunk % 2]
        )

    def store_tall(self, place):
        return pltpu.make_async_copy(
            self.tall_result.at[place % 2], self.tall_outs.at[place], self.tall_store.at[place % 2]
        )

    def start(self, phase, chunk):
        for copy in self.wide_messages(phase, chunk):
            copy.start()
        place, part, due = self.tall_turn(chunk)
        for odd in range(2):

            @pl.when(due & (part % 2 == odd))
            def _(odd=odd):
                for copy in self.tall_messages(phase, place, odd):
                    copy.start()

    def take(self, phase, chunk):
        for copy in self.wide_messages(phase, chunk):
            copy.wait()
        if phase == PHASES - 1:
            pl.when(chunk >= 2)(lambda: self.store(chunk).wait())
        self.add(
            self.wide, self.wide_slots(chunk), phase, self.wide_parts(), self.result.at[chunk % 2]
        )
        place, part, due = self.tall_turn(chunk)
        for odd in range(2):

            @pl.when(due & (part % 2 == odd))
            def _(odd=odd):
                for copy in self.tall_messages(phase, place, odd):
                    copy.wait()
                if phase == PHASES - 1:
                    pl.when(place >= 2)(lambda: self.store_tall(place).wait())
                self.add(
                    self.tall,
                    self.tall_slots(place),
                    phase,
                    self.tall_parts(odd),
                    self.tall_result.at[place % 2],
                )
                if phase == PHASES - 1:
                    self.store_tall(place).start()

        if phase == PHASES - 1:
            self.store(chunk).start()

    def older(self, step):
        for phase in range(PHASES, 0, -1):
            chunk = step - SCATTER_STEPS[phase]

            @pl.when((chunk >= 0) & (chunk < CHUNKS))
            def _(phase=phase, chunk=chunk):
                self.take(phase - 1, chunk)
                if phase < PHASES:
                    self.start(phase, chunk)

    def finish(self):
        for chunk in (CHUNKS - 2, CHUNKS - 1):
            self.store(chunk).wait()
        for place in (2 * SHRINK_PARTS - 2, 2 * SHRINK_PARTS - 1):
            self.store_tall(place).wait()


def norm_slope(values, inverse, upstream, mean):
    return inverse * (upstream - values * (inverse * inverse) * mean)


def gate_back(update, mixture, coming, first):
    inverse = lax.rsqrt(pair_mean(mixture * mixture, first) + epsilon)
    curve = logistic(update)
    back_update = coming * (mixture * inverse) * (curve * (1.0 + update * (1.0 - curve)))
    gate = coming * (update * curve)
    back_mixture = norm_slope(mixture, inverse, gate, pair_mean(gate * mixture, first))
    return back_update, back_mixture


def both_heads(values, first):
    zero = jnp.zeros_like(values)
    return jnp.concatenate([jnp.where(first, values, zero), jnp.where(first, zero, values)], axis=0)


def side_by_side(values):
    half = values.shape[0] // 2
    return jnp.concatenate([values[:half], values[half:]], axis=1)


def local_mixer_back(group, stage, attends, validity, coming, back):
    def body(turn, carry):
        rows = pl.ds(pl.multiple_of((turn // 2) * 128, 128), 128)
        lanes = pl.ds(pl.multiple_of((turn % 2) * 128, 128), 128)
        columns = pl.ds(pl.multiple_of(group * WIDTH + (turn % 2) * 128, 128), 128)
        first = first_lanes(128)

        def put(i, j, value):
            start = j * WIDTH + (turn % 2) * 128
            back[i, rows, pl.ds(pl.multiple_of(start, 128), 128)] = value.astype(LOW)

        q, k, v = stage[0, rows, lanes], stage[1, rows, lanes], stage[2, rows, lanes]
        update = stage[3, rows, lanes].astype(WIDE)
        mixture = stage[4, rows, lanes].astype(WIDE)
        back_update, back_mixture = gate_back(update, mixture, coming[rows, columns], first)
        put(1, 1, back_update)
        grad = (back_mixture.astype(LOW).astype(WIDE) * validity[rows, :]).astype(LOW)
        grads = both_heads(grad, first)
        attend_low = attends[turn].reshape(256, 128)
        attend = attend_low.astype(WIDE)
        back_attend = contract_cols(grads, v)
        total = jnp.sum(back_attend * attend, axis=-1, keepdims=True)
        back_scores = (attend * (back_attend - total)).astype(LOW)
        put(0, 0, dot(side_by_side(back_scores), both_heads(k, first)) * HEAD ** (-0.5))
        put(1, 0, contract_rows(back_scores, both_heads(q, first)) * HEAD ** (-0.5))
        put(0, 1, contract_rows(attend_low, grads))
        return carry

    lax.fori_loop(0, 2 * ROWS // 128, body, 0, unroll=4)


def linear_mixer_back(group, stage, coming, back):
    half = ROWS // 2

    def body(pair, carry):
        lanes = pl.ds(pl.multiple_of(pair * 128, 128), 128)
        columns = pl.ds(pl.multiple_of(group * WIDTH + pair * 128, 128), 128)
        first = first_lanes(ROWS)
        queries = stage[0, :, lanes].astype(WIDE)
        keys_all = stage[1, :, lanes].astype(WIDE)
        v = stage[2, :, lanes]
        fq = softplus(queries).astype(LOW)
        fk = softplus(keys_all).astype(LOW)
        update = stage[3, :, lanes].astype(WIDE)
        mixture = stage[4, :, lanes].astype(WIDE)
        back_update, back_mixture = gate_back(update, mixture, coming[:, columns], first)

        def put(i, j, rows, value):
            start = j * WIDTH + pair * 128
            back[i, rows, pl.ds(pl.multiple_of(start, 128), 128)] = value.astype(LOW)

        put(1, 1, slice(None), back_update)
        grad = back_mixture.astype(LOW)
        tiles = []
        for t in range(2):
            reach = (t + 1) * half
            i = lax.broadcasted_iota(jnp.int32, (2 * half, reach), 0) % half + t * half
            j = lax.broadcasted_iota(jnp.int32, (2 * half, reach), 1)
            pair_q = both_heads(fq[t * half : reach], first[:half])
            pair_g = both_heads(grad[t * half : reach], first[:half])
            scores = jnp.where(j <= i, contract_cols(pair_q, fk[:reach]), 0.0).astype(LOW)
            inner = jnp.where(j <= i, contract_cols(pair_g, v[:reach]), 0.0).astype(LOW)
            tiles.append(
                (
                    dot(side_by_side(inner), both_heads(fk[:reach], first[:reach])),
                    contract_rows(inner, pair_q),
                    contract_rows(scores, pair_g),
                )
            )
        for t in range(2):
            rows = pl.ds(t * half, half)
            span = slice(t * half, (t + 1) * half)
            back_q = tiles[t][0]
            back_k = tiles[1][1][span]
            back_v = tiles[1][2][span]
            if t == 0:
                back_k = back_k + tiles[0][1]
                back_v = back_v + tiles[0][2]
            put(0, 0, rows, back_q * logistic(queries[span]))
            put(1, 0, rows, back_k * logistic(keys_all[span]))
            put(0, 1, rows, back_v)
        return carry

    lax.fori_loop(0, 2, body, 0)


def over_rows(act):
    def body(t, carry):
        act(pl.ds(pl.multiple_of(t * 128, 128), 128))
        return carry

    lax.fori_loop(0, ROWS // 128, body, 0)


def backward_kernel(*refs):
    cotangent, tokens, validity = refs[:3]
    held, tall, between, middles, turns, stages, halves_in, hidden_in, attends_in = refs[3:12]
    tokens_out, outs, tall_outs = refs[12:15]
    scratch = refs[15:]
    scatter_sems, loads = scratch[:6], scratch[6:12]
    load_sem, half_sem, shrink_sem, stage_sem, turn_sem, misc_sem = loads
    wide_buffers, tall_buffers = scratch[12:19], scratch[19:26]
    (
        loaded,
        half_in,
        stage,
        attends,
        shrink,
        hidden_turned,
        branch,
        gated_branch,
        up,
        sums,
        middle,
        layer_in,
        turned,
        back,
    ) = scratch[26:]
    scatter = Scatter((outs, tall_outs), scatter_sems, wide_buffers, tall_buffers)

    class Load:
        def __init__(self, chunk, number):
            self.copies = [
                pltpu.make_async_copy(
                    held.at[chunk, f],
                    loaded.at[number % 2, :, pl.ds(f * WIDTH, WIDTH)],
                    load_sem.at[number % 2, f],
                )
                for f in range(2)
            ]

        def start(self):
            for copy in self.copies:
                copy.start()

        def wait(self):
            for copy in self.copies:
                copy.wait()

    def load_turned(layer, kind, order):
        return pltpu.make_async_copy(
            turns.at[layer, kind], turned.at[order % 2], turn_sem.at[order % 2]
        )

    def load_attends(group):
        return pltpu.make_async_copy(attends_in.at[group], attends, misc_sem.at[4])

    def load_half(layer, part, number):
        return pltpu.make_async_copy(
            halves_in.at[layer, part], half_in.at[number % 2], half_sem.at[number % 2]
        )

    def load_shrink(layer, part, number):
        rows = pl.ds(pl.multiple_of(part * WIDTH, WIDTH), WIDTH)
        return pltpu.make_async_copy(
            tall.at[layer, :, rows, :], shrink.at[number % 2], shrink_sem.at[number % 2]
        )

    def load_stage(layer, group):
        return pltpu.make_async_copy(stages.at[layer, group], stage, stage_sem)

    def fetch(kind, layer):
        source, target = (
            (None, None),
            (middles, middle),
            (hidden_in, hidden_turned),
        )[kind]
        return pltpu.make_async_copy(source.at[layer], target, misc_sem.at[kind])

    def fetch_between():
        return pltpu.make_async_copy(between, layer_in, misc_sem.at[3])

    def prefetch(number):
        layer = 1 - number // LAYER_CHUNKS
        turn = number % LAYER_CHUNKS
        base = LAYER_CHUNKS * layer

        @pl.when(turn < OUTPUT_TURN)
        def _():
            Load(base + PROJECT_CHUNKS + OUTPUT_CHUNKS + turn, number).start()
            load_half(layer, turn, number).start()
            load_shrink(layer, turn, number).start()

        @pl.when((turn >= OUTPUT_TURN) & (turn < PROJECT_TURN))
        def _():
            Load(base + PROJECT_CHUNKS + turn - OUTPUT_TURN, number).start()

        @pl.when(turn >= PROJECT_TURN)
        def _():
            Load(base + turn - PROJECT_TURN, number).start()

            @pl.when((turn - PROJECT_TURN) % 2 == 0)
            def _():
                load_stage(layer, (turn - PROJECT_TURN) // 2).start()
                pl.when(layer == 0)(lambda: load_attends((turn - PROJECT_TURN) // 2).start())

    prefetch(jnp.int32(0))
    load_turned(1, 2, 0).start()
    load_turned(1, 1, 1).start()
    fetch(2, 1).start()
    fetch(1, 1).start()
    fetch_between().start()

    def begin_rows(rows):
        up[rows, :] = cotangent[rows, :].astype(WIDE) * validity[rows, :]

    over_rows(begin_rows)
    greet(scatter.targets)

    def expand_start(layer):
        def act(rows):
            branch[rows, :] = up[rows, :].astype(LOW)
            sums[0, rows, :] = jnp.zeros((128, 1024), WIDE)

        over_rows(act)
        load_turned(0, 0, 1 - layer).wait()
        pl.when(layer == 0)(lambda: load_turned(0, 1, 4).start())

    def expand_turn(part, number):
        load_half(0, 0, number).wait()
        load_shrink(0, 0, number).wait()
        low, high = pl.ds(0, WIDTH), pl.ds(WIDTH, WIDTH)
        back_hidden = contract_cols(branch[:, :512], shrink[number % 2, 0])
        back_hidden = back_hidden + contract_cols(branch[:, 512:], shrink[number % 2, 1])
        first = half_in[number % 2, 0].astype(WIDE)
        second = half_in[number % 2, 1].astype(WIDE)
        back[0, :, low] = (back_hidden * second).astype(LOW)
        back[0, :, high] = (back_hidden * first).astype(LOW)

    def output_start(layer):
        load_turned(0, 0, 2 - layer).wait()
        load_turned(layer, 0, 3 - layer).start()
        fetch(1, 1).wait()

        def act(rows):
            values = middle[rows, :]
            back_second = sums[0, rows, :]
            new = up[rows, :] + norm_back(values, back_second)
            up[rows, :] = new
            gated_branch[rows, :] = new.astype(LOW)
            sums[1, rows, :] = jnp.zeros((128, 1024), WIDE)

        over_rows(act)

    def output_turn(part):
        for f in range(2):
            lanes = pl.ds(pl.multiple_of(f * 512 + part * WIDTH, WIDTH), WIDTH)
            back[0, :, pl.ds(f * WIDTH, WIDTH)] = gated_branch[:, lanes]

    def project_start(layer):
        @pl.when(layer == 1)
        def _():
            fetch_between().wait()
            fetch(1, 0).start()
            load_turned(0, 2, 3).start()

        @pl.when(layer == 0)
        def _():
            def act(rows):
                layer_in[rows, :] = tokens[rows, :].astype(WIDE) * validity[rows, :]

            over_rows(act)

        def clear(rows):
            sums[0, rows, :] = jnp.zeros((128, 1024), WIDE)

        over_rows(clear)
        load_turned(0, 0, 1 - layer).wait()

    def project_turn(layer, group):
        load_stage(0, 0).wait()
        coming = sums.at[1]
        pl.when(layer == 1)(lambda: linear_mixer_back(group, stage, coming, back))

        @pl.when(layer == 0)
        def _():
            load_attends(0).wait()
            local_mixer_back(group, stage, attends, validity, coming, back)

    def finish_layer(layer):
        def act(rows):
            up[rows, :] = up[rows, :] + norm_back(layer_in[rows, :], sums[0, rows, :])

        over_rows(act)

    def terms(number, which, order):
        slot = number % TERM_SLOTS
        out = wide_buffers[0]

        def body(tile, carry):
            rows = pl.ds(pl.multiple_of(tile * 512, 512), 512)
            value = dot(turned[order % 2, rows, :], back[which]).astype(LOW)
            for f in range(2):
                part = value[:, f * WIDTH : (f + 1) * WIDTH]
                out[slot, f, tile] = part.reshape(2, 2, 2, 64, WIDTH)
            return carry

        lax.fori_loop(0, 2, body, 0)

    def tall_terms(part, number):
        out = tall_buffers[0]
        pl.when(part == 0)(lambda: fetch(2, 0).wait())
        lanes = [pl.ds(pl.multiple_of(f * 512 + part * 128, 128), 128) for f in range(2)]
        both = jnp.concatenate([branch[:, lanes[0]], branch[:, lanes[1]]], axis=1)

        def body(tile, carry):
            rows = pl.ds(pl.multiple_of(tile * 8 * TALL_ROWS, 8 * TALL_ROWS), 8 * TALL_ROWS)
            value = dot(hidden_turned[rows, :], both).astype(LOW)
            for f in range(2):
                out[0, f, tile] = value[:, f * 128 : f * 128 + 128].reshape(
                    2, 2, 2, TALL_ROWS, SHRINK_WIDTH
                )
            return carry

        lax.fori_loop(0, 2, body, 0)

        @pl.when((part == SHRINK_PARTS - 1) & (number < LAYER_CHUNKS))
        def _():
            fetch(2, 0).start()

    def spread(number, which, kind):
        def body(t, carry):
            rows = pl.ds(pl.multiple_of(t * 512, 512), 512)
            value = contract_cols(back[which], loaded[number % 2, rows, :])
            sums[kind, :, rows] = sums[kind, :, rows] + value
            return carry

        lax.fori_loop(0, 2, body, 0)

    def body(step, carry):
        pl.when(step + 1 < CHUNKS)(lambda: prefetch(step + 1))
        scatter.older(step)

        @pl.when(step < CHUNKS)
        def _():
            layer = 1 - step // LAYER_CHUNKS
            turn = step % LAYER_CHUNKS
            pl.when(turn == 0)(lambda: expand_start(layer))
            pl.when(turn == OUTPUT_TURN)(lambda: output_start(layer))
            pl.when(turn == PROJECT_TURN)(lambda: project_start(layer))
            pl.when(turn < OUTPUT_TURN)(lambda: expand_turn(turn, step))
            pl.when((turn >= OUTPUT_TURN) & (turn < PROJECT_TURN))(
                lambda: output_turn(turn - OUTPUT_TURN)
            )
            pl.when((turn >= PROJECT_TURN) & ((turn - PROJECT_TURN) % 2 == 0))(
                lambda: project_turn(layer, (turn - PROJECT_TURN) // 2)
            )
            in_project = jnp.minimum(jnp.maximum(turn - PROJECT_TURN + 1, 0), 1)
            in_output = jnp.minimum(jnp.maximum(turn - OUTPUT_TURN + 1, 0), 1) - in_project
            which = in_project * ((turn + PROJECT_TURN) % 2)
            terms(step, which, 1 - layer + in_output)
            place, part, due = scatter.tall_turn(step)
            pl.when(due)(lambda: tall_terms(part, step))
            scatter.start(0, step)
            Load(0, step).wait()
            spread(step, which, in_output)
            pl.when(turn == LAYER_CHUNKS - 1)(lambda: finish_layer(layer))

            @pl.when(step == CHUNKS - 1)
            def _():
                def act(rows):
                    up[rows, :] = up[rows, :] * validity[rows, :]

                over_rows(act)
                pltpu.make_async_copy(up, tokens_out, misc_sem.at[3]).start()

        return carry

    lax.fori_loop(0, CHUNKS + SCATTER_STEPS[PHASES], body, 0)
    pltpu.make_async_copy(up, tokens_out, misc_sem.at[3]).wait()
    scatter.finish()


def scatter_buffers(terms, slots, rows, width):
    bits = [(2,) * (4 - phase) for phase in range(5)]
    return (
        [pltpu.VMEM((terms, 2, 2, 2, 2, 2, rows, width), LOW)]
        + [pltpu.VMEM((slots,) + lead + (rows, width), LOW) for lead in bits]
        + [pltpu.VMEM((2, rows, width), WIDE)]
    )


def run_backward(cotangent, tokens, validity, forward):
    struct = jax.ShapeDtypeStruct
    held, tall, mixed_out, between, middles, turns, stages, kept, hidden, attends = forward
    return pl.pallas_call(
        backward_kernel,
        out_shape=(
            struct((ROWS, 1024), WIDE),
            struct((CHUNKS, 64, WIDTH), WIDE),
            struct((2 * SHRINK_PARTS, TALL_ROWS, SHRINK_WIDTH), WIDE),
        ),
        in_specs=[FULL] * 3 + [ANY] * 9,
        out_specs=(ANY,) * 3,
        scratch_shapes=[
            pltpu.SemaphoreType.DMA((10, SCATTER_SLOTS)),
            pltpu.SemaphoreType.DMA((10, SCATTER_SLOTS)),
            pltpu.SemaphoreType.DMA((10, TALL_SLOTS)),
            pltpu.SemaphoreType.DMA((10, TALL_SLOTS)),
            pltpu.SemaphoreType.DMA((2,)),
            pltpu.SemaphoreType.DMA((2,)),
            pltpu.SemaphoreType.DMA((2, 2)),
            pltpu.SemaphoreType.DMA((2,)),
            pltpu.SemaphoreType.DMA((2,)),
            pltpu.SemaphoreType.DMA,
            pltpu.SemaphoreType.DMA((2,)),
            pltpu.SemaphoreType.DMA((5,)),
        ]
        + scatter_buffers(TERM_SLOTS, SCATTER_SLOTS, 64, WIDTH)
        + scatter_buffers(1, TALL_SLOTS, TALL_ROWS, SHRINK_WIDTH)
        + [
            pltpu.VMEM((2, 1024, 2 * WIDTH), LOW),
            pltpu.VMEM((2, 2, ROWS, WIDTH), LOW),
            pltpu.VMEM((5, ROWS, WIDTH), LOW),
            pltpu.VMEM((8, 2, 128, 128), LOW),
            pltpu.VMEM((2, 2, WIDTH, 512), LOW),
            pltpu.VMEM((2816, ROWS), LOW),
            pltpu.VMEM((ROWS, 1024), LOW),
            pltpu.VMEM((ROWS, 1024), LOW),
            pltpu.VMEM((ROWS, 1024), WIDE),
            pltpu.VMEM((2, ROWS, 1024), WIDE),
            pltpu.VMEM((ROWS, 1024), WIDE),
            pltpu.VMEM((ROWS, 1024), WIDE),
            pltpu.VMEM((2, 1024, ROWS), LOW),
            pltpu.VMEM((2, ROWS, 2 * WIDTH), LOW),
        ],
        compiler_params=pltpu.CompilerParams(
            collective_id=1, has_side_effects=True, vmem_limit_bytes=62 << 20
        ),
    )(
        cotangent,
        tokens,
        validity,
        held.reshape(CHUNKS, 2, 1024, WIDTH),
        tall.reshape(2, 2, 2816, 512),
        between,
        middles,
        turns,
        stages,
        kept,
        hidden,
        attends,
    )


def unpack_kernel(mixed_in, tokens_in, chunks, parts, *refs):
    outs, sem = refs[:-1], refs[-1]
    copies = [(mixed_in, outs[0]), (tokens_in, outs[1])]
    for order in range(2):
        layer = 1 - order
        for turn in range(LAYER_CHUNKS):
            number = order * LAYER_CHUNKS + turn
            if turn < OUTPUT_TURN:
                weight, start = 2, chunk_columns(2, turn)
            elif turn < PROJECT_TURN:
                weight, start = 1, chunk_columns(1, turn - OUTPUT_TURN)
            else:
                weight, start = 0, chunk_columns(0, turn - PROJECT_TURN)
            target = outs[2 + 4 * layer + weight].at[:, pl.ds(start, WIDTH)]
            copies.append((chunks.at[number], target))
        for part in range(SHRINK_PARTS):
            target = outs[5 + 4 * layer].at[:, pl.ds(part * SHRINK_WIDTH, SHRINK_WIDTH)]
            copies.append((parts.at[order * SHRINK_PARTS + part], target))
    copies = [
        pltpu.make_async_copy(source, target, sem.at[i])
        for i, (source, target) in enumerate(copies)
    ]
    for copy in copies:
        copy.start()
    for copy in copies:
        copy.wait()


def unpack(mixed_out, tokens_gradient, chunks, parts, shards_of):
    struct = jax.ShapeDtypeStruct
    count = 2 + CHUNKS + 2 * SHRINK_PARTS
    return pl.pallas_call(
        unpack_kernel,
        out_shape=(struct(mixed_out.shape, LOW), struct(tokens_gradient.shape, WIDE))
        + tuple(struct(item.shape, WIDE) for item in shards_of),
        in_specs=[FULL] * 4,
        out_specs=(ANY,) * (2 + WEIGHTS),
        scratch_shapes=[pltpu.SemaphoreType.DMA((count,))],
        compiler_params=pltpu.CompilerParams(vmem_limit_bytes=32 << 20),
    )(mixed_out, tokens_gradient, chunks, parts)


def gather_weights(shards_of):
    return [
        lax.all_gather(lax.all_gather(item, "fsdp", axis=1, tiled=True), "dp", axis=0, tiled=True)
        for item in shards_of
    ]


def settle_gradients(terms):
    tall = [
        lax.psum_scatter(item.astype(jnp.bfloat16), "dp", scatter_dimension=0, tiled=True)
        for item in terms
    ]
    return [
        lax.psum_scatter(item, "fsdp", scatter_dimension=1, tiled=True).astype(jnp.float32)
        for item in tall
    ]


def local_scores(queries, keys_all):
    query_blocks = split_heads(queries.astype(jnp.bfloat16))
    key_blocks = split_heads(keys_all.astype(jnp.bfloat16))
    scores = jnp.einsum(
        "bihd,bjhd->bhij", query_blocks, key_blocks, preferred_element_type=jnp.float32
    ) * HEAD ** (-0.5)
    return (query_blocks, key_blocks, jnp.where(causal_table(), scores, -1e30))


def local_forward(queries, keys_all, values_low, validity):
    query_blocks, key_blocks, scores = local_scores(queries, keys_all)
    highest_score = jnp.max(scores, axis=-1, keepdims=True)
    expweights = jnp.exp(scores - highest_score)
    row_total = jnp.sum(expweights, axis=-1, keepdims=True)
    attend = (expweights / row_total).astype(jnp.bfloat16)
    mixture = jnp.einsum(
        "bhij,bjhd->bihd", attend, split_heads(values_low), preferred_element_type=jnp.float32
    )
    return (join_heads(mixture) * validity, highest_score + jnp.log(row_total))


def local_backward(queries, keys_all, values_low, validity, logsum, back_mixture):
    query_blocks, key_blocks, scores = local_scores(queries, keys_all)
    value_blocks = split_heads(values_low)
    coming = split_heads(back_mixture * validity.astype(jnp.bfloat16))
    attend = jnp.exp(scores - logsum)
    back_values = jnp.einsum(
        "bhij,bihd->bjhd", attend.astype(jnp.bfloat16), coming, preferred_element_type=jnp.float32
    )
    back_attend = jnp.einsum(
        "bihd,bjhd->bhij", coming, value_blocks, preferred_element_type=jnp.float32
    )
    back_scores = (
        attend * (back_attend - jnp.sum(back_attend * attend, axis=-1, keepdims=True))
    ).astype(jnp.bfloat16)
    back_queries = jnp.einsum(
        "bhij,bjhd->bihd", back_scores, key_blocks, preferred_element_type=jnp.float32
    ) * HEAD ** (-0.5)
    back_keys = jnp.einsum(
        "bhij,bihd->bjhd", back_scores, query_blocks, preferred_element_type=jnp.float32
    ) * HEAD ** (-0.5)
    return (join_heads(back_queries), join_heads(back_keys), join_heads(back_values))


def linear_parts(queries, keys_all, values_low):
    feature_q = split_heads(jax.nn.softplus(queries).astype(jnp.bfloat16))
    feature_k = split_heads(jax.nn.softplus(keys_all).astype(jnp.bfloat16))
    value_blocks = split_heads(values_low)
    causal = causal_table().astype(jnp.float32)
    inner_scores = (
        jnp.einsum("bihd,bjhd->bhij", feature_q, feature_k, preferred_element_type=jnp.float32)
        * causal
    ).astype(jnp.bfloat16)
    states = jnp.einsum(
        "bjhd,bjhe->bhde", feature_k, value_blocks, preferred_element_type=jnp.float32
    )
    running = jnp.cumsum(states, axis=0)
    prior_states = jnp.concatenate([jnp.zeros_like(states[:1]), running[:-1]], axis=0)
    return (feature_q, feature_k, value_blocks, causal, inner_scores, prior_states)


def linear_forward(queries, keys_all, values_low):
    feature_q, feature_k, value_blocks, causal, inner_scores, prior_states = linear_parts(
        queries, keys_all, values_low
    )
    mixture = jnp.einsum(
        "bhij,bjhe->bihe", inner_scores, value_blocks, preferred_element_type=jnp.float32
    )
    mixture = mixture + jnp.einsum(
        "bihd,bhde->bihe", feature_q.astype(jnp.float32), prior_states, precision=highest
    )
    return join_heads(mixture)


def linear_backward(queries, keys_all, values_low, back_mixture):
    feature_q, feature_k, value_blocks, causal, inner_scores, prior_states = linear_parts(
        queries, keys_all, values_low
    )
    coming = split_heads(back_mixture)
    coming_wide = coming.astype(jnp.float32)
    back_inner = (
        jnp.einsum("bihe,bjhe->bhij", coming, value_blocks, preferred_element_type=jnp.float32)
        * causal
    ).astype(jnp.bfloat16)
    back_feature_q = jnp.einsum(
        "bhij,bjhd->bihd", back_inner, feature_k, preferred_element_type=jnp.float32
    )
    back_feature_q = back_feature_q + jnp.einsum(
        "bihe,bhde->bihd", coming_wide, prior_states, precision=highest
    )
    back_feature_k = jnp.einsum(
        "bhij,bihd->bjhd", back_inner, feature_q, preferred_element_type=jnp.float32
    )
    back_values = jnp.einsum(
        "bhij,bihe->bjhe", inner_scores, coming, preferred_element_type=jnp.float32
    )
    back_prior = jnp.einsum(
        "bihd,bihe->bhde", feature_q.astype(jnp.float32), coming_wide, precision=highest
    )
    running = jnp.cumsum(back_prior[::-1], axis=0)[::-1]
    later_states = jnp.concatenate([running[1:], jnp.zeros_like(running[:1])], axis=0)
    back_feature_k = back_feature_k + jnp.einsum(
        "bjhe,bhde->bjhd", value_blocks.astype(jnp.float32), later_states, precision=highest
    )
    back_values = back_values + jnp.einsum(
        "bjhd,bhde->bjhe", feature_k.astype(jnp.float32), later_states, precision=highest
    )
    return (
        join_heads(back_feature_q) * jax.nn.sigmoid(queries),
        join_heads(back_feature_k) * jax.nn.sigmoid(keys_all),
        join_heads(back_values),
    )


def forward_layer(layer_in, validity, weights, local):
    project, output, expand, shrink = weights
    normed = simple_norm(layer_in).astype(jnp.bfloat16)
    projected = jnp.dot(normed, project, preferred_element_type=jnp.float32)
    queries, keys_all, values, update = jnp.split(projected, 4, axis=1)
    values_low = values.astype(jnp.bfloat16)
    if local:
        mixture, logsum = local_forward(queries, keys_all, values_low, validity)
    else:
        mixture = linear_forward(queries, keys_all, values_low)
        logsum = None
    gated_rows = (head_norm(mixture) * jax.nn.silu(update)).astype(jnp.bfloat16)
    middle = layer_in + jnp.dot(gated_rows, output, preferred_element_type=jnp.float32)
    second = simple_norm(middle).astype(jnp.bfloat16)
    expanded = jnp.dot(second, expand, preferred_element_type=jnp.float32)
    half_width = expanded.shape[1] // 2
    hidden = (expanded[:, :half_width] * expanded[:, half_width:]).astype(jnp.bfloat16)
    result = middle + jnp.dot(hidden, shrink, preferred_element_type=jnp.float32)
    return (
        result,
        (layer_in, normed, projected, values_low, mixture, logsum, gated_rows, middle, second),
    )


def backward_layer(upstream, saved, weights, validity, local):
    project, output, expand, shrink = weights
    layer_in, normed, projected, values_low, mixture, logsum, gated_rows, middle, second = saved
    expanded = jnp.dot(second, expand, preferred_element_type=jnp.float32)
    half_width = expanded.shape[1] // 2
    first_half = expanded[:, :half_width]
    second_half = expanded[:, half_width:]
    hidden = (first_half * second_half).astype(jnp.bfloat16)
    back_branch = upstream.astype(jnp.bfloat16)
    shrink_term = contract_rows(hidden, back_branch)
    back_hidden = contract_cols(back_branch, shrink)
    back_expanded = jnp.concatenate(
        [back_hidden * second_half, back_hidden * first_half], axis=1
    ).astype(jnp.bfloat16)
    expand_term = contract_rows(second, back_expanded)
    back_second = contract_cols(back_expanded, expand)
    back_middle = upstream + norm_back(middle, back_second)
    back_gated = back_middle.astype(jnp.bfloat16)
    output_term = contract_rows(gated_rows, back_gated)
    back_rows_gated = contract_cols(back_gated, output)
    queries, keys_all, unused_values, update = jnp.split(projected, 4, axis=1)
    back_update = back_rows_gated * head_norm(mixture) * silu_slope(update)
    back_mixture = head_back(mixture, back_rows_gated * jax.nn.silu(update)).astype(jnp.bfloat16)
    if local:
        back_queries, back_keys, back_values = local_backward(
            queries, keys_all, values_low, validity, logsum, back_mixture
        )
    else:
        back_queries, back_keys, back_values = linear_backward(
            queries, keys_all, values_low, back_mixture
        )
    back_projected = jnp.concatenate(
        [back_queries, back_keys, back_values, back_update], axis=1
    ).astype(jnp.bfloat16)
    project_term = contract_rows(normed, back_projected)
    back_normed = contract_cols(back_projected, project)
    back_input = back_middle + norm_back(layer_in, back_normed)
    return (back_input, (project_term, output_term, expand_term, shrink_term))


def shards(
    direct,
    tokens,
    lengths,
    local_project,
    local_output,
    local_expand,
    local_shrink,
    linear_project,
    linear_output,
    linear_expand,
    linear_shrink,
    cotangent,
):
    positions = lax.broadcasted_iota(jnp.int32, (tokens.shape[1], 1), 0)
    validity = (positions < lengths[0]).astype(jnp.float32)
    shards_of = [
        local_project,
        local_output,
        local_expand,
        local_shrink,
        linear_project,
        linear_output,
        linear_expand,
        linear_shrink,
    ]
    if direct:
        forward = run_forward(shards_of, tokens[0], validity)
        back_tokens, chunks, parts = run_backward(cotangent[0], tokens[0], validity, forward)
        outs = unpack(forward[2], back_tokens, chunks, parts, shards_of)
        return (outs[0][None], outs[1][None]) + tuple(outs[2:])
    layer_in = tokens[0].astype(jnp.float32) * validity
    whole = gather_weights(shards_of)
    local_weights = whole[:4]
    linear_weights = whole[4:]
    between, local_saved = forward_layer(layer_in, validity, local_weights, True)
    result, linear_saved = forward_layer(between, validity, linear_weights, False)
    result = (result * validity).astype(jnp.bfloat16)
    upstream = cotangent[0].astype(jnp.float32) * validity
    back_between, linear_terms = backward_layer(
        upstream, linear_saved, linear_weights, validity, False
    )
    back_input, local_terms = backward_layer(
        back_between, local_saved, local_weights, validity, True
    )
    sums = settle_gradients(local_terms + linear_terms)
    return (
        result[None],
        (back_input * validity)[None],
    ) + tuple(sums)


def solution(mesh):
    in_specs = (
        P(("dp", "fsdp"), None, None),
        P(("dp", "fsdp")),
        P("dp", "fsdp"),
        P("dp", "fsdp"),
        P("dp", "fsdp"),
        P("dp", "fsdp"),
        P("dp", "fsdp"),
        P("dp", "fsdp"),
        P("dp", "fsdp"),
        P("dp", "fsdp"),
        P(("dp", "fsdp"), None, None),
    )
    out_specs = (
        P(("dp", "fsdp"), None, None),
        P(("dp", "fsdp"), None, None),
        P("dp", "fsdp"),
        P("dp", "fsdp"),
        P("dp", "fsdp"),
        P("dp", "fsdp"),
        P("dp", "fsdp"),
        P("dp", "fsdp"),
        P("dp", "fsdp"),
        P("dp", "fsdp"),
    )
    direct = dict(mesh.shape) == {"dp": 16, "fsdp": 2}
    return jax.shard_map(functools.partial(shards, direct), mesh=mesh, in_specs=in_specs, out_specs=out_specs, check_vma=False)
```

```python
import functools

import jax
import jax.numpy as jnp
from jax import lax
from jax.experimental import pallas as pl
from jax.experimental.pallas import tpu as pltpu
from jax.sharding import PartitionSpec as P

HEADS = 16
HEAD = 64
BLOCK = 64


epsilon = 1e-05
highest = lax.Precision.HIGHEST


def simple_norm(values):
    return values * lax.rsqrt(jnp.mean(values * values, axis=-1, keepdims=True) + epsilon)


def norm_back(values, upstream):
    inverse_rms = lax.rsqrt(jnp.mean(values * values, axis=-1, keepdims=True) + epsilon)
    return inverse_rms * (
        upstream
        - values * (inverse_rms * inverse_rms) * jnp.mean(upstream * values, axis=-1, keepdims=True)
    )


def head_norm(values):
    shaped = values.reshape(values.shape[0], HEADS, HEAD)
    return simple_norm(shaped).reshape(values.shape)


def head_back(values, upstream):
    shaped = values.reshape(values.shape[0], HEADS, HEAD)
    coming = upstream.reshape(values.shape[0], HEADS, HEAD)
    return norm_back(shaped, coming).reshape(values.shape)


def silu_slope(values):
    logistic = jax.nn.sigmoid(values)
    return logistic * (1.0 + values * (1.0 - logistic))


def contract_rows(first_matrix, second_matrix):
    return lax.dot_general(
        first_matrix, second_matrix, (((0,), (0,)), ((), ())), preferred_element_type=jnp.float32
    )


def contract_cols(first_matrix, second_matrix):
    return lax.dot_general(
        first_matrix, second_matrix, (((1,), (1,)), ((), ())), preferred_element_type=jnp.float32
    )


def causal_table():
    return lax.broadcasted_iota(jnp.int32, (BLOCK, BLOCK), 0) >= lax.broadcasted_iota(
        jnp.int32, (BLOCK, BLOCK), 1
    )


def split_heads(values):
    return values.reshape(values.shape[0] // BLOCK, BLOCK, HEADS, HEAD)


def join_heads(values):
    return values.reshape(values.shape[0] * BLOCK, HEADS * HEAD)


AXIS_NAMES = ("f", "zh", "zl", "y", "c")
AXIS_OF = {"c": "c", "y": "y", "x": "f", "z1": "zl", "z2": "zh"}
MESH = pl.DeviceIdType.MESH
ANY = pl.BlockSpec(memory_space=pl.ANY)
FULL = pl.BlockSpec(memory_space=pltpu.VMEM)
WEIGHTS = 8
WIDTH = 256
PHASES = 5
GATHER_STEPS = (0, 3, 6, 9, 12, 15)
HEAD_GROUPS = 4
PROJECT_CHUNKS = 8
OUTPUT_CHUNKS = 2
EXPAND_CHUNKS = 11
LAYER_CHUNKS = PROJECT_CHUNKS + OUTPUT_CHUNKS + EXPAND_CHUNKS
CHUNKS = 2 * LAYER_CHUNKS
SHRINK_PARTS = 4
SHRINK_WIDTH = 128
GATHER_SLOTS = 8
LOAD_SLOTS = 3
LOW = jnp.bfloat16
WIDE = jnp.float32
ROWS = 512


def neighbours():
    dp = lax.axis_index("dp")
    x = lax.axis_index("fsdp")
    z = dp // 4
    y = (dp // 2) % 2
    c = dp % 2
    places = {"f": x, "zh": z // 2, "zl": z % 2, "y": y, "c": c}
    targets = {
        "z1": ((z + 1 - 2 * (z % 2)) * 4 + y * 2 + c, x),
        "z2": (lax.rem(z + 2, 4) * 4 + y * 2 + c, x),
        "y": (z * 4 + (1 - y) * 2 + c, x),
        "c": (z * 4 + y * 2 + (1 - c), x),
        "x": (dp, 1 - x),
    }
    return places, targets


def greet(targets):
    barrier = pltpu.get_barrier_semaphore()
    for target in targets.values():
        pl.semaphore_signal(barrier, inc=1, device_id=target, device_id_type=MESH)
    pl.semaphore_wait(barrier, len(targets))


def dot(left, right):
    return jnp.dot(left, right, preferred_element_type=WIDE)


def softplus(values):
    return jnp.maximum(values, 0.0) + jnp.log1p(jnp.exp(-jnp.abs(values)))


def logistic(values):
    return 1.0 / (1.0 + jnp.exp(-values))


def first_lanes(rows):
    return lax.broadcasted_iota(jnp.int32, (rows, 128), 1) < HEAD


def pair_mean(values, first):
    left = jnp.sum(jnp.where(first, values, 0.0), axis=-1, keepdims=True)
    right = jnp.sum(jnp.where(first, 0.0, values), axis=-1, keepdims=True)
    return jnp.where(first, left, right) * (1.0 / HEAD)


def block_mask(rows):
    i = lax.broadcasted_iota(jnp.int32, (rows, rows), 0)
    j = lax.broadcasted_iota(jnp.int32, (rows, rows), 1)
    return (i // BLOCK == j // BLOCK) & (j <= i)


def norm_into(source, target):
    def body(t, carry):
        rows = pl.ds(pl.multiple_of(t * 128, 128), 128)
        target[rows, :] = simple_norm(source[rows, :]).astype(LOW)
        return carry

    lax.fori_loop(0, ROWS // 128, body, 0)


def local_mixer(group, parts, validity, gated, stage, attends):
    def body(turn, carry):
        t = turn // 2
        rows = pl.ds(pl.multiple_of(t * 128, 128), 128)
        pair = turn % 2
        lanes = pl.ds(pl.multiple_of(pair * 128, 128), 128)
        first = first_lanes(128)
        q = parts[0, 0, rows, lanes].astype(LOW)
        k = parts[1, 0, rows, lanes].astype(LOW)
        v = parts[0, 1, rows, lanes].astype(LOW)
        u = parts[1, 1, rows, lanes]
        keep = block_mask(128)
        mixed = []
        for head in range(2):
            mine = jnp.where(first == (head == 0), q, jnp.zeros_like(q))
            scores = contract_cols(mine, k) * HEAD ** (-0.5)
            scores = jnp.where(keep, scores, -1e30)
            highest_score = jnp.max(scores, axis=-1, keepdims=True)
            weights = jnp.exp(scores - highest_score)
            attend = (weights / jnp.sum(weights, axis=-1, keepdims=True)).astype(LOW)
            attends[turn, head] = attend
            mixed.append(dot(attend, v))
        mixture = jnp.where(first, mixed[0], mixed[1]) * validity[rows, :]
        scale = lax.rsqrt(pair_mean(mixture * mixture, first) + epsilon)
        columns = pl.ds(pl.multiple_of(group * WIDTH + pair * 128, 128), 128)
        gated[rows, columns] = (mixture * scale * (u * logistic(u))).astype(LOW)
        stage[4, rows, lanes] = mixture.astype(LOW)
        return carry

    lax.fori_loop(0, 2 * ROWS // 128, body, 0)


def linear_mixer(group, parts, gated, stage):
    half = ROWS // 2

    def body(pair, carry):
        lanes = pl.ds(pl.multiple_of(pair * 128, 128), 128)
        columns = pl.ds(pl.multiple_of(group * WIDTH + pair * 128, 128), 128)
        first = first_lanes(half)
        fk = softplus(parts[1, 0, :, lanes]).astype(LOW)
        v = parts[0, 1, :, lanes].astype(LOW)
        for t in range(2):
            rows = pl.ds(t * half, half)
            reach = (t + 1) * half
            fq = softplus(parts[0, 0, rows, lanes]).astype(LOW)
            i = lax.broadcasted_iota(jnp.int32, (half, reach), 0) + t * half
            j = lax.broadcasted_iota(jnp.int32, (half, reach), 1)
            mixed = []
            for head in range(2):
                mine = jnp.where(first == (head == 0), fq, jnp.zeros_like(fq))
                scores = jnp.where(j <= i, contract_cols(mine, fk[:reach]), 0.0).astype(LOW)
                mixed.append(dot(scores, v[:reach]))
            mixture = jnp.where(first, mixed[0], mixed[1])
            scale = lax.rsqrt(pair_mean(mixture * mixture, first) + epsilon)
            u = parts[1, 1, rows, lanes]
            gated[rows, columns] = (mixture * scale * (u * logistic(u))).astype(LOW)
            stage[4, rows, lanes] = mixture.astype(LOW)
        return carry

    lax.fori_loop(0, 2, body, 0)


def chunk_columns(weight, part):
    if weight == 0:
        return (part % 2) * 1024 + (part // 2) * WIDTH
    return part * WIDTH


class Gather:
    def __init__(self, own, held, tall, sems):
        self.own, self.held, self.tall = own, held, tall
        self.local_sem, self.send_sem, self.recv_sem, self.tall_send, self.tall_recv = sems
        self.places, self.targets = neighbours()
        self.at = tuple(self.places[name] for name in ("f", "zh", "zl", "y", "c"))

    def begin(self):
        counts = (PROJECT_CHUNKS, OUTPUT_CHUNKS, EXPAND_CHUNKS)
        for layer in range(2):
            chunk = LAYER_CHUNKS * layer
            for weight in range(3):
                for part in range(counts[weight]):
                    start = chunk_columns(weight, part)
                    pltpu.make_async_copy(
                        self.own[4 * layer + weight].at[:, pl.ds(start, WIDTH)],
                        self.held.at[(chunk,) + self.at],
                        self.local_sem.at[chunk],
                    ).start()
                    chunk += 1
            pltpu.make_async_copy(
                self.own[4 * layer + 3],
                self.tall.at[(layer,) + self.at],
                self.local_sem.at[CHUNKS + layer],
            ).start()
        greet(self.targets)

    def message(self, block, target, sems, place):
        return pltpu.make_async_remote_copy(
            src_ref=block,
            dst_ref=block,
            send_sem=sems[0].at[place],
            recv_sem=sems[1].at[place],
            device_id=self.targets[target],
            device_id_type=MESH,
        )

    def wide_messages(self, phase, chunk):
        x, zh, zl, y, c = self.at
        ref = self.held
        sems = (self.send_sem, self.recv_sem)
        slot = chunk % GATHER_SLOTS
        half = WIDTH // 2
        low, high = pl.ds(0, half), pl.ds(half, half)

        def one(index, target, part):
            return self.message(ref.at[(chunk,) + index], target, sems, (2 * phase + part, slot))

        a = slice(None)
        if phase == 0:
            return [one((x, zh, zl, y, c), "z2", 0)]
        if phase == 1:
            return [one((x, a, zl, y, c), "z1", 0)]
        if phase == 2:
            return [one((x, a, a, y, c, a, low), "x", 0), one((x, a, a, y, c, a, high), "y", 1)]
        if phase == 3:
            return [one((a, a, a, y, c, a, low), "y", 0), one((x, a, a, a, c, a, high), "x", 1)]
        return [one((a, a, a, a, c), "c", 0)]

    def tall_message(self, phase, layer, part, odd):
        x, zh, zl, y, c = self.at
        a = slice(None)
        lanes = pl.ds(pl.multiple_of(part * SHRINK_WIDTH, SHRINK_WIDTH), SHRINK_WIDTH)
        index, target = {
            (0, 0): ((x, zh, zl, y, c), "x"),
            (0, 1): ((x, zh, zl, y, c), "y"),
            (1, 0): ((a, zh, zl, y, c), "y"),
            (1, 1): ((x, zh, zl, a, c), "x"),
            (2, 0): ((a, zh, zl, a, c), "z2"),
            (3, 0): ((a, a, zl, a, c), "z1"),
            (4, 0): ((a, a, a, a, c), "c"),
        }[(phase, odd)]
        return self.message(
            self.tall.at[(layer,) + index + (a, lanes)],
            target,
            (self.tall_send, self.tall_recv),
            (phase, layer * SHRINK_PARTS + part),
        )

    def tall_turn(self, chunk):
        layer = chunk // LAYER_CHUNKS
        place = chunk % LAYER_CHUNKS
        return layer, place // 5, place % 5 == 4

    def for_tall(self, phase, chunk, act):
        layer, part, due = self.tall_turn(chunk)
        if phase >= 2:
            pl.when(due)(lambda: act(self.tall_message(phase, layer, part, 0)))
        else:
            for odd in range(2):
                pl.when(due & (part % 2 == odd))(
                    lambda odd=odd: act(self.tall_message(phase, layer, part, odd))
                )

    def step(self, step):
        for phase in range(PHASES, -1, -1):
            chunk = step - GATHER_STEPS[phase]

            @pl.when((chunk >= 0) & (chunk < CHUNKS))
            def _(phase=phase, chunk=chunk):
                if phase >= 1:
                    for copy in self.wide_messages(phase - 1, chunk):
                        copy.wait()
                    self.for_tall(phase - 1, chunk, lambda copy: copy.wait())
                else:
                    pltpu.make_async_copy(
                        self.own[0].at[:, pl.ds(0, WIDTH)],
                        self.held.at[(chunk,) + self.at],
                        self.local_sem.at[chunk],
                    ).wait()
                    layer = chunk // LAYER_CHUNKS

                    @pl.when(chunk % LAYER_CHUNKS == 4)
                    def _():
                        pltpu.make_async_copy(
                            self.own[3],
                            self.tall.at[(layer,) + self.at],
                            self.local_sem.at[CHUNKS + layer],
                        ).wait()

                if phase < PHASES:
                    for copy in self.wide_messages(phase, chunk):
                        copy.start()
                    self.for_tall(phase, chunk, lambda copy: copy.start())


def forward_kernel(*refs):
    own = refs[:WEIGHTS]
    tokens, validity = refs[WEIGHTS : WEIGHTS + 2]
    held, tall, mixed_out, between, middles, turns, stages, halves_out = refs[10:18]
    hidden_out, attends_out = refs[18:20]
    scratch = refs[20:]
    sems, (load_sem, tall_sem, stage_sem, half_sem, hidden_sem, misc_sem) = scratch[:5], scratch[5:11]
    loaded, shrink, x, middle, normed, gated, hidden, parts, stage, half_stage, final = scratch[11:22]
    turned, hidden_stage, attends = scratch[22:]
    gather = Gather(own, held, tall, sems)
    gather.begin()

    def rows_of(t):
        return pl.ds(pl.multiple_of(t * 128, 128), 128)

    def start_rows(t, carry):
        rows = rows_of(t)
        x[rows, :] = tokens[rows, :].astype(WIDE) * validity[rows, :]
        return carry

    def keep_turned(layer, kind):
        return pltpu.make_async_copy(turned, turns.at[layer, kind], misc_sem.at[0])

    def turn(source, layer, kind):
        def act(t, carry):
            rows = rows_of(t)
            turned[:, rows] = source[rows, :].T
            return carry

        lax.fori_loop(0, ROWS // 128, act, 0)
        keep_turned(layer, kind).start()

    lax.fori_loop(0, ROWS // 128, start_rows, 0)
    norm_into(x, normed)
    turn(normed, 0, 0)

    def load(chunk):
        return pltpu.make_async_copy(
            held.at[chunk], loaded.at[chunk % LOAD_SLOTS], load_sem.at[chunk % LOAD_SLOTS]
        )

    def load_tall(layer):
        return pltpu.make_async_copy(tall.at[layer], shrink, tall_sem)

    def keep_stage(layer, group):
        return pltpu.make_async_copy(stage, stages.at[layer, group], stage_sem)

    def keep_half(layer, part):
        return pltpu.make_async_copy(
            half_stage.at[part % 2], halves_out.at[layer, part], half_sem.at[part % 2]
        )

    def keep_hidden(layer, part):
        rows = pl.ds(pl.multiple_of(part * WIDTH, WIDTH), WIDTH)
        return pltpu.make_async_copy(
            hidden_stage.at[part % 2], hidden_out.at[layer, rows, :], hidden_sem.at[part % 2]
        )

    def keep_attends(group):
        return pltpu.make_async_copy(attends, attends_out.at[group], misc_sem.at[4])

    def keep_middle(layer):
        return pltpu.make_async_copy(middle, middles.at[layer], misc_sem.at[1])

    def keep_between():
        return pltpu.make_async_copy(x, between, misc_sem.at[2])

    def weight(slot, f):
        return loaded[slot, f].reshape(1024, WIDTH)

    def project_step(layer, place, slot):
        group = place // 2
        for f in range(2):
            parts[place % 2, f] = dot(normed[...], weight(slot, f))

        @pl.when(place % 2 == 1)
        def _():
            @pl.when((layer > 0) | (group > 0))
            def _():
                keep_stage(layer, group).wait()

            @pl.when((layer == 0) & (group > 0))
            def _():
                keep_attends(0).wait()

            for kind in range(4):
                stage[kind] = parts[kind % 2, kind // 2].astype(LOW)

            @pl.when(layer == 0)
            def _():
                local_mixer(group, parts, validity, gated, stage, attends)
                keep_attends(group).start()

            pl.when(layer > 0)(lambda: linear_mixer(group, parts, gated, stage))
            keep_stage(layer, group).start()

    def output_step(layer, part, slot):
        @pl.when(part == 0)
        def _():
            keep_turned(0, 0).wait()
            turn(gated, layer, 1)

            @pl.when(layer > 0)
            def _():
                keep_middle(0).wait()

        for f in range(2):
            lanes = pl.ds(pl.multiple_of(f * 512 + part * WIDTH, WIDTH), WIDTH)
            middle[:, lanes] = x[:, lanes] + dot(gated[...], weight(slot, f))

        @pl.when(part == OUTPUT_CHUNKS - 1)
        def _():
            keep_middle(layer).start()
            norm_into(middle, normed)
            keep_turned(0, 0).wait()
            turn(normed, layer, 2)

    def expand_step(layer, part, slot):
        @pl.when((layer > 0) | (part > 1))
        def _():
            keep_half(layer, part).wait()
            keep_hidden(layer, part).wait()

        first = dot(normed[...], weight(slot, 0))
        second = dot(normed[...], weight(slot, 1))
        half_stage[part % 2, 0] = first.astype(LOW)
        half_stage[part % 2, 1] = second.astype(LOW)
        both = (first * second).astype(LOW)
        hidden[:, pl.ds(pl.multiple_of(part * WIDTH, WIDTH), WIDTH)] = both
        hidden_stage[part % 2] = both.T
        keep_half(layer, part).start()
        keep_hidden(layer, part).start()

    def shrink_step(layer):
        load_tall(layer).wait()

        @pl.when(layer > 0)
        def _():
            keep_between().wait()

        def body(turn, carry):
            f = turn // 2
            columns = pl.ds(pl.multiple_of((turn % 2) * WIDTH, WIDTH), WIDTH)
            lanes = pl.ds(pl.multiple_of(turn * WIDTH, WIDTH), WIDTH)
            matrix = shrink[f, :, :, :, :, :, columns].reshape(hidden.shape[1], WIDTH)
            x[:, lanes] = middle[:, lanes] + dot(hidden[...], matrix)
            return carry

        lax.fori_loop(0, 4, body, 0)

        @pl.when(layer == 0)
        def _():
            keep_between().start()
            norm_into(x, normed)
            keep_turned(0, 0).wait()
            turn(normed, 1, 0)

        @pl.when(layer > 0)
        def _():
            def last_rows(t, carry):
                rows = rows_of(t)
                final[rows, :] = (x[rows, :] * validity[rows, :]).astype(LOW)
                return carry

            lax.fori_loop(0, ROWS // 128, last_rows, 0)

    def body(step, carry):
        gather.step(step)
        arrived = step - GATHER_STEPS[PHASES]

        @pl.when((arrived >= 0) & (arrived < CHUNKS))
        def _():
            load(arrived).start()

            @pl.when(arrived % LAYER_CHUNKS == LAYER_CHUNKS - 2)
            def _():
                load_tall(arrived // LAYER_CHUNKS).start()

        ready = arrived - 1

        @pl.when((ready >= 0) & (ready < CHUNKS))
        def _():
            load(ready).wait()
            layer = ready // LAYER_CHUNKS
            place = ready % LAYER_CHUNKS
            slot = ready % LOAD_SLOTS
            pl.when(place < PROJECT_CHUNKS)(lambda: project_step(layer, place, slot))
            pl.when((place >= PROJECT_CHUNKS) & (place < PROJECT_CHUNKS + OUTPUT_CHUNKS))(
                lambda: output_step(layer, place - PROJECT_CHUNKS, slot)
            )
            pl.when(place >= PROJECT_CHUNKS + OUTPUT_CHUNKS)(
                lambda: expand_step(layer, place - PROJECT_CHUNKS - OUTPUT_CHUNKS, slot)
            )
            pl.when(place == LAYER_CHUNKS - 1)(lambda: shrink_step(layer))

        return carry

    lax.fori_loop(0, CHUNKS + GATHER_STEPS[PHASES] + 1, body, 0)
    last = pltpu.make_async_copy(final, mixed_out, misc_sem.at[3])
    last.start()
    keep_stage(1, HEAD_GROUPS - 1).wait()
    keep_attends(0).wait()
    keep_turned(0, 0).wait()
    keep_middle(1).wait()
    keep_half(1, EXPAND_CHUNKS - 2).wait()
    keep_half(1, EXPAND_CHUNKS - 1).wait()
    keep_hidden(1, EXPAND_CHUNKS - 2).wait()
    keep_hidden(1, EXPAND_CHUNKS - 1).wait()
    last.wait()


def run_forward(shards_of, tokens, validity):
    bits = (2, 2, 2, 2, 2)
    struct = jax.ShapeDtypeStruct
    return pl.pallas_call(
        forward_kernel,
        out_shape=(
            struct((CHUNKS,) + bits + (64, WIDTH), LOW),
            struct((2,) + bits + (176, 512), LOW),
            struct((ROWS, 1024), LOW),
            struct((ROWS, 1024), WIDE),
            struct((2, ROWS, 1024), WIDE),
            struct((2, 3, 1024, ROWS), LOW),
            struct((2, HEAD_GROUPS, 5, ROWS, WIDTH), LOW),
            struct((2, EXPAND_CHUNKS, 2, ROWS, WIDTH), LOW),
            struct((2, 2816, ROWS), LOW),
            struct((HEAD_GROUPS, 8, 2, 128, 128), LOW),
        ),
        in_specs=[FULL] * (WEIGHTS + 2),
        out_specs=(ANY,) * 10,
        scratch_shapes=[
            pltpu.SemaphoreType.DMA((CHUNKS + 2,)),
            pltpu.SemaphoreType.DMA((10, GATHER_SLOTS)),
            pltpu.SemaphoreType.DMA((10, GATHER_SLOTS)),
            pltpu.SemaphoreType.DMA((PHASES, 2 * SHRINK_PARTS)),
            pltpu.SemaphoreType.DMA((PHASES, 2 * SHRINK_PARTS)),
            pltpu.SemaphoreType.DMA((LOAD_SLOTS,)),
            pltpu.SemaphoreType.DMA,
            pltpu.SemaphoreType.DMA,
            pltpu.SemaphoreType.DMA((2,)),
            pltpu.SemaphoreType.DMA((2,)),
            pltpu.SemaphoreType.DMA((5,)),
            pltpu.VMEM((LOAD_SLOTS,) + bits + (64, WIDTH), LOW),
            pltpu.VMEM(bits + (176, 512), LOW),
            pltpu.VMEM((ROWS, 1024), WIDE),
            pltpu.VMEM((ROWS, 1024), WIDE),
            pltpu.VMEM((ROWS, 1024), LOW),
            pltpu.VMEM((ROWS, 1024), LOW),
            pltpu.VMEM((ROWS, 2816), LOW),
            pltpu.VMEM((2, 2, ROWS, WIDTH), WIDE),
            pltpu.VMEM((5, ROWS, WIDTH), LOW),
            pltpu.VMEM((2, 2, ROWS, WIDTH), LOW),
            pltpu.VMEM((ROWS, 1024), LOW),
            pltpu.VMEM((1024, ROWS), LOW),
            pltpu.VMEM((2, WIDTH, ROWS), LOW),
            pltpu.VMEM((8, 2, 128, 128), LOW),
        ],
        compiler_params=pltpu.CompilerParams(
            collective_id=0, has_side_effects=True, vmem_limit_bytes=60 << 20
        ),
    )(*shards_of, tokens, validity)


SCATTER_STEPS = (0, 2, 5, 8, 11, 14)
SCATTER_SLOTS = 10
TERM_SLOTS = SCATTER_STEPS[1]
TALL_SLOTS = 3
OUTPUT_TURN = EXPAND_CHUNKS
PROJECT_TURN = EXPAND_CHUNKS + OUTPUT_CHUNKS
TALL_ROWS = 176


class Scatter:
    def __init__(self, outs, sems, wide, tall):
        self.outs, self.tall_outs = outs
        self.send_sem, self.recv_sem, self.tall_send, self.tall_recv = sems[:4]
        self.store_sem, self.tall_store = sems[4:]
        self.wide, self.tall = wide[:6], tall[:6]
        self.result, self.tall_result = wide[6], tall[6]
        self.places, self.targets = neighbours()

    def tall_turn(self, chunk):
        layer = chunk // LAYER_CHUNKS
        turn = chunk % LAYER_CHUNKS
        return layer * SHRINK_PARTS + turn // 5, turn // 5, turn % 5 == 4

    def wide_parts(self):
        half = WIDTH // 2
        return (
            (pl.ds(0, half), ("c", "y", "x", "z1", "z2")),
            (pl.ds(half, half), ("c", "x", "y", "z1", "z2")),
        )

    def tall_parts(self, odd):
        plane = ("x", "y") if odd else ("y", "x")
        return ((pl.ds(0, SHRINK_WIDTH), ("c", "z1", "z2") + plane),)

    def left(self, order, phase):
        used = set(AXIS_OF[target] for target in order[: phase + 1])
        return [name for name in AXIS_NAMES if name not in used]

    def source(self, buffers, slots, phase, order):
        if phase == 0:
            return buffers[0].at[slots[0]], list(AXIS_NAMES)
        return buffers[phase].at[slots[1]], self.left(order, phase - 1)

    def messages(self, buffers, slots, sems, phase, parts):
        if phase == 0 and len(parts) == 2:
            parts = ((pl.ds(0, WIDTH), parts[0][1]),)
        out = []
        for part, (lanes, order) in enumerate(parts):
            source, dims = self.source(buffers, slots, phase, order)
            target = order[phase]
            away = tuple(
                1 - self.places[d] if d == AXIS_OF[target] else slice(None) for d in dims
            )
            whole = tuple(slice(None) for _ in self.left(order, phase))
            place = (2 * phase + part, slots[1])
            out.append(
                pltpu.make_async_remote_copy(
                    src_ref=source.at[away + (slice(None), lanes)],
                    dst_ref=buffers[1 + phase].at[(slots[1],) + whole + (slice(None), lanes)],
                    send_sem=sems[0].at[place],
                    recv_sem=sems[1].at[place],
                    device_id=self.targets[target],
                    device_id_type=MESH,
                )
            )
        return out

    def add(self, buffers, slots, phase, parts, result):
        if phase == 0 and len(parts) == 2:
            parts = ((pl.ds(0, WIDTH), parts[0][1]),)
        for lanes, order in parts:
            source, dims = self.source(buffers, slots, phase, order)
            cut = AXIS_OF[order[phase]]
            near = tuple(self.places[d] if d == cut else slice(None) for d in dims)
            whole = tuple(slice(None) for _ in self.left(order, phase))
            ref = buffers[1 + phase].at[slots[1]]
            mine = source[near + (slice(None), lanes)]
            came = ref[whole + (slice(None), lanes)]
            if phase < 4:
                ref[whole + (slice(None), lanes)] = came + mine
            else:
                result[:, lanes] = came.astype(WIDE) + mine.astype(WIDE)

    def wide_slots(self, chunk):
        return (chunk % TERM_SLOTS, chunk % SCATTER_SLOTS)

    def tall_slots(self, place):
        return (0, place % TALL_SLOTS)

    def wide_messages(self, phase, chunk):
        return self.messages(
            self.wide,
            self.wide_slots(chunk),
            (self.send_sem, self.recv_sem),
            phase,
            self.wide_parts(),
        )

    def tall_messages(self, phase, place, odd):
        return self.messages(
            self.tall,
            self.tall_slots(place),
            (self.tall_send, self.tall_recv),
            phase,
            self.tall_parts(odd),
        )

    def store(self, chunk):
        return pltpu.make_async_copy(
            self.result.at[chunk % 2], self.outs.at[chunk], self.store_sem.at[chunk % 2]
        )

    def store_tall(self, place):
        return pltpu.make_async_copy(
            self.tall_result.at[place % 2], self.tall_outs.at[place], self.tall_store.at[place % 2]
        )

    def start(self, phase, chunk):
        for copy in self.wide_messages(phase, chunk):
            copy.start()
        place, part, due = self.tall_turn(chunk)
        for odd in range(2):

            @pl.when(due & (part % 2 == odd))
            def _(odd=odd):
                for copy in self.tall_messages(phase, place, odd):
                    copy.start()

    def take(self, phase, chunk):
        for copy in self.wide_messages(phase, chunk):
            copy.wait()
        if phase == PHASES - 1:
            pl.when(chunk >= 2)(lambda: self.store(chunk).wait())
        self.add(
            self.wide, self.wide_slots(chunk), phase, self.wide_parts(), self.result.at[chunk % 2]
        )
        place, part, due = self.tall_turn(chunk)
        for odd in range(2):

            @pl.when(due & (part % 2 == odd))
            def _(odd=odd):
                for copy in self.tall_messages(phase, place, odd):
                    copy.wait()
                if phase == PHASES - 1:
                    pl.when(place >= 2)(lambda: self.store_tall(place).wait())
                self.add(
                    self.tall,
                    self.tall_slots(place),
                    phase,
                    self.tall_parts(odd),
                    self.tall_result.at[place % 2],
                )
                if phase == PHASES - 1:
                    self.store_tall(place).start()

        if phase == PHASES - 1:
            self.store(chunk).start()

    def older(self, step):
        for phase in range(PHASES, 0, -1):
            chunk = step - SCATTER_STEPS[phase]

            @pl.when((chunk >= 0) & (chunk < CHUNKS))
            def _(phase=phase, chunk=chunk):
                self.take(phase - 1, chunk)
                if phase < PHASES:
                    self.start(phase, chunk)

    def finish(self):
        for chunk in (CHUNKS - 2, CHUNKS - 1):
            self.store(chunk).wait()
        for place in (2 * SHRINK_PARTS - 2, 2 * SHRINK_PARTS - 1):
            self.store_tall(place).wait()


def norm_slope(values, inverse, upstream, mean):
    return inverse * (upstream - values * (inverse * inverse) * mean)


def gate_back(update, mixture, coming, first):
    inverse = lax.rsqrt(pair_mean(mixture * mixture, first) + epsilon)
    curve = logistic(update)
    back_update = coming * (mixture * inverse) * (curve * (1.0 + update * (1.0 - curve)))
    gate = coming * (update * curve)
    back_mixture = norm_slope(mixture, inverse, gate, pair_mean(gate * mixture, first))
    return back_update, back_mixture


def both_heads(values, first):
    zero = jnp.zeros_like(values)
    return jnp.concatenate([jnp.where(first, values, zero), jnp.where(first, zero, values)], axis=0)


def side_by_side(values):
    half = values.shape[0] // 2
    return jnp.concatenate([values[:half], values[half:]], axis=1)


def local_mixer_back(group, stage, attends, validity, coming, back):
    def body(turn, carry):
        rows = pl.ds(pl.multiple_of((turn // 2) * 128, 128), 128)
        lanes = pl.ds(pl.multiple_of((turn % 2) * 128, 128), 128)
        columns = pl.ds(pl.multiple_of(group * WIDTH + (turn % 2) * 128, 128), 128)
        first = first_lanes(128)

        def put(i, j, value):
            start = j * WIDTH + (turn % 2) * 128
            back[i, rows, pl.ds(pl.multiple_of(start, 128), 128)] = value.astype(LOW)

        q, k, v = stage[0, rows, lanes], stage[1, rows, lanes], stage[2, rows, lanes]
        update = stage[3, rows, lanes].astype(WIDE)
        mixture = stage[4, rows, lanes].astype(WIDE)
        back_update, back_mixture = gate_back(update, mixture, coming[rows, columns], first)
        put(1, 1, back_update)
        grad = (back_mixture.astype(LOW).astype(WIDE) * validity[rows, :]).astype(LOW)
        grads = both_heads(grad, first)
        attend_low = attends[turn].reshape(256, 128)
        attend = attend_low.astype(WIDE)
        back_attend = contract_cols(grads, v)
        total = jnp.sum(back_attend * attend, axis=-1, keepdims=True)
        back_scores = (attend * (back_attend - total)).astype(LOW)
        put(0, 0, dot(side_by_side(back_scores), both_heads(k, first)) * HEAD ** (-0.5))
        put(1, 0, contract_rows(back_scores, both_heads(q, first)) * HEAD ** (-0.5))
        put(0, 1, contract_rows(attend_low, grads))
        return carry

    lax.fori_loop(0, 2 * ROWS // 128, body, 0, unroll=4)


def linear_mixer_back(group, stage, coming, back):
    half = ROWS // 2

    def body(pair, carry):
        lanes = pl.ds(pl.multiple_of(pair * 128, 128), 128)
        columns = pl.ds(pl.multiple_of(group * WIDTH + pair * 128, 128), 128)
        first = first_lanes(ROWS)
        queries = stage[0, :, lanes].astype(WIDE)
        keys_all = stage[1, :, lanes].astype(WIDE)
        v = stage[2, :, lanes]
        fq = softplus(queries).astype(LOW)
        fk = softplus(keys_all).astype(LOW)
        update = stage[3, :, lanes].astype(WIDE)
        mixture = stage[4, :, lanes].astype(WIDE)
        back_update, back_mixture = gate_back(update, mixture, coming[:, columns], first)

        def put(i, j, rows, value):
            start = j * WIDTH + pair * 128
            back[i, rows, pl.ds(pl.multiple_of(start, 128), 128)] = value.astype(LOW)

        put(1, 1, slice(None), back_update)
        grad = back_mixture.astype(LOW)
        tiles = []
        for t in range(2):
            reach = (t + 1) * half
            i = lax.broadcasted_iota(jnp.int32, (2 * half, reach), 0) % half + t * half
            j = lax.broadcasted_iota(jnp.int32, (2 * half, reach), 1)
            pair_q = both_heads(fq[t * half : reach], first[:half])
            pair_g = both_heads(grad[t * half : reach], first[:half])
            scores = jnp.where(j <= i, contract_cols(pair_q, fk[:reach]), 0.0).astype(LOW)
            inner = jnp.where(j <= i, contract_cols(pair_g, v[:reach]), 0.0).astype(LOW)
            tiles.append(
                (
                    dot(side_by_side(inner), both_heads(fk[:reach], first[:reach])),
                    contract_rows(inner, pair_q),
                    contract_rows(scores, pair_g),
                )
            )
        for t in range(2):
            rows = pl.ds(t * half, half)
            span = slice(t * half, (t + 1) * half)
            back_q = tiles[t][0]
            back_k = tiles[1][1][span]
            back_v = tiles[1][2][span]
            if t == 0:
                back_k = back_k + tiles[0][1]
                back_v = back_v + tiles[0][2]
            put(0, 0, rows, back_q * logistic(queries[span]))
            put(1, 0, rows, back_k * logistic(keys_all[span]))
            put(0, 1, rows, back_v)
        return carry

    lax.fori_loop(0, 2, body, 0)


def over_rows(act):
    def body(t, carry):
        act(pl.ds(pl.multiple_of(t * 128, 128), 128))
        return carry

    lax.fori_loop(0, ROWS // 128, body, 0)


def backward_kernel(*refs):
    cotangent, tokens, validity = refs[:3]
    held, tall, between, middles, turns, stages, halves_in, hidden_in, attends_in = refs[3:12]
    tokens_out, outs, tall_outs = refs[12:15]
    scratch = refs[15:]
    scatter_sems, loads = scratch[:6], scratch[6:12]
    load_sem, half_sem, shrink_sem, stage_sem, turn_sem, misc_sem = loads
    wide_buffers, tall_buffers = scratch[12:19], scratch[19:26]
    (
        loaded,
        half_in,
        stage,
        attends,
        shrink,
        hidden_turned,
        branch,
        gated_branch,
        up,
        sums,
        middle,
        layer_in,
        turned,
        back,
    ) = scratch[26:]
    scatter = Scatter((outs, tall_outs), scatter_sems, wide_buffers, tall_buffers)

    class Load:
        def __init__(self, chunk, number):
            self.copies = [
                pltpu.make_async_copy(
                    held.at[chunk, f],
                    loaded.at[number % 2, :, pl.ds(f * WIDTH, WIDTH)],
                    load_sem.at[number % 2, f],
                )
                for f in range(2)
            ]

        def start(self):
            for copy in self.copies:
                copy.start()

        def wait(self):
            for copy in self.copies:
                copy.wait()

    def load_turned(layer, kind, order):
        return pltpu.make_async_copy(
            turns.at[layer, kind], turned.at[order % 2], turn_sem.at[order % 2]
        )

    def load_attends(group):
        return pltpu.make_async_copy(attends_in.at[group], attends, misc_sem.at[4])

    def load_half(layer, part, number):
        return pltpu.make_async_copy(
            halves_in.at[layer, part], half_in.at[number % 2], half_sem.at[number % 2]
        )

    def load_shrink(layer, part, number):
        rows = pl.ds(pl.multiple_of(part * WIDTH, WIDTH), WIDTH)
        return pltpu.make_async_copy(
            tall.at[layer, :, rows, :], shrink.at[number % 2], shrink_sem.at[number % 2]
        )

    def load_stage(layer, group):
        return pltpu.make_async_copy(stages.at[layer, group], stage, stage_sem)

    def fetch(kind, layer):
        source, target = (
            (None, None),
            (middles, middle),
            (hidden_in, hidden_turned),
        )[kind]
        return pltpu.make_async_copy(source.at[layer], target, misc_sem.at[kind])

    def fetch_between():
        return pltpu.make_async_copy(between, layer_in, misc_sem.at[3])

    def prefetch(number):
        pl.when(number >= CHUNKS)(lambda: Load(number - CHUNKS, number).start())
        pl.when(number < CHUNKS)(lambda: prefetch_turn(number))

    def prefetch_turn(number):
        layer = 1 - number // LAYER_CHUNKS
        turn = number % LAYER_CHUNKS
        base = LAYER_CHUNKS * layer

        @pl.when(turn < OUTPUT_TURN)
        def _():
            Load(base + PROJECT_CHUNKS + OUTPUT_CHUNKS + turn, number).start()
            load_half(layer, turn, number).start()
            load_shrink(layer, turn, number).start()

        @pl.when((turn >= OUTPUT_TURN) & (turn < PROJECT_TURN))
        def _():
            Load(base + PROJECT_CHUNKS + turn - OUTPUT_TURN, number).start()

        @pl.when(turn >= PROJECT_TURN)
        def _():
            pl.when(layer == 1)(lambda: Load(base + turn - PROJECT_TURN, number).start())

            @pl.when((turn - PROJECT_TURN) % 2 == 0)
            def _():
                load_stage(layer, (turn - PROJECT_TURN) // 2).start()
                pl.when(layer == 0)(lambda: load_attends((turn - PROJECT_TURN) // 2).start())

    prefetch_turn(jnp.int32(0))
    load_turned(1, 2, 0).start()
    load_turned(1, 1, 1).start()
    fetch(2, 1).start()
    fetch(1, 1).start()
    fetch_between().start()

    def begin_rows(rows):
        up[rows, :] = cotangent[rows, :].astype(WIDE) * validity[rows, :]

    over_rows(begin_rows)
    greet(scatter.targets)

    def expand_start(layer):
        def act(rows):
            branch[rows, :] = up[rows, :].astype(LOW)
            sums[0, rows, :] = jnp.zeros((128, 1024), WIDE)

        over_rows(act)
        load_turned(0, 0, 1 - layer).wait()
        pl.when(layer == 0)(lambda: load_turned(0, 1, 4).start())

    def expand_turn(part, number):
        load_half(0, 0, number).wait()
        load_shrink(0, 0, number).wait()
        low, high = pl.ds(0, WIDTH), pl.ds(WIDTH, WIDTH)
        back_hidden = contract_cols(branch[:, :512], shrink[number % 2, 0])
        back_hidden = back_hidden + contract_cols(branch[:, 512:], shrink[number % 2, 1])
        first = half_in[number % 2, 0].astype(WIDE)
        second = half_in[number % 2, 1].astype(WIDE)
        back[0, 0, :, low] = (back_hidden * second).astype(LOW)
        back[0, 0, :, high] = (back_hidden * first).astype(LOW)

    def output_start(layer):
        load_turned(0, 0, 2 - layer).wait()
        load_turned(layer, 0, 3 - layer).start()
        fetch(1, 1).wait()

        def act(rows):
            values = middle[rows, :]
            back_second = sums[0, rows, :]
            new = up[rows, :] + norm_back(values, back_second)
            up[rows, :] = new
            gated_branch[rows, :] = new.astype(LOW)
            sums[1, rows, :] = jnp.zeros((128, 1024), WIDE)

        over_rows(act)

    def output_turn(part):
        for f in range(2):
            lanes = pl.ds(pl.multiple_of(f * 512 + part * WIDTH, WIDTH), WIDTH)
            back[0, 0, :, pl.ds(f * WIDTH, WIDTH)] = gated_branch[:, lanes]

    def project_start(layer):
        @pl.when(layer == 1)
        def _():
            fetch_between().wait()
            fetch(1, 0).start()
            load_turned(0, 2, 3).start()

        @pl.when(layer == 0)
        def _():
            def act(rows):
                layer_in[rows, :] = tokens[rows, :].astype(WIDE) * validity[rows, :]

            over_rows(act)

        def clear(rows):
            sums[0, rows, :] = jnp.zeros((128, 1024), WIDE)

        over_rows(clear)
        load_turned(0, 0, 1 - layer).wait()

    def project_turn(layer, group):
        load_stage(0, 0).wait()
        coming = sums.at[1]
        mine = back.at[group]
        pl.when(layer == 1)(lambda: linear_mixer_back(group, stage, coming, mine))

        @pl.when(layer == 0)
        def _():
            load_attends(0).wait()
            local_mixer_back(group, stage, attends, validity, coming, mine)

    def finish_layer(layer):
        def act(rows):
            up[rows, :] = up[rows, :] + norm_back(layer_in[rows, :], sums[0, rows, :])

        over_rows(act)

    def terms(number, group, which, order):
        slot = number % TERM_SLOTS
        out = wide_buffers[0]

        def body(tile, carry):
            rows = pl.ds(pl.multiple_of(tile * 512, 512), 512)
            value = dot(turned[order % 2, rows, :], back[group, which]).astype(LOW)
            for f in range(2):
                part = value[:, f * WIDTH : (f + 1) * WIDTH]
                out[slot, f, tile] = part.reshape(2, 2, 2, 64, WIDTH)
            return carry

        lax.fori_loop(0, 2, body, 0)

    def tall_terms(part, number):
        out = tall_buffers[0]
        pl.when(part == 0)(lambda: fetch(2, 0).wait())
        lanes = [pl.ds(pl.multiple_of(f * 512 + part * 128, 128), 128) for f in range(2)]
        both = jnp.concatenate([branch[:, lanes[0]], branch[:, lanes[1]]], axis=1)

        def body(tile, carry):
            rows = pl.ds(pl.multiple_of(tile * 8 * TALL_ROWS, 8 * TALL_ROWS), 8 * TALL_ROWS)
            value = dot(hidden_turned[rows, :], both).astype(LOW)
            for f in range(2):
                out[0, f, tile] = value[:, f * 128 : f * 128 + 128].reshape(
                    2, 2, 2, TALL_ROWS, SHRINK_WIDTH
                )
            return carry

        lax.fori_loop(0, 2, body, 0)

        @pl.when((part == SHRINK_PARTS - 1) & (number < LAYER_CHUNKS))
        def _():
            fetch(2, 0).start()

    def spread(number, group, which, kind):
        def body(t, carry):
            rows = pl.ds(pl.multiple_of(t * 512, 512), 512)
            value = contract_cols(back[group, which], loaded[number % 2, rows, :])
            sums[kind, :, rows] = sums[kind, :, rows] + value
            return carry

        lax.fori_loop(0, 2, body, 0)

    def body(step, carry):
        pl.when(step + 1 < CHUNKS + PROJECT_CHUNKS)(lambda: prefetch(step + 1))
        scatter.older(step)

        @pl.when(step < CHUNKS)
        def _():
            layer = 1 - step // LAYER_CHUNKS
            turn = step % LAYER_CHUNKS
            pl.when(turn == 0)(lambda: expand_start(layer))
            pl.when(turn == OUTPUT_TURN)(lambda: output_start(layer))
            pl.when(turn == PROJECT_TURN)(lambda: project_start(layer))
            pl.when(turn < OUTPUT_TURN)(lambda: expand_turn(turn, step))
            pl.when((turn >= OUTPUT_TURN) & (turn < PROJECT_TURN))(
                lambda: output_turn(turn - OUTPUT_TURN)
            )
            pl.when((turn >= PROJECT_TURN) & ((turn - PROJECT_TURN) % 2 == 0))(
                lambda: project_turn(layer, (turn - PROJECT_TURN) // 2)
            )
            in_project = jnp.minimum(jnp.maximum(turn - PROJECT_TURN + 1, 0), 1)
            in_output = jnp.minimum(jnp.maximum(turn - OUTPUT_TURN + 1, 0), 1) - in_project
            which = in_project * ((turn + PROJECT_TURN) % 2)
            group = in_project * ((turn - PROJECT_TURN) // 2)
            terms(step, group, which, 1 - layer + in_output)
            place, part, due = scatter.tall_turn(step)
            pl.when(due)(lambda: tall_terms(part, step))
            scatter.start(0, step)

            @pl.when((layer == 1) | (turn < PROJECT_TURN))
            def _():
                Load(0, step).wait()
                spread(step, group, which, in_output)

            pl.when(step == LAYER_CHUNKS - 1)(lambda: finish_layer(layer))

        @pl.when((step >= CHUNKS) & (step < CHUNKS + PROJECT_CHUNKS))
        def _():
            place = step - CHUNKS
            Load(0, step).wait()
            spread(step, place // 2, place % 2, 0)

            @pl.when(place == PROJECT_CHUNKS - 1)
            def _():
                finish_layer(0)

                def act(rows):
                    up[rows, :] = up[rows, :] * validity[rows, :]

                over_rows(act)
                pltpu.make_async_copy(up, tokens_out, misc_sem.at[3]).start()

        return carry

    lax.fori_loop(0, CHUNKS + SCATTER_STEPS[PHASES], body, 0)
    pltpu.make_async_copy(up, tokens_out, misc_sem.at[3]).wait()
    scatter.finish()


def scatter_buffers(terms, slots, rows, width):
    bits = [(2,) * (4 - phase) for phase in range(5)]
    return (
        [pltpu.VMEM((terms, 2, 2, 2, 2, 2, rows, width), LOW)]
        + [pltpu.VMEM((slots,) + lead + (rows, width), LOW) for lead in bits]
        + [pltpu.VMEM((2, rows, width), WIDE)]
    )


def run_backward(cotangent, tokens, validity, forward):
    struct = jax.ShapeDtypeStruct
    held, tall, mixed_out, between, middles, turns, stages, kept, hidden, attends = forward
    return pl.pallas_call(
        backward_kernel,
        out_shape=(
            struct((ROWS, 1024), WIDE),
            struct((CHUNKS, 64, WIDTH), WIDE),
            struct((2 * SHRINK_PARTS, TALL_ROWS, SHRINK_WIDTH), WIDE),
        ),
        in_specs=[FULL] * 3 + [ANY] * 9,
        out_specs=(ANY,) * 3,
        scratch_shapes=[
            pltpu.SemaphoreType.DMA((10, SCATTER_SLOTS)),
            pltpu.SemaphoreType.DMA((10, SCATTER_SLOTS)),
            pltpu.SemaphoreType.DMA((10, TALL_SLOTS)),
            pltpu.SemaphoreType.DMA((10, TALL_SLOTS)),
            pltpu.SemaphoreType.DMA((2,)),
            pltpu.SemaphoreType.DMA((2,)),
            pltpu.SemaphoreType.DMA((2, 2)),
            pltpu.SemaphoreType.DMA((2,)),
            pltpu.SemaphoreType.DMA((2,)),
            pltpu.SemaphoreType.DMA,
            pltpu.SemaphoreType.DMA((2,)),
            pltpu.SemaphoreType.DMA((5,)),
        ]
        + scatter_buffers(TERM_SLOTS, SCATTER_SLOTS, 64, WIDTH)
        + scatter_buffers(1, TALL_SLOTS, TALL_ROWS, SHRINK_WIDTH)
        + [
            pltpu.VMEM((2, 1024, 2 * WIDTH), LOW),
            pltpu.VMEM((2, 2, ROWS, WIDTH), LOW),
            pltpu.VMEM((5, ROWS, WIDTH), LOW),
            pltpu.VMEM((8, 2, 128, 128), LOW),
            pltpu.VMEM((2, 2, WIDTH, 512), LOW),
            pltpu.VMEM((2816, ROWS), LOW),
            pltpu.VMEM((ROWS, 1024), LOW),
            pltpu.VMEM((ROWS, 1024), LOW),
            pltpu.VMEM((ROWS, 1024), WIDE),
            pltpu.VMEM((2, ROWS, 1024), WIDE),
            pltpu.VMEM((ROWS, 1024), WIDE),
            pltpu.VMEM((ROWS, 1024), WIDE),
            pltpu.VMEM((2, 1024, ROWS), LOW),
            pltpu.VMEM((HEAD_GROUPS, 2, ROWS, 2 * WIDTH), LOW),
        ],
        compiler_params=pltpu.CompilerParams(
            collective_id=1, has_side_effects=True, vmem_limit_bytes=62 << 20
        ),
    )(
        cotangent,
        tokens,
        validity,
        held.reshape(CHUNKS, 2, 1024, WIDTH),
        tall.reshape(2, 2, 2816, 512),
        between,
        middles,
        turns,
        stages,
        kept,
        hidden,
        attends,
    )


def unpack_kernel(*refs):
    outs, held, sem, load_sem = refs[4 : 6 + WEIGHTS], refs[6 + WEIGHTS : -2], refs[-2], refs[-1]
    loads = [
        pltpu.make_async_copy(source, target, load_sem.at[i])
        for i, (source, target) in enumerate(zip(refs[:4], held))
    ]
    for copy in loads:
        copy.start()
    mixed_in, tokens_in, chunks, parts = held
    copies = [(mixed_in, outs[0]), (tokens_in, outs[1])]
    for order in range(2):
        layer = 1 - order
        for turn in range(LAYER_CHUNKS):
            number = order * LAYER_CHUNKS + turn
            if turn < OUTPUT_TURN:
                weight, start = 2, chunk_columns(2, turn)
            elif turn < PROJECT_TURN:
                weight, start = 1, chunk_columns(1, turn - OUTPUT_TURN)
            else:
                weight, start = 0, chunk_columns(0, turn - PROJECT_TURN)
            target = outs[2 + 4 * layer + weight].at[:, pl.ds(start, WIDTH)]
            copies.append((chunks.at[number], target))
        for part in range(SHRINK_PARTS):
            target = outs[5 + 4 * layer].at[:, pl.ds(part * SHRINK_WIDTH, SHRINK_WIDTH)]
            copies.append((parts.at[order * SHRINK_PARTS + part], target))
    copies = [
        pltpu.make_async_copy(source, target, sem.at[i])
        for i, (source, target) in enumerate(copies)
    ]
    groups = ([0], [1], range(2, len(copies)))
    for group, waited in zip(groups, (loads[:1], loads[1:2], loads[2:])):
        for copy in waited:
            copy.wait()
        for i in group:
            copies[i].start()
    for copy in copies:
        copy.wait()


def unpack(mixed_out, tokens_gradient, chunks, parts, shards_of):
    struct = jax.ShapeDtypeStruct
    count = 2 + CHUNKS + 2 * SHRINK_PARTS
    return pl.pallas_call(
        unpack_kernel,
        out_shape=(struct(mixed_out.shape, LOW), struct(tokens_gradient.shape, WIDE))
        + tuple(struct(item.shape, WIDE) for item in shards_of),
        in_specs=[ANY] * 4,
        out_specs=(ANY,) * (2 + WEIGHTS),
        scratch_shapes=[
            pltpu.VMEM(item.shape, item.dtype)
            for item in (mixed_out, tokens_gradient, chunks, parts)
        ]
        + [pltpu.SemaphoreType.DMA((count,)), pltpu.SemaphoreType.DMA((4,))],
        compiler_params=pltpu.CompilerParams(vmem_limit_bytes=60 << 20),
    )(mixed_out, tokens_gradient, chunks, parts)


def gather_weights(shards_of):
    return [
        lax.all_gather(lax.all_gather(item, "fsdp", axis=1, tiled=True), "dp", axis=0, tiled=True)
        for item in shards_of
    ]


def settle_gradients(terms):
    tall = [
        lax.psum_scatter(item.astype(jnp.bfloat16), "dp", scatter_dimension=0, tiled=True)
        for item in terms
    ]
    return [
        lax.psum_scatter(item, "fsdp", scatter_dimension=1, tiled=True).astype(jnp.float32)
        for item in tall
    ]


def local_scores(queries, keys_all):
    query_blocks = split_heads(queries.astype(jnp.bfloat16))
    key_blocks = split_heads(keys_all.astype(jnp.bfloat16))
    scores = jnp.einsum(
        "bihd,bjhd->bhij", query_blocks, key_blocks, preferred_element_type=jnp.float32
    ) * HEAD ** (-0.5)
    return (query_blocks, key_blocks, jnp.where(causal_table(), scores, -1e30))


def local_forward(queries, keys_all, values_low, validity):
    query_blocks, key_blocks, scores = local_scores(queries, keys_all)
    highest_score = jnp.max(scores, axis=-1, keepdims=True)
    expweights = jnp.exp(scores - highest_score)
    row_total = jnp.sum(expweights, axis=-1, keepdims=True)
    attend = (expweights / row_total).astype(jnp.bfloat16)
    mixture = jnp.einsum(
        "bhij,bjhd->bihd", attend, split_heads(values_low), preferred_element_type=jnp.float32
    )
    return (join_heads(mixture) * validity, highest_score + jnp.log(row_total))


def local_backward(queries, keys_all, values_low, validity, logsum, back_mixture):
    query_blocks, key_blocks, scores = local_scores(queries, keys_all)
    value_blocks = split_heads(values_low)
    coming = split_heads(back_mixture * validity.astype(jnp.bfloat16))
    attend = jnp.exp(scores - logsum)
    back_values = jnp.einsum(
        "bhij,bihd->bjhd", attend.astype(jnp.bfloat16), coming, preferred_element_type=jnp.float32
    )
    back_attend = jnp.einsum(
        "bihd,bjhd->bhij", coming, value_blocks, preferred_element_type=jnp.float32
    )
    back_scores = (
        attend * (back_attend - jnp.sum(back_attend * attend, axis=-1, keepdims=True))
    ).astype(jnp.bfloat16)
    back_queries = jnp.einsum(
        "bhij,bjhd->bihd", back_scores, key_blocks, preferred_element_type=jnp.float32
    ) * HEAD ** (-0.5)
    back_keys = jnp.einsum(
        "bhij,bihd->bjhd", back_scores, query_blocks, preferred_element_type=jnp.float32
    ) * HEAD ** (-0.5)
    return (join_heads(back_queries), join_heads(back_keys), join_heads(back_values))


def linear_parts(queries, keys_all, values_low):
    feature_q = split_heads(jax.nn.softplus(queries).astype(jnp.bfloat16))
    feature_k = split_heads(jax.nn.softplus(keys_all).astype(jnp.bfloat16))
    value_blocks = split_heads(values_low)
    causal = causal_table().astype(jnp.float32)
    inner_scores = (
        jnp.einsum("bihd,bjhd->bhij", feature_q, feature_k, preferred_element_type=jnp.float32)
        * causal
    ).astype(jnp.bfloat16)
    states = jnp.einsum(
        "bjhd,bjhe->bhde", feature_k, value_blocks, preferred_element_type=jnp.float32
    )
    running = jnp.cumsum(states, axis=0)
    prior_states = jnp.concatenate([jnp.zeros_like(states[:1]), running[:-1]], axis=0)
    return (feature_q, feature_k, value_blocks, causal, inner_scores, prior_states)


def linear_forward(queries, keys_all, values_low):
    feature_q, feature_k, value_blocks, causal, inner_scores, prior_states = linear_parts(
        queries, keys_all, values_low
    )
    mixture = jnp.einsum(
        "bhij,bjhe->bihe", inner_scores, value_blocks, preferred_element_type=jnp.float32
    )
    mixture = mixture + jnp.einsum(
        "bihd,bhde->bihe", feature_q.astype(jnp.float32), prior_states, precision=highest
    )
    return join_heads(mixture)


def linear_backward(queries, keys_all, values_low, back_mixture):
    feature_q, feature_k, value_blocks, causal, inner_scores, prior_states = linear_parts(
        queries, keys_all, values_low
    )
    coming = split_heads(back_mixture)
    coming_wide = coming.astype(jnp.float32)
    back_inner = (
        jnp.einsum("bihe,bjhe->bhij", coming, value_blocks, preferred_element_type=jnp.float32)
        * causal
    ).astype(jnp.bfloat16)
    back_feature_q = jnp.einsum(
        "bhij,bjhd->bihd", back_inner, feature_k, preferred_element_type=jnp.float32
    )
    back_feature_q = back_feature_q + jnp.einsum(
        "bihe,bhde->bihd", coming_wide, prior_states, precision=highest
    )
    back_feature_k = jnp.einsum(
        "bhij,bihd->bjhd", back_inner, feature_q, preferred_element_type=jnp.float32
    )
    back_values = jnp.einsum(
        "bhij,bihe->bjhe", inner_scores, coming, preferred_element_type=jnp.float32
    )
    back_prior = jnp.einsum(
        "bihd,bihe->bhde", feature_q.astype(jnp.float32), coming_wide, precision=highest
    )
    running = jnp.cumsum(back_prior[::-1], axis=0)[::-1]
    later_states = jnp.concatenate([running[1:], jnp.zeros_like(running[:1])], axis=0)
    back_feature_k = back_feature_k + jnp.einsum(
        "bjhe,bhde->bjhd", value_blocks.astype(jnp.float32), later_states, precision=highest
    )
    back_values = back_values + jnp.einsum(
        "bjhd,bhde->bjhe", feature_k.astype(jnp.float32), later_states, precision=highest
    )
    return (
        join_heads(back_feature_q) * jax.nn.sigmoid(queries),
        join_heads(back_feature_k) * jax.nn.sigmoid(keys_all),
        join_heads(back_values),
    )


def forward_layer(layer_in, validity, weights, local):
    project, output, expand, shrink = weights
    normed = simple_norm(layer_in).astype(jnp.bfloat16)
    projected = jnp.dot(normed, project, preferred_element_type=jnp.float32)
    queries, keys_all, values, update = jnp.split(projected, 4, axis=1)
    values_low = values.astype(jnp.bfloat16)
    if local:
        mixture, logsum = local_forward(queries, keys_all, values_low, validity)
    else:
        mixture = linear_forward(queries, keys_all, values_low)
        logsum = None
    gated_rows = (head_norm(mixture) * jax.nn.silu(update)).astype(jnp.bfloat16)
    middle = layer_in + jnp.dot(gated_rows, output, preferred_element_type=jnp.float32)
    second = simple_norm(middle).astype(jnp.bfloat16)
    expanded = jnp.dot(second, expand, preferred_element_type=jnp.float32)
    half_width = expanded.shape[1] // 2
    hidden = (expanded[:, :half_width] * expanded[:, half_width:]).astype(jnp.bfloat16)
    result = middle + jnp.dot(hidden, shrink, preferred_element_type=jnp.float32)
    return (
        result,
        (layer_in, normed, projected, values_low, mixture, logsum, gated_rows, middle, second),
    )


def backward_layer(upstream, saved, weights, validity, local):
    project, output, expand, shrink = weights
    layer_in, normed, projected, values_low, mixture, logsum, gated_rows, middle, second = saved
    expanded = jnp.dot(second, expand, preferred_element_type=jnp.float32)
    half_width = expanded.shape[1] // 2
    first_half = expanded[:, :half_width]
    second_half = expanded[:, half_width:]
    hidden = (first_half * second_half).astype(jnp.bfloat16)
    back_branch = upstream.astype(jnp.bfloat16)
    shrink_term = contract_rows(hidden, back_branch)
    back_hidden = contract_cols(back_branch, shrink)
    back_expanded = jnp.concatenate(
        [back_hidden * second_half, back_hidden * first_half], axis=1
    ).astype(jnp.bfloat16)
    expand_term = contract_rows(second, back_expanded)
    back_second = contract_cols(back_expanded, expand)
    back_middle = upstream + norm_back(middle, back_second)
    back_gated = back_middle.astype(jnp.bfloat16)
    output_term = contract_rows(gated_rows, back_gated)
    back_rows_gated = contract_cols(back_gated, output)
    queries, keys_all, unused_values, update = jnp.split(projected, 4, axis=1)
    back_update = back_rows_gated * head_norm(mixture) * silu_slope(update)
    back_mixture = head_back(mixture, back_rows_gated * jax.nn.silu(update)).astype(jnp.bfloat16)
    if local:
        back_queries, back_keys, back_values = local_backward(
            queries, keys_all, values_low, validity, logsum, back_mixture
        )
    else:
        back_queries, back_keys, back_values = linear_backward(
            queries, keys_all, values_low, back_mixture
        )
    back_projected = jnp.concatenate(
        [back_queries, back_keys, back_values, back_update], axis=1
    ).astype(jnp.bfloat16)
    project_term = contract_rows(normed, back_projected)
    back_normed = contract_cols(back_projected, project)
    back_input = back_middle + norm_back(layer_in, back_normed)
    return (back_input, (project_term, output_term, expand_term, shrink_term))


def shards(
    direct,
    tokens,
    lengths,
    local_project,
    local_output,
    local_expand,
    local_shrink,
    linear_project,
    linear_output,
    linear_expand,
    linear_shrink,
    cotangent,
):
    positions = lax.broadcasted_iota(jnp.int32, (tokens.shape[1], 1), 0)
    validity = (positions < lengths[0]).astype(jnp.float32)
    shards_of = [
        local_project,
        local_output,
        local_expand,
        local_shrink,
        linear_project,
        linear_output,
        linear_expand,
        linear_shrink,
    ]
    if direct:
        forward = run_forward(shards_of, tokens[0], validity)
        back_tokens, chunks, parts = run_backward(cotangent[0], tokens[0], validity, forward)
        outs = unpack(forward[2], back_tokens, chunks, parts, shards_of)
        return (outs[0][None], outs[1][None]) + tuple(outs[2:])
    layer_in = tokens[0].astype(jnp.float32) * validity
    whole = gather_weights(shards_of)
    local_weights = whole[:4]
    linear_weights = whole[4:]
    between, local_saved = forward_layer(layer_in, validity, local_weights, True)
    result, linear_saved = forward_layer(between, validity, linear_weights, False)
    result = (result * validity).astype(jnp.bfloat16)
    upstream = cotangent[0].astype(jnp.float32) * validity
    back_between, linear_terms = backward_layer(
        upstream, linear_saved, linear_weights, validity, False
    )
    back_input, local_terms = backward_layer(
        back_between, local_saved, local_weights, validity, True
    )
    sums = settle_gradients(local_terms + linear_terms)
    return (
        result[None],
        (back_input * validity)[None],
    ) + tuple(sums)


def solution(mesh):
    in_specs = (
        P(("dp", "fsdp"), None, None),
        P(("dp", "fsdp")),
        P("dp", "fsdp"),
        P("dp", "fsdp"),
        P("dp", "fsdp"),
        P("dp", "fsdp"),
        P("dp", "fsdp"),
        P("dp", "fsdp"),
        P("dp", "fsdp"),
        P("dp", "fsdp"),
        P(("dp", "fsdp"), None, None),
    )
    out_specs = (
        P(("dp", "fsdp"), None, None),
        P(("dp", "fsdp"), None, None),
        P("dp", "fsdp"),
        P("dp", "fsdp"),
        P("dp", "fsdp"),
        P("dp", "fsdp"),
        P("dp", "fsdp"),
        P("dp", "fsdp"),
        P("dp", "fsdp"),
        P("dp", "fsdp"),
    )
    direct = dict(mesh.shape) == {"dp": 16, "fsdp": 2}
    return jax.shard_map(functools.partial(shards, direct), mesh=mesh, in_specs=in_specs, out_specs=out_specs, check_vma=False)
```

```python
import functools

import jax
import jax.numpy as jnp
from jax import lax
from jax.experimental import pallas as pl
from jax.experimental.pallas import tpu as pltpu
from jax.sharding import PartitionSpec as P

HEADS = 16
HEAD = 64
BLOCK = 64


epsilon = 1e-05
highest = lax.Precision.HIGHEST


def simple_norm(values):
    return values * lax.rsqrt(jnp.mean(values * values, axis=-1, keepdims=True) + epsilon)


def norm_back(values, upstream):
    inverse_rms = lax.rsqrt(jnp.mean(values * values, axis=-1, keepdims=True) + epsilon)
    return inverse_rms * (
        upstream
        - values * (inverse_rms * inverse_rms) * jnp.mean(upstream * values, axis=-1, keepdims=True)
    )


def head_norm(values):
    shaped = values.reshape(values.shape[0], HEADS, HEAD)
    return simple_norm(shaped).reshape(values.shape)


def head_back(values, upstream):
    shaped = values.reshape(values.shape[0], HEADS, HEAD)
    coming = upstream.reshape(values.shape[0], HEADS, HEAD)
    return norm_back(shaped, coming).reshape(values.shape)


def silu_slope(values):
    logistic = jax.nn.sigmoid(values)
    return logistic * (1.0 + values * (1.0 - logistic))


def contract_rows(first_matrix, second_matrix):
    return lax.dot_general(
        first_matrix, second_matrix, (((0,), (0,)), ((), ())), preferred_element_type=jnp.float32
    )


def contract_cols(first_matrix, second_matrix):
    return lax.dot_general(
        first_matrix, second_matrix, (((1,), (1,)), ((), ())), preferred_element_type=jnp.float32
    )


def causal_table():
    return lax.broadcasted_iota(jnp.int32, (BLOCK, BLOCK), 0) >= lax.broadcasted_iota(
        jnp.int32, (BLOCK, BLOCK), 1
    )


def split_heads(values):
    return values.reshape(values.shape[0] // BLOCK, BLOCK, HEADS, HEAD)


def join_heads(values):
    return values.reshape(values.shape[0] * BLOCK, HEADS * HEAD)


AXIS_NAMES = ("f", "zh", "zl", "y", "c")
AXIS_OF = {"c": "c", "y": "y", "x": "f", "z1": "zl", "z2": "zh"}
MESH = pl.DeviceIdType.MESH
ANY = pl.BlockSpec(memory_space=pl.ANY)
FULL = pl.BlockSpec(memory_space=pltpu.VMEM)
WEIGHTS = 8
WIDTH = 256
PHASES = 5
GATHER_STEPS = (0, 3, 6, 9, 12, 15)
HEAD_GROUPS = 4
PROJECT_CHUNKS = 8
OUTPUT_CHUNKS = 2
EXPAND_CHUNKS = 11
LAYER_CHUNKS = PROJECT_CHUNKS + OUTPUT_CHUNKS + EXPAND_CHUNKS
CHUNKS = 2 * LAYER_CHUNKS
SHRINK_PARTS = 4
SHRINK_WIDTH = 128
GATHER_SLOTS = 8
LOAD_SLOTS = 3
LOW = jnp.bfloat16
WIDE = jnp.float32
ROWS = 512


def neighbours():
    dp = lax.axis_index("dp")
    x = lax.axis_index("fsdp")
    z = dp // 4
    y = (dp // 2) % 2
    c = dp % 2
    places = {"f": x, "zh": z // 2, "zl": z % 2, "y": y, "c": c}
    targets = {
        "z1": ((z + 1 - 2 * (z % 2)) * 4 + y * 2 + c, x),
        "z2": (lax.rem(z + 2, 4) * 4 + y * 2 + c, x),
        "y": (z * 4 + (1 - y) * 2 + c, x),
        "c": (z * 4 + y * 2 + (1 - c), x),
        "x": (dp, 1 - x),
    }
    return places, targets


def greet(targets):
    barrier = pltpu.get_barrier_semaphore()
    for target in targets.values():
        pl.semaphore_signal(barrier, inc=1, device_id=target, device_id_type=MESH)
    pl.semaphore_wait(barrier, len(targets))


def dot(left, right):
    return jnp.dot(left, right, preferred_element_type=WIDE)


def softplus(values):
    return jnp.maximum(values, 0.0) + jnp.log1p(jnp.exp(-jnp.abs(values)))


def logistic(values):
    return 1.0 / (1.0 + jnp.exp(-values))


def first_lanes(rows):
    return lax.broadcasted_iota(jnp.int32, (rows, 128), 1) < HEAD


def pair_mean(values, first):
    left = jnp.sum(jnp.where(first, values, 0.0), axis=-1, keepdims=True)
    right = jnp.sum(jnp.where(first, 0.0, values), axis=-1, keepdims=True)
    return jnp.where(first, left, right) * (1.0 / HEAD)


def block_mask(rows):
    i = lax.broadcasted_iota(jnp.int32, (rows, rows), 0)
    j = lax.broadcasted_iota(jnp.int32, (rows, rows), 1)
    return (i // BLOCK == j // BLOCK) & (j <= i)


def norm_into(source, target):
    def body(t, carry):
        rows = pl.ds(pl.multiple_of(t * 128, 128), 128)
        target[rows, :] = simple_norm(source[rows, :]).astype(LOW)
        return carry

    lax.fori_loop(0, ROWS // 128, body, 0)


def local_mixer(group, parts, validity, gated, stage, attends):
    def body(turn, carry):
        t = turn // 2
        rows = pl.ds(pl.multiple_of(t * 128, 128), 128)
        pair = turn % 2
        lanes = pl.ds(pl.multiple_of(pair * 128, 128), 128)
        first = first_lanes(128)
        q = parts[0, 0, rows, lanes].astype(LOW)
        k = parts[1, 0, rows, lanes].astype(LOW)
        v = parts[0, 1, rows, lanes].astype(LOW)
        u = parts[1, 1, rows, lanes]
        keep = block_mask(128)
        mixed = []
        for head in range(2):
            mine = jnp.where(first == (head == 0), q, jnp.zeros_like(q))
            scores = contract_cols(mine, k) * HEAD ** (-0.5)
            scores = jnp.where(keep, scores, -1e30)
            highest_score = jnp.max(scores, axis=-1, keepdims=True)
            weights = jnp.exp(scores - highest_score)
            attend = (weights / jnp.sum(weights, axis=-1, keepdims=True)).astype(LOW)
            attends[turn, head] = attend
            mixed.append(dot(attend, v))
        mixture = jnp.where(first, mixed[0], mixed[1]) * validity[rows, :]
        scale = lax.rsqrt(pair_mean(mixture * mixture, first) + epsilon)
        columns = pl.ds(pl.multiple_of(group * WIDTH + pair * 128, 128), 128)
        gated[rows, columns] = (mixture * scale * (u * logistic(u))).astype(LOW)
        stage[4, rows, lanes] = mixture.astype(LOW)
        return carry

    lax.fori_loop(0, 2 * ROWS // 128, body, 0)


def linear_mixer(group, parts, gated, stage):
    half = ROWS // 2

    def body(pair, carry):
        lanes = pl.ds(pl.multiple_of(pair * 128, 128), 128)
        columns = pl.ds(pl.multiple_of(group * WIDTH + pair * 128, 128), 128)
        first = first_lanes(half)
        fk = softplus(parts[1, 0, :, lanes]).astype(LOW)
        v = parts[0, 1, :, lanes].astype(LOW)
        for t in range(2):
            rows = pl.ds(t * half, half)
            reach = (t + 1) * half
            fq = softplus(parts[0, 0, rows, lanes]).astype(LOW)
            i = lax.broadcasted_iota(jnp.int32, (half, reach), 0) + t * half
            j = lax.broadcasted_iota(jnp.int32, (half, reach), 1)
            mixed = []
            for head in range(2):
                mine = jnp.where(first == (head == 0), fq, jnp.zeros_like(fq))
                scores = jnp.where(j <= i, contract_cols(mine, fk[:reach]), 0.0).astype(LOW)
                mixed.append(dot(scores, v[:reach]))
            mixture = jnp.where(first, mixed[0], mixed[1])
            scale = lax.rsqrt(pair_mean(mixture * mixture, first) + epsilon)
            u = parts[1, 1, rows, lanes]
            gated[rows, columns] = (mixture * scale * (u * logistic(u))).astype(LOW)
            stage[4, rows, lanes] = mixture.astype(LOW)
        return carry

    lax.fori_loop(0, 2, body, 0)


def chunk_columns(weight, part):
    if weight == 0:
        return (part % 2) * 1024 + (part // 2) * WIDTH
    return part * WIDTH


class Gather:
    def __init__(self, own, held, tall, sems):
        self.own, self.held, self.tall = own, held, tall
        self.local_sem, self.send_sem, self.recv_sem, self.tall_send, self.tall_recv = sems
        self.places, self.targets = neighbours()
        self.at = tuple(self.places[name] for name in ("f", "zh", "zl", "y", "c"))

    def begin(self):
        counts = (PROJECT_CHUNKS, OUTPUT_CHUNKS, EXPAND_CHUNKS)
        for layer in range(2):
            chunk = LAYER_CHUNKS * layer
            for weight in range(3):
                for part in range(counts[weight]):
                    start = chunk_columns(weight, part)
                    pltpu.make_async_copy(
                        self.own[4 * layer + weight].at[:, pl.ds(start, WIDTH)],
                        self.held.at[(chunk,) + self.at],
                        self.local_sem.at[chunk],
                    ).start()
                    chunk += 1
            pltpu.make_async_copy(
                self.own[4 * layer + 3],
                self.tall.at[(layer,) + self.at],
                self.local_sem.at[CHUNKS + layer],
            ).start()
        greet(self.targets)

    def message(self, block, target, sems, place):
        return pltpu.make_async_remote_copy(
            src_ref=block,
            dst_ref=block,
            send_sem=sems[0].at[place],
            recv_sem=sems[1].at[place],
            device_id=self.targets[target],
            device_id_type=MESH,
        )

    def wide_messages(self, phase, chunk):
        x, zh, zl, y, c = self.at
        ref = self.held
        sems = (self.send_sem, self.recv_sem)
        slot = chunk % GATHER_SLOTS
        half = WIDTH // 2
        low, high = pl.ds(0, half), pl.ds(half, half)

        def one(index, target, part):
            return self.message(ref.at[(chunk,) + index], target, sems, (2 * phase + part, slot))

        a = slice(None)
        if phase == 0:
            return [one((x, zh, zl, y, c), "z2", 0)]
        if phase == 1:
            return [one((x, a, zl, y, c), "z1", 0)]
        if phase == 2:
            return [one((x, a, a, y, c, a, low), "x", 0), one((x, a, a, y, c, a, high), "y", 1)]
        if phase == 3:
            return [one((a, a, a, y, c, a, low), "y", 0), one((x, a, a, a, c, a, high), "x", 1)]
        return [one((a, a, a, a, c), "c", 0)]

    def tall_message(self, phase, layer, part, odd):
        x, zh, zl, y, c = self.at
        a = slice(None)
        lanes = pl.ds(pl.multiple_of(part * SHRINK_WIDTH, SHRINK_WIDTH), SHRINK_WIDTH)
        index, target = {
            (0, 0): ((x, zh, zl, y, c), "x"),
            (0, 1): ((x, zh, zl, y, c), "y"),
            (1, 0): ((a, zh, zl, y, c), "y"),
            (1, 1): ((x, zh, zl, a, c), "x"),
            (2, 0): ((a, zh, zl, a, c), "z2"),
            (3, 0): ((a, a, zl, a, c), "z1"),
            (4, 0): ((a, a, a, a, c), "c"),
        }[(phase, odd)]
        return self.message(
            self.tall.at[(layer,) + index + (a, lanes)],
            target,
            (self.tall_send, self.tall_recv),
            (phase, layer * SHRINK_PARTS + part),
        )

    def tall_turn(self, chunk):
        layer = chunk // LAYER_CHUNKS
        place = chunk % LAYER_CHUNKS
        return layer, place // 5, place % 5 == 4

    def for_tall(self, phase, chunk, act):
        layer, part, due = self.tall_turn(chunk)
        if phase >= 2:
            pl.when(due)(lambda: act(self.tall_message(phase, layer, part, 0)))
        else:
            for odd in range(2):
                pl.when(due & (part % 2 == odd))(
                    lambda odd=odd: act(self.tall_message(phase, layer, part, odd))
                )

    def step(self, step):
        for phase in range(PHASES, -1, -1):
            chunk = step - GATHER_STEPS[phase]

            @pl.when((chunk >= 0) & (chunk < CHUNKS))
            def _(phase=phase, chunk=chunk):
                if phase >= 1:
                    for copy in self.wide_messages(phase - 1, chunk):
                        copy.wait()
                    self.for_tall(phase - 1, chunk, lambda copy: copy.wait())
                else:
                    pltpu.make_async_copy(
                        self.own[0].at[:, pl.ds(0, WIDTH)],
                        self.held.at[(chunk,) + self.at],
                        self.local_sem.at[chunk],
                    ).wait()
                    layer = chunk // LAYER_CHUNKS

                    @pl.when(chunk % LAYER_CHUNKS == 4)
                    def _():
                        pltpu.make_async_copy(
                            self.own[3],
                            self.tall.at[(layer,) + self.at],
                            self.local_sem.at[CHUNKS + layer],
                        ).wait()

                if phase < PHASES:
                    for copy in self.wide_messages(phase, chunk):
                        copy.start()
                    self.for_tall(phase, chunk, lambda copy: copy.start())


def forward_kernel(*refs):
    own = refs[:WEIGHTS]
    tokens, validity = refs[WEIGHTS : WEIGHTS + 2]
    held, tall, mixed_out, between, middles, turns, stages, halves_out = refs[10:18]
    hidden_out, attends_out = refs[18:20]
    scratch = refs[20:]
    sems, (load_sem, tall_sem, stage_sem, half_sem, hidden_sem, misc_sem) = scratch[:5], scratch[5:11]
    loaded, shrink, x, middle, normed, gated, hidden, parts, stage, half_stage, final = scratch[11:22]
    turned, hidden_stage, attends = scratch[22:]
    gather = Gather(own, held, tall, sems)
    gather.begin()

    def rows_of(t):
        return pl.ds(pl.multiple_of(t * 128, 128), 128)

    def start_rows(t, carry):
        rows = rows_of(t)
        x[rows, :] = tokens[rows, :].astype(WIDE) * validity[rows, :]
        return carry

    def keep_turned(layer, kind):
        return pltpu.make_async_copy(turned, turns.at[layer, kind], misc_sem.at[0])

    def turn(source, layer, kind):
        def act(t, carry):
            rows = rows_of(t)
            turned[:, rows] = source[rows, :].T
            return carry

        lax.fori_loop(0, ROWS // 128, act, 0)
        keep_turned(layer, kind).start()

    def start_layers():
        lax.fori_loop(0, ROWS // 128, start_rows, 0)
        norm_into(x, normed)
        turn(normed, 0, 0)

    def load(chunk):
        return pltpu.make_async_copy(
            held.at[chunk], loaded.at[chunk % LOAD_SLOTS], load_sem.at[chunk % LOAD_SLOTS]
        )

    def load_tall(layer):
        return pltpu.make_async_copy(tall.at[layer], shrink, tall_sem)

    def keep_stage(layer, group):
        return pltpu.make_async_copy(stage, stages.at[layer, group], stage_sem)

    def keep_half(layer, part):
        return pltpu.make_async_copy(
            half_stage.at[part % 2], halves_out.at[layer, part], half_sem.at[part % 2]
        )

    def keep_hidden(layer, part):
        rows = pl.ds(pl.multiple_of(part * WIDTH, WIDTH), WIDTH)
        return pltpu.make_async_copy(
            hidden_stage.at[part % 2], hidden_out.at[layer, rows, :], hidden_sem.at[part % 2]
        )

    def keep_attends(group):
        return pltpu.make_async_copy(attends, attends_out.at[group], misc_sem.at[4])

    def keep_middle(layer):
        return pltpu.make_async_copy(middle, middles.at[layer], misc_sem.at[1])

    def keep_between():
        return pltpu.make_async_copy(x, between, misc_sem.at[2])

    def weight(slot, f):
        return loaded[slot, f].reshape(1024, WIDTH)

    def project_step(layer, place, slot):
        group = place // 2
        for f in range(2):
            parts[place % 2, f] = dot(normed[...], weight(slot, f))

        @pl.when(place % 2 == 1)
        def _():
            @pl.when((layer > 0) | (group > 0))
            def _():
                keep_stage(layer, group).wait()

            @pl.when((layer == 0) & (group > 0))
            def _():
                keep_attends(0).wait()

            for kind in range(4):
                stage[kind] = parts[kind % 2, kind // 2].astype(LOW)

            @pl.when(layer == 0)
            def _():
                local_mixer(group, parts, validity, gated, stage, attends)
                keep_attends(group).start()

            pl.when(layer > 0)(lambda: linear_mixer(group, parts, gated, stage))
            keep_stage(layer, group).start()

    def output_step(layer, part, slot):
        @pl.when(part == 0)
        def _():
            keep_turned(0, 0).wait()
            turn(gated, layer, 1)

            @pl.when(layer > 0)
            def _():
                keep_middle(0).wait()

        for f in range(2):
            lanes = pl.ds(pl.multiple_of(f * 512 + part * WIDTH, WIDTH), WIDTH)
            middle[:, lanes] = x[:, lanes] + dot(gated[...], weight(slot, f))

        @pl.when(part == OUTPUT_CHUNKS - 1)
        def _():
            keep_middle(layer).start()
            norm_into(middle, normed)
            keep_turned(0, 0).wait()
            turn(normed, layer, 2)

    def expand_step(layer, part, slot):
        @pl.when((layer > 0) | (part > 1))
        def _():
            keep_half(layer, part).wait()
            keep_hidden(layer, part).wait()

        first = dot(normed[...], weight(slot, 0))
        second = dot(normed[...], weight(slot, 1))
        half_stage[part % 2, 0] = first.astype(LOW)
        half_stage[part % 2, 1] = second.astype(LOW)
        both = (first * second).astype(LOW)
        hidden[:, pl.ds(pl.multiple_of(part * WIDTH, WIDTH), WIDTH)] = both
        hidden_stage[part % 2] = both.T
        keep_half(layer, part).start()
        keep_hidden(layer, part).start()

    def shrink_step(layer):
        load_tall(layer).wait()

        @pl.when(layer > 0)
        def _():
            keep_between().wait()

        def body(turn, carry):
            f = turn // 2
            columns = pl.ds(pl.multiple_of((turn % 2) * WIDTH, WIDTH), WIDTH)
            lanes = pl.ds(pl.multiple_of(turn * WIDTH, WIDTH), WIDTH)
            matrix = shrink[f, :, :, :, :, :, columns].reshape(hidden.shape[1], WIDTH)
            x[:, lanes] = middle[:, lanes] + dot(hidden[...], matrix)
            return carry

        lax.fori_loop(0, 4, body, 0)

        @pl.when(layer == 0)
        def _():
            keep_between().start()
            norm_into(x, normed)
            keep_turned(0, 0).wait()
            turn(normed, 1, 0)

        @pl.when(layer > 0)
        def _():
            def last_rows(t, carry):
                rows = rows_of(t)
                final[rows, :] = (x[rows, :] * validity[rows, :]).astype(LOW)
                return carry

            lax.fori_loop(0, ROWS // 128, last_rows, 0)

    def body(step, carry):
        gather.step(step)
        pl.when(step == 2)(start_layers)
        arrived = step - GATHER_STEPS[PHASES]

        @pl.when((arrived >= 0) & (arrived < CHUNKS))
        def _():
            load(arrived).start()

            @pl.when(arrived % LAYER_CHUNKS == LAYER_CHUNKS - 2)
            def _():
                load_tall(arrived // LAYER_CHUNKS).start()

        ready = arrived - 1

        @pl.when((ready >= 0) & (ready < CHUNKS))
        def _():
            load(ready).wait()
            layer = ready // LAYER_CHUNKS
            place = ready % LAYER_CHUNKS
            slot = ready % LOAD_SLOTS
            pl.when(place < PROJECT_CHUNKS)(lambda: project_step(layer, place, slot))
            pl.when((place >= PROJECT_CHUNKS) & (place < PROJECT_CHUNKS + OUTPUT_CHUNKS))(
                lambda: output_step(layer, place - PROJECT_CHUNKS, slot)
            )
            pl.when(place >= PROJECT_CHUNKS + OUTPUT_CHUNKS)(
                lambda: expand_step(layer, place - PROJECT_CHUNKS - OUTPUT_CHUNKS, slot)
            )
            pl.when(place == LAYER_CHUNKS - 1)(lambda: shrink_step(layer))

        return carry

    lax.fori_loop(0, CHUNKS + GATHER_STEPS[PHASES] + 1, body, 0)
    last = pltpu.make_async_copy(final, mixed_out, misc_sem.at[3])
    last.start()
    keep_stage(1, HEAD_GROUPS - 1).wait()
    keep_attends(0).wait()
    keep_turned(0, 0).wait()
    keep_middle(1).wait()
    keep_half(1, EXPAND_CHUNKS - 2).wait()
    keep_half(1, EXPAND_CHUNKS - 1).wait()
    keep_hidden(1, EXPAND_CHUNKS - 2).wait()
    keep_hidden(1, EXPAND_CHUNKS - 1).wait()
    last.wait()


def run_forward(shards_of, tokens, validity):
    bits = (2, 2, 2, 2, 2)
    struct = jax.ShapeDtypeStruct
    return pl.pallas_call(
        forward_kernel,
        out_shape=(
            struct((CHUNKS,) + bits + (64, WIDTH), LOW),
            struct((2,) + bits + (176, 512), LOW),
            struct((ROWS, 1024), LOW),
            struct((ROWS, 1024), WIDE),
            struct((2, ROWS, 1024), WIDE),
            struct((2, 3, 1024, ROWS), LOW),
            struct((2, HEAD_GROUPS, 5, ROWS, WIDTH), LOW),
            struct((2, EXPAND_CHUNKS, 2, ROWS, WIDTH), LOW),
            struct((2, 2816, ROWS), LOW),
            struct((HEAD_GROUPS, 8, 2, 128, 128), LOW),
        ),
        in_specs=[FULL] * (WEIGHTS + 2),
        out_specs=(ANY,) * 10,
        scratch_shapes=[
            pltpu.SemaphoreType.DMA((CHUNKS + 2,)),
            pltpu.SemaphoreType.DMA((10, GATHER_SLOTS)),
            pltpu.SemaphoreType.DMA((10, GATHER_SLOTS)),
            pltpu.SemaphoreType.DMA((PHASES, 2 * SHRINK_PARTS)),
            pltpu.SemaphoreType.DMA((PHASES, 2 * SHRINK_PARTS)),
            pltpu.SemaphoreType.DMA((LOAD_SLOTS,)),
            pltpu.SemaphoreType.DMA,
            pltpu.SemaphoreType.DMA,
            pltpu.SemaphoreType.DMA((2,)),
            pltpu.SemaphoreType.DMA((2,)),
            pltpu.SemaphoreType.DMA((5,)),
            pltpu.VMEM((LOAD_SLOTS,) + bits + (64, WIDTH), LOW),
            pltpu.VMEM(bits + (176, 512), LOW),
            pltpu.VMEM((ROWS, 1024), WIDE),
            pltpu.VMEM((ROWS, 1024), WIDE),
            pltpu.VMEM((ROWS, 1024), LOW),
            pltpu.VMEM((ROWS, 1024), LOW),
            pltpu.VMEM((ROWS, 2816), LOW),
            pltpu.VMEM((2, 2, ROWS, WIDTH), WIDE),
            pltpu.VMEM((5, ROWS, WIDTH), LOW),
            pltpu.VMEM((2, 2, ROWS, WIDTH), LOW),
            pltpu.VMEM((ROWS, 1024), LOW),
            pltpu.VMEM((1024, ROWS), LOW),
            pltpu.VMEM((2, WIDTH, ROWS), LOW),
            pltpu.VMEM((8, 2, 128, 128), LOW),
        ],
        compiler_params=pltpu.CompilerParams(
            collective_id=0, has_side_effects=True, vmem_limit_bytes=60 << 20
        ),
    )(*shards_of, tokens, validity)


SCATTER_STEPS = (0, 2, 5, 8, 11, 14)
SCATTER_SLOTS = 10
TERM_SLOTS = SCATTER_STEPS[1]
TALL_SLOTS = 3
OUTPUT_TURN = EXPAND_CHUNKS
PROJECT_TURN = EXPAND_CHUNKS + OUTPUT_CHUNKS
TALL_ROWS = 176


class Scatter:
    def __init__(self, outs, sems, wide, tall):
        self.outs, self.tall_outs = outs
        self.send_sem, self.recv_sem, self.tall_send, self.tall_recv = sems[:4]
        self.store_sem, self.tall_store = sems[4:]
        self.wide, self.tall = wide[:6], tall[:6]
        self.result, self.tall_result = wide[6], tall[6]
        self.places, self.targets = neighbours()

    def tall_turn(self, chunk):
        layer = chunk // LAYER_CHUNKS
        turn = chunk % LAYER_CHUNKS
        return layer * SHRINK_PARTS + turn // 5, turn // 5, turn % 5 == 4

    def wide_parts(self):
        half = WIDTH // 2
        return (
            (pl.ds(0, half), ("c", "y", "x", "z1", "z2")),
            (pl.ds(half, half), ("c", "x", "y", "z1", "z2")),
        )

    def tall_parts(self, odd):
        plane = ("x", "y") if odd else ("y", "x")
        return ((pl.ds(0, SHRINK_WIDTH), ("c", "z1", "z2") + plane),)

    def left(self, order, phase):
        used = set(AXIS_OF[target] for target in order[: phase + 1])
        return [name for name in AXIS_NAMES if name not in used]

    def source(self, buffers, slots, phase, order):
        if phase == 0:
            return buffers[0].at[slots[0]], list(AXIS_NAMES)
        return buffers[phase].at[slots[1]], self.left(order, phase - 1)

    def messages(self, buffers, slots, sems, phase, parts):
        if phase == 0 and len(parts) == 2:
            parts = ((pl.ds(0, WIDTH), parts[0][1]),)
        out = []
        for part, (lanes, order) in enumerate(parts):
            source, dims = self.source(buffers, slots, phase, order)
            target = order[phase]
            away = tuple(
                1 - self.places[d] if d == AXIS_OF[target] else slice(None) for d in dims
            )
            whole = tuple(slice(None) for _ in self.left(order, phase))
            place = (2 * phase + part, slots[1])
            out.append(
                pltpu.make_async_remote_copy(
                    src_ref=source.at[away + (slice(None), lanes)],
                    dst_ref=buffers[1 + phase].at[(slots[1],) + whole + (slice(None), lanes)],
                    send_sem=sems[0].at[place],
                    recv_sem=sems[1].at[place],
                    device_id=self.targets[target],
                    device_id_type=MESH,
                )
            )
        return out

    def add(self, buffers, slots, phase, parts, result):
        if phase == 0 and len(parts) == 2:
            parts = ((pl.ds(0, WIDTH), parts[0][1]),)
        for lanes, order in parts:
            source, dims = self.source(buffers, slots, phase, order)
            cut = AXIS_OF[order[phase]]
            near = tuple(self.places[d] if d == cut else slice(None) for d in dims)
            whole = tuple(slice(None) for _ in self.left(order, phase))
            ref = buffers[1 + phase].at[slots[1]]
            mine = source[near + (slice(None), lanes)]
            came = ref[whole + (slice(None), lanes)]
            if phase < 4:
                ref[whole + (slice(None), lanes)] = came + mine
            else:
                result[:, lanes] = came.astype(WIDE) + mine.astype(WIDE)

    def wide_slots(self, chunk):
        return (chunk % TERM_SLOTS, chunk % SCATTER_SLOTS)

    def tall_slots(self, place):
        return (0, place % TALL_SLOTS)

    def wide_messages(self, phase, chunk):
        return self.messages(
            self.wide,
            self.wide_slots(chunk),
            (self.send_sem, self.recv_sem),
            phase,
            self.wide_parts(),
        )

    def tall_messages(self, phase, place, odd):
        return self.messages(
            self.tall,
            self.tall_slots(place),
            (self.tall_send, self.tall_recv),
            phase,
            self.tall_parts(odd),
        )

    def store(self, chunk):
        return pltpu.make_async_copy(
            self.result.at[chunk % 2], self.outs.at[chunk], self.store_sem.at[chunk % 2]
        )

    def store_tall(self, place):
        return pltpu.make_async_copy(
            self.tall_result.at[place % 2], self.tall_outs.at[place], self.tall_store.at[place % 2]
        )

    def start(self, phase, chunk):
        for copy in self.wide_messages(phase, chunk):
            copy.start()
        place, part, due = self.tall_turn(chunk)
        for odd in range(2):

            @pl.when(due & (part % 2 == odd))
            def _(odd=odd):
                for copy in self.tall_messages(phase, place, odd):
                    copy.start()

    def take(self, phase, chunk):
        for copy in self.wide_messages(phase, chunk):
            copy.wait()
        if phase == PHASES - 1:
            pl.when(chunk >= 2)(lambda: self.store(chunk).wait())
        self.add(
            self.wide, self.wide_slots(chunk), phase, self.wide_parts(), self.result.at[chunk % 2]
        )
        place, part, due = self.tall_turn(chunk)
        for odd in range(2):

            @pl.when(due & (part % 2 == odd))
            def _(odd=odd):
                for copy in self.tall_messages(phase, place, odd):
                    copy.wait()
                if phase == PHASES - 1:
                    pl.when(place >= 2)(lambda: self.store_tall(place).wait())
                self.add(
                    self.tall,
                    self.tall_slots(place),
                    phase,
                    self.tall_parts(odd),
                    self.tall_result.at[place % 2],
                )
                if phase == PHASES - 1:
                    self.store_tall(place).start()

        if phase == PHASES - 1:
            self.store(chunk).start()

    def older(self, step):
        for phase in range(PHASES, 0, -1):
            chunk = step - SCATTER_STEPS[phase]

            @pl.when((chunk >= 0) & (chunk < CHUNKS))
            def _(phase=phase, chunk=chunk):
                self.take(phase - 1, chunk)
                if phase < PHASES:
                    self.start(phase, chunk)

    def finish(self):
        for chunk in (CHUNKS - 2, CHUNKS - 1):
            self.store(chunk).wait()
        for place in (2 * SHRINK_PARTS - 2, 2 * SHRINK_PARTS - 1):
            self.store_tall(place).wait()


def norm_slope(values, inverse, upstream, mean):
    return inverse * (upstream - values * (inverse * inverse) * mean)


def gate_back(update, mixture, coming, first):
    inverse = lax.rsqrt(pair_mean(mixture * mixture, first) + epsilon)
    curve = logistic(update)
    back_update = coming * (mixture * inverse) * (curve * (1.0 + update * (1.0 - curve)))
    gate = coming * (update * curve)
    back_mixture = norm_slope(mixture, inverse, gate, pair_mean(gate * mixture, first))
    return back_update, back_mixture


def both_heads(values, first):
    zero = jnp.zeros_like(values)
    return jnp.concatenate([jnp.where(first, values, zero), jnp.where(first, zero, values)], axis=0)


def side_by_side(values):
    half = values.shape[0] // 2
    return jnp.concatenate([values[:half], values[half:]], axis=1)


def local_mixer_back(group, stage, attends, validity, coming, back):
    def body(turn, carry):
        rows = pl.ds(pl.multiple_of((turn // 2) * 128, 128), 128)
        lanes = pl.ds(pl.multiple_of((turn % 2) * 128, 128), 128)
        columns = pl.ds(pl.multiple_of(group * WIDTH + (turn % 2) * 128, 128), 128)
        first = first_lanes(128)

        def put(i, j, value):
            start = j * WIDTH + (turn % 2) * 128
            back[i, rows, pl.ds(pl.multiple_of(start, 128), 128)] = value.astype(LOW)

        q, k, v = stage[0, rows, lanes], stage[1, rows, lanes], stage[2, rows, lanes]
        update = stage[3, rows, lanes].astype(WIDE)
        mixture = stage[4, rows, lanes].astype(WIDE)
        back_update, back_mixture = gate_back(update, mixture, coming[rows, columns], first)
        put(1, 1, back_update)
        grad = (back_mixture.astype(LOW).astype(WIDE) * validity[rows, :]).astype(LOW)
        grads = both_heads(grad, first)
        attend_low = attends[turn].reshape(256, 128)
        attend = attend_low.astype(WIDE)
        back_attend = contract_cols(grads, v)
        total = jnp.sum(back_attend * attend, axis=-1, keepdims=True)
        back_scores = (attend * (back_attend - total)).astype(LOW)
        put(0, 0, dot(side_by_side(back_scores), both_heads(k, first)) * HEAD ** (-0.5))
        put(1, 0, contract_rows(back_scores, both_heads(q, first)) * HEAD ** (-0.5))
        put(0, 1, contract_rows(attend_low, grads))
        return carry

    lax.fori_loop(0, 2 * ROWS // 128, body, 0, unroll=4)


def linear_mixer_back(group, stage, coming, back):
    half = ROWS // 2

    def body(pair, carry):
        lanes = pl.ds(pl.multiple_of(pair * 128, 128), 128)
        columns = pl.ds(pl.multiple_of(group * WIDTH + pair * 128, 128), 128)
        first = first_lanes(ROWS)
        queries = stage[0, :, lanes].astype(WIDE)
        keys_all = stage[1, :, lanes].astype(WIDE)
        v = stage[2, :, lanes]
        fq = softplus(queries).astype(LOW)
        fk = softplus(keys_all).astype(LOW)
        update = stage[3, :, lanes].astype(WIDE)
        mixture = stage[4, :, lanes].astype(WIDE)
        back_update, back_mixture = gate_back(update, mixture, coming[:, columns], first)

        def put(i, j, rows, value):
            start = j * WIDTH + pair * 128
            back[i, rows, pl.ds(pl.multiple_of(start, 128), 128)] = value.astype(LOW)

        put(1, 1, slice(None), back_update)
        grad = back_mixture.astype(LOW)
        tiles = []
        for t in range(2):
            reach = (t + 1) * half
            i = lax.broadcasted_iota(jnp.int32, (2 * half, reach), 0) % half + t * half
            j = lax.broadcasted_iota(jnp.int32, (2 * half, reach), 1)
            pair_q = both_heads(fq[t * half : reach], first[:half])
            pair_g = both_heads(grad[t * half : reach], first[:half])
            scores = jnp.where(j <= i, contract_cols(pair_q, fk[:reach]), 0.0).astype(LOW)
            inner = jnp.where(j <= i, contract_cols(pair_g, v[:reach]), 0.0).astype(LOW)
            tiles.append(
                (
                    dot(side_by_side(inner), both_heads(fk[:reach], first[:reach])),
                    contract_rows(inner, pair_q),
                    contract_rows(scores, pair_g),
                )
            )
        for t in range(2):
            rows = pl.ds(t * half, half)
            span = slice(t * half, (t + 1) * half)
            back_q = tiles[t][0]
            back_k = tiles[1][1][span]
            back_v = tiles[1][2][span]
            if t == 0:
                back_k = back_k + tiles[0][1]
                back_v = back_v + tiles[0][2]
            put(0, 0, rows, back_q * logistic(queries[span]))
            put(1, 0, rows, back_k * logistic(keys_all[span]))
            put(0, 1, rows, back_v)
        return carry

    lax.fori_loop(0, 2, body, 0)


def over_rows(act):
    def body(t, carry):
        act(pl.ds(pl.multiple_of(t * 128, 128), 128))
        return carry

    lax.fori_loop(0, ROWS // 128, body, 0)


def backward_kernel(*refs):
    cotangent, tokens, validity = refs[:3]
    held, tall, between, middles, turns, stages, halves_in, hidden_in, attends_in = refs[3:12]
    tokens_out, outs, tall_outs = refs[12:15]
    scratch = refs[15:]
    scatter_sems, loads = scratch[:6], scratch[6:12]
    load_sem, half_sem, shrink_sem, stage_sem, turn_sem, misc_sem = loads
    wide_buffers, tall_buffers = scratch[12:19], scratch[19:26]
    (
        loaded,
        half_in,
        stage,
        attends,
        shrink,
        hidden_turned,
        branch,
        gated_branch,
        up,
        sums,
        middle,
        layer_in,
        turned,
        back,
    ) = scratch[26:]
    scatter = Scatter((outs, tall_outs), scatter_sems, wide_buffers, tall_buffers)

    class Load:
        def __init__(self, chunk, number):
            self.copies = [
                pltpu.make_async_copy(
                    held.at[chunk, f],
                    loaded.at[number % 2, :, pl.ds(f * WIDTH, WIDTH)],
                    load_sem.at[number % 2, f],
                )
                for f in range(2)
            ]

        def start(self):
            for copy in self.copies:
                copy.start()

        def wait(self):
            for copy in self.copies:
                copy.wait()

    def load_turned(layer, kind, order):
        return pltpu.make_async_copy(
            turns.at[layer, kind], turned.at[order % 2], turn_sem.at[order % 2]
        )

    def load_attends(group):
        return pltpu.make_async_copy(attends_in.at[group], attends, misc_sem.at[4])

    def load_half(layer, part, number):
        return pltpu.make_async_copy(
            halves_in.at[layer, part], half_in.at[number % 2], half_sem.at[number % 2]
        )

    def load_shrink(layer, part, number):
        rows = pl.ds(pl.multiple_of(part * WIDTH, WIDTH), WIDTH)
        return pltpu.make_async_copy(
            tall.at[layer, :, rows, :], shrink.at[number % 2], shrink_sem.at[number % 2]
        )

    def load_stage(layer, group):
        return pltpu.make_async_copy(stages.at[layer, group], stage, stage_sem)

    def fetch(kind, layer):
        source, target = (
            (None, None),
            (middles, middle),
            (hidden_in, hidden_turned),
        )[kind]
        return pltpu.make_async_copy(source.at[layer], target, misc_sem.at[kind])

    def fetch_between():
        return pltpu.make_async_copy(between, layer_in, misc_sem.at[3])

    def prefetch(number):
        pl.when(number >= CHUNKS)(lambda: Load(number - CHUNKS, number).start())
        pl.when(number < CHUNKS)(lambda: prefetch_turn(number))

    def prefetch_turn(number):
        layer = 1 - number // LAYER_CHUNKS
        turn = number % LAYER_CHUNKS
        base = LAYER_CHUNKS * layer

        @pl.when(turn < OUTPUT_TURN)
        def _():
            Load(base + PROJECT_CHUNKS + OUTPUT_CHUNKS + turn, number).start()
            load_half(layer, turn, number).start()
            load_shrink(layer, turn, number).start()

        @pl.when((turn >= OUTPUT_TURN) & (turn < PROJECT_TURN))
        def _():
            Load(base + PROJECT_CHUNKS + turn - OUTPUT_TURN, number).start()

        @pl.when(turn >= PROJECT_TURN)
        def _():
            pl.when(layer == 1)(lambda: Load(base + turn - PROJECT_TURN, number).start())

            @pl.when((turn - PROJECT_TURN) % 2 == 0)
            def _():
                load_stage(layer, (turn - PROJECT_TURN) // 2).start()
                pl.when(layer == 0)(lambda: load_attends((turn - PROJECT_TURN) // 2).start())

    prefetch_turn(jnp.int32(0))
    load_turned(1, 2, 0).start()
    load_turned(1, 1, 1).start()
    fetch(2, 1).start()
    fetch(1, 1).start()
    fetch_between().start()

    def begin_rows(rows):
        up[rows, :] = cotangent[rows, :].astype(WIDE) * validity[rows, :]

    over_rows(begin_rows)
    greet(scatter.targets)

    def expand_start(layer):
        def act(rows):
            branch[rows, :] = up[rows, :].astype(LOW)
            sums[0, rows, :] = jnp.zeros((128, 1024), WIDE)

        over_rows(act)
        load_turned(0, 0, 1 - layer).wait()
        pl.when(layer == 0)(lambda: load_turned(0, 1, 4).start())

    def expand_turn(part, number):
        load_half(0, 0, number).wait()
        load_shrink(0, 0, number).wait()
        low, high = pl.ds(0, WIDTH), pl.ds(WIDTH, WIDTH)
        back_hidden = contract_cols(branch[:, :512], shrink[number % 2, 0])
        back_hidden = back_hidden + contract_cols(branch[:, 512:], shrink[number % 2, 1])
        first = half_in[number % 2, 0].astype(WIDE)
        second = half_in[number % 2, 1].astype(WIDE)
        back[0, 0, :, low] = (back_hidden * second).astype(LOW)
        back[0, 0, :, high] = (back_hidden * first).astype(LOW)

    def output_start(layer):
        load_turned(0, 0, 2 - layer).wait()
        load_turned(layer, 0, 3 - layer).start()
        fetch(1, 1).wait()

        def act(rows):
            values = middle[rows, :]
            back_second = sums[0, rows, :]
            new = up[rows, :] + norm_back(values, back_second)
            up[rows, :] = new
            gated_branch[rows, :] = new.astype(LOW)
            sums[1, rows, :] = jnp.zeros((128, 1024), WIDE)

        over_rows(act)

    def output_turn(part):
        for f in range(2):
            lanes = pl.ds(pl.multiple_of(f * 512 + part * WIDTH, WIDTH), WIDTH)
            back[0, 0, :, pl.ds(f * WIDTH, WIDTH)] = gated_branch[:, lanes]

    def project_start(layer):
        @pl.when(layer == 1)
        def _():
            fetch_between().wait()
            fetch(1, 0).start()
            load_turned(0, 2, 3).start()

        @pl.when(layer == 0)
        def _():
            def act(rows):
                layer_in[rows, :] = tokens[rows, :].astype(WIDE) * validity[rows, :]

            over_rows(act)

        def clear(rows):
            sums[0, rows, :] = jnp.zeros((128, 1024), WIDE)

        over_rows(clear)
        load_turned(0, 0, 1 - layer).wait()

    def project_turn(layer, group):
        load_stage(0, 0).wait()
        coming = sums.at[1]
        mine = back.at[group]
        pl.when(layer == 1)(lambda: linear_mixer_back(group, stage, coming, mine))

        @pl.when(layer == 0)
        def _():
            load_attends(0).wait()
            local_mixer_back(group, stage, attends, validity, coming, mine)

    def finish_layer(layer):
        def act(rows):
            up[rows, :] = up[rows, :] + norm_back(layer_in[rows, :], sums[0, rows, :])

        over_rows(act)

    def terms(number, group, which, order):
        slot = number % TERM_SLOTS
        out = wide_buffers[0]

        def body(tile, carry):
            rows = pl.ds(pl.multiple_of(tile * 512, 512), 512)
            value = dot(turned[order % 2, rows, :], back[group, which]).astype(LOW)
            for f in range(2):
                part = value[:, f * WIDTH : (f + 1) * WIDTH]
                out[slot, f, tile] = part.reshape(2, 2, 2, 64, WIDTH)
            return carry

        lax.fori_loop(0, 2, body, 0)

    def tall_terms(part, number):
        out = tall_buffers[0]
        pl.when(part == 0)(lambda: fetch(2, 0).wait())
        lanes = [pl.ds(pl.multiple_of(f * 512 + part * 128, 128), 128) for f in range(2)]
        both = jnp.concatenate([branch[:, lanes[0]], branch[:, lanes[1]]], axis=1)

        def body(tile, carry):
            rows = pl.ds(pl.multiple_of(tile * 8 * TALL_ROWS, 8 * TALL_ROWS), 8 * TALL_ROWS)
            value = dot(hidden_turned[rows, :], both).astype(LOW)
            for f in range(2):
                out[0, f, tile] = value[:, f * 128 : f * 128 + 128].reshape(
                    2, 2, 2, TALL_ROWS, SHRINK_WIDTH
                )
            return carry

        lax.fori_loop(0, 2, body, 0)

        @pl.when((part == SHRINK_PARTS - 1) & (number < LAYER_CHUNKS))
        def _():
            fetch(2, 0).start()

    def spread(number, group, which, kind):
        def body(t, carry):
            rows = pl.ds(pl.multiple_of(t * 512, 512), 512)
            value = contract_cols(back[group, which], loaded[number % 2, rows, :])
            sums[kind, :, rows] = sums[kind, :, rows] + value
            return carry

        lax.fori_loop(0, 2, body, 0)

    def body(step, carry):
        pl.when(step + 1 < CHUNKS + PROJECT_CHUNKS)(lambda: prefetch(step + 1))
        scatter.older(step)

        @pl.when(step < CHUNKS)
        def _():
            layer = 1 - step // LAYER_CHUNKS
            turn = step % LAYER_CHUNKS
            pl.when(turn == 0)(lambda: expand_start(layer))
            pl.when(turn == OUTPUT_TURN)(lambda: output_start(layer))
            pl.when(turn == PROJECT_TURN)(lambda: project_start(layer))
            pl.when(turn < OUTPUT_TURN)(lambda: expand_turn(turn, step))
            pl.when((turn >= OUTPUT_TURN) & (turn < PROJECT_TURN))(
                lambda: output_turn(turn - OUTPUT_TURN)
            )
            pl.when((turn >= PROJECT_TURN) & ((turn - PROJECT_TURN) % 2 == 0))(
                lambda: project_turn(layer, (turn - PROJECT_TURN) // 2)
            )
            in_project = jnp.minimum(jnp.maximum(turn - PROJECT_TURN + 1, 0), 1)
            in_output = jnp.minimum(jnp.maximum(turn - OUTPUT_TURN + 1, 0), 1) - in_project
            which = in_project * ((turn + PROJECT_TURN) % 2)
            group = in_project * ((turn - PROJECT_TURN) // 2)
            terms(step, group, which, 1 - layer + in_output)
            place, part, due = scatter.tall_turn(step)
            pl.when(due)(lambda: tall_terms(part, step))
            scatter.start(0, step)

            @pl.when((layer == 1) | (turn < PROJECT_TURN))
            def _():
                Load(0, step).wait()
                spread(step, group, which, in_output)

            pl.when(step == LAYER_CHUNKS - 1)(lambda: finish_layer(layer))

        @pl.when((step >= CHUNKS) & (step < CHUNKS + PROJECT_CHUNKS))
        def _():
            place = step - CHUNKS
            Load(0, step).wait()
            spread(step, place // 2, place % 2, 0)

            @pl.when(place == PROJECT_CHUNKS - 1)
            def _():
                finish_layer(0)

                def act(rows):
                    up[rows, :] = up[rows, :] * validity[rows, :]

                over_rows(act)
                pltpu.make_async_copy(up, tokens_out, misc_sem.at[3]).start()

        return carry

    lax.fori_loop(0, CHUNKS + SCATTER_STEPS[PHASES], body, 0)
    pltpu.make_async_copy(up, tokens_out, misc_sem.at[3]).wait()
    scatter.finish()


def scatter_buffers(terms, slots, rows, width):
    bits = [(2,) * (4 - phase) for phase in range(5)]
    return (
        [pltpu.VMEM((terms, 2, 2, 2, 2, 2, rows, width), LOW)]
        + [pltpu.VMEM((slots,) + lead + (rows, width), LOW) for lead in bits]
        + [pltpu.VMEM((2, rows, width), WIDE)]
    )


def run_backward(cotangent, tokens, validity, forward):
    struct = jax.ShapeDtypeStruct
    held, tall, mixed_out, between, middles, turns, stages, kept, hidden, attends = forward
    return pl.pallas_call(
        backward_kernel,
        out_shape=(
            struct((ROWS, 1024), WIDE),
            struct((CHUNKS, 64, WIDTH), WIDE),
            struct((2 * SHRINK_PARTS, TALL_ROWS, SHRINK_WIDTH), WIDE),
        ),
        in_specs=[FULL] * 3 + [ANY] * 9,
        out_specs=(ANY,) * 3,
        scratch_shapes=[
            pltpu.SemaphoreType.DMA((10, SCATTER_SLOTS)),
            pltpu.SemaphoreType.DMA((10, SCATTER_SLOTS)),
            pltpu.SemaphoreType.DMA((10, TALL_SLOTS)),
            pltpu.SemaphoreType.DMA((10, TALL_SLOTS)),
            pltpu.SemaphoreType.DMA((2,)),
            pltpu.SemaphoreType.DMA((2,)),
            pltpu.SemaphoreType.DMA((2, 2)),
            pltpu.SemaphoreType.DMA((2,)),
            pltpu.SemaphoreType.DMA((2,)),
            pltpu.SemaphoreType.DMA,
            pltpu.SemaphoreType.DMA((2,)),
            pltpu.SemaphoreType.DMA((5,)),
        ]
        + scatter_buffers(TERM_SLOTS, SCATTER_SLOTS, 64, WIDTH)
        + scatter_buffers(1, TALL_SLOTS, TALL_ROWS, SHRINK_WIDTH)
        + [
            pltpu.VMEM((2, 1024, 2 * WIDTH), LOW),
            pltpu.VMEM((2, 2, ROWS, WIDTH), LOW),
            pltpu.VMEM((5, ROWS, WIDTH), LOW),
            pltpu.VMEM((8, 2, 128, 128), LOW),
            pltpu.VMEM((2, 2, WIDTH, 512), LOW),
            pltpu.VMEM((2816, ROWS), LOW),
            pltpu.VMEM((ROWS, 1024), LOW),
            pltpu.VMEM((ROWS, 1024), LOW),
            pltpu.VMEM((ROWS, 1024), WIDE),
            pltpu.VMEM((2, ROWS, 1024), WIDE),
            pltpu.VMEM((ROWS, 1024), WIDE),
            pltpu.VMEM((ROWS, 1024), WIDE),
            pltpu.VMEM((2, 1024, ROWS), LOW),
            pltpu.VMEM((HEAD_GROUPS, 2, ROWS, 2 * WIDTH), LOW),
        ],
        compiler_params=pltpu.CompilerParams(
            collective_id=1, has_side_effects=True, vmem_limit_bytes=62 << 20
        ),
    )(
        cotangent,
        tokens,
        validity,
        held.reshape(CHUNKS, 2, 1024, WIDTH),
        tall.reshape(2, 2, 2816, 512),
        between,
        middles,
        turns,
        stages,
        kept,
        hidden,
        attends,
    )


def unpack_kernel(*refs):
    outs, held, sem, load_sem = refs[4 : 6 + WEIGHTS], refs[6 + WEIGHTS : -2], refs[-2], refs[-1]
    loads = [
        pltpu.make_async_copy(source, target, load_sem.at[i])
        for i, (source, target) in enumerate(zip(refs[:4], held))
    ]
    for copy in loads:
        copy.start()
    mixed_in, tokens_in, chunks, parts = held
    copies = [(mixed_in, outs[0]), (tokens_in, outs[1])]
    for order in range(2):
        layer = 1 - order
        for turn in range(LAYER_CHUNKS):
            number = order * LAYER_CHUNKS + turn
            if turn < OUTPUT_TURN:
                weight, start = 2, chunk_columns(2, turn)
            elif turn < PROJECT_TURN:
                weight, start = 1, chunk_columns(1, turn - OUTPUT_TURN)
            else:
                weight, start = 0, chunk_columns(0, turn - PROJECT_TURN)
            target = outs[2 + 4 * layer + weight].at[:, pl.ds(start, WIDTH)]
            copies.append((chunks.at[number], target))
        for part in range(SHRINK_PARTS):
            target = outs[5 + 4 * layer].at[:, pl.ds(part * SHRINK_WIDTH, SHRINK_WIDTH)]
            copies.append((parts.at[order * SHRINK_PARTS + part], target))
    copies = [
        pltpu.make_async_copy(source, target, sem.at[i])
        for i, (source, target) in enumerate(copies)
    ]
    groups = ([0], [1], range(2, len(copies)))
    for group, waited in zip(groups, (loads[:1], loads[1:2], loads[2:])):
        for copy in waited:
            copy.wait()
        for i in group:
            copies[i].start()
    for copy in copies:
        copy.wait()


def unpack(mixed_out, tokens_gradient, chunks, parts, shards_of):
    struct = jax.ShapeDtypeStruct
    count = 2 + CHUNKS + 2 * SHRINK_PARTS
    return pl.pallas_call(
        unpack_kernel,
        out_shape=(struct(mixed_out.shape, LOW), struct(tokens_gradient.shape, WIDE))
        + tuple(struct(item.shape, WIDE) for item in shards_of),
        in_specs=[ANY] * 4,
        out_specs=(ANY,) * (2 + WEIGHTS),
        scratch_shapes=[
            pltpu.VMEM(item.shape, item.dtype)
            for item in (mixed_out, tokens_gradient, chunks, parts)
        ]
        + [pltpu.SemaphoreType.DMA((count,)), pltpu.SemaphoreType.DMA((4,))],
        compiler_params=pltpu.CompilerParams(vmem_limit_bytes=60 << 20),
    )(mixed_out, tokens_gradient, chunks, parts)


def gather_weights(shards_of):
    return [
        lax.all_gather(lax.all_gather(item, "fsdp", axis=1, tiled=True), "dp", axis=0, tiled=True)
        for item in shards_of
    ]


def settle_gradients(terms):
    tall = [
        lax.psum_scatter(item.astype(jnp.bfloat16), "dp", scatter_dimension=0, tiled=True)
        for item in terms
    ]
    return [
        lax.psum_scatter(item, "fsdp", scatter_dimension=1, tiled=True).astype(jnp.float32)
        for item in tall
    ]


def local_scores(queries, keys_all):
    query_blocks = split_heads(queries.astype(jnp.bfloat16))
    key_blocks = split_heads(keys_all.astype(jnp.bfloat16))
    scores = jnp.einsum(
        "bihd,bjhd->bhij", query_blocks, key_blocks, preferred_element_type=jnp.float32
    ) * HEAD ** (-0.5)
    return (query_blocks, key_blocks, jnp.where(causal_table(), scores, -1e30))


def local_forward(queries, keys_all, values_low, validity):
    query_blocks, key_blocks, scores = local_scores(queries, keys_all)
    highest_score = jnp.max(scores, axis=-1, keepdims=True)
    expweights = jnp.exp(scores - highest_score)
    row_total = jnp.sum(expweights, axis=-1, keepdims=True)
    attend = (expweights / row_total).astype(jnp.bfloat16)
    mixture = jnp.einsum(
        "bhij,bjhd->bihd", attend, split_heads(values_low), preferred_element_type=jnp.float32
    )
    return (join_heads(mixture) * validity, highest_score + jnp.log(row_total))


def local_backward(queries, keys_all, values_low, validity, logsum, back_mixture):
    query_blocks, key_blocks, scores = local_scores(queries, keys_all)
    value_blocks = split_heads(values_low)
    coming = split_heads(back_mixture * validity.astype(jnp.bfloat16))
    attend = jnp.exp(scores - logsum)
    back_values = jnp.einsum(
        "bhij,bihd->bjhd", attend.astype(jnp.bfloat16), coming, preferred_element_type=jnp.float32
    )
    back_attend = jnp.einsum(
        "bihd,bjhd->bhij", coming, value_blocks, preferred_element_type=jnp.float32
    )
    back_scores = (
        attend * (back_attend - jnp.sum(back_attend * attend, axis=-1, keepdims=True))
    ).astype(jnp.bfloat16)
    back_queries = jnp.einsum(
        "bhij,bjhd->bihd", back_scores, key_blocks, preferred_element_type=jnp.float32
    ) * HEAD ** (-0.5)
    back_keys = jnp.einsum(
        "bhij,bihd->bjhd", back_scores, query_blocks, preferred_element_type=jnp.float32
    ) * HEAD ** (-0.5)
    return (join_heads(back_queries), join_heads(back_keys), join_heads(back_values))


def linear_parts(queries, keys_all, values_low):
    feature_q = split_heads(jax.nn.softplus(queries).astype(jnp.bfloat16))
    feature_k = split_heads(jax.nn.softplus(keys_all).astype(jnp.bfloat16))
    value_blocks = split_heads(values_low)
    causal = causal_table().astype(jnp.float32)
    inner_scores = (
        jnp.einsum("bihd,bjhd->bhij", feature_q, feature_k, preferred_element_type=jnp.float32)
        * causal
    ).astype(jnp.bfloat16)
    states = jnp.einsum(
        "bjhd,bjhe->bhde", feature_k, value_blocks, preferred_element_type=jnp.float32
    )
    running = jnp.cumsum(states, axis=0)
    prior_states = jnp.concatenate([jnp.zeros_like(states[:1]), running[:-1]], axis=0)
    return (feature_q, feature_k, value_blocks, causal, inner_scores, prior_states)


def linear_forward(queries, keys_all, values_low):
    feature_q, feature_k, value_blocks, causal, inner_scores, prior_states = linear_parts(
        queries, keys_all, values_low
    )
    mixture = jnp.einsum(
        "bhij,bjhe->bihe", inner_scores, value_blocks, preferred_element_type=jnp.float32
    )
    mixture = mixture + jnp.einsum(
        "bihd,bhde->bihe", feature_q.astype(jnp.float32), prior_states, precision=highest
    )
    return join_heads(mixture)


def linear_backward(queries, keys_all, values_low, back_mixture):
    feature_q, feature_k, value_blocks, causal, inner_scores, prior_states = linear_parts(
        queries, keys_all, values_low
    )
    coming = split_heads(back_mixture)
    coming_wide = coming.astype(jnp.float32)
    back_inner = (
        jnp.einsum("bihe,bjhe->bhij", coming, value_blocks, preferred_element_type=jnp.float32)
        * causal
    ).astype(jnp.bfloat16)
    back_feature_q = jnp.einsum(
        "bhij,bjhd->bihd", back_inner, feature_k, preferred_element_type=jnp.float32
    )
    back_feature_q = back_feature_q + jnp.einsum(
        "bihe,bhde->bihd", coming_wide, prior_states, precision=highest
    )
    back_feature_k = jnp.einsum(
        "bhij,bihd->bjhd", back_inner, feature_q, preferred_element_type=jnp.float32
    )
    back_values = jnp.einsum(
        "bhij,bihe->bjhe", inner_scores, coming, preferred_element_type=jnp.float32
    )
    back_prior = jnp.einsum(
        "bihd,bihe->bhde", feature_q.astype(jnp.float32), coming_wide, precision=highest
    )
    running = jnp.cumsum(back_prior[::-1], axis=0)[::-1]
    later_states = jnp.concatenate([running[1:], jnp.zeros_like(running[:1])], axis=0)
    back_feature_k = back_feature_k + jnp.einsum(
        "bjhe,bhde->bjhd", value_blocks.astype(jnp.float32), later_states, precision=highest
    )
    back_values = back_values + jnp.einsum(
        "bjhd,bhde->bjhe", feature_k.astype(jnp.float32), later_states, precision=highest
    )
    return (
        join_heads(back_feature_q) * jax.nn.sigmoid(queries),
        join_heads(back_feature_k) * jax.nn.sigmoid(keys_all),
        join_heads(back_values),
    )


def forward_layer(layer_in, validity, weights, local):
    project, output, expand, shrink = weights
    normed = simple_norm(layer_in).astype(jnp.bfloat16)
    projected = jnp.dot(normed, project, preferred_element_type=jnp.float32)
    queries, keys_all, values, update = jnp.split(projected, 4, axis=1)
    values_low = values.astype(jnp.bfloat16)
    if local:
        mixture, logsum = local_forward(queries, keys_all, values_low, validity)
    else:
        mixture = linear_forward(queries, keys_all, values_low)
        logsum = None
    gated_rows = (head_norm(mixture) * jax.nn.silu(update)).astype(jnp.bfloat16)
    middle = layer_in + jnp.dot(gated_rows, output, preferred_element_type=jnp.float32)
    second = simple_norm(middle).astype(jnp.bfloat16)
    expanded = jnp.dot(second, expand, preferred_element_type=jnp.float32)
    half_width = expanded.shape[1] // 2
    hidden = (expanded[:, :half_width] * expanded[:, half_width:]).astype(jnp.bfloat16)
    result = middle + jnp.dot(hidden, shrink, preferred_element_type=jnp.float32)
    return (
        result,
        (layer_in, normed, projected, values_low, mixture, logsum, gated_rows, middle, second),
    )


def backward_layer(upstream, saved, weights, validity, local):
    project, output, expand, shrink = weights
    layer_in, normed, projected, values_low, mixture, logsum, gated_rows, middle, second = saved
    expanded = jnp.dot(second, expand, preferred_element_type=jnp.float32)
    half_width = expanded.shape[1] // 2
    first_half = expanded[:, :half_width]
    second_half = expanded[:, half_width:]
    hidden = (first_half * second_half).astype(jnp.bfloat16)
    back_branch = upstream.astype(jnp.bfloat16)
    shrink_term = contract_rows(hidden, back_branch)
    back_hidden = contract_cols(back_branch, shrink)
    back_expanded = jnp.concatenate(
        [back_hidden * second_half, back_hidden * first_half], axis=1
    ).astype(jnp.bfloat16)
    expand_term = contract_rows(second, back_expanded)
    back_second = contract_cols(back_expanded, expand)
    back_middle = upstream + norm_back(middle, back_second)
    back_gated = back_middle.astype(jnp.bfloat16)
    output_term = contract_rows(gated_rows, back_gated)
    back_rows_gated = contract_cols(back_gated, output)
    queries, keys_all, unused_values, update = jnp.split(projected, 4, axis=1)
    back_update = back_rows_gated * head_norm(mixture) * silu_slope(update)
    back_mixture = head_back(mixture, back_rows_gated * jax.nn.silu(update)).astype(jnp.bfloat16)
    if local:
        back_queries, back_keys, back_values = local_backward(
            queries, keys_all, values_low, validity, logsum, back_mixture
        )
    else:
        back_queries, back_keys, back_values = linear_backward(
            queries, keys_all, values_low, back_mixture
        )
    back_projected = jnp.concatenate(
        [back_queries, back_keys, back_values, back_update], axis=1
    ).astype(jnp.bfloat16)
    project_term = contract_rows(normed, back_projected)
    back_normed = contract_cols(back_projected, project)
    back_input = back_middle + norm_back(layer_in, back_normed)
    return (back_input, (project_term, output_term, expand_term, shrink_term))


def shards(
    direct,
    tokens,
    lengths,
    local_project,
    local_output,
    local_expand,
    local_shrink,
    linear_project,
    linear_output,
    linear_expand,
    linear_shrink,
    cotangent,
):
    positions = lax.broadcasted_iota(jnp.int32, (tokens.shape[1], 1), 0)
    validity = (positions < lengths[0]).astype(jnp.float32)
    shards_of = [
        local_project,
        local_output,
        local_expand,
        local_shrink,
        linear_project,
        linear_output,
        linear_expand,
        linear_shrink,
    ]
    if direct:
        forward = run_forward(shards_of, tokens[0], validity)
        back_tokens, chunks, parts = run_backward(cotangent[0], tokens[0], validity, forward)
        outs = unpack(forward[2], back_tokens, chunks, parts, shards_of)
        return (outs[0][None], outs[1][None]) + tuple(outs[2:])
    layer_in = tokens[0].astype(jnp.float32) * validity
    whole = gather_weights(shards_of)
    local_weights = whole[:4]
    linear_weights = whole[4:]
    between, local_saved = forward_layer(layer_in, validity, local_weights, True)
    result, linear_saved = forward_layer(between, validity, linear_weights, False)
    result = (result * validity).astype(jnp.bfloat16)
    upstream = cotangent[0].astype(jnp.float32) * validity
    back_between, linear_terms = backward_layer(
        upstream, linear_saved, linear_weights, validity, False
    )
    back_input, local_terms = backward_layer(
        back_between, local_saved, local_weights, validity, True
    )
    sums = settle_gradients(local_terms + linear_terms)
    return (
        result[None],
        (back_input * validity)[None],
    ) + tuple(sums)


def solution(mesh):
    in_specs = (
        P(("dp", "fsdp"), None, None),
        P(("dp", "fsdp")),
        P("dp", "fsdp"),
        P("dp", "fsdp"),
        P("dp", "fsdp"),
        P("dp", "fsdp"),
        P("dp", "fsdp"),
        P("dp", "fsdp"),
        P("dp", "fsdp"),
        P("dp", "fsdp"),
        P(("dp", "fsdp"), None, None),
    )
    out_specs = (
        P(("dp", "fsdp"), None, None),
        P(("dp", "fsdp"), None, None),
        P("dp", "fsdp"),
        P("dp", "fsdp"),
        P("dp", "fsdp"),
        P("dp", "fsdp"),
        P("dp", "fsdp"),
        P("dp", "fsdp"),
        P("dp", "fsdp"),
        P("dp", "fsdp"),
    )
    direct = dict(mesh.shape) == {"dp": 16, "fsdp": 2}
    return jax.shard_map(functools.partial(shards, direct), mesh=mesh, in_specs=in_specs, out_specs=out_specs, check_vma=False)
```

```python
import functools

import jax
import jax.numpy as jnp
from jax import lax
from jax.experimental import pallas as pl
from jax.experimental.pallas import tpu as pltpu
from jax.sharding import PartitionSpec as P

HEADS = 16
HEAD = 64
BLOCK = 64


epsilon = 1e-05
highest = lax.Precision.HIGHEST


def simple_norm(values):
    return values * lax.rsqrt(jnp.mean(values * values, axis=-1, keepdims=True) + epsilon)


def norm_back(values, upstream):
    inverse_rms = lax.rsqrt(jnp.mean(values * values, axis=-1, keepdims=True) + epsilon)
    return inverse_rms * (
        upstream
        - values * (inverse_rms * inverse_rms) * jnp.mean(upstream * values, axis=-1, keepdims=True)
    )


def head_norm(values):
    shaped = values.reshape(values.shape[0], HEADS, HEAD)
    return simple_norm(shaped).reshape(values.shape)


def head_back(values, upstream):
    shaped = values.reshape(values.shape[0], HEADS, HEAD)
    coming = upstream.reshape(values.shape[0], HEADS, HEAD)
    return norm_back(shaped, coming).reshape(values.shape)


def silu_slope(values):
    logistic = jax.nn.sigmoid(values)
    return logistic * (1.0 + values * (1.0 - logistic))


def contract_rows(first_matrix, second_matrix):
    return lax.dot_general(
        first_matrix, second_matrix, (((0,), (0,)), ((), ())), preferred_element_type=jnp.float32
    )


def contract_cols(first_matrix, second_matrix):
    return lax.dot_general(
        first_matrix, second_matrix, (((1,), (1,)), ((), ())), preferred_element_type=jnp.float32
    )


def causal_table():
    return lax.broadcasted_iota(jnp.int32, (BLOCK, BLOCK), 0) >= lax.broadcasted_iota(
        jnp.int32, (BLOCK, BLOCK), 1
    )


def split_heads(values):
    return values.reshape(values.shape[0] // BLOCK, BLOCK, HEADS, HEAD)


def join_heads(values):
    return values.reshape(values.shape[0] * BLOCK, HEADS * HEAD)


AXIS_NAMES = ("f", "zh", "zl", "y", "c")
AXIS_OF = {"c": "c", "y": "y", "x": "f", "z1": "zl", "z2": "zh"}
MESH = pl.DeviceIdType.MESH
ANY = pl.BlockSpec(memory_space=pl.ANY)
FULL = pl.BlockSpec(memory_space=pltpu.VMEM)
WEIGHTS = 8
WIDTH = 256
PHASES = 5
GATHER_STEPS = (0, 3, 6, 9, 12, 15)
HEAD_GROUPS = 4
PROJECT_CHUNKS = 8
OUTPUT_CHUNKS = 2
EXPAND_CHUNKS = 11
LAYER_CHUNKS = PROJECT_CHUNKS + OUTPUT_CHUNKS + EXPAND_CHUNKS
CHUNKS = 2 * LAYER_CHUNKS
SHRINK_PARTS = 4
SHRINK_WIDTH = 128
GATHER_SLOTS = 8
LOAD_SLOTS = 3
LOW = jnp.bfloat16
WIDE = jnp.float32
ROWS = 512


def neighbours():
    dp = lax.axis_index("dp")
    x = lax.axis_index("fsdp")
    z = dp // 4
    y = (dp // 2) % 2
    c = dp % 2
    places = {"f": x, "zh": z // 2, "zl": z % 2, "y": y, "c": c}
    targets = {
        "z1": ((z + 1 - 2 * (z % 2)) * 4 + y * 2 + c, x),
        "z2": (lax.rem(z + 2, 4) * 4 + y * 2 + c, x),
        "y": (z * 4 + (1 - y) * 2 + c, x),
        "c": (z * 4 + y * 2 + (1 - c), x),
        "x": (dp, 1 - x),
    }
    return places, targets


def greet(targets):
    barrier = pltpu.get_barrier_semaphore()
    for target in targets.values():
        pl.semaphore_signal(barrier, inc=1, device_id=target, device_id_type=MESH)
    return lambda: pl.semaphore_wait(barrier, len(targets))


def dot(left, right):
    return jnp.dot(left, right, preferred_element_type=WIDE)


def softplus(values):
    return jnp.maximum(values, 0.0) + jnp.log1p(jnp.exp(-jnp.abs(values)))


def logistic(values):
    return 1.0 / (1.0 + jnp.exp(-values))


def first_lanes(rows):
    return lax.broadcasted_iota(jnp.int32, (rows, 128), 1) < HEAD


def pair_mean(values, first):
    left = jnp.sum(jnp.where(first, values, 0.0), axis=-1, keepdims=True)
    right = jnp.sum(jnp.where(first, 0.0, values), axis=-1, keepdims=True)
    return jnp.where(first, left, right) * (1.0 / HEAD)


def block_mask(rows):
    i = lax.broadcasted_iota(jnp.int32, (rows, rows), 0)
    j = lax.broadcasted_iota(jnp.int32, (rows, rows), 1)
    return (i // BLOCK == j // BLOCK) & (j <= i)


def norm_into(source, target):
    def body(t, carry):
        rows = pl.ds(pl.multiple_of(t * 128, 128), 128)
        target[rows, :] = simple_norm(source[rows, :]).astype(LOW)
        return carry

    lax.fori_loop(0, ROWS // 128, body, 0)


def local_mixer(group, parts, validity, gated, stage, attends):
    def body(turn, carry):
        t = turn // 2
        rows = pl.ds(pl.multiple_of(t * 128, 128), 128)
        pair = turn % 2
        lanes = pl.ds(pl.multiple_of(pair * 128, 128), 128)
        first = first_lanes(128)
        q = parts[0, 0, rows, lanes].astype(LOW)
        k = parts[1, 0, rows, lanes].astype(LOW)
        v = parts[0, 1, rows, lanes].astype(LOW)
        u = parts[1, 1, rows, lanes]
        keep = block_mask(128)
        mixed = []
        for head in range(2):
            mine = jnp.where(first == (head == 0), q, jnp.zeros_like(q))
            scores = contract_cols(mine, k) * HEAD ** (-0.5)
            scores = jnp.where(keep, scores, -1e30)
            highest_score = jnp.max(scores, axis=-1, keepdims=True)
            weights = jnp.exp(scores - highest_score)
            attend = (weights / jnp.sum(weights, axis=-1, keepdims=True)).astype(LOW)
            attends[turn, head] = attend
            mixed.append(dot(attend, v))
        mixture = jnp.where(first, mixed[0], mixed[1]) * validity[rows, :]
        scale = lax.rsqrt(pair_mean(mixture * mixture, first) + epsilon)
        columns = pl.ds(pl.multiple_of(group * WIDTH + pair * 128, 128), 128)
        gated[rows, columns] = (mixture * scale * (u * logistic(u))).astype(LOW)
        stage[4, rows, lanes] = mixture.astype(LOW)
        return carry

    lax.fori_loop(0, 2 * ROWS // 128, body, 0)


def linear_mixer(group, parts, gated, stage):
    half = ROWS // 2

    def body(pair, carry):
        lanes = pl.ds(pl.multiple_of(pair * 128, 128), 128)
        columns = pl.ds(pl.multiple_of(group * WIDTH + pair * 128, 128), 128)
        first = first_lanes(half)
        fk = softplus(parts[1, 0, :, lanes]).astype(LOW)
        v = parts[0, 1, :, lanes].astype(LOW)
        for t in range(2):
            rows = pl.ds(t * half, half)
            reach = (t + 1) * half
            fq = softplus(parts[0, 0, rows, lanes]).astype(LOW)
            i = lax.broadcasted_iota(jnp.int32, (half, reach), 0) + t * half
            j = lax.broadcasted_iota(jnp.int32, (half, reach), 1)
            mixed = []
            for head in range(2):
                mine = jnp.where(first == (head == 0), fq, jnp.zeros_like(fq))
                scores = jnp.where(j <= i, contract_cols(mine, fk[:reach]), 0.0).astype(LOW)
                mixed.append(dot(scores, v[:reach]))
            mixture = jnp.where(first, mixed[0], mixed[1])
            scale = lax.rsqrt(pair_mean(mixture * mixture, first) + epsilon)
            u = parts[1, 1, rows, lanes]
            gated[rows, columns] = (mixture * scale * (u * logistic(u))).astype(LOW)
            stage[4, rows, lanes] = mixture.astype(LOW)
        return carry

    lax.fori_loop(0, 2, body, 0)


def chunk_columns(weight, part):
    if weight == 0:
        return (part % 2) * 1024 + (part // 2) * WIDTH
    return part * WIDTH


class Gather:
    def __init__(self, own, held, tall, sems):
        self.own, self.held, self.tall = own, held, tall
        self.local_sem, self.send_sem, self.recv_sem, self.tall_send, self.tall_recv = sems
        self.places, self.targets = neighbours()
        self.at = tuple(self.places[name] for name in ("f", "zh", "zl", "y", "c"))

    def begin(self):
        met = greet(self.targets)
        counts = (PROJECT_CHUNKS, OUTPUT_CHUNKS, EXPAND_CHUNKS)
        for layer in range(2):
            chunk = LAYER_CHUNKS * layer
            for weight in range(3):
                for part in range(counts[weight]):
                    start = chunk_columns(weight, part)
                    pltpu.make_async_copy(
                        self.own[4 * layer + weight].at[:, pl.ds(start, WIDTH)],
                        self.held.at[(chunk,) + self.at],
                        self.local_sem.at[chunk],
                    ).start()
                    chunk += 1
            pltpu.make_async_copy(
                self.own[4 * layer + 3],
                self.tall.at[(layer,) + self.at],
                self.local_sem.at[CHUNKS + layer],
            ).start()
        met()

    def message(self, block, target, sems, place):
        return pltpu.make_async_remote_copy(
            src_ref=block,
            dst_ref=block,
            send_sem=sems[0].at[place],
            recv_sem=sems[1].at[place],
            device_id=self.targets[target],
            device_id_type=MESH,
        )

    def wide_messages(self, phase, chunk):
        x, zh, zl, y, c = self.at
        ref = self.held
        sems = (self.send_sem, self.recv_sem)
        slot = chunk % GATHER_SLOTS
        half = WIDTH // 2
        low, high = pl.ds(0, half), pl.ds(half, half)

        def one(index, target, part):
            return self.message(ref.at[(chunk,) + index], target, sems, (2 * phase + part, slot))

        a = slice(None)
        if phase == 0:
            return [one((x, zh, zl, y, c), "z2", 0)]
        if phase == 1:
            return [one((x, a, zl, y, c), "z1", 0)]
        if phase == 2:
            return [one((x, a, a, y, c, a, low), "x", 0), one((x, a, a, y, c, a, high), "y", 1)]
        if phase == 3:
            return [one((a, a, a, y, c, a, low), "y", 0), one((x, a, a, a, c, a, high), "x", 1)]
        return [one((a, a, a, a, c), "c", 0)]

    def tall_message(self, phase, layer, part, odd):
        x, zh, zl, y, c = self.at
        a = slice(None)
        lanes = pl.ds(pl.multiple_of(part * SHRINK_WIDTH, SHRINK_WIDTH), SHRINK_WIDTH)
        index, target = {
            (0, 0): ((x, zh, zl, y, c), "x"),
            (0, 1): ((x, zh, zl, y, c), "y"),
            (1, 0): ((a, zh, zl, y, c), "y"),
            (1, 1): ((x, zh, zl, a, c), "x"),
            (2, 0): ((a, zh, zl, a, c), "z2"),
            (3, 0): ((a, a, zl, a, c), "z1"),
            (4, 0): ((a, a, a, a, c), "c"),
        }[(phase, odd)]
        return self.message(
            self.tall.at[(layer,) + index + (a, lanes)],
            target,
            (self.tall_send, self.tall_recv),
            (phase, layer * SHRINK_PARTS + part),
        )

    def tall_turn(self, chunk):
        layer = chunk // LAYER_CHUNKS
        place = chunk % LAYER_CHUNKS
        return layer, place // 5, place % 5 == 4

    def for_tall(self, phase, chunk, act):
        layer, part, due = self.tall_turn(chunk)
        if phase >= 2:
            pl.when(due)(lambda: act(self.tall_message(phase, layer, part, 0)))
        else:
            for odd in range(2):
                pl.when(due & (part % 2 == odd))(
                    lambda odd=odd: act(self.tall_message(phase, layer, part, odd))
                )

    def step(self, step):
        for phase in range(PHASES, -1, -1):
            chunk = step - GATHER_STEPS[phase]

            @pl.when((chunk >= 0) & (chunk < CHUNKS))
            def _(phase=phase, chunk=chunk):
                if phase >= 1:
                    for copy in self.wide_messages(phase - 1, chunk):
                        copy.wait()
                    self.for_tall(phase - 1, chunk, lambda copy: copy.wait())
                else:
                    pltpu.make_async_copy(
                        self.own[0].at[:, pl.ds(0, WIDTH)],
                        self.held.at[(chunk,) + self.at],
                        self.local_sem.at[chunk],
                    ).wait()
                    layer = chunk // LAYER_CHUNKS

                    @pl.when(chunk % LAYER_CHUNKS == 4)
                    def _():
                        pltpu.make_async_copy(
                            self.own[3],
                            self.tall.at[(layer,) + self.at],
                            self.local_sem.at[CHUNKS + layer],
                        ).wait()

                if phase < PHASES:
                    for copy in self.wide_messages(phase, chunk):
                        copy.start()
                    self.for_tall(phase, chunk, lambda copy: copy.start())


def forward_kernel(*refs):
    own = refs[:WEIGHTS]
    tokens, validity = refs[WEIGHTS : WEIGHTS + 2]
    held, tall, mixed_out, between, middles, turns, stages, halves_out = refs[10:18]
    hidden_out, attends_out = refs[18:20]
    scratch = refs[20:]
    sems, (load_sem, tall_sem, stage_sem, half_sem, hidden_sem, misc_sem) = scratch[:5], scratch[5:11]
    loaded, shrink, x, middle, normed, gated, hidden, parts, stage, half_stage, final = scratch[11:22]
    turned, hidden_stage, attends = scratch[22:]
    gather = Gather(own, held, tall, sems)
    gather.begin()

    def rows_of(t):
        return pl.ds(pl.multiple_of(t * 128, 128), 128)

    def start_rows(t, carry):
        rows = rows_of(t)
        x[rows, :] = tokens[rows, :].astype(WIDE) * validity[rows, :]
        return carry

    def keep_turned(layer, kind):
        return pltpu.make_async_copy(turned, turns.at[layer, kind], misc_sem.at[0])

    def turn(source, layer, kind):
        def act(t, carry):
            rows = rows_of(t)
            turned[:, rows] = source[rows, :].T
            return carry

        lax.fori_loop(0, ROWS // 128, act, 0)
        keep_turned(layer, kind).start()

    def start_layers():
        lax.fori_loop(0, ROWS // 128, start_rows, 0)
        norm_into(x, normed)
        turn(normed, 0, 0)

    def load(chunk):
        return pltpu.make_async_copy(
            held.at[chunk], loaded.at[chunk % LOAD_SLOTS], load_sem.at[chunk % LOAD_SLOTS]
        )

    def load_tall(layer):
        return pltpu.make_async_copy(tall.at[layer], shrink, tall_sem)

    def keep_stage(layer, group):
        return pltpu.make_async_copy(stage, stages.at[layer, group], stage_sem)

    def keep_half(layer, part):
        return pltpu.make_async_copy(
            half_stage.at[part % 2], halves_out.at[layer, part], half_sem.at[part % 2]
        )

    def keep_hidden(layer, part):
        rows = pl.ds(pl.multiple_of(part * WIDTH, WIDTH), WIDTH)
        return pltpu.make_async_copy(
            hidden_stage.at[part % 2], hidden_out.at[layer, rows, :], hidden_sem.at[part % 2]
        )

    def keep_attends(group):
        return pltpu.make_async_copy(attends, attends_out.at[group], misc_sem.at[4])

    def keep_middle(layer):
        return pltpu.make_async_copy(middle, middles.at[layer], misc_sem.at[1])

    def keep_between():
        return pltpu.make_async_copy(x, between, misc_sem.at[2])

    def weight(slot, f):
        return loaded[slot, f].reshape(1024, WIDTH)

    def project_step(layer, place, slot):
        group = place // 2
        for f in range(2):
            parts[place % 2, f] = dot(normed[...], weight(slot, f))

        @pl.when(place % 2 == 1)
        def _():
            @pl.when((layer > 0) | (group > 0))
            def _():
                keep_stage(layer, group).wait()

            @pl.when((layer == 0) & (group > 0))
            def _():
                keep_attends(0).wait()

            for kind in range(4):
                stage[kind] = parts[kind % 2, kind // 2].astype(LOW)

            @pl.when(layer == 0)
            def _():
                local_mixer(group, parts, validity, gated, stage, attends)
                keep_attends(group).start()

            pl.when(layer > 0)(lambda: linear_mixer(group, parts, gated, stage))
            keep_stage(layer, group).start()

    def output_step(layer, part, slot):
        @pl.when(part == 0)
        def _():
            keep_turned(0, 0).wait()
            turn(gated, layer, 1)

            @pl.when(layer > 0)
            def _():
                keep_middle(0).wait()

        for f in range(2):
            lanes = pl.ds(pl.multiple_of(f * 512 + part * WIDTH, WIDTH), WIDTH)
            middle[:, lanes] = x[:, lanes] + dot(gated[...], weight(slot, f))

        @pl.when(part == OUTPUT_CHUNKS - 1)
        def _():
            keep_middle(layer).start()
            norm_into(middle, normed)
            keep_turned(0, 0).wait()
            turn(normed, layer, 2)

    def expand_step(layer, part, slot):
        @pl.when((layer > 0) | (part > 1))
        def _():
            keep_half(layer, part).wait()
            keep_hidden(layer, part).wait()

        first = dot(normed[...], weight(slot, 0))
        second = dot(normed[...], weight(slot, 1))
        half_stage[part % 2, 0] = first.astype(LOW)
        half_stage[part % 2, 1] = second.astype(LOW)
        both = (first * second).astype(LOW)
        hidden[:, pl.ds(pl.multiple_of(part * WIDTH, WIDTH), WIDTH)] = both
        hidden_stage[part % 2] = both.T
        keep_half(layer, part).start()
        keep_hidden(layer, part).start()

    def shrink_step(layer):
        load_tall(layer).wait()

        @pl.when(layer > 0)
        def _():
            keep_between().wait()

        def body(turn, carry):
            f = turn // 2
            columns = pl.ds(pl.multiple_of((turn % 2) * WIDTH, WIDTH), WIDTH)
            lanes = pl.ds(pl.multiple_of(turn * WIDTH, WIDTH), WIDTH)
            matrix = shrink[f, :, :, :, :, :, columns].reshape(hidden.shape[1], WIDTH)
            x[:, lanes] = middle[:, lanes] + dot(hidden[...], matrix)
            return carry

        lax.fori_loop(0, 4, body, 0)

        @pl.when(layer == 0)
        def _():
            keep_between().start()
            norm_into(x, normed)
            keep_turned(0, 0).wait()
            turn(normed, 1, 0)

        @pl.when(layer > 0)
        def _():
            def last_rows(t, carry):
                rows = rows_of(t)
                final[rows, :] = (x[rows, :] * validity[rows, :]).astype(LOW)
                return carry

            lax.fori_loop(0, ROWS // 128, last_rows, 0)

    def body(step, carry):
        gather.step(step)
        pl.when(step == 2)(start_layers)
        arrived = step - GATHER_STEPS[PHASES]

        @pl.when((arrived >= 0) & (arrived < CHUNKS))
        def _():
            load(arrived).start()

            @pl.when(arrived % LAYER_CHUNKS == LAYER_CHUNKS - 2)
            def _():
                load_tall(arrived // LAYER_CHUNKS).start()

        ready = arrived - 1

        @pl.when((ready >= 0) & (ready < CHUNKS))
        def _():
            load(ready).wait()
            layer = ready // LAYER_CHUNKS
            place = ready % LAYER_CHUNKS
            slot = ready % LOAD_SLOTS
            pl.when(place < PROJECT_CHUNKS)(lambda: project_step(layer, place, slot))
            pl.when((place >= PROJECT_CHUNKS) & (place < PROJECT_CHUNKS + OUTPUT_CHUNKS))(
                lambda: output_step(layer, place - PROJECT_CHUNKS, slot)
            )
            pl.when(place >= PROJECT_CHUNKS + OUTPUT_CHUNKS)(
                lambda: expand_step(layer, place - PROJECT_CHUNKS - OUTPUT_CHUNKS, slot)
            )
            pl.when(place == LAYER_CHUNKS - 1)(lambda: shrink_step(layer))

        return carry

    lax.fori_loop(0, CHUNKS + GATHER_STEPS[PHASES] + 1, body, 0)
    last = pltpu.make_async_copy(final, mixed_out, misc_sem.at[3])
    last.start()
    keep_stage(1, HEAD_GROUPS - 1).wait()
    keep_attends(0).wait()
    keep_turned(0, 0).wait()
    keep_middle(1).wait()
    keep_half(1, EXPAND_CHUNKS - 2).wait()
    keep_half(1, EXPAND_CHUNKS - 1).wait()
    keep_hidden(1, EXPAND_CHUNKS - 2).wait()
    keep_hidden(1, EXPAND_CHUNKS - 1).wait()
    last.wait()


def run_forward(shards_of, tokens, validity):
    bits = (2, 2, 2, 2, 2)
    struct = jax.ShapeDtypeStruct
    return pl.pallas_call(
        forward_kernel,
        out_shape=(
            struct((CHUNKS,) + bits + (64, WIDTH), LOW),
            struct((2,) + bits + (176, 512), LOW),
            struct((ROWS, 1024), LOW),
            struct((ROWS, 1024), WIDE),
            struct((2, ROWS, 1024), WIDE),
            struct((2, 3, 1024, ROWS), LOW),
            struct((2, HEAD_GROUPS, 5, ROWS, WIDTH), LOW),
            struct((2, EXPAND_CHUNKS, 2, ROWS, WIDTH), LOW),
            struct((2, 2816, ROWS), LOW),
            struct((HEAD_GROUPS, 8, 2, 128, 128), LOW),
        ),
        in_specs=[FULL] * (WEIGHTS + 2),
        out_specs=(ANY,) * 10,
        scratch_shapes=[
            pltpu.SemaphoreType.DMA((CHUNKS + 2,)),
            pltpu.SemaphoreType.DMA((10, GATHER_SLOTS)),
            pltpu.SemaphoreType.DMA((10, GATHER_SLOTS)),
            pltpu.SemaphoreType.DMA((PHASES, 2 * SHRINK_PARTS)),
            pltpu.SemaphoreType.DMA((PHASES, 2 * SHRINK_PARTS)),
            pltpu.SemaphoreType.DMA((LOAD_SLOTS,)),
            pltpu.SemaphoreType.DMA,
            pltpu.SemaphoreType.DMA,
            pltpu.SemaphoreType.DMA((2,)),
            pltpu.SemaphoreType.DMA((2,)),
            pltpu.SemaphoreType.DMA((5,)),
            pltpu.VMEM((LOAD_SLOTS,) + bits + (64, WIDTH), LOW),
            pltpu.VMEM(bits + (176, 512), LOW),
            pltpu.VMEM((ROWS, 1024), WIDE),
            pltpu.VMEM((ROWS, 1024), WIDE),
            pltpu.VMEM((ROWS, 1024), LOW),
            pltpu.VMEM((ROWS, 1024), LOW),
            pltpu.VMEM((ROWS, 2816), LOW),
            pltpu.VMEM((2, 2, ROWS, WIDTH), WIDE),
            pltpu.VMEM((5, ROWS, WIDTH), LOW),
            pltpu.VMEM((2, 2, ROWS, WIDTH), LOW),
            pltpu.VMEM((ROWS, 1024), LOW),
            pltpu.VMEM((1024, ROWS), LOW),
            pltpu.VMEM((2, WIDTH, ROWS), LOW),
            pltpu.VMEM((8, 2, 128, 128), LOW),
        ],
        compiler_params=pltpu.CompilerParams(
            collective_id=0, has_side_effects=True, vmem_limit_bytes=60 << 20
        ),
    )(*shards_of, tokens, validity)


SCATTER_STEPS = (0, 2, 5, 8, 11, 14)
SCATTER_SLOTS = 10
TERM_SLOTS = SCATTER_STEPS[1]
TALL_SLOTS = 3
OUTPUT_TURN = EXPAND_CHUNKS
PROJECT_TURN = EXPAND_CHUNKS + OUTPUT_CHUNKS
TALL_ROWS = 176


class Scatter:
    def __init__(self, outs, sems, wide, tall):
        self.outs, self.tall_outs = outs
        self.send_sem, self.recv_sem, self.tall_send, self.tall_recv = sems[:4]
        self.store_sem, self.tall_store = sems[4:]
        self.wide, self.tall = wide[:6], tall[:6]
        self.result, self.tall_result = wide[6], tall[6]
        self.places, self.targets = neighbours()

    def tall_turn(self, chunk):
        layer = chunk // LAYER_CHUNKS
        turn = chunk % LAYER_CHUNKS
        return layer * SHRINK_PARTS + turn // 5, turn // 5, turn % 5 == 4

    def wide_parts(self):
        half = WIDTH // 2
        return (
            (pl.ds(0, half), ("c", "y", "x", "z1", "z2")),
            (pl.ds(half, half), ("c", "x", "y", "z1", "z2")),
        )

    def tall_parts(self, odd):
        plane = ("x", "y") if odd else ("y", "x")
        return ((pl.ds(0, SHRINK_WIDTH), ("c", "z1", "z2") + plane),)

    def left(self, order, phase):
        used = set(AXIS_OF[target] for target in order[: phase + 1])
        return [name for name in AXIS_NAMES if name not in used]

    def source(self, buffers, slots, phase, order):
        if phase == 0:
            return buffers[0].at[slots[0]], list(AXIS_NAMES)
        return buffers[phase].at[slots[1]], self.left(order, phase - 1)

    def messages(self, buffers, slots, sems, phase, parts):
        if phase == 0 and len(parts) == 2:
            parts = ((pl.ds(0, WIDTH), parts[0][1]),)
        out = []
        for part, (lanes, order) in enumerate(parts):
            source, dims = self.source(buffers, slots, phase, order)
            target = order[phase]
            away = tuple(
                1 - self.places[d] if d == AXIS_OF[target] else slice(None) for d in dims
            )
            whole = tuple(slice(None) for _ in self.left(order, phase))
            place = (2 * phase + part, slots[1])
            out.append(
                pltpu.make_async_remote_copy(
                    src_ref=source.at[away + (slice(None), lanes)],
                    dst_ref=buffers[1 + phase].at[(slots[1],) + whole + (slice(None), lanes)],
                    send_sem=sems[0].at[place],
                    recv_sem=sems[1].at[place],
                    device_id=self.targets[target],
                    device_id_type=MESH,
                )
            )
        return out

    def add(self, buffers, slots, phase, parts, result):
        if phase == 0 and len(parts) == 2:
            parts = ((pl.ds(0, WIDTH), parts[0][1]),)
        for lanes, order in parts:
            source, dims = self.source(buffers, slots, phase, order)
            cut = AXIS_OF[order[phase]]
            near = tuple(self.places[d] if d == cut else slice(None) for d in dims)
            whole = tuple(slice(None) for _ in self.left(order, phase))
            ref = buffers[1 + phase].at[slots[1]]
            mine = source[near + (slice(None), lanes)]
            came = ref[whole + (slice(None), lanes)]
            if phase < 4:
                ref[whole + (slice(None), lanes)] = came + mine
            else:
                result[:, lanes] = came.astype(WIDE) + mine.astype(WIDE)

    def wide_slots(self, chunk):
        return (chunk % TERM_SLOTS, chunk % SCATTER_SLOTS)

    def tall_slots(self, place):
        return (0, place % TALL_SLOTS)

    def wide_messages(self, phase, chunk):
        return self.messages(
            self.wide,
            self.wide_slots(chunk),
            (self.send_sem, self.recv_sem),
            phase,
            self.wide_parts(),
        )

    def tall_messages(self, phase, place, odd):
        return self.messages(
            self.tall,
            self.tall_slots(place),
            (self.tall_send, self.tall_recv),
            phase,
            self.tall_parts(odd),
        )

    def store(self, chunk):
        return pltpu.make_async_copy(
            self.result.at[chunk % 2], self.outs.at[chunk], self.store_sem.at[chunk % 2]
        )

    def store_tall(self, place):
        return pltpu.make_async_copy(
            self.tall_result.at[place % 2], self.tall_outs.at[place], self.tall_store.at[place % 2]
        )

    def start(self, phase, chunk):
        for copy in self.wide_messages(phase, chunk):
            copy.start()
        place, part, due = self.tall_turn(chunk)
        for odd in range(2):

            @pl.when(due & (part % 2 == odd))
            def _(odd=odd):
                for copy in self.tall_messages(phase, place, odd):
                    copy.start()

    def take(self, phase, chunk):
        for copy in self.wide_messages(phase, chunk):
            copy.wait()
        if phase == PHASES - 1:
            pl.when(chunk >= 2)(lambda: self.store(chunk).wait())
        self.add(
            self.wide, self.wide_slots(chunk), phase, self.wide_parts(), self.result.at[chunk % 2]
        )
        place, part, due = self.tall_turn(chunk)
        for odd in range(2):

            @pl.when(due & (part % 2 == odd))
            def _(odd=odd):
                for copy in self.tall_messages(phase, place, odd):
                    copy.wait()
                if phase == PHASES - 1:
                    pl.when(place >= 2)(lambda: self.store_tall(place).wait())
                self.add(
                    self.tall,
                    self.tall_slots(place),
                    phase,
                    self.tall_parts(odd),
                    self.tall_result.at[place % 2],
                )
                if phase == PHASES - 1:
                    self.store_tall(place).start()

        if phase == PHASES - 1:
            self.store(chunk).start()

    def older(self, step):
        for phase in range(PHASES, 0, -1):
            chunk = step - SCATTER_STEPS[phase]

            @pl.when((chunk >= 0) & (chunk < CHUNKS))
            def _(phase=phase, chunk=chunk):
                self.take(phase - 1, chunk)
                if phase < PHASES:
                    self.start(phase, chunk)

    def finish(self):
        for chunk in (CHUNKS - 2, CHUNKS - 1):
            self.store(chunk).wait()
        for place in (2 * SHRINK_PARTS - 2, 2 * SHRINK_PARTS - 1):
            self.store_tall(place).wait()


def norm_slope(values, inverse, upstream, mean):
    return inverse * (upstream - values * (inverse * inverse) * mean)


def gate_back(update, mixture, coming, first):
    inverse = lax.rsqrt(pair_mean(mixture * mixture, first) + epsilon)
    curve = logistic(update)
    back_update = coming * (mixture * inverse) * (curve * (1.0 + update * (1.0 - curve)))
    gate = coming * (update * curve)
    back_mixture = norm_slope(mixture, inverse, gate, pair_mean(gate * mixture, first))
    return back_update, back_mixture


def both_heads(values, first):
    zero = jnp.zeros_like(values)
    return jnp.concatenate([jnp.where(first, values, zero), jnp.where(first, zero, values)], axis=0)


def side_by_side(values):
    half = values.shape[0] // 2
    return jnp.concatenate([values[:half], values[half:]], axis=1)


def local_mixer_back(group, stage, attends, validity, coming, back):
    def body(turn, carry):
        rows = pl.ds(pl.multiple_of((turn // 2) * 128, 128), 128)
        lanes = pl.ds(pl.multiple_of((turn % 2) * 128, 128), 128)
        columns = pl.ds(pl.multiple_of(group * WIDTH + (turn % 2) * 128, 128), 128)
        first = first_lanes(128)

        def put(i, j, value):
            start = j * WIDTH + (turn % 2) * 128
            back[i, rows, pl.ds(pl.multiple_of(start, 128), 128)] = value.astype(LOW)

        q, k, v = stage[0, rows, lanes], stage[1, rows, lanes], stage[2, rows, lanes]
        update = stage[3, rows, lanes].astype(WIDE)
        mixture = stage[4, rows, lanes].astype(WIDE)
        back_update, back_mixture = gate_back(update, mixture, coming[rows, columns], first)
        put(1, 1, back_update)
        grad = (back_mixture.astype(LOW).astype(WIDE) * validity[rows, :]).astype(LOW)
        grads = both_heads(grad, first)
        attend_low = attends[turn].reshape(256, 128)
        attend = attend_low.astype(WIDE)
        back_attend = contract_cols(grads, v)
        total = jnp.sum(back_attend * attend, axis=-1, keepdims=True)
        back_scores = (attend * (back_attend - total)).astype(LOW)
        put(0, 0, dot(side_by_side(back_scores), both_heads(k, first)) * HEAD ** (-0.5))
        put(1, 0, contract_rows(back_scores, both_heads(q, first)) * HEAD ** (-0.5))
        put(0, 1, contract_rows(attend_low, grads))
        return carry

    lax.fori_loop(0, 2 * ROWS // 128, body, 0, unroll=4)


def linear_mixer_back(group, stage, coming, back):
    half = ROWS // 2

    def body(pair, carry):
        lanes = pl.ds(pl.multiple_of(pair * 128, 128), 128)
        columns = pl.ds(pl.multiple_of(group * WIDTH + pair * 128, 128), 128)
        first = first_lanes(ROWS)
        queries = stage[0, :, lanes].astype(WIDE)
        keys_all = stage[1, :, lanes].astype(WIDE)
        v = stage[2, :, lanes]
        fq = softplus(queries).astype(LOW)
        fk = softplus(keys_all).astype(LOW)
        update = stage[3, :, lanes].astype(WIDE)
        mixture = stage[4, :, lanes].astype(WIDE)
        back_update, back_mixture = gate_back(update, mixture, coming[:, columns], first)

        def put(i, j, rows, value):
            start = j * WIDTH + pair * 128
            back[i, rows, pl.ds(pl.multiple_of(start, 128), 128)] = value.astype(LOW)

        put(1, 1, slice(None), back_update)
        grad = back_mixture.astype(LOW)
        tiles = []
        for t in range(2):
            reach = (t + 1) * half
            i = lax.broadcasted_iota(jnp.int32, (2 * half, reach), 0) % half + t * half
            j = lax.broadcasted_iota(jnp.int32, (2 * half, reach), 1)
            pair_q = both_heads(fq[t * half : reach], first[:half])
            pair_g = both_heads(grad[t * half : reach], first[:half])
            scores = jnp.where(j <= i, contract_cols(pair_q, fk[:reach]), 0.0).astype(LOW)
            inner = jnp.where(j <= i, contract_cols(pair_g, v[:reach]), 0.0).astype(LOW)
            tiles.append(
                (
                    dot(side_by_side(inner), both_heads(fk[:reach], first[:reach])),
                    contract_rows(inner, pair_q),
                    contract_rows(scores, pair_g),
                )
            )
        for t in range(2):
            rows = pl.ds(t * half, half)
            span = slice(t * half, (t + 1) * half)
            back_q = tiles[t][0]
            back_k = tiles[1][1][span]
            back_v = tiles[1][2][span]
            if t == 0:
                back_k = back_k + tiles[0][1]
                back_v = back_v + tiles[0][2]
            put(0, 0, rows, back_q * logistic(queries[span]))
            put(1, 0, rows, back_k * logistic(keys_all[span]))
            put(0, 1, rows, back_v)
        return carry

    lax.fori_loop(0, 2, body, 0)


def over_rows(act):
    def body(t, carry):
        act(pl.ds(pl.multiple_of(t * 128, 128), 128))
        return carry

    lax.fori_loop(0, ROWS // 128, body, 0)


def backward_kernel(*refs):
    cotangent, tokens, validity = refs[:3]
    held, tall, between, middles, turns, stages, halves_in, hidden_in, attends_in = refs[3:12]
    tokens_out, outs, tall_outs = refs[12:15]
    scratch = refs[15:]
    scatter_sems, loads = scratch[:6], scratch[6:12]
    load_sem, half_sem, shrink_sem, stage_sem, turn_sem, misc_sem = loads
    wide_buffers, tall_buffers = scratch[12:19], scratch[19:26]
    (
        loaded,
        half_in,
        stage,
        attends,
        shrink,
        hidden_turned,
        branch,
        gated_branch,
        up,
        sums,
        middle,
        layer_in,
        turned,
        back,
    ) = scratch[26:]
    scatter = Scatter((outs, tall_outs), scatter_sems, wide_buffers, tall_buffers)

    class Load:
        def __init__(self, chunk, number):
            self.copies = [
                pltpu.make_async_copy(
                    held.at[chunk, f],
                    loaded.at[number % 2, :, pl.ds(f * WIDTH, WIDTH)],
                    load_sem.at[number % 2, f],
                )
                for f in range(2)
            ]

        def start(self):
            for copy in self.copies:
                copy.start()

        def wait(self):
            for copy in self.copies:
                copy.wait()

    def load_turned(layer, kind, order):
        return pltpu.make_async_copy(
            turns.at[layer, kind], turned.at[order % 2], turn_sem.at[order % 2]
        )

    def load_attends(group):
        return pltpu.make_async_copy(attends_in.at[group], attends, misc_sem.at[4])

    def load_half(layer, part, number):
        return pltpu.make_async_copy(
            halves_in.at[layer, part], half_in.at[number % 2], half_sem.at[number % 2]
        )

    def load_shrink(layer, part, number):
        rows = pl.ds(pl.multiple_of(part * WIDTH, WIDTH), WIDTH)
        return pltpu.make_async_copy(
            tall.at[layer, :, rows, :], shrink.at[number % 2], shrink_sem.at[number % 2]
        )

    def load_stage(layer, group):
        return pltpu.make_async_copy(stages.at[layer, group], stage, stage_sem)

    def fetch(kind, layer):
        source, target = (
            (None, None),
            (middles, middle),
            (hidden_in, hidden_turned),
        )[kind]
        return pltpu.make_async_copy(source.at[layer], target, misc_sem.at[kind])

    def fetch_between():
        return pltpu.make_async_copy(between, layer_in, misc_sem.at[3])

    def prefetch(number):
        pl.when(number >= CHUNKS)(lambda: Load(number - CHUNKS, number).start())
        pl.when(number < CHUNKS)(lambda: prefetch_turn(number))

    def prefetch_turn(number):
        layer = 1 - number // LAYER_CHUNKS
        turn = number % LAYER_CHUNKS
        base = LAYER_CHUNKS * layer

        @pl.when(turn < OUTPUT_TURN)
        def _():
            Load(base + PROJECT_CHUNKS + OUTPUT_CHUNKS + turn, number).start()
            load_half(layer, turn, number).start()
            load_shrink(layer, turn, number).start()

        @pl.when((turn >= OUTPUT_TURN) & (turn < PROJECT_TURN))
        def _():
            Load(base + PROJECT_CHUNKS + turn - OUTPUT_TURN, number).start()

        @pl.when(turn >= PROJECT_TURN)
        def _():
            pl.when(layer == 1)(lambda: Load(base + turn - PROJECT_TURN, number).start())

            @pl.when((turn - PROJECT_TURN) % 2 == 0)
            def _():
                load_stage(layer, (turn - PROJECT_TURN) // 2).start()
                pl.when(layer == 0)(lambda: load_attends((turn - PROJECT_TURN) // 2).start())

    met = greet(scatter.targets)
    prefetch_turn(jnp.int32(0))
    load_turned(1, 2, 0).start()
    load_turned(1, 1, 1).start()
    fetch(2, 1).start()
    fetch(1, 1).start()
    fetch_between().start()

    def begin_rows(rows):
        up[rows, :] = cotangent[rows, :].astype(WIDE) * validity[rows, :]

    over_rows(begin_rows)
    met()

    def expand_start(layer):
        def act(rows):
            branch[rows, :] = up[rows, :].astype(LOW)
            sums[0, rows, :] = jnp.zeros((128, 1024), WIDE)

        over_rows(act)
        load_turned(0, 0, 1 - layer).wait()
        pl.when(layer == 0)(lambda: load_turned(0, 1, 4).start())

    def expand_turn(part, number):
        load_half(0, 0, number).wait()
        load_shrink(0, 0, number).wait()
        low, high = pl.ds(0, WIDTH), pl.ds(WIDTH, WIDTH)
        back_hidden = contract_cols(branch[:, :512], shrink[number % 2, 0])
        back_hidden = back_hidden + contract_cols(branch[:, 512:], shrink[number % 2, 1])
        first = half_in[number % 2, 0].astype(WIDE)
        second = half_in[number % 2, 1].astype(WIDE)
        back[0, 0, :, low] = (back_hidden * second).astype(LOW)
        back[0, 0, :, high] = (back_hidden * first).astype(LOW)

    def output_start(layer):
        load_turned(0, 0, 2 - layer).wait()
        load_turned(layer, 0, 3 - layer).start()
        fetch(1, 1).wait()

        def act(rows):
            values = middle[rows, :]
            back_second = sums[0, rows, :]
            new = up[rows, :] + norm_back(values, back_second)
            up[rows, :] = new
            gated_branch[rows, :] = new.astype(LOW)
            sums[1, rows, :] = jnp.zeros((128, 1024), WIDE)

        over_rows(act)

    def output_turn(part):
        for f in range(2):
            lanes = pl.ds(pl.multiple_of(f * 512 + part * WIDTH, WIDTH), WIDTH)
            back[0, 0, :, pl.ds(f * WIDTH, WIDTH)] = gated_branch[:, lanes]

    def project_start(layer):
        @pl.when(layer == 1)
        def _():
            fetch_between().wait()
            fetch(1, 0).start()
            load_turned(0, 2, 3).start()

        @pl.when(layer == 0)
        def _():
            def act(rows):
                layer_in[rows, :] = tokens[rows, :].astype(WIDE) * validity[rows, :]

            over_rows(act)

        def clear(rows):
            sums[0, rows, :] = jnp.zeros((128, 1024), WIDE)

        over_rows(clear)
        load_turned(0, 0, 1 - layer).wait()

    def project_turn(layer, group):
        load_stage(0, 0).wait()
        coming = sums.at[1]
        mine = back.at[group]
        pl.when(layer == 1)(lambda: linear_mixer_back(group, stage, coming, mine))

        @pl.when(layer == 0)
        def _():
            load_attends(0).wait()
            local_mixer_back(group, stage, attends, validity, coming, mine)

    def finish_layer(layer):
        def act(rows):
            up[rows, :] = up[rows, :] + norm_back(layer_in[rows, :], sums[0, rows, :])

        over_rows(act)

    def terms(number, group, which, order):
        slot = number % TERM_SLOTS
        out = wide_buffers[0]

        def body(tile, carry):
            rows = pl.ds(pl.multiple_of(tile * 512, 512), 512)
            value = dot(turned[order % 2, rows, :], back[group, which]).astype(LOW)
            for f in range(2):
                part = value[:, f * WIDTH : (f + 1) * WIDTH]
                out[slot, f, tile] = part.reshape(2, 2, 2, 64, WIDTH)
            return carry

        lax.fori_loop(0, 2, body, 0)

    def tall_terms(part, number):
        out = tall_buffers[0]
        pl.when(part == 0)(lambda: fetch(2, 0).wait())
        lanes = [pl.ds(pl.multiple_of(f * 512 + part * 128, 128), 128) for f in range(2)]
        both = jnp.concatenate([branch[:, lanes[0]], branch[:, lanes[1]]], axis=1)

        def body(tile, carry):
            rows = pl.ds(pl.multiple_of(tile * 8 * TALL_ROWS, 8 * TALL_ROWS), 8 * TALL_ROWS)
            value = dot(hidden_turned[rows, :], both).astype(LOW)
            for f in range(2):
                out[0, f, tile] = value[:, f * 128 : f * 128 + 128].reshape(
                    2, 2, 2, TALL_ROWS, SHRINK_WIDTH
                )
            return carry

        lax.fori_loop(0, 2, body, 0)

        @pl.when((part == SHRINK_PARTS - 1) & (number < LAYER_CHUNKS))
        def _():
            fetch(2, 0).start()

    def spread(number, group, which, kind):
        def body(t, carry):
            rows = pl.ds(pl.multiple_of(t * 512, 512), 512)
            value = contract_cols(back[group, which], loaded[number % 2, rows, :])
            sums[kind, :, rows] = sums[kind, :, rows] + value
            return carry

        lax.fori_loop(0, 2, body, 0)

    def body(step, carry):
        pl.when(step + 1 < CHUNKS + PROJECT_CHUNKS)(lambda: prefetch(step + 1))
        scatter.older(step)

        @pl.when(step < CHUNKS)
        def _():
            layer = 1 - step // LAYER_CHUNKS
            turn = step % LAYER_CHUNKS
            pl.when(turn == 0)(lambda: expand_start(layer))
            pl.when(turn == OUTPUT_TURN)(lambda: output_start(layer))
            pl.when(turn == PROJECT_TURN)(lambda: project_start(layer))
            pl.when(turn < OUTPUT_TURN)(lambda: expand_turn(turn, step))
            pl.when((turn >= OUTPUT_TURN) & (turn < PROJECT_TURN))(
                lambda: output_turn(turn - OUTPUT_TURN)
            )
            pl.when((turn >= PROJECT_TURN) & ((turn - PROJECT_TURN) % 2 == 0))(
                lambda: project_turn(layer, (turn - PROJECT_TURN) // 2)
            )
            in_project = jnp.minimum(jnp.maximum(turn - PROJECT_TURN + 1, 0), 1)
            in_output = jnp.minimum(jnp.maximum(turn - OUTPUT_TURN + 1, 0), 1) - in_project
            which = in_project * ((turn + PROJECT_TURN) % 2)
            group = in_project * ((turn - PROJECT_TURN) // 2)
            terms(step, group, which, 1 - layer + in_output)
            place, part, due = scatter.tall_turn(step)
            pl.when(due)(lambda: tall_terms(part, step))
            scatter.start(0, step)

            @pl.when((layer == 1) | (turn < PROJECT_TURN))
            def _():
                Load(0, step).wait()
                spread(step, group, which, in_output)

            pl.when(step == LAYER_CHUNKS - 1)(lambda: finish_layer(layer))

        @pl.when((step >= CHUNKS) & (step < CHUNKS + PROJECT_CHUNKS))
        def _():
            place = step - CHUNKS
            Load(0, step).wait()
            spread(step, place // 2, place % 2, 0)

            @pl.when(place == PROJECT_CHUNKS - 1)
            def _():
                finish_layer(0)

                def act(rows):
                    up[rows, :] = up[rows, :] * validity[rows, :]

                over_rows(act)
                pltpu.make_async_copy(up, tokens_out, misc_sem.at[3]).start()

        return carry

    lax.fori_loop(0, CHUNKS + SCATTER_STEPS[PHASES], body, 0)
    pltpu.make_async_copy(up, tokens_out, misc_sem.at[3]).wait()
    scatter.finish()


def scatter_buffers(terms, slots, rows, width):
    bits = [(2,) * (4 - phase) for phase in range(5)]
    return (
        [pltpu.VMEM((terms, 2, 2, 2, 2, 2, rows, width), LOW)]
        + [pltpu.VMEM((slots,) + lead + (rows, width), LOW) for lead in bits]
        + [pltpu.VMEM((2, rows, width), WIDE)]
    )


def run_backward(cotangent, tokens, validity, forward):
    struct = jax.ShapeDtypeStruct
    held, tall, mixed_out, between, middles, turns, stages, kept, hidden, attends = forward
    return pl.pallas_call(
        backward_kernel,
        out_shape=(
            struct((ROWS, 1024), WIDE),
            struct((CHUNKS, 64, WIDTH), WIDE),
            struct((2 * SHRINK_PARTS, TALL_ROWS, SHRINK_WIDTH), WIDE),
        ),
        in_specs=[FULL] * 3 + [ANY] * 9,
        out_specs=(ANY,) * 3,
        scratch_shapes=[
            pltpu.SemaphoreType.DMA((10, SCATTER_SLOTS)),
            pltpu.SemaphoreType.DMA((10, SCATTER_SLOTS)),
            pltpu.SemaphoreType.DMA((10, TALL_SLOTS)),
            pltpu.SemaphoreType.DMA((10, TALL_SLOTS)),
            pltpu.SemaphoreType.DMA((2,)),
            pltpu.SemaphoreType.DMA((2,)),
            pltpu.SemaphoreType.DMA((2, 2)),
            pltpu.SemaphoreType.DMA((2,)),
            pltpu.SemaphoreType.DMA((2,)),
            pltpu.SemaphoreType.DMA,
            pltpu.SemaphoreType.DMA((2,)),
            pltpu.SemaphoreType.DMA((5,)),
        ]
        + scatter_buffers(TERM_SLOTS, SCATTER_SLOTS, 64, WIDTH)
        + scatter_buffers(1, TALL_SLOTS, TALL_ROWS, SHRINK_WIDTH)
        + [
            pltpu.VMEM((2, 1024, 2 * WIDTH), LOW),
            pltpu.VMEM((2, 2, ROWS, WIDTH), LOW),
            pltpu.VMEM((5, ROWS, WIDTH), LOW),
            pltpu.VMEM((8, 2, 128, 128), LOW),
            pltpu.VMEM((2, 2, WIDTH, 512), LOW),
            pltpu.VMEM((2816, ROWS), LOW),
            pltpu.VMEM((ROWS, 1024), LOW),
            pltpu.VMEM((ROWS, 1024), LOW),
            pltpu.VMEM((ROWS, 1024), WIDE),
            pltpu.VMEM((2, ROWS, 1024), WIDE),
            pltpu.VMEM((ROWS, 1024), WIDE),
            pltpu.VMEM((ROWS, 1024), WIDE),
            pltpu.VMEM((2, 1024, ROWS), LOW),
            pltpu.VMEM((HEAD_GROUPS, 2, ROWS, 2 * WIDTH), LOW),
        ],
        compiler_params=pltpu.CompilerParams(
            collective_id=1, has_side_effects=True, vmem_limit_bytes=62 << 20
        ),
    )(
        cotangent,
        tokens,
        validity,
        held.reshape(CHUNKS, 2, 1024, WIDTH),
        tall.reshape(2, 2, 2816, 512),
        between,
        middles,
        turns,
        stages,
        kept,
        hidden,
        attends,
    )


def unpack_kernel(*refs):
    outs, held, sem, load_sem = refs[4 : 6 + WEIGHTS], refs[6 + WEIGHTS : -2], refs[-2], refs[-1]
    loads = [
        pltpu.make_async_copy(source, target, load_sem.at[i])
        for i, (source, target) in enumerate(zip(refs[:4], held))
    ]
    for copy in loads:
        copy.start()
    mixed_in, tokens_in, chunks, parts = held
    copies = [(mixed_in, outs[0]), (tokens_in, outs[1])]
    for order in range(2):
        layer = 1 - order
        for turn in range(LAYER_CHUNKS):
            number = order * LAYER_CHUNKS + turn
            if turn < OUTPUT_TURN:
                weight, start = 2, chunk_columns(2, turn)
            elif turn < PROJECT_TURN:
                weight, start = 1, chunk_columns(1, turn - OUTPUT_TURN)
            else:
                weight, start = 0, chunk_columns(0, turn - PROJECT_TURN)
            target = outs[2 + 4 * layer + weight].at[:, pl.ds(start, WIDTH)]
            copies.append((chunks.at[number], target))
        for part in range(SHRINK_PARTS):
            target = outs[5 + 4 * layer].at[:, pl.ds(part * SHRINK_WIDTH, SHRINK_WIDTH)]
            copies.append((parts.at[order * SHRINK_PARTS + part], target))
    copies = [
        pltpu.make_async_copy(source, target, sem.at[i])
        for i, (source, target) in enumerate(copies)
    ]
    groups = ([0], [1], range(2, len(copies)))
    for group, waited in zip(groups, (loads[:1], loads[1:2], loads[2:])):
        for copy in waited:
            copy.wait()
        for i in group:
            copies[i].start()
    for copy in copies:
        copy.wait()


def unpack(mixed_out, tokens_gradient, chunks, parts, shards_of):
    struct = jax.ShapeDtypeStruct
    count = 2 + CHUNKS + 2 * SHRINK_PARTS
    return pl.pallas_call(
        unpack_kernel,
        out_shape=(struct(mixed_out.shape, LOW), struct(tokens_gradient.shape, WIDE))
        + tuple(struct(item.shape, WIDE) for item in shards_of),
        in_specs=[ANY] * 4,
        out_specs=(ANY,) * (2 + WEIGHTS),
        scratch_shapes=[
            pltpu.VMEM(item.shape, item.dtype)
            for item in (mixed_out, tokens_gradient, chunks, parts)
        ]
        + [pltpu.SemaphoreType.DMA((count,)), pltpu.SemaphoreType.DMA((4,))],
        compiler_params=pltpu.CompilerParams(vmem_limit_bytes=60 << 20),
    )(mixed_out, tokens_gradient, chunks, parts)


def gather_weights(shards_of):
    return [
        lax.all_gather(lax.all_gather(item, "fsdp", axis=1, tiled=True), "dp", axis=0, tiled=True)
        for item in shards_of
    ]


def settle_gradients(terms):
    tall = [
        lax.psum_scatter(item.astype(jnp.bfloat16), "dp", scatter_dimension=0, tiled=True)
        for item in terms
    ]
    return [
        lax.psum_scatter(item, "fsdp", scatter_dimension=1, tiled=True).astype(jnp.float32)
        for item in tall
    ]


def local_scores(queries, keys_all):
    query_blocks = split_heads(queries.astype(jnp.bfloat16))
    key_blocks = split_heads(keys_all.astype(jnp.bfloat16))
    scores = jnp.einsum(
        "bihd,bjhd->bhij", query_blocks, key_blocks, preferred_element_type=jnp.float32
    ) * HEAD ** (-0.5)
    return (query_blocks, key_blocks, jnp.where(causal_table(), scores, -1e30))


def local_forward(queries, keys_all, values_low, validity):
    query_blocks, key_blocks, scores = local_scores(queries, keys_all)
    highest_score = jnp.max(scores, axis=-1, keepdims=True)
    expweights = jnp.exp(scores - highest_score)
    row_total = jnp.sum(expweights, axis=-1, keepdims=True)
    attend = (expweights / row_total).astype(jnp.bfloat16)
    mixture = jnp.einsum(
        "bhij,bjhd->bihd", attend, split_heads(values_low), preferred_element_type=jnp.float32
    )
    return (join_heads(mixture) * validity, highest_score + jnp.log(row_total))


def local_backward(queries, keys_all, values_low, validity, logsum, back_mixture):
    query_blocks, key_blocks, scores = local_scores(queries, keys_all)
    value_blocks = split_heads(values_low)
    coming = split_heads(back_mixture * validity.astype(jnp.bfloat16))
    attend = jnp.exp(scores - logsum)
    back_values = jnp.einsum(
        "bhij,bihd->bjhd", attend.astype(jnp.bfloat16), coming, preferred_element_type=jnp.float32
    )
    back_attend = jnp.einsum(
        "bihd,bjhd->bhij", coming, value_blocks, preferred_element_type=jnp.float32
    )
    back_scores = (
        attend * (back_attend - jnp.sum(back_attend * attend, axis=-1, keepdims=True))
    ).astype(jnp.bfloat16)
    back_queries = jnp.einsum(
        "bhij,bjhd->bihd", back_scores, key_blocks, preferred_element_type=jnp.float32
    ) * HEAD ** (-0.5)
    back_keys = jnp.einsum(
        "bhij,bihd->bjhd", back_scores, query_blocks, preferred_element_type=jnp.float32
    ) * HEAD ** (-0.5)
    return (join_heads(back_queries), join_heads(back_keys), join_heads(back_values))


def linear_parts(queries, keys_all, values_low):
    feature_q = split_heads(jax.nn.softplus(queries).astype(jnp.bfloat16))
    feature_k = split_heads(jax.nn.softplus(keys_all).astype(jnp.bfloat16))
    value_blocks = split_heads(values_low)
    causal = causal_table().astype(jnp.float32)
    inner_scores = (
        jnp.einsum("bihd,bjhd->bhij", feature_q, feature_k, preferred_element_type=jnp.float32)
        * causal
    ).astype(jnp.bfloat16)
    states = jnp.einsum(
        "bjhd,bjhe->bhde", feature_k, value_blocks, preferred_element_type=jnp.float32
    )
    running = jnp.cumsum(states, axis=0)
    prior_states = jnp.concatenate([jnp.zeros_like(states[:1]), running[:-1]], axis=0)
    return (feature_q, feature_k, value_blocks, causal, inner_scores, prior_states)


def linear_forward(queries, keys_all, values_low):
    feature_q, feature_k, value_blocks, causal, inner_scores, prior_states = linear_parts(
        queries, keys_all, values_low
    )
    mixture = jnp.einsum(
        "bhij,bjhe->bihe", inner_scores, value_blocks, preferred_element_type=jnp.float32
    )
    mixture = mixture + jnp.einsum(
        "bihd,bhde->bihe", feature_q.astype(jnp.float32), prior_states, precision=highest
    )
    return join_heads(mixture)


def linear_backward(queries, keys_all, values_low, back_mixture):
    feature_q, feature_k, value_blocks, causal, inner_scores, prior_states = linear_parts(
        queries, keys_all, values_low
    )
    coming = split_heads(back_mixture)
    coming_wide = coming.astype(jnp.float32)
    back_inner = (
        jnp.einsum("bihe,bjhe->bhij", coming, value_blocks, preferred_element_type=jnp.float32)
        * causal
    ).astype(jnp.bfloat16)
    back_feature_q = jnp.einsum(
        "bhij,bjhd->bihd", back_inner, feature_k, preferred_element_type=jnp.float32
    )
    back_feature_q = back_feature_q + jnp.einsum(
        "bihe,bhde->bihd", coming_wide, prior_states, precision=highest
    )
    back_feature_k = jnp.einsum(
        "bhij,bihd->bjhd", back_inner, feature_q, preferred_element_type=jnp.float32
    )
    back_values = jnp.einsum(
        "bhij,bihe->bjhe", inner_scores, coming, preferred_element_type=jnp.float32
    )
    back_prior = jnp.einsum(
        "bihd,bihe->bhde", feature_q.astype(jnp.float32), coming_wide, precision=highest
    )
    running = jnp.cumsum(back_prior[::-1], axis=0)[::-1]
    later_states = jnp.concatenate([running[1:], jnp.zeros_like(running[:1])], axis=0)
    back_feature_k = back_feature_k + jnp.einsum(
        "bjhe,bhde->bjhd", value_blocks.astype(jnp.float32), later_states, precision=highest
    )
    back_values = back_values + jnp.einsum(
        "bjhd,bhde->bjhe", feature_k.astype(jnp.float32), later_states, precision=highest
    )
    return (
        join_heads(back_feature_q) * jax.nn.sigmoid(queries),
        join_heads(back_feature_k) * jax.nn.sigmoid(keys_all),
        join_heads(back_values),
    )


def forward_layer(layer_in, validity, weights, local):
    project, output, expand, shrink = weights
    normed = simple_norm(layer_in).astype(jnp.bfloat16)
    projected = jnp.dot(normed, project, preferred_element_type=jnp.float32)
    queries, keys_all, values, update = jnp.split(projected, 4, axis=1)
    values_low = values.astype(jnp.bfloat16)
    if local:
        mixture, logsum = local_forward(queries, keys_all, values_low, validity)
    else:
        mixture = linear_forward(queries, keys_all, values_low)
        logsum = None
    gated_rows = (head_norm(mixture) * jax.nn.silu(update)).astype(jnp.bfloat16)
    middle = layer_in + jnp.dot(gated_rows, output, preferred_element_type=jnp.float32)
    second = simple_norm(middle).astype(jnp.bfloat16)
    expanded = jnp.dot(second, expand, preferred_element_type=jnp.float32)
    half_width = expanded.shape[1] // 2
    hidden = (expanded[:, :half_width] * expanded[:, half_width:]).astype(jnp.bfloat16)
    result = middle + jnp.dot(hidden, shrink, preferred_element_type=jnp.float32)
    return (
        result,
        (layer_in, normed, projected, values_low, mixture, logsum, gated_rows, middle, second),
    )


def backward_layer(upstream, saved, weights, validity, local):
    project, output, expand, shrink = weights
    layer_in, normed, projected, values_low, mixture, logsum, gated_rows, middle, second = saved
    expanded = jnp.dot(second, expand, preferred_element_type=jnp.float32)
    half_width = expanded.shape[1] // 2
    first_half = expanded[:, :half_width]
    second_half = expanded[:, half_width:]
    hidden = (first_half * second_half).astype(jnp.bfloat16)
    back_branch = upstream.astype(jnp.bfloat16)
    shrink_term = contract_rows(hidden, back_branch)
    back_hidden = contract_cols(back_branch, shrink)
    back_expanded = jnp.concatenate(
        [back_hidden * second_half, back_hidden * first_half], axis=1
    ).astype(jnp.bfloat16)
    expand_term = contract_rows(second, back_expanded)
    back_second = contract_cols(back_expanded, expand)
    back_middle = upstream + norm_back(middle, back_second)
    back_gated = back_middle.astype(jnp.bfloat16)
    output_term = contract_rows(gated_rows, back_gated)
    back_rows_gated = contract_cols(back_gated, output)
    queries, keys_all, unused_values, update = jnp.split(projected, 4, axis=1)
    back_update = back_rows_gated * head_norm(mixture) * silu_slope(update)
    back_mixture = head_back(mixture, back_rows_gated * jax.nn.silu(update)).astype(jnp.bfloat16)
    if local:
        back_queries, back_keys, back_values = local_backward(
            queries, keys_all, values_low, validity, logsum, back_mixture
        )
    else:
        back_queries, back_keys, back_values = linear_backward(
            queries, keys_all, values_low, back_mixture
        )
    back_projected = jnp.concatenate(
        [back_queries, back_keys, back_values, back_update], axis=1
    ).astype(jnp.bfloat16)
    project_term = contract_rows(normed, back_projected)
    back_normed = contract_cols(back_projected, project)
    back_input = back_middle + norm_back(layer_in, back_normed)
    return (back_input, (project_term, output_term, expand_term, shrink_term))


def shards(
    direct,
    tokens,
    lengths,
    local_project,
    local_output,
    local_expand,
    local_shrink,
    linear_project,
    linear_output,
    linear_expand,
    linear_shrink,
    cotangent,
):
    positions = lax.broadcasted_iota(jnp.int32, (tokens.shape[1], 1), 0)
    validity = (positions < lengths[0]).astype(jnp.float32)
    shards_of = [
        local_project,
        local_output,
        local_expand,
        local_shrink,
        linear_project,
        linear_output,
        linear_expand,
        linear_shrink,
    ]
    if direct:
        forward = run_forward(shards_of, tokens[0], validity)
        back_tokens, chunks, parts = run_backward(cotangent[0], tokens[0], validity, forward)
        outs = unpack(forward[2], back_tokens, chunks, parts, shards_of)
        return (outs[0][None], outs[1][None]) + tuple(outs[2:])
    layer_in = tokens[0].astype(jnp.float32) * validity
    whole = gather_weights(shards_of)
    local_weights = whole[:4]
    linear_weights = whole[4:]
    between, local_saved = forward_layer(layer_in, validity, local_weights, True)
    result, linear_saved = forward_layer(between, validity, linear_weights, False)
    result = (result * validity).astype(jnp.bfloat16)
    upstream = cotangent[0].astype(jnp.float32) * validity
    back_between, linear_terms = backward_layer(
        upstream, linear_saved, linear_weights, validity, False
    )
    back_input, local_terms = backward_layer(
        back_between, local_saved, local_weights, validity, True
    )
    sums = settle_gradients(local_terms + linear_terms)
    return (
        result[None],
        (back_input * validity)[None],
    ) + tuple(sums)


def solution(mesh):
    in_specs = (
        P(("dp", "fsdp"), None, None),
        P(("dp", "fsdp")),
        P("dp", "fsdp"),
        P("dp", "fsdp"),
        P("dp", "fsdp"),
        P("dp", "fsdp"),
        P("dp", "fsdp"),
        P("dp", "fsdp"),
        P("dp", "fsdp"),
        P("dp", "fsdp"),
        P(("dp", "fsdp"), None, None),
    )
    out_specs = (
        P(("dp", "fsdp"), None, None),
        P(("dp", "fsdp"), None, None),
        P("dp", "fsdp"),
        P("dp", "fsdp"),
        P("dp", "fsdp"),
        P("dp", "fsdp"),
        P("dp", "fsdp"),
        P("dp", "fsdp"),
        P("dp", "fsdp"),
        P("dp", "fsdp"),
    )
    direct = dict(mesh.shape) == {"dp": 16, "fsdp": 2}
    return jax.shard_map(functools.partial(shards, direct), mesh=mesh, in_specs=in_specs, out_specs=out_specs, check_vma=False)
```
